128 devices in a mesh: dp: 16 (over x, z), tx: 2 (over core), ty: 4 (over y).
Axes of the slice: x: 4, y: 4, z: 4, core: 2. Of those that a mesh axis runs over, the one named last changes fastest.
Arguments:
- latent: bfloat16 [16, 64, 64, 4], P('dp', 'tx', 'ty'), may hold values from -6 to 6
- condition: bfloat16 [16, 1152], P(None, ('dp', 'tx', 'ty')), may hold values from -6 to 6
- routed_ids: int32 [16, 512], P('dp'), may hold values from 0 to 1023, as said below
- embed_weight: bfloat16 [16, 1152], P(None, ('dp', 'tx', 'ty')), may hold values from -1.5 to 1.5
- embed_bias: bfloat16 [1152], P(('dp', 'tx', 'ty')), may hold values from -1.5 to 1.5
- modulation_weight: bfloat16 [2, 1152, 6912], P(None, ('dp', 'tx', 'ty')), may hold values from -0.1875 to 0.1875
- modulation_bias: bfloat16 [2, 6912], P(None, ('dp', 'tx', 'ty')), may hold values from -1.5 to 1.5
- attention_weight: bfloat16 [2, 1152, 3, 1152], P(None, ('dp', 'tx', 'ty')), may hold values from -0.1875 to 0.1875
- attention_bias: bfloat16 [2, 2304], P(None, ('dp', 'tx', 'ty')), may hold values from -1.5 to 1.5
- merge_weight: bfloat16 [2, 1152, 1152], P(None, ('dp', 'tx', 'ty')), may hold values from -0.75 to 0.75
- merge_bias: bfloat16 [2, 1152], P(None, ('dp', 'tx', 'ty')), may hold values from -1.5 to 1.5
- expand_weight: bfloat16 [2, 1152, 4608], P(None, ('dp', 'tx', 'ty')), may hold values from -0.1875 to 0.1875
- expand_bias: bfloat16 [2, 4608], P(None, ('dp', 'tx', 'ty')), may hold values from -1.5 to 1.5
- reduce_weight: bfloat16 [2, 1152, 4608], P(None, ('dp', 'tx', 'ty')), may hold values from -0.09375 to 0.09375
- reduce_bias: bfloat16 [2, 1152], P(None, ('dp', 'tx', 'ty')), may hold values from -1.5 to 1.5
- final_modulation: bfloat16 [1152, 2304], P(('dp', 'tx', 'ty')), may hold values from -0.1875 to 0.1875
- final_offsets: bfloat16 [2304], P(('dp', 'tx', 'ty')), may hold values from -1.5 to 1.5
- unpatch_weight: bfloat16 [1152, 32], P(('dp', 'tx', 'ty')), may hold values from -0.1875 to 0.1875
- unpatch_bias: bfloat16 [32], replicated, may hold values from -1.5 to 1.5
- pred_cotangent: bfloat16 [16, 64, 64, 8], P('dp', 'tx', 'ty'), may hold values from -6 to 6
Outputs:
- predicted: bfloat16 [16, 64, 64, 8], P('dp', 'tx', 'ty')
- latent_grad: float32 [16, 64, 64, 4], P('dp', 'tx', 'ty')
- condition_grad: float32 [16, 1152], P(None, ('dp', 'tx', 'ty'))
- embed_weight_grad: float32 [16, 1152], P(None, ('dp', 'tx', 'ty'))
- embed_bias_grad: float32 [1152], P(('dp', 'tx', 'ty'))
- modulation_weight_grad: float32 [2, 1152, 6912], P(None, ('dp', 'tx', 'ty'))
- modulation_bias_grad: float32 [2, 6912], P(None, ('dp', 'tx', 'ty'))
- attention_weight_grad: float32 [2, 1152, 3, 1152], P(None, ('dp', 'tx', 'ty'))
- attention_bias_grad: float32 [2, 2304], P(None, ('dp', 'tx', 'ty'))
- merge_weight_grad: float32 [2, 1152, 1152], P(None, ('dp', 'tx', 'ty'))
- merge_bias_grad: float32 [2, 1152], P(None, ('dp', 'tx', 'ty'))
- expand_weight_grad: float32 [2, 1152, 4608], P(None, ('dp', 'tx', 'ty'))
- expand_bias_grad: float32 [2, 4608], P(None, ('dp', 'tx', 'ty'))
- reduce_weight_grad: float32 [2, 1152, 4608], P(None, ('dp', 'tx', 'ty'))
- reduce_bias_grad: float32 [2, 1152], P(None, ('dp', 'tx', 'ty'))
- final_modulation_grad: float32 [1152, 2304], P(('dp', 'tx', 'ty'))
- final_offsets_grad: float32 [2304], P(('dp', 'tx', 'ty'))
- unpatch_weight_grad: float32 [1152, 32], P(('dp', 'tx', 'ty'))
- unpatch_bias_grad: float32 [32], replicated
The draws below stay inside these ranges and needn't reach their ends.
Inputs may be any that keep to these rules, and one draw needn't show every extreme that they name: `routed_ids`: each row lists 512 different token numbers of one image in rising order, token r * 32 + c sitting at patch row r and column c; of the 128 tokens of one device's tile (patch rows split over tx, columns over ty) at most 112 and at least 16 are listed, and in every image some tile holds exactly 112.
All inputs are finite; a program needn't handle non-finite values.
Results may differ from the reference program's by a relative error of at most 0.024.
Values may be sent and summed in bfloat16 or wider, within the bound.
A program may use at most 192 MiB of HBM per device.

```python
import jax
import jax.numpy as jnp
from jax import lax

D = 1152
HEADS = 16
FF = 4608
HEAD = 72
CHAN = 4
OUT_CHAN = 8
GRID = 32
IMAGES = 16
TOK_IMG = 1024
KEEP = 512
N_TX = 2
N_TY = 4


def routed_row(key):
    first_key, second_key, third_key = jax.random.split(key, 3)
    tiles = N_TX * N_TY
    size = TOK_IMG // tiles
    light = size // 8
    heavy = 7 * size // 8
    order = jax.random.permutation(first_key, tiles)
    firsts = jax.random.randint(second_key, (tiles // 2,), light, heavy + 1, dtype=jnp.int32)
    firsts = firsts.at[0].set(heavy)
    loads = jnp.zeros((tiles,), jnp.int32).at[order[0::2]].set(firsts).at[order[1::2]].set(size - firsts)
    index = jnp.arange(TOK_IMG, dtype=jnp.int32)
    rows = index // GRID
    cols = index % GRID
    tile = rows // (GRID // N_TX) * N_TY + cols // (GRID // N_TY)
    noise = jax.random.randint(third_key, (TOK_IMG,), 0, 2 ** 17, dtype=jnp.int32)
    score = (tile * 2 ** 17 + noise) * TOK_IMG + index
    ranked = jnp.argsort(score)
    rank = jnp.zeros((TOK_IMG,), jnp.int32).at[ranked].set(index) - tile * size
    keep = rank < loads[tile]
    picked = jnp.argsort(jnp.where(keep, index, index + TOK_IMG))[:KEEP]
    return picked.astype(jnp.int32)


def draw_routed_ids(key, part):
    key = jax.random.fold_in(key, 7)
    return jax.vmap(routed_row)(jax.random.split(key, IMAGES)).astype(jnp.int32)


def level_of(own_key, dims, cuts, low, largest):
    gain = 1.0
    for dim, blocks in cuts:
        steps = jax.random.uniform(jax.random.fold_in(jax.random.fold_in(own_key, 6), dim), (blocks,), jnp.float32, low / len(cuts), largest / len(cuts))
        gain = gain * jnp.repeat(jnp.exp(steps), dims[dim] // blocks).reshape((-1,) + (1,) * (len(dims) - 1 - dim))
    return gain


def normal_values(key, dims, scale, reach, cuts=(), kind=jnp.bfloat16):
    drawn = scale * jax.random.normal(key, dims, jnp.float32)
    if cuts:
        drawn = drawn * level_of(key, dims, cuts, -0.22, 0.18)
    return jnp.clip(drawn, -reach, reach).astype(kind)


def setup_inputs(seed: int = 0) -> dict:
    arg_keys = jax.random.split(jax.random.key(seed), 21)
    latent = normal_values(arg_keys[0], (IMAGES, 2 * GRID, 2 * GRID, CHAN), 1.0, 6.0, ((0, 16), (1, 2), (2, 4)))
    condition = normal_values(arg_keys[1], (IMAGES, D), 1.0, 6.0, ((1, 128),))
    routed_ids = draw_routed_ids(jax.random.fold_in(arg_keys[20], 71), 0)
    embed_weight = normal_values(arg_keys[3], (4 * CHAN, D), (4 * CHAN) ** -0.5, 1.5, ((1, 128),))
    embed_bias = normal_values(arg_keys[4], (D,), 0.3, 1.5, ((0, 128),))
    modulation_weight = normal_values(arg_keys[5], (2, D, 6 * D), D ** -0.5, 0.1875, ((1, 128),))
    modulation_bias = normal_values(arg_keys[6], (2, 6 * D), 0.3, 1.5, ((1, 128),))
    attention_weight = normal_values(arg_keys[7], (2, D, 3, D), D ** -0.5, 0.1875, ((1, 128),))
    attention_bias = normal_values(arg_keys[8], (2, 2 * D), 0.3, 1.5, ((1, 128),))
    merge_weight = normal_values(arg_keys[9], (2, D, D), (D // 16) ** -0.5, 0.75, ((1, 128),))
    merge_bias = normal_values(arg_keys[10], (2, D), 0.3, 1.5, ((1, 128),))
    expand_weight = normal_values(arg_keys[11], (2, D, FF), D ** -0.5, 0.1875, ((1, 128),))
    expand_bias = normal_values(arg_keys[12], (2, FF), 0.3, 1.5, ((1, 128),))
    reduce_weight = normal_values(arg_keys[13], (2, D, FF), FF ** -0.5, 0.09375, ((1, 128),))
    reduce_bias = normal_values(arg_keys[14], (2, D), 0.3, 1.5, ((1, 128),))
    final_modulation = normal_values(arg_keys[15], (D, 2 * D), D ** -0.5, 0.1875, ((0, 128),))
    final_offsets = normal_values(arg_keys[16], (2 * D,), 0.3, 1.5, ((0, 128),))
    unpatch_weight = normal_values(arg_keys[17], (D, 4 * OUT_CHAN), D ** -0.5, 0.1875, ((0, 128),))
    unpatch_bias = normal_values(arg_keys[18], (4 * OUT_CHAN,), 0.3, 1.5)
    pred_cotangent = normal_values(arg_keys[19], (IMAGES, 2 * GRID, 2 * GRID, OUT_CHAN), 1.0, 6.0, ((0, 16), (1, 2), (2, 4)))
    return {"latent": latent, "condition": condition, "routed_ids": routed_ids, "embed_weight": embed_weight, "embed_bias": embed_bias, "modulation_weight": modulation_weight, "modulation_bias": modulation_bias, "attention_weight": attention_weight, "attention_bias": attention_bias, "merge_weight": merge_weight, "merge_bias": merge_bias, "expand_weight": expand_weight, "expand_bias": expand_bias, "reduce_weight": reduce_weight, "reduce_bias": reduce_bias, "final_modulation": final_modulation, "final_offsets": final_offsets, "unpatch_weight": unpatch_weight, "unpatch_bias": unpatch_bias, "pred_cotangent": pred_cotangent}


@jax.custom_vjp
def low(v):
    return lax.optimization_barrier(v.astype(jnp.bfloat16)).astype(jnp.float32)

@jax.custom_vjp
def low_back(v):
    return v

def low_keep(v):
    return (low(v), None)

def low_pass(kept, grad):
    return (grad,)

def back_keep(v):
    return (v, None)

def back_low(kept, grad):
    return (low(grad),)
low.defvjp(low_keep, low_pass)
low_back.defvjp(back_keep, back_low)

def matmul(left, right):
    return jnp.dot(left, right, precision=lax.Precision.HIGHEST)

def layer_norm(value_rows):
    centered = value_rows - lax.optimization_barrier(jnp.mean(value_rows, axis=-1, keepdims=True))
    return centered * lax.rsqrt(lax.optimization_barrier(jnp.mean(centered * centered, axis=-1, keepdims=True)) + 1e-06)

def sincos_table(row_pos, col_pos, width):
    quarter = width // 4
    freqs = jnp.power(10000.0, -jnp.arange(quarter, dtype=jnp.float32) / quarter)
    row_angle = row_pos[:, None] * freqs[None, :]
    col_angle = col_pos[:, None] * freqs[None, :]
    row_embed = jnp.concatenate([jnp.sin(row_angle), jnp.cos(row_angle)], axis=-1)
    col_embed = jnp.concatenate([jnp.sin(col_angle), jnp.cos(col_angle)], axis=-1)
    row_full = jnp.broadcast_to(row_embed[:, None, :], (row_pos.shape[0], col_pos.shape[0], width // 2))
    col_full = jnp.broadcast_to(col_embed[None, :, :], (row_pos.shape[0], col_pos.shape[0], width // 2))
    return jnp.concatenate([row_full, col_full], axis=-1).reshape(row_pos.shape[0] * col_pos.shape[0], width)

def diffusion_block(value_rows, condition_activated, layer_params):
    mod_w, mod_b, attn_w, attn_b, merge_w, merge_b, expand_w, expand_b, reduce_w, reduce_b = layer_params
    count = value_rows.shape[0]
    mod = low_back(matmul(condition_activated, mod_w) + mod_b)
    shift1 = mod[0:D]
    scale1 = mod[D:2 * D]
    gate1 = mod[2 * D:3 * D]
    shift2 = mod[3 * D:4 * D]
    scale2 = mod[4 * D:5 * D]
    gate2 = mod[5 * D:6 * D]
    normed1 = low(layer_norm(value_rows) * (1.0 + scale1) + shift1)
    joined = jnp.einsum('td,dke->tke', normed1, attn_w, precision=lax.Precision.HIGHEST)
    query = low(low_back(joined[:, 0] + attn_b[:D]))
    keys = low(low_back(joined[:, 1]))
    vals = low(low_back(joined[:, 2] + attn_b[D:]))
    q_heads = query.reshape(count, HEADS, HEAD)
    k_heads = keys.reshape(count, HEADS, HEAD)
    v_heads = vals.reshape(count, HEADS, HEAD)
    scores = jnp.einsum('qhe,khe->hqk', q_heads, k_heads, precision=lax.Precision.HIGHEST) * HEAD ** (-0.5)
    scores = low_back(scores)
    shifted = jnp.exp(scores - lax.optimization_barrier(jnp.max(scores, axis=-1, keepdims=True)))
    probs = low(shifted / lax.optimization_barrier(jnp.sum(shifted, axis=-1, keepdims=True)))
    attended = jnp.einsum('hqk,khe->qhe', probs, v_heads, precision=lax.Precision.HIGHEST).reshape(count, D)
    attended = low(low_back(attended))
    branch = low_back(matmul(attended, merge_w.T) + merge_b)
    middle = value_rows + gate1 * branch
    normed2 = low(layer_norm(middle) * (1.0 + scale2) + shift2)
    pre = low_back(matmul(normed2, expand_w) + expand_b)
    hidden = low(jax.nn.gelu(pre, approximate=True))
    mlp = low_back(matmul(hidden, reduce_w.T) + reduce_b)
    return middle + gate2 * mlp

def one_image(pixels, cond, picks, weights):
    embed_w, embed_b, mod_w, mod_b, attn_w, attn_b, merge_w, merge_b, expand_w, expand_b, reduce_w, reduce_b, head_mod_w, head_mod_b, unpatch_w, unpatch_b = weights
    patches = pixels.reshape(GRID, 2, GRID, 2, CHAN).transpose(0, 2, 1, 3, 4).reshape(TOK_IMG, 4 * CHAN)
    condition_activated = low(jax.nn.silu(cond))
    grid_pos = jnp.arange(GRID, dtype=jnp.float32)
    initial_tokens = low_back(matmul(patches, embed_w) + embed_b) + sincos_table(grid_pos, grid_pos, D)
    stacked_groups = (mod_w, mod_b, attn_w, attn_b, merge_w, merge_b, expand_w, expand_b, reduce_w, reduce_b)
    leading_block = diffusion_block(initial_tokens, condition_activated, tuple((stack_arrays[0] for stack_arrays in stacked_groups)))
    selected_rows = leading_block[picks]
    trailing_block = diffusion_block(selected_rows, condition_activated, tuple((stack_arrays[1] for stack_arrays in stacked_groups)))
    ended = leading_block.at[picks].set(trailing_block)
    head_mod = low_back(matmul(condition_activated, head_mod_w) + head_mod_b)
    normed = low(layer_norm(ended) * (1.0 + head_mod[D:]) + head_mod[:D])
    outputs = matmul(normed, unpatch_w) + unpatch_b
    return outputs.reshape(GRID, GRID, 2, 2, OUT_CHAN).transpose(0, 2, 1, 3, 4).reshape(2 * GRID, 2 * GRID, OUT_CHAN)

def reference(latent, condition, routed_ids, embed_weight, embed_bias, modulation_weight, modulation_bias, attention_weight, attention_bias, merge_weight, merge_bias, expand_weight, expand_bias, reduce_weight, reduce_bias, final_modulation, final_offsets, unpatch_weight, unpatch_bias, pred_cotangent):
    weights = tuple((weight.astype(jnp.float32) for weight in (embed_weight, embed_bias, modulation_weight, modulation_bias, attention_weight, attention_bias, merge_weight, merge_bias, expand_weight, expand_bias, reduce_weight, reduce_bias, final_modulation, final_offsets, unpatch_weight, unpatch_bias)))

    def forward(pixels, conds, *weights_f):

        def per_image(entry):
            return one_image(entry[0], entry[1], entry[2], weights_f)
        return lax.map(jax.checkpoint(per_image), (pixels, conds, routed_ids))
    preds, pullback = jax.vjp(forward, latent.astype(jnp.float32), condition.astype(jnp.float32), *weights)
    grads = pullback(pred_cotangent.astype(jnp.float32))
    return (preds.astype(jnp.bfloat16), grads[0], grads[1], grads[2], grads[3], grads[4], grads[5], grads[6], grads[7], grads[8], grads[9], grads[10], grads[11], grads[12], grads[13], grads[14], grads[15], grads[16], grads[17])
```

```python
import functools

import jax
import jax.numpy as jnp
from jax import lax
from jax.experimental import pallas as pl
from jax.experimental.pallas import tpu as pltpu
from jax.sharding import Mesh
from jax.sharding import PartitionSpec as P

D = 1152
HEADS = 16
FF = 4608
HW = D // 8
FW = FF // 8
DP = ("dp_0", "dp_1")
DP_TX_TY = ("dp_0", "dp_1", "tx", "ty")
MESH = pl.DeviceIdType.MESH
VMEM = pl.BlockSpec(memory_space=pltpu.VMEM)
F32 = jnp.float32
BF16 = jnp.bfloat16
ATT_COLS = 640
FFN_COLS = 2 * FW
ALL_COLS = 2 * (ATT_COLS + FFN_COLS)
PIECE = 512
PIECES = ALL_COLS // PIECE
MOD_ALL = 14 * D
SMALL_IN = (16 * 9, 9, 9 * 32, 2 * 18, 2 * 9, 2 * 36, 2 * 9)


def enter(peers):
    barrier = pltpu.get_barrier_semaphore()
    for peer in peers:
        pl.semaphore_signal(barrier, inc=1, device_id=peer, device_id_type=MESH)
    pl.semaphore_wait(barrier, len(peers))


def send(src, dst, sems, k, peer):
    copy = pltpu.make_async_remote_copy(
        src_ref=src,
        dst_ref=dst,
        send_sem=sems[0].at[k],
        recv_sem=sems[1].at[k],
        device_id=peer,
        device_id_type=MESH,
    )
    copy.start()
    return copy


def group_peers():
    c, y = lax.axis_index("tx"), lax.axis_index("ty")
    found = []
    for dc in range(2):
        for dy in range(4):
            if dc or dy:
                oc, oy = lax.rem(c + dc, 2), lax.rem(y + dy, 4)
                found.append(({"tx": oc, "ty": oy}, oc * 4 + oy))
    return found


def image_peers():
    x, z = lax.axis_index("dp_0"), lax.axis_index("dp_1")
    found = []
    for dx in range(4):
        for dz in range(4):
            if dx or dz:
                ox, oz = lax.rem(x + dx, 4), lax.rem(z + dz, 4)
                found.append(({"dp_0": ox, "dp_1": oz}, ox * 4 + oz))
    return found


def own_group():
    return lax.axis_index("tx") * 4 + lax.axis_index("ty")


def own_image():
    return lax.axis_index("dp_0") * 4 + lax.axis_index("dp_1")


def dma_sems(n):
    return [pltpu.SemaphoreType.DMA((n,)), pltpu.SemaphoreType.DMA((n,))]


def collective(kernel, cid, outs, scratch, *operands, vmem=48 << 20):
    return pl.pallas_call(
        kernel,
        out_shape=outs,
        in_specs=[VMEM] * len(operands),
        out_specs=jax.tree.map(lambda _: VMEM, outs),
        scratch_shapes=scratch,
        compiler_params=pltpu.CompilerParams(
            collective_id=cid, has_side_effects=True, vmem_limit_bytes=vmem
        ),
    )(*operands)


def ring_peers():
    c, y = lax.axis_index("tx"), lax.axis_index("ty")
    return (
        {"tx": 1 - c},
        {"ty": lax.rem(y + 1, 4)},
        {"ty": lax.rem(y + 3, 4)},
        {"ty": lax.rem(y + 2, 4)},
    )


def gather_kernel(x_ref, o_ref, ss, rs):
    tokens = x_ref.shape[0]
    half = (tokens // 2 + 15) // 16 * 16
    c, y = lax.axis_index("tx"), lax.axis_index("ty")
    sib, up, down, _ = ring_peers()
    enter([sib, up, down])
    sems = (ss, rs)
    me = c * 4 + y
    above, below, across = (c * 4 + lax.rem(y + k, 4) for k in (1, 3, 2))
    a1 = send(x_ref.at[0:half], o_ref.at[me, 0:half], sems, 0, up)
    b1 = send(x_ref.at[half:tokens], o_ref.at[me, half:tokens], sems, 1, down)
    a2 = send(x_ref.at[half:tokens], o_ref.at[me, half:tokens], sems, 2, up)
    b2 = send(x_ref.at[0:half], o_ref.at[me, 0:half], sems, 3, down)
    s0 = send(x_ref, o_ref.at[me], sems, 4, sib)
    o_ref[me] = x_ref[...]
    a1.wait_recv()
    f1 = send(o_ref.at[below, 0:half], o_ref.at[below, 0:half], sems, 5, up)
    b1.wait_recv()
    f2 = send(o_ref.at[above, half:tokens], o_ref.at[above, half:tokens], sems, 6, down)
    a2.wait_recv()
    s1 = send(o_ref.at[below], o_ref.at[below], sems, 7, sib)
    b2.wait_recv()
    s2 = send(o_ref.at[above], o_ref.at[above], sems, 8, sib)
    f1.wait_recv()
    f2.wait_recv()
    s3 = send(o_ref.at[across], o_ref.at[across], sems, 9, sib)
    for copy in (s0, s1, s2, s3):
        copy.wait()
    for copy in (a1, a2, b1, b2, f1, f2):
        copy.wait_send()


def sum_kernel(x_ref, o_ref, sib_buf, mine, got, ss, rs):
    c, y = lax.axis_index("tx"), lax.axis_index("ty")
    sib, up, down, far = ring_peers()
    enter([sib, up, down, far])
    sems = (ss, rs)
    to = {1: up, 2: far, 3: down}
    order = (2, 1, 3, 0)
    swaps = [
        send(x_ref.at[(1 - c) * 4 + lax.rem(y + d, 4)], sib_buf.at[d], sems, d, sib) for d in order
    ]
    sends = {}
    for d, swap in zip(order, swaps):
        swap.wait_recv()
        total = x_ref[c * 4 + lax.rem(y + d, 4)].astype(F32) + sib_buf[d].astype(F32)
        if d:
            mine[d] = total.astype(BF16)
            sends[d] = send(mine.at[d], got.at[d], sems, 3 + d, to[d])
        else:
            o_ref[...] = total
    for d in (1, 3, 2):
        sends[d].wait_recv()
        o_ref[...] = o_ref[...] + got[d].astype(F32)
    for d in (1, 3, 2):
        sends[d].wait_send()
    for swap in swaps:
        swap.wait_send()


def gather_image(rows16, cid):
    tokens = rows16.shape[1]
    out = jax.ShapeDtypeStruct((8, tokens, D), BF16)
    parts = collective(gather_kernel, cid, out, dma_sems(10), rows16[0])
    return parts.reshape(1, 8 * tokens, D)


def sum_image(partial_value, cid):
    tokens = partial_value.shape[1] // 8
    out = jax.ShapeDtypeStruct((tokens, D), F32)
    scratch = [pltpu.VMEM((4, tokens, D), BF16)] * 3 + dma_sems(8)
    parts = partial_value.astype(BF16).reshape(8, tokens, D)
    return collective(sum_kernel, cid, out, scratch, parts)[None]


def spread_kernel(w_ref, m_ref, s_ref, w_out, m_out, s_out, m_got, m_two, ss, rs):
    group, image = group_peers(), image_peers()
    enter([peer for peer, _ in group + image])
    sems = (ss, rs)
    me, mine = own_group(), own_image()
    first = []
    for k, (peer, at) in enumerate(image):
        first.append(send(m_ref.at[at], m_got.at[mine], sems, k, peer))
        first.append(send(s_ref, s_out.at[me, mine], sems, 15 + k, peer))
    weights = [send(w_ref.at[at], w_out.at[me], sems, 30 + k, p) for k, (p, at) in enumerate(group)]
    w_out[me] = w_ref[me]
    s_out[me, mine] = s_ref[...]
    m_got[mine] = m_ref[mine]
    for copy in first:
        copy.wait_recv()
    total = m_got[0]
    for k in range(1, 16):
        total = total + m_got[k]
    m_two[me] = total
    second = []
    for k, (peer, _) in enumerate(group):
        second.append(send(m_two.at[me], m_two.at[me], sems, 37 + k, peer))
        second.append(send(s_out.at[me], s_out.at[me], sems, 44 + k, peer))
    for copy in second:
        copy.wait_recv()
    total = m_two[0]
    for k in range(1, 8):
        total = total + m_two[k]
    m_out[...] = total
    for copy in weights:
        copy.wait_recv()
    for copy in first + second + weights:
        copy.wait_send()


def spread(weights, mods, small):
    outs = (
        jax.ShapeDtypeStruct(weights.shape, BF16),
        jax.ShapeDtypeStruct((128, 128), F32),
        jax.ShapeDtypeStruct((8, 16, *small.shape), BF16),
    )
    scratch = [pltpu.VMEM((16, 128, 128), F32), pltpu.VMEM((8, 128, 128), F32)] + dma_sems(51)
    return collective(spread_kernel, 1, outs, scratch, weights, mods, small)


def fetch_kernel(w_ref, o_ref, ss, rs):
    image = image_peers()
    enter([peer for peer, _ in image])
    mine = own_image()
    copies = [
        send(w_ref, o_ref.at[mine], (ss, rs), k, peer) for k, (peer, _) in enumerate(image)
    ]
    o_ref[mine] = w_ref[...]
    for copy in copies:
        copy.wait()


def fetch_rows(rows, cid):
    padded = jnp.pad(rows, [(0, 8), (0, 0)])
    out = jax.ShapeDtypeStruct((16, *padded.shape), BF16)
    slabs = collective(fetch_kernel, cid, out, dma_sems(15), padded)
    return slabs[:, :72].reshape(D, rows.shape[1])


def reduce_kernel(g_ref, o_ref, got, ss, rs):
    image = image_peers()
    enter([peer for peer, _ in image])
    mine = own_image()
    copies = [
        send(g_ref.at[at], got.at[mine], (ss, rs), k, peer) for k, (peer, at) in enumerate(image)
    ]
    got[mine] = g_ref[mine]
    for copy in copies:
        copy.wait_recv()

    @pl.loop(0, g_ref.shape[1] // 16)
    def _(piece):
        rows = pl.ds(pl.multiple_of(piece * 16, 16), 16)
        total = got[0, rows, :].astype(F32)
        for k in range(1, 16):
            total = total + got[k, rows, :].astype(F32)
        o_ref[rows, :] = total.astype(BF16)

    for copy in copies:
        copy.wait_send()


def reduce_rows(grads, cid):
    slabs = jnp.pad(grads.reshape(16, 72, -1), [(0, 0), (0, 8), (0, 0)])
    out = jax.ShapeDtypeStruct(slabs.shape[1:], BF16)
    scratch = [pltpu.VMEM(slabs.shape, BF16)] + dma_sems(15)
    return collective(reduce_kernel, cid, out, scratch, slabs)[:72]


def finish_kernel(g_ref, m_ref, s_ref, g_out, m_out, s_out, m_got, s_got, s_mine, s_two, ss, rs):
    group, image = group_peers(), image_peers()
    enter([peer for peer, _ in group + image])
    sems = (ss, rs)
    me, mine = own_group(), own_image()
    first = [send(m_ref.at[at], m_got.at[me], sems, k, p) for k, (p, at) in enumerate(group)]
    small = [send(s_ref.at[at], s_got.at[mine], sems, 7 + k, p) for k, (p, at) in enumerate(image)]
    weights = [send(g_ref.at[at], g_out.at[me], sems, 22 + k, p) for k, (p, at) in enumerate(group)]
    m_got[me] = m_ref[me]
    s_got[mine] = s_ref[mine]
    g_out[me] = g_ref[me]
    for copy in first:
        copy.wait_recv()
    total = m_got[0]
    for k in range(1, 8):
        total = total + m_got[k]
    m_out[me, mine] = total.astype(BF16)
    second = [
        send(m_out.at[me, mine], m_out.at[me, mine], sems, 29 + k, p)
        for k, (p, _) in enumerate(image)
    ]
    for copy in small:
        copy.wait_recv()
    total = s_got[0]
    for k in range(1, 16):
        total = total + s_got[k]
    s_mine[...] = total
    pieces = [send(s_mine.at[at], s_two.at[me], sems, 44 + k, p) for k, (p, at) in enumerate(group)]
    s_two[me] = s_mine[me]
    for copy in second:
        copy.wait_recv()
    third = [send(m_out.at[me], m_out.at[me], sems, 51 + k, p) for k, (p, _) in enumerate(group)]
    for copy in pieces:
        copy.wait_recv()
    total = s_two[0]
    for k in range(1, 8):
        total = total + s_two[k]
    s_out[...] = total
    for copy in weights + third:
        copy.wait_recv()
    for copy in first + small + weights + second + pieces + third:
        copy.wait_send()


def finish(grads, mods, small):
    outs = (
        jax.ShapeDtypeStruct(grads.shape, BF16),
        jax.ShapeDtypeStruct((8, 16, 16, 128), BF16),
        jax.ShapeDtypeStruct((8, 128), F32),
    )
    scratch = [
        pltpu.VMEM((8, 16, 128), F32),
        pltpu.VMEM((16, 8, 8, 128), F32),
        pltpu.VMEM((8, 8, 128), F32),
        pltpu.VMEM((8, 8, 128), F32),
    ] + dma_sems(58)
    return collective(finish_kernel, 2, outs, scratch, grads, mods, small)


def layer_stats(value_rows):
    centered = value_rows - jnp.mean(value_rows, axis=-1, keepdims=True)
    inv_std = lax.rsqrt(jnp.mean(centered * centered, axis=-1, keepdims=True) + 1e-06)
    return (centered * inv_std, inv_std)


def layer_back(upstream, normed, inv_std):
    return inv_std * (
        upstream
        - jnp.mean(upstream, axis=-1, keepdims=True)
        - normed * jnp.mean(upstream * normed, axis=-1, keepdims=True)
    )


def smooth_gate(value_rows):
    return jax.nn.gelu(value_rows, approximate=True)


def sincos_table(row_pos, col_pos, width):
    quarter = width // 4
    freqs = jnp.power(10000.0, -jnp.arange(quarter, dtype=jnp.float32) / quarter)
    row_angle = row_pos[:, None] * freqs[None, :]
    col_angle = col_pos[:, None] * freqs[None, :]
    row_embed = jnp.concatenate([jnp.sin(row_angle), jnp.cos(row_angle)], axis=-1)
    col_embed = jnp.concatenate([jnp.sin(col_angle), jnp.cos(col_angle)], axis=-1)
    row_full = jnp.broadcast_to(
        row_embed[:, None, :], (row_pos.shape[0], col_pos.shape[0], width // 2)
    )
    col_full = jnp.broadcast_to(
        col_embed[None, :, :], (row_pos.shape[0], col_pos.shape[0], width // 2)
    )
    return jnp.concatenate([row_full, col_full], axis=-1).reshape(
        row_pos.shape[0] * col_pos.shape[0], width
    )


def to_patches(pixels):
    count, height, breadth, depth = pixels.shape
    shaped = pixels.reshape(count, height // 2, 2, breadth // 2, 2, depth)
    return shaped.transpose(0, 1, 3, 2, 4, 5).reshape(
        count, height // 2 * (breadth // 2), 4 * depth
    )


def from_patches(token_rows, tile_rows, tile_cols):
    count = token_rows.shape[0]
    depth = token_rows.shape[2] // 4
    shaped = token_rows.reshape(count, tile_rows, tile_cols, 2, 2, depth)
    return shaped.transpose(0, 1, 3, 2, 4, 5).reshape(count, 2 * tile_rows, 2 * tile_cols, depth)


def split_mod(mod, width):
    return [mod[:, None, piece * width : (piece + 1) * width] for piece in range(6)]


def compact_plan(routed, capacity):
    count, tokens = routed.shape
    flags = routed > 0
    position = jnp.cumsum(flags.astype(jnp.int32), axis=1) - 1
    slots = jnp.where(flags, position, capacity)
    batch_index = jnp.broadcast_to(jnp.arange(count, dtype=jnp.int32)[:, None], (count, tokens))
    token_ids = jnp.arange(tokens, dtype=jnp.int32)[None, :]
    owner = (
        jnp.zeros((count, capacity), jnp.int32).at[batch_index, slots].set(token_ids, mode="drop")
    )
    filled = jnp.sum(flags.astype(jnp.int32), axis=1, keepdims=True)
    valid = (jnp.arange(capacity, dtype=jnp.int32)[None, :] < filled).astype(jnp.float32)
    return (jnp.where(flags, position, 0), owner, valid)


def pick_rows(value_rows, index):
    return jax.vmap(lambda table, where: jnp.take(table, where, axis=0))(value_rows, index)


def score_block(query, keys, key_marks, heads, scale):
    count, rows, width = query.shape
    size = width // heads
    q_heads = query.reshape(count, rows, heads, size)
    k_heads = keys.reshape(count, keys.shape[1], heads, size)
    scores = (
        jnp.einsum("bqhe,bkhe->bhqk", q_heads, k_heads, preferred_element_type=jnp.float32) * scale
    )
    return jnp.where(key_marks[:, None, None, :] > 0, scores, -1e30)


def attend(query, keys, vals, key_marks, heads, scale):
    count, rows, width = query.shape
    size = width // heads
    scores = score_block(query, keys, key_marks, heads, scale)
    highest = jnp.max(scores, axis=-1, keepdims=True)
    shifted = jnp.exp(scores - highest)
    summed = jnp.sum(shifted, axis=-1, keepdims=True)
    probs16 = (shifted / summed).astype(jnp.bfloat16)
    log_sum = highest + jnp.log(summed)
    v_heads = vals.reshape(count, vals.shape[1], heads, size)
    attended = jnp.einsum("bhqk,bkhe->bqhe", probs16, v_heads, preferred_element_type=jnp.float32)
    return (attended.reshape(count, rows, width).astype(jnp.bfloat16), log_sum)


def attend_back(query, keys, vals, key_marks, log_sum, attended_grad16, heads, scale):
    count, rows, width = query.shape
    size = width // heads
    key_count = keys.shape[1]
    scores = score_block(query, keys, key_marks, heads, scale)
    probs = jnp.exp(scores - log_sum)
    probs16 = probs.astype(jnp.bfloat16)
    grad_heads = attended_grad16.reshape(count, rows, heads, size)
    v_heads = vals.reshape(count, key_count, heads, size)
    k_heads = keys.reshape(count, key_count, heads, size)
    q_heads = query.reshape(count, rows, heads, size)
    grad_probs = jnp.einsum(
        "bqhe,bkhe->bhqk", grad_heads, v_heads, preferred_element_type=jnp.float32
    )
    grad_values = jnp.einsum(
        "bhqk,bqhe->bkhe", probs16, grad_heads, preferred_element_type=jnp.float32
    )
    weighted = jnp.sum(probs * grad_probs, axis=-1, keepdims=True)
    score_grad16 = (probs * (grad_probs - weighted)).astype(jnp.bfloat16)
    grad_query = (
        jnp.einsum("bhqk,bkhe->bqhe", score_grad16, k_heads, preferred_element_type=jnp.float32)
        * scale
    )
    grad_keys = (
        jnp.einsum("bhqk,bqhe->bkhe", score_grad16, q_heads, preferred_element_type=jnp.float32)
        * scale
    )
    return (
        grad_query.reshape(count, rows, width),
        grad_keys.reshape(count, key_count, width),
        grad_values.reshape(count, key_count, width),
    )


def spread_forward(value_rows, mod, params, biases, marks_all, scale, cid):
    attn_p, merge_p, expand_p, reduce_p = params
    attn_b, merge_b, expand_b, reduce_b = biases
    width = value_rows.shape[2]
    head_width = attn_p.shape[2]
    hidden_width = expand_p.shape[1]
    heads = head_width // (D // HEADS)
    group = lax.axis_index(("tx", "ty"))
    shift1, scale1, gate1, shift2, scale2, gate2 = split_mod(mod, width)
    normed1, inv_one = layer_stats(value_rows)
    input16 = (normed1 * (1.0 + scale1) + shift1).astype(jnp.bfloat16)
    input_all = gather_image(input16, cid + 0)
    joined = jnp.einsum("btd,dke->btke", input_all, attn_p, preferred_element_type=jnp.float32)
    q_bias = lax.dynamic_slice_in_dim(attn_b, group * head_width, head_width).astype(jnp.float32)
    v_bias = lax.dynamic_slice_in_dim(attn_b, width + group * head_width, head_width).astype(
        jnp.float32
    )
    query = (joined[:, :, 0] + q_bias).astype(jnp.bfloat16)
    keys = joined[:, :, 1].astype(jnp.bfloat16)
    vals = (joined[:, :, 2] + v_bias).astype(jnp.bfloat16)
    attended, log_sum = attend(query, keys, vals, marks_all, heads, scale)
    branch = sum_image(
        jnp.einsum("bth,dh->btd", attended, merge_p, preferred_element_type=jnp.float32),
        cid + 2,
    )
    branch = branch + merge_b.astype(jnp.float32)
    middle = value_rows + gate1 * branch
    normed2, inv_two = layer_stats(middle)
    second16 = (normed2 * (1.0 + scale2) + shift2).astype(jnp.bfloat16)
    second_all = gather_image(second16, cid + 1)
    e_bias = lax.dynamic_slice_in_dim(expand_b, group * hidden_width, hidden_width).astype(
        jnp.float32
    )
    pre = (
        jnp.einsum("btd,df->btf", second_all, expand_p, preferred_element_type=jnp.float32)
        + e_bias
    )
    hidden16 = smooth_gate(pre).astype(jnp.bfloat16)
    mlp = sum_image(
        jnp.einsum("btf,df->btd", hidden16, reduce_p, preferred_element_type=jnp.float32),
        cid + 3,
    )
    mlp = mlp + reduce_b.astype(jnp.float32)
    output = middle + gate2 * mlp
    saved = (
        normed1,
        inv_one,
        input_all,
        query,
        keys,
        vals,
        marks_all,
        log_sum,
        attended,
        branch,
        normed2,
        inv_two,
        second_all,
        pre,
        hidden16,
        mlp,
    )
    return (output, saved)


def spread_backward(upstream, saved, mod, params, marks, scale, cid):
    attn_p, merge_p, expand_p, reduce_p = params
    (
        normed1,
        inv_one,
        input_all,
        query,
        keys,
        vals,
        marks_all,
        log_sum,
        attended,
        branch,
        normed2,
        inv_two,
        second_all,
        pre,
        hidden16,
        mlp,
    ) = saved
    width = upstream.shape[2]
    head_width = attn_p.shape[2]
    hidden_width = expand_p.shape[1]
    heads = head_width // (D // HEADS)
    group = lax.axis_index(("tx", "ty"))
    shift1, scale1, gate1, shift2, scale2, gate2 = split_mod(mod, width)
    grad_out = upstream * marks[:, :, None]
    grad_gate2 = jnp.sum(grad_out * mlp, axis=1)
    mlp_grad16 = (grad_out * gate2).astype(jnp.bfloat16)
    grad_reduce_b = jnp.sum(mlp_grad16.astype(jnp.float32), axis=(0, 1))
    mlp_grad_all = gather_image(mlp_grad16, cid + 4)
    grad_reduce_p = jnp.einsum(
        "btd,btf->df", mlp_grad_all, hidden16, preferred_element_type=jnp.float32
    )
    grad_hidden = jnp.einsum(
        "btd,df->btf", mlp_grad_all, reduce_p, preferred_element_type=jnp.float32
    )
    gate_value, gate_pull = jax.vjp(smooth_gate, pre)
    pre_grad16 = gate_pull(grad_hidden)[0].astype(jnp.bfloat16)
    grad_expand_p = jnp.einsum(
        "btd,btf->df", second_all, pre_grad16, preferred_element_type=jnp.float32
    )
    grad_expand_b = lax.dynamic_update_slice_in_dim(
        jnp.zeros((FF,), jnp.float32),
        jnp.sum(pre_grad16.astype(jnp.float32), axis=(0, 1)),
        group * hidden_width,
        0,
    )
    grad_second = sum_image(
        jnp.einsum("btf,df->btd", pre_grad16, expand_p, preferred_element_type=jnp.float32),
        cid + 5,
    )
    grad_shift2 = jnp.sum(grad_second, axis=1)
    grad_scale2 = jnp.sum(grad_second * normed2, axis=1)
    grad_middle = grad_out + layer_back(grad_second * (1.0 + scale2), normed2, inv_two)
    grad_gate1 = jnp.sum(grad_middle * branch, axis=1)
    branch_grad16 = (grad_middle * gate1).astype(jnp.bfloat16)
    grad_merge_b = jnp.sum(branch_grad16.astype(jnp.float32), axis=(0, 1))
    branch_grad_all = gather_image(branch_grad16, cid + 6)
    grad_merge_p = jnp.einsum(
        "btd,bth->dh", branch_grad_all, attended, preferred_element_type=jnp.float32
    )
    attended_grad16 = jnp.einsum(
        "btd,dh->bth", branch_grad_all, merge_p, preferred_element_type=jnp.float32
    ).astype(jnp.bfloat16)
    grad_query, grad_keys, grad_values = attend_back(
        query, keys, vals, marks_all, log_sum, attended_grad16, heads, scale
    )
    joined_grad16 = jnp.stack([grad_query, grad_keys, grad_values], axis=2).astype(jnp.bfloat16)
    grad_attn_p = jnp.einsum(
        "btd,btke->dke", input_all, joined_grad16, preferred_element_type=jnp.float32
    )
    bias_zero = jnp.zeros((2 * width,), jnp.float32)
    grad_attn_b = lax.dynamic_update_slice_in_dim(
        bias_zero,
        jnp.sum(joined_grad16[:, :, 0].astype(jnp.float32), axis=(0, 1)),
        group * head_width,
        0,
    )
    grad_attn_b = lax.dynamic_update_slice_in_dim(
        grad_attn_b,
        jnp.sum(joined_grad16[:, :, 2].astype(jnp.float32), axis=(0, 1)),
        width + group * head_width,
        0,
    )
    grad_input = sum_image(
        jnp.einsum("btke,dke->btd", joined_grad16, attn_p, preferred_element_type=jnp.float32),
        cid + 7,
    )
    grad_shift1 = jnp.sum(grad_input, axis=1)
    grad_scale1 = jnp.sum(grad_input * normed1, axis=1)
    grad_values_in = grad_middle + layer_back(grad_input * (1.0 + scale1), normed1, inv_one)
    grad_mod = jnp.concatenate(
        [grad_shift1, grad_scale1, grad_gate1, grad_shift2, grad_scale2, grad_gate2], axis=-1
    )
    return (
        grad_values_in,
        grad_mod,
        (grad_attn_p, grad_merge_p, grad_expand_p, grad_reduce_p),
        (grad_attn_b, grad_merge_b, grad_expand_b, grad_reduce_b),
    )


def pack_weights(attention_weight, merge_weight, expand_weight, reduce_weight):
    def by_group(array):
        parts = array.reshape(*array.shape[:-1], 8, array.shape[-1] // 8)
        return jnp.moveaxis(parts, -2, 0)

    attn, merge = by_group(attention_weight), by_group(merge_weight)
    expand, reduce = by_group(expand_weight), by_group(reduce_weight)
    spare = jnp.zeros((8, 9, ATT_COLS - 4 * HW), BF16)
    columns = []
    for b in range(2):
        columns += [attn[:, b].reshape(8, 9, 3 * HW), merge[:, b], spare]
    for b in range(2):
        columns += [expand[:, b], reduce[:, b]]
    return pack_pieces(jnp.concatenate(columns, axis=2))


def pack_pieces(columns):
    pieces = columns.reshape(8, 9, PIECES, PIECE).swapaxes(1, 2)
    return jnp.pad(pieces.reshape(8, 9 * PIECES, PIECE), [(0, 0), (0, 1), (0, 0)])


def unpack_pieces(packed):
    pieces = packed[:, : 9 * PIECES].reshape(8, PIECES, 9, PIECE)
    return pieces.swapaxes(1, 2).reshape(8, 9, ALL_COLS)


def unpack_rows(packed):
    return unpack_pieces(packed).reshape(72, ALL_COLS)


def block_params(attn, ffn):
    return (
        attn[:, : 3 * HW].reshape(D, 3, HW),
        attn[:, 3 * HW : 4 * HW],
        ffn[:, :FW],
        ffn[:, FW:],
    )


def join_grads(grads):
    attn, merge, expand, reduce = (g.astype(BF16) for g in grads)
    spare = jnp.zeros((D, ATT_COLS - 4 * HW), BF16)
    return jnp.concatenate([attn.reshape(D, 3 * HW), merge, spare, expand, reduce], axis=1)


def pack_grads(one, two):
    columns = jnp.concatenate(
        [one[:, :ATT_COLS], two[:, :ATT_COLS], one[:, ATT_COLS:], two[:, ATT_COLS:]], axis=1
    )
    return pack_pieces(columns.reshape(8, 9, ALL_COLS))


def unpack_grads(packed):
    columns = unpack_pieces(packed)

    def whole(at, width, inner):
        parts = columns[:, :, at : at + inner * width].reshape(8, 9, inner, width)
        return parts.transpose(1, 2, 0, 3).reshape(9, inner, 8 * width).astype(F32)

    starts = (0, ATT_COLS), (2 * ATT_COLS, 2 * ATT_COLS + FFN_COLS)
    return (
        jnp.stack([whole(at, HW, 3) for at in starts[0]]),
        jnp.stack([whole(at + 3 * HW, HW, 1)[:, 0] for at in starts[0]]),
        jnp.stack([whole(at, FW, 1)[:, 0] for at in starts[1]]),
        jnp.stack([whole(at + FW, FW, 1)[:, 0] for at in starts[1]]),
    )


def pack_small(parts):
    flat = jnp.concatenate([part.reshape(-1) for part in parts])
    return jnp.pad(flat, (0, 2048 - flat.shape[0])).reshape(16, 128)


def by_owner(array, dim):
    before, after = array.shape[:dim], array.shape[dim + 1 :]
    parts = array.reshape(*before, 128, array.shape[dim] // 128, *after)
    return jnp.moveaxis(parts, dim, 0).reshape(128, -1)


def from_owner(parts, shape, dim):
    split = parts.reshape(128, *shape[:dim], shape[dim] // 128, *shape[dim + 1 :])
    return jnp.moveaxis(split, 0, dim).reshape(shape)


def shards(
    latent,
    condition,
    routed_ids,
    embed_weight,
    embed_bias,
    modulation_weight,
    modulation_bias,
    attention_weight,
    attention_bias,
    merge_weight,
    merge_bias,
    expand_weight,
    expand_bias,
    reduce_weight,
    reduce_bias,
    final_modulation,
    final_offsets,
    unpatch_weight,
    unpatch_bias,
    pred_cotangent,
):
    count = latent.shape[0]
    tile_rows = latent.shape[1] // 2
    tile_cols = latent.shape[2] // 2
    tile_tokens = tile_rows * tile_cols
    rows_tiles = lax.axis_size("tx")
    cols_tiles = lax.axis_size("ty")
    tiles = rows_tiles * cols_tiles
    grid_side = tile_rows * rows_tiles
    row_index = lax.axis_index("tx") * tile_rows + jnp.arange(tile_rows, dtype=jnp.int32)
    col_index = lax.axis_index("ty") * tile_cols + jnp.arange(tile_cols, dtype=jnp.int32)
    token_index = (row_index[:, None] * grid_side + col_index[None, :]).reshape(tile_tokens)
    routed = jnp.sum(
        (routed_ids[:, :, None] == token_index[None, None, :]).astype(jnp.float32), axis=1
    )
    capacity = 7 * tile_tokens // 8
    id_tiles = (
        routed_ids // grid_side // tile_rows * cols_tiles + routed_ids % grid_side // tile_cols
    )
    tile_loads = jnp.sum(
        (id_tiles[:, :, None] == jnp.arange(tiles, dtype=jnp.int32)[None, None, :]).astype(
            jnp.int32
        ),
        axis=1,
    )
    routed_marks = jnp.arange(capacity, dtype=jnp.int32)[None, None, :] < tile_loads[:, :, None]
    routed_marks = routed_marks.astype(jnp.float32).reshape(count, tiles * capacity)
    everyone = jnp.ones((count, tile_tokens), jnp.float32)
    everyone_all = jnp.ones((count, tiles * tile_tokens), jnp.float32)
    position, owner, valid = compact_plan(routed, capacity)
    width = D
    scale = (D // HEADS) ** (-0.5)
    whole_index = lax.axis_index(DP_TX_TY)
    small_parts = (
        embed_weight,
        embed_bias,
        unpatch_weight,
        attention_bias,
        merge_bias,
        expand_bias,
        reduce_bias,
    )
    cond_rows = jax.nn.silu(condition.astype(F32)).astype(BF16)
    mod_cuts = (6 * D, 12 * D, 14 * D)
    mod_piece = modulation_bias.shape[1]
    final_piece = final_offsets.shape[0]
    placed_bias = jnp.zeros((MOD_ALL,), F32)
    for bias, at in (
        (modulation_bias[0], whole_index * mod_piece),
        (modulation_bias[1], 6 * D + whole_index * mod_piece),
        (final_offsets, 12 * D + whole_index * final_piece),
    ):
        placed_bias = lax.dynamic_update_slice_in_dim(placed_bias, bias.astype(F32), at, 0)
    mod_parts = jnp.concatenate(
        [
            jnp.dot(cond_rows, modulation_weight[0], preferred_element_type=F32),
            jnp.dot(cond_rows, modulation_weight[1], preferred_element_type=F32),
            jnp.dot(cond_rows, final_modulation, preferred_element_type=F32),
        ],
        axis=1,
    )
    mod_parts = jnp.pad(mod_parts + placed_bias[None], [(0, 0), (0, 16384 - MOD_ALL)])
    packed = pack_weights(attention_weight, merge_weight, expand_weight, reduce_weight)
    packed, mods, small = spread(packed, mod_parts.reshape(16, 128, 128), pack_small(small_parts))
    mods = mods.reshape(1, 16384)
    mod_one = mods[:, : 6 * D]
    mod_two = mods[:, 6 * D : 12 * D]
    head_mod = mods[:, 12 * D : 14 * D]
    small = small.transpose(1, 0, 2, 3).reshape(128, 2048)
    pieces = jnp.split(small, [sum(SMALL_IN[:k]) for k in range(1, 8)], axis=1)
    embed_w = from_owner(pieces[0], (16, D), 1)
    embed_b = from_owner(pieces[1], (D,), 0)
    unpatch_w = from_owner(pieces[2], (D, 32), 0)
    attn_b = from_owner(pieces[3], (2, 2 * D), 1)
    merge_b = from_owner(pieces[4], (2, D), 1)
    expand_b = from_owner(pieces[5], (2, FF), 1)
    reduce_b = from_owner(pieces[6], (2, D), 1)
    rows = unpack_rows(packed)
    first_attn = fetch_rows(rows[:, :ATT_COLS], 3)
    first_ffn = lax.all_gather(
        rows[:, 2 * ATT_COLS : 2 * ATT_COLS + FFN_COLS], DP, axis=0, tiled=True
    )
    second_all = lax.all_gather(
        jnp.concatenate(
            [rows[:, ATT_COLS : 2 * ATT_COLS], rows[:, 2 * ATT_COLS + FFN_COLS :]], axis=1
        ),
        DP,
        axis=0,
        tiled=True,
    )
    placed = sincos_table(row_index.astype(jnp.float32), col_index.astype(jnp.float32), width)
    patches = to_patches(latent)
    initial_tokens = (
        jnp.einsum("btp,pd->btd", patches, embed_w, preferred_element_type=jnp.float32)
        + embed_b.astype(jnp.float32)
        + placed[None, :, :]
    )
    first_params = block_params(first_attn, first_ffn)
    second_params = block_params(second_all[:, :ATT_COLS], second_all[:, ATT_COLS:])
    first_biases = (attn_b[0], merge_b[0], expand_b[0], reduce_b[0])
    second_biases = (attn_b[1], merge_b[1], expand_b[1], reduce_b[1])
    middle_one, saved_one = spread_forward(
        initial_tokens, mod_one, first_params, first_biases, everyone_all, scale, 10
    )
    selected_rows = pick_rows(middle_one, owner)
    middle_two, saved_two = spread_forward(
        selected_rows, mod_two, second_params, second_biases, routed_marks, scale, 20
    )
    keep_mask = routed[:, :, None] > 0
    ended = jnp.where(keep_mask, pick_rows(middle_two, position), middle_one)
    head_shift = head_mod[:, None, :width]
    head_scale = head_mod[:, None, width:]
    normed_end, inv_end = layer_stats(ended)
    final16 = (normed_end * (1.0 + head_scale) + head_shift).astype(jnp.bfloat16)
    outputs = jnp.einsum(
        "btd,do->bto", final16, unpatch_w, preferred_element_type=jnp.float32
    ) + unpatch_bias.astype(jnp.float32)
    predicted = from_patches(outputs.astype(jnp.bfloat16), tile_rows, tile_cols)
    cotangent = to_patches(pred_cotangent)
    grad_unpatch_w = jnp.einsum(
        "btd,bto->do", final16, cotangent, preferred_element_type=jnp.float32
    )
    grad_unpatch_b = jnp.sum(cotangent.astype(jnp.float32), axis=(0, 1))
    grad_final = jnp.einsum("bto,do->btd", cotangent, unpatch_w, preferred_element_type=jnp.float32)
    head_grad_mod = jnp.concatenate(
        [jnp.sum(grad_final, axis=1), jnp.sum(grad_final * normed_end, axis=1)], axis=-1
    )
    grad_ended = layer_back(grad_final * (1.0 + head_scale), normed_end, inv_end)
    grad_chosen = pick_rows(grad_ended, owner)
    grad_two, mod_grad_two, weights_two, biases_two = spread_backward(
        grad_chosen, saved_two, mod_two, second_params, valid, scale, 20
    )
    summed_two = reduce_rows(join_grads(weights_two), 4)
    grad_middle = jnp.where(keep_mask, pick_rows(grad_two, position), grad_ended)
    grad_start, mod_grad_one, weights_one, biases_one = spread_backward(
        grad_middle, saved_one, mod_one, first_params, everyone, scale, 10
    )
    summed_one = reduce_rows(join_grads(weights_one), 5)
    start_grad16 = grad_start.astype(jnp.bfloat16)
    grad_embed_w = jnp.einsum(
        "btp,btd->pd", patches, start_grad16, preferred_element_type=jnp.float32
    )
    grad_embed_b = jnp.sum(start_grad16.astype(jnp.float32), axis=(0, 1))
    latent_tokens = jnp.einsum(
        "btd,pd->btp", start_grad16, embed_w, preferred_element_type=jnp.float32
    )
    latent_grad = from_patches(latent_tokens, tile_rows, tile_cols)
    bias_grads = [jnp.stack([biases_one[member], biases_two[member]]) for member in range(4)]
    small_out = jnp.concatenate(
        [
            by_owner(grad_embed_w, 1),
            by_owner(grad_embed_b, 0),
            by_owner(grad_unpatch_w, 0),
            by_owner(bias_grads[0], 1),
            by_owner(bias_grads[1], 1),
            by_owner(bias_grads[2], 1),
            by_owner(bias_grads[3], 1),
            jnp.broadcast_to(grad_unpatch_b[None], (128, 32)),
        ],
        axis=1,
    )
    small_out = jnp.pad(small_out, [(0, 0), (0, 1024 - small_out.shape[1])])
    grad_mods = jnp.concatenate([mod_grad_one, mod_grad_two, head_grad_mod], axis=1)
    grad_mods = jnp.pad(grad_mods.reshape(8, MOD_ALL // 8), [(0, 0), (0, 2048 - MOD_ALL // 8)])
    packed_grads, mod_back, small_back = finish(
        pack_grads(summed_one, summed_two),
        grad_mods.reshape(8, 16, 128),
        small_out.reshape(16, 8, 8, 128),
    )
    small_back = small_back.reshape(1024)
    small_sizes = (*SMALL_IN, 32)
    small_sums = jnp.split(small_back, [sum(small_sizes[:k]) for k in range(1, 9)])
    mod_back = mod_back.reshape(8, 16, 2048)[:, :, : MOD_ALL // 8]
    mod_back = mod_back.transpose(1, 0, 2).reshape(16, MOD_ALL)
    one16 = mod_back[:, : mod_cuts[0]]
    two16 = mod_back[:, mod_cuts[0] : mod_cuts[1]]
    head16 = mod_back[:, mod_cuts[1] :]
    stacked = unpack_grads(packed_grads)
    mod_weight_grad = jnp.stack(
        [
            jnp.einsum("id,ie->de", cond_rows, one16, preferred_element_type=jnp.float32),
            jnp.einsum("id,ie->de", cond_rows, two16, preferred_element_type=jnp.float32),
        ]
    )
    mod_bias_grad = jnp.stack(
        [
            lax.dynamic_slice_in_dim(
                jnp.sum(one16.astype(jnp.float32), axis=0), whole_index * mod_piece, mod_piece
            ),
            lax.dynamic_slice_in_dim(
                jnp.sum(two16.astype(jnp.float32), axis=0), whole_index * mod_piece, mod_piece
            ),
        ]
    )
    final_mod_grad = jnp.einsum("id,ie->de", cond_rows, head16, preferred_element_type=jnp.float32)
    final_bias_grad = lax.dynamic_slice_in_dim(
        jnp.sum(head16.astype(jnp.float32), axis=0), whole_index * final_piece, final_piece
    )
    cond_terms = (
        jnp.einsum("ie,de->id", one16, modulation_weight[0], preferred_element_type=jnp.float32)
        + jnp.einsum("ie,de->id", two16, modulation_weight[1], preferred_element_type=jnp.float32)
        + jnp.einsum("ie,de->id", head16, final_modulation, preferred_element_type=jnp.float32)
    )
    silu_value, silu_pull = jax.vjp(jax.nn.silu, condition.astype(jnp.float32))
    condition_grad = silu_pull(cond_terms)[0]
    return (
        predicted,
        latent_grad,
        condition_grad,
        small_sums[0].reshape(16, 9),
        small_sums[1],
        mod_weight_grad,
        mod_bias_grad,
        stacked[0],
        small_sums[3].reshape(2, 18),
        stacked[1],
        small_sums[4].reshape(2, 9),
        stacked[2],
        small_sums[5].reshape(2, 36),
        stacked[3],
        small_sums[6].reshape(2, 9),
        final_mod_grad,
        final_bias_grad,
        small_sums[2].reshape(9, 32),
        small_sums[7],
    )


def solution(mesh):
    torus = Mesh(
        mesh.devices.reshape(4, 4, mesh.shape["tx"], mesh.shape["ty"]), ("dp_0", "dp_1", "tx", "ty")
    )
    return jax.shard_map(
        shards,
        mesh=torus,
        in_specs=(
            P(DP, "tx", "ty", None),
            P(None, DP_TX_TY),
            P(DP, None),
            P(None, DP_TX_TY),
            P(DP_TX_TY),
            P(None, DP_TX_TY, None),
            P(None, DP_TX_TY),
            P(None, DP_TX_TY, None, None),
            P(None, DP_TX_TY),
            P(None, DP_TX_TY, None),
            P(None, DP_TX_TY),
            P(None, DP_TX_TY, None),
            P(None, DP_TX_TY),
            P(None, DP_TX_TY, None),
            P(None, DP_TX_TY),
            P(DP_TX_TY, None),
            P(DP_TX_TY),
            P(DP_TX_TY, None),
            P(),
            P(DP, "tx", "ty", None),
        ),
        out_specs=(
            P(DP, "tx", "ty", None),
            P(DP, "tx", "ty", None),
            P(None, DP_TX_TY),
            P(None, DP_TX_TY),
            P(DP_TX_TY),
            P(None, DP_TX_TY, None),
            P(None, DP_TX_TY),
            P(None, DP_TX_TY, None, None),
            P(None, DP_TX_TY),
            P(None, DP_TX_TY, None),
            P(None, DP_TX_TY),
            P(None, DP_TX_TY, None),
            P(None, DP_TX_TY),
            P(None, DP_TX_TY, None),
            P(None, DP_TX_TY),
            P(DP_TX_TY, None),
            P(DP_TX_TY),
            P(DP_TX_TY, None),
            P(),
        ),
        check_vma=False,
    )
```

```python
import functools

import jax
import jax.numpy as jnp
from jax import lax
from jax.experimental import pallas as pl
from jax.experimental.pallas import tpu as pltpu
from jax.sharding import Mesh
from jax.sharding import PartitionSpec as P

D = 1152
HEADS = 16
FF = 4608
HW = D // 8
FW = FF // 8
DP = ("dp_0", "dp_1")
DP_TX_TY = ("dp_0", "dp_1", "tx", "ty")
MESH = pl.DeviceIdType.MESH
VMEM = pl.BlockSpec(memory_space=pltpu.VMEM)
F32 = jnp.float32
BF16 = jnp.bfloat16
ATT_COLS = 640
FFN_COLS = 2 * FW
ALL_COLS = 2 * (ATT_COLS + FFN_COLS)
PIECE = 512
PIECES = ALL_COLS // PIECE
MOD_ALL = 14 * D
SMALL_IN = (16 * 9, 9, 9 * 32, 2 * 18, 2 * 9, 2 * 36, 2 * 9)


def enter(peers):
    barrier = pltpu.get_barrier_semaphore()
    for peer in peers:
        pl.semaphore_signal(barrier, inc=1, device_id=peer, device_id_type=MESH)
    pl.semaphore_wait(barrier, len(peers))


def send(src, dst, sems, k, peer):
    copy = pltpu.make_async_remote_copy(
        src_ref=src,
        dst_ref=dst,
        send_sem=sems[0].at[k],
        recv_sem=sems[1].at[k],
        device_id=peer,
        device_id_type=MESH,
    )
    copy.start()
    return copy


def group_peers():
    c, y = lax.axis_index("tx"), lax.axis_index("ty")
    found = []
    for dc in range(2):
        for dy in range(4):
            if dc or dy:
                oc, oy = lax.rem(c + dc, 2), lax.rem(y + dy, 4)
                found.append(({"tx": oc, "ty": oy}, oc * 4 + oy))
    return found


def image_peers():
    x, z = lax.axis_index("dp_0"), lax.axis_index("dp_1")
    found = []
    for dx in range(4):
        for dz in range(4):
            if dx or dz:
                ox, oz = lax.rem(x + dx, 4), lax.rem(z + dz, 4)
                found.append(({"dp_0": ox, "dp_1": oz}, ox * 4 + oz))
    return found


def own_group():
    return lax.axis_index("tx") * 4 + lax.axis_index("ty")


def own_image():
    return lax.axis_index("dp_0") * 4 + lax.axis_index("dp_1")


def dma_sems(n):
    return [pltpu.SemaphoreType.DMA((n,)), pltpu.SemaphoreType.DMA((n,))]


def collective(kernel, cid, outs, scratch, *operands, vmem=48 << 20):
    return pl.pallas_call(
        kernel,
        out_shape=outs,
        in_specs=[VMEM] * len(operands),
        out_specs=jax.tree.map(lambda _: VMEM, outs),
        scratch_shapes=scratch,
        compiler_params=pltpu.CompilerParams(
            collective_id=cid, has_side_effects=True, vmem_limit_bytes=vmem
        ),
    )(*operands)


def ring_peers():
    c, y = lax.axis_index("tx"), lax.axis_index("ty")
    return (
        {"tx": 1 - c},
        {"ty": lax.rem(y + 1, 4)},
        {"ty": lax.rem(y + 3, 4)},
        {"ty": lax.rem(y + 2, 4)},
    )


def spread_kernel(w_ref, m_ref, s_ref, w_out, m_out, s_out, m_got, m_two, ss, rs):
    group, image = group_peers(), image_peers()
    enter([peer for peer, _ in group + image])
    sems = (ss, rs)
    me, mine = own_group(), own_image()
    first = []
    for k, (peer, at) in enumerate(image):
        first.append(send(m_ref.at[at], m_got.at[mine], sems, k, peer))
        first.append(send(s_ref, s_out.at[me, mine], sems, 15 + k, peer))
    weights = [send(w_ref.at[at], w_out.at[me], sems, 30 + k, p) for k, (p, at) in enumerate(group)]
    w_out[me] = w_ref[me]
    s_out[me, mine] = s_ref[...]
    m_got[mine] = m_ref[mine]
    for copy in first:
        copy.wait_recv()
    total = m_got[0]
    for k in range(1, 16):
        total = total + m_got[k]
    m_two[me] = total
    second = []
    for k, (peer, _) in enumerate(group):
        second.append(send(m_two.at[me], m_two.at[me], sems, 37 + k, peer))
        second.append(send(s_out.at[me], s_out.at[me], sems, 44 + k, peer))
    for copy in second:
        copy.wait_recv()
    total = m_two[0]
    for k in range(1, 8):
        total = total + m_two[k]
    m_out[...] = total
    for copy in weights:
        copy.wait_recv()
    for copy in first + second + weights:
        copy.wait_send()


def spread(weights, mods, small):
    outs = (
        jax.ShapeDtypeStruct(weights.shape, BF16),
        jax.ShapeDtypeStruct((128, 128), F32),
        jax.ShapeDtypeStruct((8, 16, *small.shape), BF16),
    )
    scratch = [pltpu.VMEM((16, 128, 128), F32), pltpu.VMEM((8, 128, 128), F32)] + dma_sems(51)
    return collective(spread_kernel, 1, outs, scratch, weights, mods, small)


def fetch_kernel(w_ref, o_ref, ss, rs):
    image = image_peers()
    enter([peer for peer, _ in image])
    mine = own_image()
    copies = [
        send(w_ref, o_ref.at[mine], (ss, rs), k, peer) for k, (peer, _) in enumerate(image)
    ]
    o_ref[mine] = w_ref[...]
    for copy in copies:
        copy.wait()


def fetch_rows(rows, cid):
    padded = jnp.pad(rows, [(0, 8), (0, 0)])
    out = jax.ShapeDtypeStruct((16, *padded.shape), BF16)
    slabs = collective(fetch_kernel, cid, out, dma_sems(15), padded)
    return slabs[:, :72].reshape(D, rows.shape[1])


def reduce_kernel(g_ref, o_ref, got, ss, rs):
    image = image_peers()
    enter([peer for peer, _ in image])
    mine = own_image()
    copies = [
        send(g_ref.at[at], got.at[mine], (ss, rs), k, peer) for k, (peer, at) in enumerate(image)
    ]
    got[mine] = g_ref[mine]
    for copy in copies:
        copy.wait_recv()

    @pl.loop(0, g_ref.shape[1] // 16)
    def _(piece):
        rows = pl.ds(pl.multiple_of(piece * 16, 16), 16)
        total = got[0, rows, :].astype(F32)
        for k in range(1, 16):
            total = total + got[k, rows, :].astype(F32)
        o_ref[rows, :] = total.astype(BF16)

    for copy in copies:
        copy.wait_send()


def reduce_rows(grads, cid):
    slabs = jnp.pad(grads.reshape(16, 72, -1), [(0, 0), (0, 8), (0, 0)])
    out = jax.ShapeDtypeStruct(slabs.shape[1:], BF16)
    scratch = [pltpu.VMEM(slabs.shape, BF16)] + dma_sems(15)
    return collective(reduce_kernel, cid, out, scratch, slabs)[:72]


def finish_kernel(g_ref, m_ref, s_ref, g_out, m_out, s_out, m_got, s_got, s_mine, s_two, ss, rs):
    group, image = group_peers(), image_peers()
    enter([peer for peer, _ in group + image])
    sems = (ss, rs)
    me, mine = own_group(), own_image()
    first = [send(m_ref.at[at], m_got.at[me], sems, k, p) for k, (p, at) in enumerate(group)]
    small = [send(s_ref.at[at], s_got.at[mine], sems, 7 + k, p) for k, (p, at) in enumerate(image)]
    weights = [send(g_ref.at[at], g_out.at[me], sems, 22 + k, p) for k, (p, at) in enumerate(group)]
    m_got[me] = m_ref[me]
    s_got[mine] = s_ref[mine]
    g_out[me] = g_ref[me]
    for copy in first:
        copy.wait_recv()
    total = m_got[0]
    for k in range(1, 8):
        total = total + m_got[k]
    m_out[me, mine] = total.astype(BF16)
    second = [
        send(m_out.at[me, mine], m_out.at[me, mine], sems, 29 + k, p)
        for k, (p, _) in enumerate(image)
    ]
    for copy in small:
        copy.wait_recv()
    total = s_got[0]
    for k in range(1, 16):
        total = total + s_got[k]
    s_mine[...] = total
    pieces = [send(s_mine.at[at], s_two.at[me], sems, 44 + k, p) for k, (p, at) in enumerate(group)]
    s_two[me] = s_mine[me]
    for copy in second:
        copy.wait_recv()
    third = [send(m_out.at[me], m_out.at[me], sems, 51 + k, p) for k, (p, _) in enumerate(group)]
    for copy in pieces:
        copy.wait_recv()
    total = s_two[0]
    for k in range(1, 8):
        total = total + s_two[k]
    s_out[...] = total
    for copy in weights + third:
        copy.wait_recv()
    for copy in first + small + weights + second + pieces + third:
        copy.wait_send()


def finish(grads, mods, small):
    outs = (
        jax.ShapeDtypeStruct(grads.shape, BF16),
        jax.ShapeDtypeStruct((8, 16, 16, 128), BF16),
        jax.ShapeDtypeStruct((8, 128), F32),
    )
    scratch = [
        pltpu.VMEM((8, 16, 128), F32),
        pltpu.VMEM((16, 8, 8, 128), F32),
        pltpu.VMEM((8, 8, 128), F32),
        pltpu.VMEM((8, 8, 128), F32),
    ] + dma_sems(58)
    return collective(finish_kernel, 2, outs, scratch, grads, mods, small)


def layer_stats(value_rows):
    centered = value_rows - jnp.mean(value_rows, axis=-1, keepdims=True)
    inv_std = lax.rsqrt(jnp.mean(centered * centered, axis=-1, keepdims=True) + 1e-06)
    return (centered * inv_std, inv_std)


def layer_back(upstream, normed, inv_std):
    return inv_std * (
        upstream
        - jnp.mean(upstream, axis=-1, keepdims=True)
        - normed * jnp.mean(upstream * normed, axis=-1, keepdims=True)
    )


def sincos_table(row_pos, col_pos, width):
    quarter = width // 4
    freqs = jnp.power(10000.0, -jnp.arange(quarter, dtype=jnp.float32) / quarter)
    row_angle = row_pos[:, None] * freqs[None, :]
    col_angle = col_pos[:, None] * freqs[None, :]
    row_embed = jnp.concatenate([jnp.sin(row_angle), jnp.cos(row_angle)], axis=-1)
    col_embed = jnp.concatenate([jnp.sin(col_angle), jnp.cos(col_angle)], axis=-1)
    row_full = jnp.broadcast_to(
        row_embed[:, None, :], (row_pos.shape[0], col_pos.shape[0], width // 2)
    )
    col_full = jnp.broadcast_to(
        col_embed[None, :, :], (row_pos.shape[0], col_pos.shape[0], width // 2)
    )
    return jnp.concatenate([row_full, col_full], axis=-1).reshape(
        row_pos.shape[0] * col_pos.shape[0], width
    )


def to_patches(pixels):
    count, height, breadth, depth = pixels.shape
    shaped = pixels.reshape(count, height // 2, 2, breadth // 2, 2, depth)
    return shaped.transpose(0, 1, 3, 2, 4, 5).reshape(
        count, height // 2 * (breadth // 2), 4 * depth
    )


def from_patches(token_rows, tile_rows, tile_cols):
    count = token_rows.shape[0]
    depth = token_rows.shape[2] // 4
    shaped = token_rows.reshape(count, tile_rows, tile_cols, 2, 2, depth)
    return shaped.transpose(0, 1, 3, 2, 4, 5).reshape(count, 2 * tile_rows, 2 * tile_cols, depth)


def compact_plan(routed, capacity):
    count, tokens = routed.shape
    flags = routed > 0
    position = jnp.cumsum(flags.astype(jnp.int32), axis=1) - 1
    slots = jnp.where(flags, position, capacity)
    batch_index = jnp.broadcast_to(jnp.arange(count, dtype=jnp.int32)[:, None], (count, tokens))
    token_ids = jnp.arange(tokens, dtype=jnp.int32)[None, :]
    owner = (
        jnp.zeros((count, capacity), jnp.int32).at[batch_index, slots].set(token_ids, mode="drop")
    )
    filled = jnp.sum(flags.astype(jnp.int32), axis=1, keepdims=True)
    valid = (jnp.arange(capacity, dtype=jnp.int32)[None, :] < filled).astype(jnp.float32)
    return (jnp.where(flags, position, 0), owner, valid)


def pick_rows(value_rows, index):
    return jax.vmap(lambda table, where: jnp.take(table, where, axis=0))(value_rows, index)


def rows_at(index, tokens):
    return pl.ds(pl.multiple_of(index * tokens, 16), tokens)


def ring_scratch(tokens):
    half = (tokens // 2 + 15) // 16 * 16
    return [
        pltpu.VMEM((4, tokens, D), F32),
        pltpu.VMEM((4, tokens, D), BF16),
        pltpu.VMEM((4, tokens, D), BF16),
        pltpu.VMEM((3, tokens, D), BF16),
        pltpu.VMEM((2, tokens, D), BF16),
        pltpu.VMEM((half, D), BF16),
        pltpu.VMEM((tokens - half, D), BF16),
        pltpu.SemaphoreType.DMA((20,)),
        pltpu.SemaphoreType.DMA((20,)),
    ]


class Ring:
    def __init__(self, tokens, scratch):
        self.tokens = tokens
        self.half = (tokens // 2 + 15) // 16 * 16
        self.kept, self.sib_out, self.sib_in, self.out, self.got = scratch[:5]
        self.far_low, self.far_high = scratch[5:7]
        self.sems = tuple(scratch[7:9])
        c, y = lax.axis_index("tx"), lax.axis_index("ty")
        self.sib, self.up, self.down, _ = ring_peers()
        self.own = [c * 4 + lax.rem(y + d, 4) for d in range(4)]
        self.other = [(1 - c) * 4 + lax.rem(y + d, 4) for d in range(4)]
        self.sent = []

    def enter(self):
        enter([self.sib, self.up, self.down])

    def send(self, src, dst, k, peer):
        copy = send(src, dst, self.sems, k, peer)
        self.sent.append(copy)
        return copy

    def rows(self, index, start=0, stop=None):
        stop = self.tokens if stop is None else stop
        at = pl.multiple_of(index * self.tokens + start, 16)
        return pl.ds(at, stop - start)

    def gather(self, x_ref, all_ref, visit):
        half, tokens = self.half, self.tokens
        me, above, across, below = self.own
        first, last = slice(0, half), slice(half, tokens)

        def pass_on(index, k, peer, start=0, stop=None):
            part = all_ref.at[self.rows(index, start, stop)]
            return self.send(part, part, k, peer)

        def own_part(rows, k, peer):
            part = all_ref.at[self.rows(me, rows.start, rows.stop)]
            return self.send(x_ref.at[rows], part, k, peer)

        a1 = own_part(first, 0, self.up)
        b1 = own_part(last, 1, self.down)
        a2 = own_part(last, 2, self.up)
        b2 = own_part(first, 3, self.down)
        s0 = self.send(x_ref, all_ref.at[self.rows(me)], 4, self.sib)
        all_ref[self.rows(me), :] = x_ref[...]
        visit(True, 0)
        s0.wait_recv()
        visit(False, 0)
        a1.wait_recv()
        f1 = pass_on(below, 5, self.up, 0, half)
        b1.wait_recv()
        f2 = pass_on(above, 6, self.down, half, tokens)
        a2.wait_recv()
        s1 = pass_on(below, 7, self.sib)
        b2.wait_recv()
        s2 = pass_on(above, 8, self.sib)
        visit(True, 3)
        visit(True, 1)
        s1.wait_recv()
        visit(False, 3)
        s2.wait_recv()
        visit(False, 1)
        f1.wait_recv()
        f2.wait_recv()
        s3 = pass_on(across, 9, self.sib)
        visit(True, 2)
        s3.wait_recv()
        visit(False, 2)

    def put(self, own, d, value):
        if own:
            self.kept[d] = value
        else:
            self.sib_out[d] = value.astype(BF16)
            self.swaps[d] = self.send(self.sib_out.at[d], self.sib_in.at[d], 10 + d, self.sib)

    def start_sums(self):
        self.swaps = {}

    def chip_sum(self, d):
        self.swaps[d].wait_recv()
        return self.kept[d] + self.sib_in[d].astype(F32)

    def near(self):
        half = self.half
        first, last = slice(0, half), slice(half, self.tokens)
        total = self.chip_sum(1)
        self.kept[1] = total
        self.out[0, last] = total[half:].astype(BF16)
        self.n1 = self.send(self.out.at[0, last], self.got.at[0, last], 14, self.up)
        total = self.chip_sum(3)
        self.kept[3] = total
        self.out[1, first] = total[:half].astype(BF16)
        self.n2 = self.send(self.out.at[1, first], self.got.at[1, first], 15, self.down)

    def far(self):
        half = self.half
        self.out[2] = self.chip_sum(2).astype(BF16)
        self.f1 = self.send(self.out.at[2, 0:half], self.far_low, 16, self.up)
        self.f2 = self.send(self.out.at[2, half : self.tokens], self.far_high, 17, self.down)

    def relay(self):
        half = self.half
        first, last = slice(0, half), slice(half, self.tokens)
        self.f1.wait_recv()
        self.out[0, first] = (self.kept[1, first] + self.far_low[...].astype(F32)).astype(BF16)
        self.r1 = self.send(self.out.at[0, first], self.got.at[0, first], 18, self.up)
        self.f2.wait_recv()
        self.out[1, last] = (self.kept[3, last] + self.far_high[...].astype(F32)).astype(BF16)
        self.r2 = self.send(self.out.at[1, last], self.got.at[1, last], 19, self.down)

    def total(self):
        value = self.chip_sum(0)
        for copy in (self.n1, self.n2, self.r1, self.r2):
            copy.wait_recv()
        return value + self.got[0].astype(F32) + self.got[1].astype(F32)

    def leave(self):
        for copy in self.sent:
            copy.wait_send()


def dot_nn(left, right):
    return lax.dot_general(left, right, (((1,), (0,)), ((), ())), preferred_element_type=F32)


def dot_nt(left, right):
    return lax.dot_general(left, right, (((1,), (1,)), ((), ())), preferred_element_type=F32)


def dot_tn(left, right):
    return lax.dot_general(left, right, (((0,), (0,)), ((), ())), preferred_element_type=F32)


def gelu_both(pre):
    root = 0.7978845608028654
    square = pre * pre
    bent = jnp.tanh(root * pre * (1.0 + 0.044715 * square))
    value = 0.5 * pre * (1.0 + bent)
    slope = 0.5 * (1.0 + bent) + 0.5 * pre * (1.0 - bent * bent) * root * (1.0 + 0.134145 * square)
    return value, slope


def ffn_forward_kernel(
    x_ref, vec_ref, bias_ref, we_ref, wr_ref, out_ref, mlp_ref, all_ref, hid_ref, slope_ref, x16, *scratch
):
    tokens = x_ref.shape[0]
    ring = Ring(tokens, scratch)
    normed, _ = layer_stats(x_ref[...])
    x16[...] = (normed * (1.0 + vec_ref[1:2]) + vec_ref[0:1]).astype(BF16)
    ring.enter()
    ring.start_sums()

    def visit(own, d):
        rows = ring.rows((ring.own if own else ring.other)[d])
        pre = dot_nn(all_ref[rows, :], we_ref[...]) + bias_ref[...]
        value, slope = gelu_both(pre)
        hidden = value.astype(BF16)
        hid_ref[rows, :] = hidden
        slope_ref[rows, :] = slope.astype(BF16)
        ring.put(own, d, dot_nt(hidden, wr_ref[...]))
        if not own and d == 1:
            ring.near()

    ring.gather(x16, all_ref, visit)
    ring.far()
    ring.relay()
    mlp = ring.total() + vec_ref[3:4]
    mlp_ref[...] = mlp
    out_ref[...] = x_ref[...] + vec_ref[2:3] * mlp
    ring.leave()


def ffn_forward(x, vecs, bias, we, wr, cid):
    tokens = x.shape[0]
    outs = (
        jax.ShapeDtypeStruct((tokens, D), F32),
        jax.ShapeDtypeStruct((tokens, D), F32),
        jax.ShapeDtypeStruct((8 * tokens, D), BF16),
        jax.ShapeDtypeStruct((8 * tokens, FW), BF16),
        jax.ShapeDtypeStruct((8 * tokens, FW), BF16),
    )
    scratch = [pltpu.VMEM((tokens, D), BF16)] + ring_scratch(tokens)
    return collective(ffn_forward_kernel, cid, outs, scratch, x, vecs, bias, we, wr)


def sum_rows(value):
    return jnp.sum(value, axis=0, keepdims=True)


def ffn_backward_kernel(
    g_ref, x_ref, mlp_ref, vec_ref, valid_ref, second_ref, hid_ref, slope_ref, we_ref, wr_ref,
    out_ref, vecs_ref, bias_ref, dw_ref, g16, g_all, pre_all, *scratch
):
    tokens = x_ref.shape[0]
    ring = Ring(tokens, scratch)
    grad = g_ref[...] * valid_ref[...]
    g16[...] = (grad * vec_ref[2:3]).astype(BF16)
    ring.enter()
    ring.start_sums()
    bias_ref[...] = jnp.zeros_like(bias_ref)

    def visit(own, d):
        rows = ring.rows((ring.own if own else ring.other)[d])
        pre_grad = (
            dot_nn(g_all[rows, :], wr_ref[...]) * slope_ref[rows, :].astype(F32)
        ).astype(BF16)
        pre_all[rows, :] = pre_grad
        bias_ref[...] += sum_rows(pre_grad.astype(F32))
        ring.put(own, d, dot_nt(pre_grad, we_ref[...]))
        if not own and d == 1:
            ring.near()

    ring.gather(g16, g_all, visit)
    ring.far()
    vecs_ref[2:3] = sum_rows(grad * mlp_ref[...])
    vecs_ref[3:4] = sum_rows(g16[...].astype(F32))
    vecs_ref[4:8] = jnp.zeros((4, D), F32)
    ring.relay()

    @pl.loop(0, D // 128)
    def _(k):
        at = pl.ds(pl.multiple_of(k * 128, 128), 128)
        dw_ref[at, :] = jnp.concatenate(
            [
                dot_tn(second_ref[:, at], pre_all[...]),
                dot_tn(g_all[:, at], hid_ref[...]),
            ],
            axis=1,
        ).astype(BF16)

    second_grad = ring.total()
    normed, inv_std = layer_stats(x_ref[...])
    vecs_ref[0:1] = sum_rows(second_grad)
    vecs_ref[1:2] = sum_rows(second_grad * normed)
    out_ref[...] = grad + layer_back(second_grad * (1.0 + vec_ref[1:2]), normed, inv_std)
    ring.leave()


def ffn_backward(g, x, mlp, vecs, valid, second, hid, slope, we, wr, cid):
    tokens = x.shape[0]
    outs = (
        jax.ShapeDtypeStruct((tokens, D), F32),
        jax.ShapeDtypeStruct((8, D), F32),
        jax.ShapeDtypeStruct((1, FW), F32),
        jax.ShapeDtypeStruct((D, FFN_COLS), BF16),
    )
    scratch = [
        pltpu.VMEM((tokens, D), BF16),
        pltpu.VMEM((8 * tokens, D), BF16),
        pltpu.VMEM((8 * tokens, FW), BF16),
    ] + ring_scratch(tokens)
    return collective(
        ffn_backward_kernel, cid, outs, scratch, g, x, mlp, vecs, valid, second, hid, slope, we, wr
    )


HEAD = D // HEADS
SCALE = HEAD ** (-0.5)


def head_cols(h, start=0):
    return slice(start + h * HEAD, start + (h + 1) * HEAD)


def attn_forward_kernel(
    x_ref, vec_ref, bias_ref, mask_ref, wqkv_ref, wm_ref,
    out_ref, branch_ref, all_ref, q_ref, k_ref, v_ref, lse_ref, att_ref, x16, *scratch
):
    tokens = x_ref.shape[0]
    ring = Ring(tokens, scratch)
    normed, _ = layer_stats(x_ref[...])
    x16[...] = (normed * (1.0 + vec_ref[1:2]) + vec_ref[0:1]).astype(BF16)
    ring.enter()
    ring.start_sums()

    def visit(own, d):
        rows = ring.rows((ring.own if own else ring.other)[d])
        joined = (dot_nn(all_ref[rows, :], wqkv_ref[...]) + bias_ref[...]).astype(BF16)
        for h in range(2):
            q_ref[h, rows, :] = joined[:, head_cols(h)]
            k_ref[h, rows, :] = joined[:, head_cols(h, HW)]
            v_ref[h, rows, :] = joined[:, head_cols(h, 2 * HW)]

    def attend(own, d):
        rows = ring.rows((ring.own if own else ring.other)[d])
        parts = []
        for h in range(2):
            scores = dot_nt(q_ref[h, rows, :], k_ref[h]) * SCALE + mask_ref[...]
            highest = jnp.max(scores, axis=-1, keepdims=True)
            shifted = jnp.exp(scores - highest)
            summed = jnp.sum(shifted, axis=-1, keepdims=True)
            probs = (shifted * (1.0 / summed)).astype(BF16)
            lse_ref[rows, h : h + 1] = highest + jnp.log(summed)
            parts.append(dot_nn(probs, v_ref[h]).astype(BF16))
        attended = jnp.concatenate(parts, axis=1)
        att_ref[rows, :] = attended
        ring.put(own, d, dot_nt(attended, wm_ref[...]))

    ring.gather(x16, all_ref, visit)
    attend(False, 2)
    attend(True, 2)
    ring.far()
    for d in (1, 3):
        attend(False, d)
        attend(True, d)
    ring.near()
    ring.relay()
    attend(False, 0)
    attend(True, 0)
    branch = ring.total() + vec_ref[3:4]
    branch_ref[...] = branch
    out_ref[...] = x_ref[...] + vec_ref[2:3] * branch
    ring.leave()


def attn_forward(x, vecs, bias, mask, wqkv, wm, cid):
    tokens = x.shape[0]
    heads = jax.ShapeDtypeStruct((2, 8 * tokens, HEAD), BF16)
    outs = (
        jax.ShapeDtypeStruct((tokens, D), F32),
        jax.ShapeDtypeStruct((tokens, D), F32),
        jax.ShapeDtypeStruct((8 * tokens, D), BF16),
        heads,
        heads,
        heads,
        jax.ShapeDtypeStruct((8 * tokens, 2), F32),
        jax.ShapeDtypeStruct((8 * tokens, HW), BF16),
    )
    scratch = [pltpu.VMEM((tokens, D), BF16)] + ring_scratch(tokens)
    return collective(attn_forward_kernel, cid, outs, scratch, x, vecs, bias, mask, wqkv, wm)


def attn_backward_kernel(
    g_ref, x_ref, branch_ref, vec_ref, mask_ref, in_ref, q_ref, k_ref, v_ref, lse_ref, att_ref,
    wqkv_ref, wm_ref, out_ref, vecs_ref, bias_ref, dw_ref,
    g16, g_all, joined, dk, dv, *scratch
):
    tokens = x_ref.shape[0]
    ring = Ring(tokens, scratch)
    g16[...] = (g_ref[...] * vec_ref[2:3]).astype(BF16)
    ring.enter()
    ring.start_sums()
    dk[...] = jnp.zeros_like(dk)
    dv[...] = jnp.zeros_like(dv)

    def visit(own, d):
        rows = ring.rows((ring.own if own else ring.other)[d])
        grad = dot_nn(g_all[rows, :], wm_ref[...]).astype(BF16)
        queries = []
        for h in range(2):
            part = grad[:, head_cols(h)]
            query = q_ref[h, rows, :]
            scores = dot_nt(query, k_ref[h]) * SCALE + mask_ref[...]
            probs = jnp.exp(scores - lse_ref[rows, h : h + 1])
            grad_probs = dot_nt(part, v_ref[h])
            weighted = jnp.sum(probs * grad_probs, axis=-1, keepdims=True)
            score_grad = (probs * (grad_probs - weighted)).astype(BF16)
            queries.append((dot_nn(score_grad, k_ref[h]) * SCALE).astype(BF16))
            dk[h] += dot_tn(score_grad, query)
            dv[h] += dot_tn(probs.astype(BF16), part)
        joined[rows, 0:HW] = jnp.concatenate(queries, axis=1)

    def back(own, d):
        rows = ring.rows((ring.own if own else ring.other)[d])
        ring.put(own, d, dot_nt(joined[rows, :], wqkv_ref[...]))

    ring.gather(g16, g_all, visit)
    later = [(dk[h] * SCALE).astype(BF16) for h in range(2)] + [dv[h].astype(BF16) for h in range(2)]
    joined[:, HW : 3 * HW] = jnp.concatenate(later, axis=1)
    back(False, 2)
    back(True, 2)
    ring.far()
    for d in (1, 3):
        back(False, d)
        back(True, d)
    ring.near()
    back(False, 0)
    back(True, 0)
    bias_ref[...] = sum_rows(joined[...].astype(F32))
    vecs_ref[2:3] = sum_rows(g_ref[...] * branch_ref[...])
    vecs_ref[3:4] = sum_rows(g16[...].astype(F32))
    vecs_ref[4:8] = jnp.zeros((4, D), F32)
    ring.relay()

    @pl.loop(0, D // 128)
    def _(k):
        at = pl.ds(pl.multiple_of(k * 128, 128), 128)
        dw_ref[at, :] = jnp.concatenate(
            [
                dot_tn(in_ref[:, at], joined[...]),
                dot_tn(g_all[:, at], att_ref[...]),
                jnp.zeros((128, ATT_COLS - 4 * HW), F32),
            ],
            axis=1,
        ).astype(BF16)

    input_grad = ring.total()
    normed, inv_std = layer_stats(x_ref[...])
    vecs_ref[0:1] = sum_rows(input_grad)
    vecs_ref[1:2] = sum_rows(input_grad * normed)
    out_ref[...] = g_ref[...] + layer_back(input_grad * (1.0 + vec_ref[1:2]), normed, inv_std)
    ring.leave()


def attn_backward(g, x, branch, vecs, mask, inputs, q, k, v, lse, att, wqkv, wm, cid):
    tokens = x.shape[0]
    outs = (
        jax.ShapeDtypeStruct((tokens, D), F32),
        jax.ShapeDtypeStruct((8, D), F32),
        jax.ShapeDtypeStruct((1, 3 * HW), F32),
        jax.ShapeDtypeStruct((D, ATT_COLS), BF16),
    )
    scratch = [
        pltpu.VMEM((tokens, D), BF16),
        pltpu.VMEM((8 * tokens, D), BF16),
        pltpu.VMEM((8 * tokens, 3 * HW), BF16),
        pltpu.VMEM((2, 8 * tokens, HEAD), F32),
        pltpu.VMEM((2, 8 * tokens, HEAD), F32),
    ] + ring_scratch(tokens)
    operands = (g, x, branch, vecs, mask, inputs, q, k, v, lse, att, wqkv, wm)
    return collective(attn_backward_kernel, cid, outs, scratch, *operands)


def block_forward(x, mod, params, biases, mask, cid):
    wqkv, wm, we, wr = params
    attn_b, merge_b, expand_b, reduce_b = (b.astype(F32) for b in biases)
    group = own_group()
    zeros = jnp.zeros((4, D), F32)
    vec_one = jnp.concatenate([mod[0:3], merge_b[None], zeros])
    vec_two = jnp.concatenate([mod[3:6], reduce_b[None], zeros])
    bias = jnp.concatenate(
        [
            lax.dynamic_slice_in_dim(attn_b, group * HW, HW),
            jnp.zeros((HW,), F32),
            lax.dynamic_slice_in_dim(attn_b, D + group * HW, HW),
        ]
    )[None]
    middle, branch, *kept = attn_forward(x, vec_one, bias, mask, wqkv, wm, cid)
    e_bias = lax.dynamic_slice_in_dim(expand_b, group * FW, FW)[None]
    output, mlp, *more = ffn_forward(middle, vec_two, e_bias, we, wr, cid + 1)
    return output, (x, vec_one, mask, middle, branch, kept, vec_two, mlp, more)


def block_backward(grad, saved, params, valid, cid):
    x, vec_one, mask, middle, branch, kept, vec_two, mlp, more = saved
    wqkv, wm, we, wr = params
    group = own_group()
    grad, mod_two, bias_two, dw_ffn = ffn_backward(
        grad, middle, mlp, vec_two, valid, *more, we, wr, cid + 2
    )
    grad, mod_one, bias_one, dw_attn = attn_backward(
        grad, x, branch, vec_one, mask, *kept, wqkv, wm, cid + 3
    )
    grad_expand_b = lax.dynamic_update_slice_in_dim(
        jnp.zeros((FF,), F32), bias_two[0], group * FW, 0
    )
    grad_attn_b = lax.dynamic_update_slice_in_dim(
        jnp.zeros((2 * D,), F32), bias_one[0, :HW], group * HW, 0
    )
    grad_attn_b = lax.dynamic_update_slice_in_dim(
        grad_attn_b, bias_one[0, 2 * HW :], D + group * HW, 0
    )
    mod_grad = jnp.concatenate([mod_one[0:3].reshape(-1), mod_two[0:3].reshape(-1)])
    biases = (grad_attn_b, mod_one[3], grad_expand_b, mod_two[3])
    return grad, mod_grad, (dw_attn, dw_ffn), biases


def pack_weights(attention_weight, merge_weight, expand_weight, reduce_weight):
    def by_group(array):
        parts = array.reshape(*array.shape[:-1], 8, array.shape[-1] // 8)
        return jnp.moveaxis(parts, -2, 0)

    attn, merge = by_group(attention_weight), by_group(merge_weight)
    expand, reduce = by_group(expand_weight), by_group(reduce_weight)
    spare = jnp.zeros((8, 9, ATT_COLS - 4 * HW), BF16)
    columns = []
    for b in range(2):
        columns += [attn[:, b].reshape(8, 9, 3 * HW), merge[:, b], spare]
    for b in range(2):
        columns += [expand[:, b], reduce[:, b]]
    return pack_pieces(jnp.concatenate(columns, axis=2))


def pack_pieces(columns):
    pieces = columns.reshape(8, 9, PIECES, PIECE).swapaxes(1, 2)
    return jnp.pad(pieces.reshape(8, 9 * PIECES, PIECE), [(0, 0), (0, 1), (0, 0)])


def unpack_pieces(packed):
    pieces = packed[:, : 9 * PIECES].reshape(8, PIECES, 9, PIECE)
    return pieces.swapaxes(1, 2).reshape(8, 9, ALL_COLS)


def unpack_rows(packed):
    return unpack_pieces(packed).reshape(72, ALL_COLS)


def block_params(attn, ffn):
    return attn[:, : 3 * HW], attn[:, 3 * HW : 4 * HW], ffn[:, :FW], ffn[:, FW:]


def pack_grads(one, two):
    columns = jnp.concatenate(
        [one[:, :ATT_COLS], two[:, :ATT_COLS], one[:, ATT_COLS:], two[:, ATT_COLS:]], axis=1
    )
    return pack_pieces(columns.reshape(8, 9, ALL_COLS))


def unpack_grads(packed):
    columns = unpack_pieces(packed)

    def whole(at, width, inner):
        parts = columns[:, :, at : at + inner * width].reshape(8, 9, inner, width)
        return parts.transpose(1, 2, 0, 3).reshape(9, inner, 8 * width).astype(F32)

    starts = (0, ATT_COLS), (2 * ATT_COLS, 2 * ATT_COLS + FFN_COLS)
    return (
        jnp.stack([whole(at, HW, 3) for at in starts[0]]),
        jnp.stack([whole(at + 3 * HW, HW, 1)[:, 0] for at in starts[0]]),
        jnp.stack([whole(at, FW, 1)[:, 0] for at in starts[1]]),
        jnp.stack([whole(at + FW, FW, 1)[:, 0] for at in starts[1]]),
    )


def pack_small(parts):
    flat = jnp.concatenate([part.reshape(-1) for part in parts])
    return jnp.pad(flat, (0, 2048 - flat.shape[0])).reshape(16, 128)


def by_owner(array, dim):
    before, after = array.shape[:dim], array.shape[dim + 1 :]
    parts = array.reshape(*before, 128, array.shape[dim] // 128, *after)
    return jnp.moveaxis(parts, dim, 0).reshape(128, -1)


def from_owner(parts, shape, dim):
    split = parts.reshape(128, *shape[:dim], shape[dim] // 128, *shape[dim + 1 :])
    return jnp.moveaxis(split, 0, dim).reshape(shape)


def shards(
    latent,
    condition,
    routed_ids,
    embed_weight,
    embed_bias,
    modulation_weight,
    modulation_bias,
    attention_weight,
    attention_bias,
    merge_weight,
    merge_bias,
    expand_weight,
    expand_bias,
    reduce_weight,
    reduce_bias,
    final_modulation,
    final_offsets,
    unpatch_weight,
    unpatch_bias,
    pred_cotangent,
):
    count = latent.shape[0]
    tile_rows = latent.shape[1] // 2
    tile_cols = latent.shape[2] // 2
    tile_tokens = tile_rows * tile_cols
    rows_tiles = lax.axis_size("tx")
    cols_tiles = lax.axis_size("ty")
    tiles = rows_tiles * cols_tiles
    grid_side = tile_rows * rows_tiles
    row_index = lax.axis_index("tx") * tile_rows + jnp.arange(tile_rows, dtype=jnp.int32)
    col_index = lax.axis_index("ty") * tile_cols + jnp.arange(tile_cols, dtype=jnp.int32)
    token_index = (row_index[:, None] * grid_side + col_index[None, :]).reshape(tile_tokens)
    routed = jnp.sum(
        (routed_ids[:, :, None] == token_index[None, None, :]).astype(jnp.float32), axis=1
    )
    capacity = 7 * tile_tokens // 8
    id_tiles = (
        routed_ids // grid_side // tile_rows * cols_tiles + routed_ids % grid_side // tile_cols
    )
    tile_loads = jnp.sum(
        (id_tiles[:, :, None] == jnp.arange(tiles, dtype=jnp.int32)[None, None, :]).astype(
            jnp.int32
        ),
        axis=1,
    )
    routed_marks = jnp.arange(capacity, dtype=jnp.int32)[None, None, :] < tile_loads[:, :, None]
    routed_marks = routed_marks.astype(jnp.float32).reshape(count, tiles * capacity)
    everyone = jnp.ones((count, tile_tokens), jnp.float32)
    position, owner, valid = compact_plan(routed, capacity)
    width = D
    whole_index = lax.axis_index(DP_TX_TY)
    small_parts = (
        embed_weight,
        embed_bias,
        unpatch_weight,
        attention_bias,
        merge_bias,
        expand_bias,
        reduce_bias,
    )
    cond_rows = jax.nn.silu(condition.astype(F32)).astype(BF16)
    mod_cuts = (6 * D, 12 * D, 14 * D)
    mod_piece = modulation_bias.shape[1]
    final_piece = final_offsets.shape[0]
    placed_bias = jnp.zeros((MOD_ALL,), F32)
    for bias, at in (
        (modulation_bias[0], whole_index * mod_piece),
        (modulation_bias[1], 6 * D + whole_index * mod_piece),
        (final_offsets, 12 * D + whole_index * final_piece),
    ):
        placed_bias = lax.dynamic_update_slice_in_dim(placed_bias, bias.astype(F32), at, 0)
    mod_parts = jnp.concatenate(
        [
            jnp.dot(cond_rows, modulation_weight[0], preferred_element_type=F32),
            jnp.dot(cond_rows, modulation_weight[1], preferred_element_type=F32),
            jnp.dot(cond_rows, final_modulation, preferred_element_type=F32),
        ],
        axis=1,
    )
    mod_parts = jnp.pad(mod_parts + placed_bias[None], [(0, 0), (0, 16384 - MOD_ALL)])
    packed = pack_weights(attention_weight, merge_weight, expand_weight, reduce_weight)
    packed, mods, small = spread(packed, mod_parts.reshape(16, 128, 128), pack_small(small_parts))
    mods = mods.reshape(1, 16384)
    mod_one = mods[:, : 6 * D]
    mod_two = mods[:, 6 * D : 12 * D]
    head_mod = mods[:, 12 * D : 14 * D]
    small = small.transpose(1, 0, 2, 3).reshape(128, 2048)
    pieces = jnp.split(small, [sum(SMALL_IN[:k]) for k in range(1, 8)], axis=1)
    embed_w = from_owner(pieces[0], (16, D), 1)
    embed_b = from_owner(pieces[1], (D,), 0)
    unpatch_w = from_owner(pieces[2], (D, 32), 0)
    attn_b = from_owner(pieces[3], (2, 2 * D), 1)
    merge_b = from_owner(pieces[4], (2, D), 1)
    expand_b = from_owner(pieces[5], (2, FF), 1)
    reduce_b = from_owner(pieces[6], (2, D), 1)
    rows = unpack_rows(packed)
    first_attn = fetch_rows(rows[:, :ATT_COLS], 3)
    first_ffn = lax.all_gather(
        rows[:, 2 * ATT_COLS : 2 * ATT_COLS + FFN_COLS], DP, axis=0, tiled=True
    )
    second_all = lax.all_gather(
        jnp.concatenate(
            [rows[:, ATT_COLS : 2 * ATT_COLS], rows[:, 2 * ATT_COLS + FFN_COLS :]], axis=1
        ),
        DP,
        axis=0,
        tiled=True,
    )
    placed = sincos_table(row_index.astype(jnp.float32), col_index.astype(jnp.float32), width)
    patches = to_patches(latent)
    initial_tokens = (
        jnp.einsum("btp,pd->btd", patches, embed_w, preferred_element_type=jnp.float32)
        + embed_b.astype(jnp.float32)
        + placed[None, :, :]
    )
    first_params = block_params(first_attn, first_ffn)
    second_params = block_params(second_all[:, :ATT_COLS], second_all[:, ATT_COLS:])
    first_biases = (attn_b[0], merge_b[0], expand_b[0], reduce_b[0])
    second_biases = (attn_b[1], merge_b[1], expand_b[1], reduce_b[1])
    mask_one = jnp.zeros((1, tiles * tile_tokens), F32)
    mask_two = jnp.where(routed_marks > 0, 0.0, -1e30).astype(F32)
    middle_one, saved_one = block_forward(
        initial_tokens[0], mod_one.reshape(6, D), first_params, first_biases, mask_one, 10
    )
    middle_one = middle_one[None]
    selected_rows = pick_rows(middle_one, owner)
    middle_two, saved_two = block_forward(
        selected_rows[0], mod_two.reshape(6, D), second_params, second_biases, mask_two, 20
    )
    middle_two = middle_two[None]
    keep_mask = routed[:, :, None] > 0
    ended = jnp.where(keep_mask, pick_rows(middle_two, position), middle_one)
    head_shift = head_mod[:, None, :width]
    head_scale = head_mod[:, None, width:]
    normed_end, inv_end = layer_stats(ended)
    final16 = (normed_end * (1.0 + head_scale) + head_shift).astype(jnp.bfloat16)
    outputs = jnp.einsum(
        "btd,do->bto", final16, unpatch_w, preferred_element_type=jnp.float32
    ) + unpatch_bias.astype(jnp.float32)
    predicted = from_patches(outputs.astype(jnp.bfloat16), tile_rows, tile_cols)
    cotangent = to_patches(pred_cotangent)
    grad_unpatch_w = jnp.einsum(
        "btd,bto->do", final16, cotangent, preferred_element_type=jnp.float32
    )
    grad_unpatch_b = jnp.sum(cotangent.astype(jnp.float32), axis=(0, 1))
    grad_final = jnp.einsum("bto,do->btd", cotangent, unpatch_w, preferred_element_type=jnp.float32)
    head_grad_mod = jnp.concatenate(
        [jnp.sum(grad_final, axis=1), jnp.sum(grad_final * normed_end, axis=1)], axis=-1
    )
    grad_ended = layer_back(grad_final * (1.0 + head_scale), normed_end, inv_end)
    grad_chosen = pick_rows(grad_ended, owner)
    grad_two, mod_grad_two, weights_two, biases_two = block_backward(
        grad_chosen[0], saved_two, second_params, valid[0][:, None], 20
    )
    summed_two = reduce_rows(jnp.concatenate(weights_two, axis=1), 4)
    grad_middle = jnp.where(keep_mask, pick_rows(grad_two[None], position), grad_ended)
    grad_start, mod_grad_one, weights_one, biases_one = block_backward(
        grad_middle[0], saved_one, first_params, everyone[0][:, None], 10
    )
    grad_start = grad_start[None]
    summed_one = reduce_rows(jnp.concatenate(weights_one, axis=1), 5)
    start_grad16 = grad_start.astype(jnp.bfloat16)
    grad_embed_w = jnp.einsum(
        "btp,btd->pd", patches, start_grad16, preferred_element_type=jnp.float32
    )
    grad_embed_b = jnp.sum(start_grad16.astype(jnp.float32), axis=(0, 1))
    latent_tokens = jnp.einsum(
        "btd,pd->btp", start_grad16, embed_w, preferred_element_type=jnp.float32
    )
    latent_grad = from_patches(latent_tokens, tile_rows, tile_cols)
    bias_grads = [jnp.stack([biases_one[member], biases_two[member]]) for member in range(4)]
    small_out = jnp.concatenate(
        [
            by_owner(grad_embed_w, 1),
            by_owner(grad_embed_b, 0),
            by_owner(grad_unpatch_w, 0),
            by_owner(bias_grads[0], 1),
            by_owner(bias_grads[1], 1),
            by_owner(bias_grads[2], 1),
            by_owner(bias_grads[3], 1),
            jnp.broadcast_to(grad_unpatch_b[None], (128, 32)),
        ],
        axis=1,
    )
    small_out = jnp.pad(small_out, [(0, 0), (0, 1024 - small_out.shape[1])])
    grad_mods = jnp.concatenate([mod_grad_one, mod_grad_two, head_grad_mod[0]])
    grad_mods = jnp.pad(grad_mods.reshape(8, MOD_ALL // 8), [(0, 0), (0, 2048 - MOD_ALL // 8)])
    packed_grads, mod_back, small_back = finish(
        pack_grads(summed_one, summed_two),
        grad_mods.reshape(8, 16, 128),
        small_out.reshape(16, 8, 8, 128),
    )
    small_back = small_back.reshape(1024)
    small_sizes = (*SMALL_IN, 32)
    small_sums = jnp.split(small_back, [sum(small_sizes[:k]) for k in range(1, 9)])
    mod_back = mod_back.reshape(8, 16, 2048)[:, :, : MOD_ALL // 8]
    mod_back = mod_back.transpose(1, 0, 2).reshape(16, MOD_ALL)
    one16 = mod_back[:, : mod_cuts[0]]
    two16 = mod_back[:, mod_cuts[0] : mod_cuts[1]]
    head16 = mod_back[:, mod_cuts[1] :]
    stacked = unpack_grads(packed_grads)
    mod_weight_grad = jnp.stack(
        [
            jnp.einsum("id,ie->de", cond_rows, one16, preferred_element_type=jnp.float32),
            jnp.einsum("id,ie->de", cond_rows, two16, preferred_element_type=jnp.float32),
        ]
    )
    mod_bias_grad = jnp.stack(
        [
            lax.dynamic_slice_in_dim(
                jnp.sum(one16.astype(jnp.float32), axis=0), whole_index * mod_piece, mod_piece
            ),
            lax.dynamic_slice_in_dim(
                jnp.sum(two16.astype(jnp.float32), axis=0), whole_index * mod_piece, mod_piece
            ),
        ]
    )
    final_mod_grad = jnp.einsum("id,ie->de", cond_rows, head16, preferred_element_type=jnp.float32)
    final_bias_grad = lax.dynamic_slice_in_dim(
        jnp.sum(head16.astype(jnp.float32), axis=0), whole_index * final_piece, final_piece
    )
    cond_terms = (
        jnp.einsum("ie,de->id", one16, modulation_weight[0], preferred_element_type=jnp.float32)
        + jnp.einsum("ie,de->id", two16, modulation_weight[1], preferred_element_type=jnp.float32)
        + jnp.einsum("ie,de->id", head16, final_modulation, preferred_element_type=jnp.float32)
    )
    silu_value, silu_pull = jax.vjp(jax.nn.silu, condition.astype(jnp.float32))
    condition_grad = silu_pull(cond_terms)[0]
    return (
        predicted,
        latent_grad,
        condition_grad,
        small_sums[0].reshape(16, 9),
        small_sums[1],
        mod_weight_grad,
        mod_bias_grad,
        stacked[0],
        small_sums[3].reshape(2, 18),
        stacked[1],
        small_sums[4].reshape(2, 9),
        stacked[2],
        small_sums[5].reshape(2, 36),
        stacked[3],
        small_sums[6].reshape(2, 9),
        final_mod_grad,
        final_bias_grad,
        small_sums[2].reshape(9, 32),
        small_sums[7],
    )


def solution(mesh):
    torus = Mesh(
        mesh.devices.reshape(4, 4, mesh.shape["tx"], mesh.shape["ty"]), ("dp_0", "dp_1", "tx", "ty")
    )
    return jax.shard_map(
        shards,
        mesh=torus,
        in_specs=(
            P(DP, "tx", "ty", None),
            P(None, DP_TX_TY),
            P(DP, None),
            P(None, DP_TX_TY),
            P(DP_TX_TY),
            P(None, DP_TX_TY, None),
            P(None, DP_TX_TY),
            P(None, DP_TX_TY, None, None),
            P(None, DP_TX_TY),
            P(None, DP_TX_TY, None),
            P(None, DP_TX_TY),
            P(None, DP_TX_TY, None),
            P(None, DP_TX_TY),
            P(None, DP_TX_TY, None),
            P(None, DP_TX_TY),
            P(DP_TX_TY, None),
            P(DP_TX_TY),
            P(DP_TX_TY, None),
            P(),
            P(DP, "tx", "ty", None),
        ),
        out_specs=(
            P(DP, "tx", "ty", None),
            P(DP, "tx", "ty", None),
            P(None, DP_TX_TY),
            P(None, DP_TX_TY),
            P(DP_TX_TY),
            P(None, DP_TX_TY, None),
            P(None, DP_TX_TY),
            P(None, DP_TX_TY, None, None),
            P(None, DP_TX_TY),
            P(None, DP_TX_TY, None),
            P(None, DP_TX_TY),
            P(None, DP_TX_TY, None),
            P(None, DP_TX_TY),
            P(None, DP_TX_TY, None),
            P(None, DP_TX_TY),
            P(DP_TX_TY, None),
            P(DP_TX_TY),
            P(DP_TX_TY, None),
            P(),
        ),
        check_vma=False,
    )
```

```python
import functools

import jax
import jax.numpy as jnp
from jax import lax
from jax.experimental import pallas as pl
from jax.experimental.pallas import tpu as pltpu
from jax.sharding import Mesh
from jax.sharding import PartitionSpec as P

D = 1152
HEADS = 16
FF = 4608
HW = D // 8
FW = FF // 8
DP = ("dp_0", "dp_1")
DP_TX_TY = ("dp_0", "dp_1", "tx", "ty")
MESH = pl.DeviceIdType.MESH
VMEM = pl.BlockSpec(memory_space=pltpu.VMEM)
FAR = pl.BlockSpec(memory_space=pl.ANY)
F32 = jnp.float32
BF16 = jnp.bfloat16
ATT_COLS = 640
FFN_COLS = 2 * FW
ALL_COLS = 2 * (ATT_COLS + FFN_COLS)
PIECE = 512
PIECES = ALL_COLS // PIECE
MOD_ALL = 14 * D
SMALL_IN = (16 * 9, 9, 9 * 32, 2 * 18, 2 * 9, 2 * 36, 2 * 9)


def greet(peers):
    barrier = pltpu.get_barrier_semaphore()
    for peer in peers:
        pl.semaphore_signal(barrier, inc=1, device_id=peer, device_id_type=MESH)


def met(peers):
    pl.semaphore_wait(pltpu.get_barrier_semaphore(), len(peers))


def enter(peers):
    greet(peers)
    met(peers)


def send(src, dst, sems, k, peer):
    copy = pltpu.make_async_remote_copy(
        src_ref=src,
        dst_ref=dst,
        send_sem=sems[0].at[k],
        recv_sem=sems[1].at[k],
        device_id=peer,
        device_id_type=MESH,
    )
    copy.start()
    return copy


def group_peers():
    c, y = lax.axis_index("tx"), lax.axis_index("ty")
    found = []
    for dc in range(2):
        for dy in range(4):
            if dc or dy:
                oc, oy = lax.rem(c + dc, 2), lax.rem(y + dy, 4)
                found.append(({"tx": oc, "ty": oy}, oc * 4 + oy))
    return found


def image_peers():
    x, z = lax.axis_index("dp_0"), lax.axis_index("dp_1")
    found = []
    for dx in range(4):
        for dz in range(4):
            if dx or dz:
                ox, oz = lax.rem(x + dx, 4), lax.rem(z + dz, 4)
                found.append(({"dp_0": ox, "dp_1": oz}, ox * 4 + oz))
    return found


def own_group():
    return lax.axis_index("tx") * 4 + lax.axis_index("ty")


def own_image():
    return lax.axis_index("dp_0") * 4 + lax.axis_index("dp_1")


def dma_sems(n):
    return [pltpu.SemaphoreType.DMA((n,)), pltpu.SemaphoreType.DMA((n,))]


def collective(kernel, cid, outs, scratch, *operands, far_in=0, far_out=0, vmem=56 << 20):
    many = isinstance(outs, tuple)
    near_in = len(operands) - far_in
    near_out = (len(outs) if many else 1) - far_out
    out_specs = (VMEM,) * near_out + (FAR,) * far_out
    return pl.pallas_call(
        kernel,
        out_shape=outs,
        in_specs=[VMEM] * near_in + [FAR] * far_in,
        out_specs=out_specs if many else out_specs[0],
        scratch_shapes=scratch,
        compiler_params=pltpu.CompilerParams(
            collective_id=cid, has_side_effects=True, vmem_limit_bytes=vmem
        ),
    )(*operands)


class Moves:
    def __init__(self, sems):
        self.sems, self.copies = sems, {}

    def start(self, k, src, dst):
        self.copies[k] = pltpu.make_async_copy(src, dst, self.sems.at[k])
        self.copies[k].start()

    def wait(self, *which):
        for k in which:
            self.copies.pop(k).wait()

    def finish(self):
        self.wait(*list(self.copies))


def ring_peers():
    c, y = lax.axis_index("tx"), lax.axis_index("ty")
    return (
        {"tx": 1 - c},
        {"ty": lax.rem(y + 1, 4)},
        {"ty": lax.rem(y + 3, 4)},
        {"ty": lax.rem(y + 2, 4)},
    )


def spread_kernel(w_ref, m_ref, s_ref, w_out, m_out, s_out, m_got, m_two, ss, rs):
    group, image = group_peers(), image_peers()
    enter([peer for peer, _ in group + image])
    sems = (ss, rs)
    me, mine = own_group(), own_image()
    first = []
    for k, (peer, at) in enumerate(image):
        first.append(send(m_ref.at[at], m_got.at[mine], sems, k, peer))
        first.append(send(s_ref, s_out.at[me, mine], sems, 15 + k, peer))
    weights = [send(w_ref.at[at], w_out.at[me], sems, 30 + k, p) for k, (p, at) in enumerate(group)]
    w_out[me] = w_ref[me]
    s_out[me, mine] = s_ref[...]
    m_got[mine] = m_ref[mine]
    for copy in first:
        copy.wait_recv()
    total = m_got[0]
    for k in range(1, 16):
        total = total + m_got[k]
    m_two[me] = total
    second = []
    for k, (peer, _) in enumerate(group):
        second.append(send(m_two.at[me], m_two.at[me], sems, 37 + k, peer))
        second.append(send(s_out.at[me], s_out.at[me], sems, 44 + k, peer))
    for copy in second:
        copy.wait_recv()
    total = m_two[0]
    for k in range(1, 8):
        total = total + m_two[k]
    m_out[...] = total
    for copy in weights:
        copy.wait_recv()
    for copy in first + second + weights:
        copy.wait_send()


def spread(weights, mods, small):
    outs = (
        jax.ShapeDtypeStruct(weights.shape, BF16),
        jax.ShapeDtypeStruct((128, 128), F32),
        jax.ShapeDtypeStruct((8, 16, *small.shape), BF16),
    )
    scratch = [pltpu.VMEM((16, 128, 128), F32), pltpu.VMEM((8, 128, 128), F32)] + dma_sems(51)
    return collective(spread_kernel, 1, outs, scratch, weights, mods, small)


def finish_kernel(g_ref, m_ref, s_ref, g_out, m_out, s_out, m_got, s_got, s_mine, s_two, ss, rs):
    group, image = group_peers(), image_peers()
    enter([peer for peer, _ in group + image])
    sems = (ss, rs)
    me, mine = own_group(), own_image()
    first = [send(m_ref.at[at], m_got.at[me], sems, k, p) for k, (p, at) in enumerate(group)]
    small = [send(s_ref.at[at], s_got.at[mine], sems, 7 + k, p) for k, (p, at) in enumerate(image)]
    weights = [send(g_ref.at[at], g_out.at[me], sems, 22 + k, p) for k, (p, at) in enumerate(group)]
    m_got[me] = m_ref[me]
    s_got[mine] = s_ref[mine]
    g_out[me] = g_ref[me]
    for copy in first:
        copy.wait_recv()
    total = m_got[0]
    for k in range(1, 8):
        total = total + m_got[k]
    m_out[me, mine] = total.astype(BF16)
    second = [
        send(m_out.at[me, mine], m_out.at[me, mine], sems, 29 + k, p)
        for k, (p, _) in enumerate(image)
    ]
    for copy in small:
        copy.wait_recv()
    total = s_got[0]
    for k in range(1, 16):
        total = total + s_got[k]
    s_mine[...] = total
    pieces = [send(s_mine.at[at], s_two.at[me], sems, 44 + k, p) for k, (p, at) in enumerate(group)]
    s_two[me] = s_mine[me]
    for copy in second:
        copy.wait_recv()
    third = [send(m_out.at[me], m_out.at[me], sems, 51 + k, p) for k, (p, _) in enumerate(group)]
    for copy in pieces:
        copy.wait_recv()
    total = s_two[0]
    for k in range(1, 8):
        total = total + s_two[k]
    s_out[...] = total
    for copy in weights + third:
        copy.wait_recv()
    for copy in first + small + weights + second + pieces + third:
        copy.wait_send()


def finish(grads, mods, small):
    outs = (
        jax.ShapeDtypeStruct(grads.shape, BF16),
        jax.ShapeDtypeStruct((8, 16, 16, 128), BF16),
        jax.ShapeDtypeStruct((8, 128), F32),
    )
    scratch = [
        pltpu.VMEM((8, 16, 128), F32),
        pltpu.VMEM((16, 8, 8, 128), F32),
        pltpu.VMEM((8, 8, 128), F32),
        pltpu.VMEM((8, 8, 128), F32),
    ] + dma_sems(58)
    return collective(finish_kernel, 2, outs, scratch, grads, mods, small)


def layer_stats(value_rows):
    centered = value_rows - jnp.mean(value_rows, axis=-1, keepdims=True)
    inv_std = lax.rsqrt(jnp.mean(centered * centered, axis=-1, keepdims=True) + 1e-06)
    return (centered * inv_std, inv_std)


def layer_back(upstream, normed, inv_std):
    return inv_std * (
        upstream
        - jnp.mean(upstream, axis=-1, keepdims=True)
        - normed * jnp.mean(upstream * normed, axis=-1, keepdims=True)
    )


def sincos_table(row_pos, col_pos, width):
    quarter = width // 4
    freqs = jnp.power(10000.0, -jnp.arange(quarter, dtype=jnp.float32) / quarter)
    row_angle = row_pos[:, None] * freqs[None, :]
    col_angle = col_pos[:, None] * freqs[None, :]
    row_embed = jnp.concatenate([jnp.sin(row_angle), jnp.cos(row_angle)], axis=-1)
    col_embed = jnp.concatenate([jnp.sin(col_angle), jnp.cos(col_angle)], axis=-1)
    row_full = jnp.broadcast_to(
        row_embed[:, None, :], (row_pos.shape[0], col_pos.shape[0], width // 2)
    )
    col_full = jnp.broadcast_to(
        col_embed[None, :, :], (row_pos.shape[0], col_pos.shape[0], width // 2)
    )
    return jnp.concatenate([row_full, col_full], axis=-1).reshape(
        row_pos.shape[0] * col_pos.shape[0], width
    )


def to_patches(pixels):
    count, height, breadth, depth = pixels.shape
    shaped = pixels.reshape(count, height // 2, 2, breadth // 2, 2, depth)
    return shaped.transpose(0, 1, 3, 2, 4, 5).reshape(
        count, height // 2 * (breadth // 2), 4 * depth
    )


def from_patches(token_rows, tile_rows, tile_cols):
    count = token_rows.shape[0]
    depth = token_rows.shape[2] // 4
    shaped = token_rows.reshape(count, tile_rows, tile_cols, 2, 2, depth)
    return shaped.transpose(0, 1, 3, 2, 4, 5).reshape(count, 2 * tile_rows, 2 * tile_cols, depth)


def compact_plan(routed, capacity):
    count, tokens = routed.shape
    flags = routed > 0
    position = jnp.cumsum(flags.astype(jnp.int32), axis=1) - 1
    slots = jnp.where(flags, position, capacity)
    batch_index = jnp.broadcast_to(jnp.arange(count, dtype=jnp.int32)[:, None], (count, tokens))
    token_ids = jnp.arange(tokens, dtype=jnp.int32)[None, :]
    owner = (
        jnp.zeros((count, capacity), jnp.int32).at[batch_index, slots].set(token_ids, mode="drop")
    )
    filled = jnp.sum(flags.astype(jnp.int32), axis=1, keepdims=True)
    valid = (jnp.arange(capacity, dtype=jnp.int32)[None, :] < filled).astype(jnp.float32)
    return (jnp.where(flags, position, 0), owner, valid)


def pick_rows(value_rows, index):
    return jax.vmap(lambda table, where: jnp.take(table, where, axis=0))(value_rows, index)


def rows_at(index, tokens):
    return pl.ds(pl.multiple_of(index * tokens, 16), tokens)


def ring_scratch(tokens):
    half = (tokens // 2 + 15) // 16 * 16
    return [
        pltpu.VMEM((4, tokens, D), F32),
        pltpu.VMEM((4, tokens, D), BF16),
        pltpu.VMEM((4, tokens, D), BF16),
        pltpu.VMEM((3, tokens, D), BF16),
        pltpu.VMEM((2, tokens, D), BF16),
        pltpu.VMEM((half, D), BF16),
        pltpu.VMEM((tokens - half, D), BF16),
        pltpu.SemaphoreType.DMA((20,)),
        pltpu.SemaphoreType.DMA((20,)),
    ]


SLAB = 80
PART = D // 16
CUT = {ATT_COLS: 384, FFN_COLS: 640}


def line_peers():
    x, z = lax.axis_index("dp_0"), lax.axis_index("dp_1")
    along_x = [({"dp_0": lax.rem(x + d, 4)}, lax.rem(x + d, 4)) for d in (2, 1, 3)]
    along_z = [({"dp_1": lax.rem(z + d, 4)}, lax.rem(z + d, 4)) for d in (2, 1, 3)]
    return along_x, along_z


class RowsIn:
    def __init__(self, left_ref, right_ref, scratch):
        self.left, self.right = left_ref, right_ref
        self.all_left, self.all_right = scratch[:2]
        self.sems = tuple(scratch[2:4])
        self.x, self.z = lax.axis_index("dp_0"), lax.axis_index("dp_1")
        self.along_x, self.along_z = line_peers()

    def peers(self):
        return [peer for peer, _ in self.along_x + self.along_z]

    def start(self):
        x, z = self.x, self.z
        self.first = []
        for k, (peer, _) in enumerate(self.along_z):
            self.first.append(send(self.left, self.all_left.at[x, z], self.sems, k, peer))
        for k, (peer, _) in enumerate(self.along_x):
            self.first.append(send(self.right, self.all_right.at[x, z], self.sems, 3 + k, peer))
        self.all_left[x, z] = self.left[...]
        self.all_right[x, z] = self.right[...]

    def middle(self):
        left, right = self.all_left.at[self.x], self.all_right.at[:, self.z]
        self.second = []
        for copy in self.first[:3]:
            copy.wait_recv()
        for k, (peer, _) in enumerate(self.along_x):
            self.second.append(send(left, left, self.sems, 6 + k, peer))
        for copy in self.first[3:]:
            copy.wait_recv()
        for k, (peer, _) in enumerate(self.along_z):
            self.second.append(send(right, right, self.sems, 9 + k, peer))

    def end(self, one_ref, two_ref):
        for copy in self.second:
            copy.wait_recv()
        width, other = one_ref.shape[1], two_ref.shape[1]
        cut = self.left.shape[1]

        @pl.loop(0, 8)
        def _(pair):
            x, z = pair // 2, 2 * lax.rem(pair, 2)
            both = []
            for k in range(2):
                parts = [self.all_left[x, z + k], self.all_right[x, z + k]]
                both.append(jnp.concatenate(parts, axis=1).astype(F32)[:PART])
            value = jnp.concatenate(both, axis=0).astype(BF16)
            at = pl.ds(pl.multiple_of(pair * 2 * PART, 16), 2 * PART)
            one_ref[at, :] = value[:, :width]
            two_ref[at, :] = value[:, width : width + other]

        for copy in self.first + self.second:
            copy.wait_send()


def rows_in_scratch(cols):
    left = CUT[cols]
    return [
        pltpu.VMEM((4, 4, SLAB, left), BF16),
        pltpu.VMEM((4, 4, SLAB, cols - left), BF16),
    ] + dma_sems(12)


class RowsOut:
    def __init__(self, left_ref, right_ref, scratch):
        self.left, self.right = left_ref, right_ref
        self.got = scratch[0:2]
        self.mine = scratch[2:4]
        self.last = scratch[4:6]
        self.sems = tuple(scratch[6:8])
        self.x, self.z = lax.axis_index("dp_0"), lax.axis_index("dp_1")
        self.along_x, self.along_z = line_peers()

    def peers(self):
        return [peer for peer, _ in self.along_x + self.along_z]

    def start(self):
        self.first = []
        for k, (peer, at) in enumerate(self.along_x):
            part = self.left.at[at]
            self.first.append(send(part, self.got[0].at[k], self.sems, k, peer))
        for k, (peer, at) in enumerate(self.along_z):
            part = self.right.at[:, at]
            self.first.append(send(part, self.got[1].at[k], self.sems, 3 + k, peer))

    def middle(self):
        self.second = []
        for side, peers in ((0, self.along_z), (1, self.along_x)):
            for copy in self.first[3 * side : 3 * side + 3]:
                copy.wait_recv()
            got, mine = self.got[side], self.mine[side]

            @pl.loop(0, 4)
            def _(k):
                own = self.right[k, self.z] if side else self.left[self.x, k]
                total = own.astype(F32)
                for source in range(3):
                    total = total + got[source, k].astype(F32)
                mine[k] = total.astype(BF16)

            for k, (peer, at) in enumerate(peers):
                part = mine.at[at]
                copy = send(part, self.last[side].at[k], self.sems, 6 + 3 * side + k, peer)
                self.second.append(copy)

    def end(self, out_ref):
        cut = self.left.shape[3]
        for copy in self.second:
            copy.wait_recv()
        for side, own, cols in ((0, self.z, slice(0, cut)), (1, self.x, slice(cut, None))):
            total = self.mine[side][own].astype(F32)
            for source in range(3):
                total = total + self.last[side][source].astype(F32)
            out_ref[:, cols] = total.astype(BF16)
        for copy in self.first + self.second:
            copy.wait_send()


def rows_out_scratch(cols):
    widths = (CUT[cols], cols - CUT[cols])
    return (
        [pltpu.VMEM((3, 4, SLAB, w), BF16) for w in widths]
        + [pltpu.VMEM((4, SLAB, w), BF16) for w in widths]
        + [pltpu.VMEM((3, SLAB, w), BF16) for w in widths]
        + dma_sems(12)
    )


def slab_shapes(cols):
    widths = (CUT[cols], cols - CUT[cols])
    return tuple(jax.ShapeDtypeStruct((16, SLAB, w), BF16) for w in widths)


def slabs(pair):
    return [part.reshape(4, 4, *part.shape[1:]) for part in pair]


def write_slabs(whole, left_ref, right_ref):
    cut = left_ref.shape[2]

    @pl.loop(0, 16)
    def _(k):
        rows = whole[pl.ds(pl.multiple_of(k * PART, 8), PART), :]
        rows = jnp.concatenate([rows, jnp.zeros((SLAB - PART, rows.shape[1]), F32)], axis=0)
        rows = rows.astype(BF16)
        left_ref[k] = rows[:, :cut]
        right_ref[k] = rows[:, cut:]


def fetch_kernel(left_ref, right_ref, one_ref, two_ref, *scratch):
    rows = RowsIn(left_ref, right_ref, scratch)
    enter(rows.peers())
    rows.start()
    rows.middle()
    rows.end(one_ref, two_ref)


def weight_shapes(cols):
    widths = (3 * HW, HW) if cols == ATT_COLS else (FW, FW)
    return tuple(jax.ShapeDtypeStruct((D, w), BF16) for w in widths)


def fetch_rows(pair, cols, cid):
    return collective(fetch_kernel, cid, weight_shapes(cols), rows_in_scratch(cols), *pair)


def reduce_kernel(left_ref, right_ref, out_ref, *scratch):
    rows = RowsOut(left_ref, right_ref, scratch)
    enter(rows.peers())
    rows.start()
    rows.middle()
    rows.end(out_ref)


def reduce_rows(pair, cols, cid):
    out = jax.ShapeDtypeStruct((SLAB, cols), BF16)
    return collective(reduce_kernel, cid, out, rows_out_scratch(cols), *slabs(pair))


class Ring:
    def __init__(self, tokens, scratch):
        self.tokens = tokens
        self.half = (tokens // 2 + 15) // 16 * 16
        self.kept, self.sib_out, self.sib_in, self.out, self.got = scratch[:5]
        self.far_low, self.far_high = scratch[5:7]
        self.sems = tuple(scratch[7:9])
        c, y = lax.axis_index("tx"), lax.axis_index("ty")
        self.sib, self.up, self.down, _ = ring_peers()
        self.own = [c * 4 + lax.rem(y + d, 4) for d in range(4)]
        self.other = [(1 - c) * 4 + lax.rem(y + d, 4) for d in range(4)]
        self.sent = []

    def peers(self):
        return [self.sib, self.up, self.down]

    def send(self, src, dst, k, peer):
        copy = send(src, dst, self.sems, k, peer)
        self.sent.append(copy)
        return copy

    def rows(self, index, start=0, stop=None):
        stop = self.tokens if stop is None else stop
        at = pl.multiple_of(index * self.tokens + start, 16)
        return pl.ds(at, stop - start)

    def gather(self, x_ref, all_ref, prepare, visit, between=None):
        half, tokens = self.half, self.tokens
        me, above, across, below = self.own
        first, last = slice(0, half), slice(half, tokens)

        def pass_on(index, k, peer, start=0, stop=None):
            part = all_ref.at[self.rows(index, start, stop)]
            return self.send(part, part, k, peer)

        def own_part(rows, k, peer):
            part = all_ref.at[self.rows(me, rows.start, rows.stop)]
            return self.send(x_ref.at[rows], part, k, peer)

        a1 = own_part(first, 0, self.up)
        b1 = own_part(last, 1, self.down)
        a2 = own_part(last, 2, self.up)
        b2 = own_part(first, 3, self.down)
        s0 = self.send(x_ref, all_ref.at[self.rows(me)], 4, self.sib)
        all_ref[self.rows(me), :] = x_ref[...]
        prepare()
        visit(True, 0)
        s0.wait_recv()
        visit(False, 0)
        a1.wait_recv()
        f1 = pass_on(below, 5, self.up, 0, half)
        b1.wait_recv()
        f2 = pass_on(above, 6, self.down, half, tokens)
        a2.wait_recv()
        s1 = pass_on(below, 7, self.sib)
        b2.wait_recv()
        s2 = pass_on(above, 8, self.sib)
        if between:
            between()
        visit(True, 3)
        visit(True, 1)
        s1.wait_recv()
        visit(False, 3)
        s2.wait_recv()
        visit(False, 1)
        f1.wait_recv()
        f2.wait_recv()
        s3 = pass_on(across, 9, self.sib)
        visit(True, 2)
        s3.wait_recv()
        visit(False, 2)

    def put(self, own, d, value):
        if own:
            self.kept[d] = value
        else:
            self.sib_out[d] = value.astype(BF16)
            self.swaps[d] = self.send(self.sib_out.at[d], self.sib_in.at[d], 10 + d, self.sib)

    def start_sums(self):
        self.swaps = {}

    def chip_sum(self, d):
        self.swaps[d].wait_recv()
        return self.kept[d] + self.sib_in[d].astype(F32)

    def near(self):
        half = self.half
        first, last = slice(0, half), slice(half, self.tokens)
        total = self.chip_sum(1)
        self.kept[1] = total
        self.out[0, last] = total[half:].astype(BF16)
        self.n1 = self.send(self.out.at[0, last], self.got.at[0, last], 14, self.up)
        total = self.chip_sum(3)
        self.kept[3] = total
        self.out[1, first] = total[:half].astype(BF16)
        self.n2 = self.send(self.out.at[1, first], self.got.at[1, first], 15, self.down)

    def far(self):
        half = self.half
        self.out[2] = self.chip_sum(2).astype(BF16)
        self.f1 = self.send(self.out.at[2, 0:half], self.far_low, 16, self.up)
        self.f2 = self.send(self.out.at[2, half : self.tokens], self.far_high, 17, self.down)

    def relay(self):
        half = self.half
        first, last = slice(0, half), slice(half, self.tokens)
        self.f1.wait_recv()
        self.out[0, first] = (self.kept[1, first] + self.far_low[...].astype(F32)).astype(BF16)
        self.r1 = self.send(self.out.at[0, first], self.got.at[0, first], 18, self.up)
        self.f2.wait_recv()
        self.out[1, last] = (self.kept[3, last] + self.far_high[...].astype(F32)).astype(BF16)
        self.r2 = self.send(self.out.at[1, last], self.got.at[1, last], 19, self.down)

    def total(self):
        value = self.chip_sum(0)
        for copy in (self.n1, self.n2, self.r1, self.r2):
            copy.wait_recv()
        return value + self.got[0].astype(F32) + self.got[1].astype(F32)

    def leave(self):
        for copy in self.sent:
            copy.wait_send()


def dot_nn(left, right):
    return lax.dot_general(left, right, (((1,), (0,)), ((), ())), preferred_element_type=F32)


def dot_nt(left, right):
    return lax.dot_general(left, right, (((1,), (1,)), ((), ())), preferred_element_type=F32)


def dot_tn(left, right):
    return lax.dot_general(left, right, (((0,), (0,)), ((), ())), preferred_element_type=F32)


def gelu_both(pre):
    root = 0.7978845608028654
    square = pre * pre
    bent = jnp.tanh(root * pre * (1.0 + 0.044715 * square))
    value = 0.5 * pre * (1.0 + bent)
    slope = 0.5 * (1.0 + bent) + 0.5 * pre * (1.0 - bent * bent) * root * (1.0 + 0.134145 * square)
    return value, slope


def sum_rows(value):
    return jnp.sum(value, axis=0, keepdims=True)


def ffn_forward_kernel(
    x_ref, vec_ref, bias_ref, we_ref, wr_ref, next_left, next_right,
    out_ref, mlp_ref, next_one, next_two, all_out, hid_out, slope_out,
    x16, all_ref, hid_ref, slope_ref, move_sems, *scratch
):
    tokens = x_ref.shape[0]
    ring = Ring(tokens, scratch[:9])
    rows_in = RowsIn(next_left, next_right, scratch[9:]) if scratch[9:] else None
    moves = Moves(move_sems)
    peers = ring.peers() + (rows_in.peers() if rows_in else [])
    greet(peers)
    normed, _ = layer_stats(x_ref[...])
    x16[...] = (normed * (1.0 + vec_ref[1:2]) + vec_ref[0:1]).astype(BF16)
    met(peers)
    ring.start_sums()

    def prepare():
        if rows_in:
            rows_in.start()

    def visit(own, d):
        rows = ring.rows((ring.own if own else ring.other)[d])
        pre = dot_nn(all_ref[rows, :], we_ref[...]) + bias_ref[...]
        value, slope = gelu_both(pre)
        hidden = value.astype(BF16)
        hid_ref[rows, :] = hidden
        slope_ref[rows, :] = slope.astype(BF16)
        ring.put(own, d, dot_nt(hidden, wr_ref[...]))
        if not own and d == 1:
            ring.near()

    ring.gather(x16, all_ref, prepare, visit, rows_in.middle if rows_in else None)
    ring.far()
    moves.start(0, all_ref, all_out)
    moves.start(1, hid_ref, hid_out)
    moves.start(2, slope_ref, slope_out)
    ring.relay()
    if rows_in:
        rows_in.end(next_one, next_two)
    mlp = ring.total() + vec_ref[3:4]
    mlp_ref[...] = mlp
    out_ref[...] = x_ref[...] + vec_ref[2:3] * mlp
    ring.leave()
    moves.finish()


def ffn_forward_last_kernel(
    x_ref, vec_ref, bias_ref, we_ref, wr_ref, out_ref, mlp_ref, all_out, hid_out, slope_out, *scratch
):
    ffn_forward_kernel(
        x_ref, vec_ref, bias_ref, we_ref, wr_ref, None, None,
        out_ref, mlp_ref, None, None, all_out, hid_out, slope_out, *scratch
    )


def ffn_forward(x, vecs, bias, we, wr, following, cid):
    tokens = x.shape[0]
    saved = [(8 * tokens, D), (8 * tokens, FW), (8 * tokens, FW)]
    outs = (
        jax.ShapeDtypeStruct((tokens, D), F32),
        jax.ShapeDtypeStruct((tokens, D), F32),
        *(weight_shapes(ATT_COLS) if following else ()),
        *(jax.ShapeDtypeStruct(shape, BF16) for shape in saved),
    )
    scratch = [pltpu.VMEM((tokens, D), BF16)]
    scratch += [pltpu.VMEM(shape, BF16) for shape in saved]
    scratch += [pltpu.SemaphoreType.DMA((3,))] + ring_scratch(tokens)
    kernel = ffn_forward_last_kernel
    if following:
        scratch += rows_in_scratch(ATT_COLS)
        kernel = ffn_forward_kernel
    operands = (x, vecs, bias, we, wr, *following)
    return collective(kernel, cid, outs, scratch, *operands, far_out=3)


def ffn_backward_kernel(
    g_ref, x_ref, mlp_ref, vec_ref, valid_ref, we_ref, wr_ref, *refs
):
    tokens = x_ref.shape[0]
    refs = list(refs)
    pending = (refs.pop(0), refs.pop(0)) if len(refs) > 30 else None
    second_in, hid_in, slope_in, out_ref, vecs_ref, bias_ref, dw_left, dw_right = refs[:8]
    refs = refs[8:]
    summed = refs.pop(0) if pending else None
    g16, g_all, pre_all, second_ref, hid_ref, slope_ref, whole, move_sems = refs[:8]
    ring = Ring(tokens, refs[8:17])
    rows_out = RowsOut(*pending, refs[17:]) if pending else None
    moves = Moves(move_sems)
    peers = ring.peers() + (rows_out.peers() if rows_out else [])
    greet(peers)
    moves.start(0, slope_in, slope_ref)
    moves.start(1, hid_in, hid_ref)
    moves.start(2, second_in, second_ref)
    grad = g_ref[...] * valid_ref[...]
    g16[...] = (grad * vec_ref[2:3]).astype(BF16)
    met(peers)
    ring.start_sums()
    bias_ref[...] = jnp.zeros_like(bias_ref)

    def prepare():
        if rows_out:
            rows_out.start()
        moves.wait(0)

    def visit(own, d):
        rows = ring.rows((ring.own if own else ring.other)[d])
        pre_grad = (
            dot_nn(g_all[rows, :], wr_ref[...]) * slope_ref[rows, :].astype(F32)
        ).astype(BF16)
        pre_all[rows, :] = pre_grad
        bias_ref[...] += sum_rows(pre_grad.astype(F32))
        ring.put(own, d, dot_nt(pre_grad, we_ref[...]))
        if not own and d == 1:
            ring.near()

    ring.gather(g16, g_all, prepare, visit)
    ring.far()
    vecs_ref[2:3] = sum_rows(grad * mlp_ref[...])
    vecs_ref[3:4] = sum_rows(g16[...].astype(F32))
    vecs_ref[4:8] = jnp.zeros((4, D), F32)
    if rows_out:
        rows_out.middle()
    ring.relay()
    moves.finish()

    @pl.loop(0, D // 128)
    def _(k):
        at = pl.ds(pl.multiple_of(k * 128, 128), 128)
        whole[at, :] = jnp.concatenate(
            [
                dot_tn(second_ref[:, at], pre_all[...]),
                dot_tn(g_all[:, at], hid_ref[...]),
            ],
            axis=1,
        )

    write_slabs(whole, dw_left, dw_right)
    if rows_out:
        rows_out.end(summed)
    second_grad = ring.total()
    normed, inv_std = layer_stats(x_ref[...])
    vecs_ref[0:1] = sum_rows(second_grad)
    vecs_ref[1:2] = sum_rows(second_grad * normed)
    out_ref[...] = grad + layer_back(second_grad * (1.0 + vec_ref[1:2]), normed, inv_std)
    ring.leave()


def ffn_backward(g, x, mlp, vecs, valid, second, hid, slope, we, wr, pending, cid):
    tokens = x.shape[0]
    outs = (
        jax.ShapeDtypeStruct((tokens, D), F32),
        jax.ShapeDtypeStruct((8, D), F32),
        jax.ShapeDtypeStruct((1, FW), F32),
        *slab_shapes(FFN_COLS),
        *((jax.ShapeDtypeStruct((SLAB, ATT_COLS), BF16),) if pending else ()),
    )
    scratch = [
        pltpu.VMEM((tokens, D), BF16),
        pltpu.VMEM((8 * tokens, D), BF16),
        pltpu.VMEM((8 * tokens, FW), BF16),
        pltpu.VMEM((8 * tokens, D), BF16),
        pltpu.VMEM((8 * tokens, FW), BF16),
        pltpu.VMEM((8 * tokens, FW), BF16),
        pltpu.VMEM((D, FFN_COLS), F32),
        pltpu.SemaphoreType.DMA((3,)),
    ] + ring_scratch(tokens)
    if pending:
        scratch += rows_out_scratch(ATT_COLS)
    operands = (g, x, mlp, vecs, valid, we, wr, *pending, second, hid, slope)
    return collective(ffn_backward_kernel, cid, outs, scratch, *operands, far_in=3)


HEAD = D // HEADS
SCALE = HEAD ** (-0.5)


def head_cols(h, start=0):
    return slice(start + h * HEAD, start + (h + 1) * HEAD)


def attn_forward_kernel(
    x_ref, vec_ref, bias_ref, mask_ref, wqkv_ref, wm_ref, next_left, next_right,
    out_ref, branch_ref, next_one, next_two, *refs
):
    outs, (x16, *kept, move_sems), scratch = refs[:6], refs[6:14], refs[14:]
    all_ref, q_ref, k_ref, v_ref, lse_ref, att_ref = kept
    tokens = x_ref.shape[0]
    ring = Ring(tokens, scratch[:9])
    rows_in = RowsIn(next_left, next_right, scratch[9:])
    moves = Moves(move_sems)
    peers = ring.peers() + rows_in.peers()
    greet(peers)
    normed, _ = layer_stats(x_ref[...])
    x16[...] = (normed * (1.0 + vec_ref[1:2]) + vec_ref[0:1]).astype(BF16)
    met(peers)
    ring.start_sums()

    def visit(own, d):
        rows = ring.rows((ring.own if own else ring.other)[d])
        joined = (dot_nn(all_ref[rows, :], wqkv_ref[...]) + bias_ref[...]).astype(BF16)
        for h in range(2):
            q_ref[h, rows, :] = joined[:, head_cols(h)]
            k_ref[h, rows, :] = joined[:, head_cols(h, HW)]
            v_ref[h, rows, :] = joined[:, head_cols(h, 2 * HW)]

    def attend(own, d):
        rows = ring.rows((ring.own if own else ring.other)[d])
        parts = []
        for h in range(2):
            scores = dot_nt(q_ref[h, rows, :], k_ref[h]) * SCALE + mask_ref[...]
            highest = jnp.max(scores, axis=-1, keepdims=True)
            shifted = jnp.exp(scores - highest)
            summed = jnp.sum(shifted, axis=-1, keepdims=True)
            probs = (shifted * (1.0 / summed)).astype(BF16)
            lse_ref[rows, h : h + 1] = highest + jnp.log(summed)
            parts.append(dot_nn(probs, v_ref[h]).astype(BF16))
        attended = jnp.concatenate(parts, axis=1)
        att_ref[rows, :] = attended
        ring.put(own, d, dot_nt(attended, wm_ref[...]))

    ring.gather(x16, all_ref, rows_in.start, visit, rows_in.middle)
    attend(False, 2)
    attend(True, 2)
    ring.far()
    for k in range(4):
        moves.start(k, kept[k], outs[k])
    for d in (1, 3):
        attend(False, d)
        attend(True, d)
    ring.near()
    ring.relay()
    attend(False, 0)
    attend(True, 0)
    for k in range(4, 6):
        moves.start(k, kept[k], outs[k])
    rows_in.end(next_one, next_two)
    branch = ring.total() + vec_ref[3:4]
    branch_ref[...] = branch
    out_ref[...] = x_ref[...] + vec_ref[2:3] * branch
    ring.leave()
    moves.finish()


def kept_shapes(tokens):
    heads = ((2, 8 * tokens, HEAD), BF16)
    return (
        ((8 * tokens, D), BF16),
        heads,
        heads,
        heads,
        ((8 * tokens, 2), F32),
        ((8 * tokens, HW), BF16),
    )


def attn_forward(x, vecs, bias, mask, wqkv, wm, following, cid):
    tokens = x.shape[0]
    outs = (
        jax.ShapeDtypeStruct((tokens, D), F32),
        jax.ShapeDtypeStruct((tokens, D), F32),
        *weight_shapes(FFN_COLS),
        *(jax.ShapeDtypeStruct(*shape) for shape in kept_shapes(tokens)),
    )
    scratch = [pltpu.VMEM((tokens, D), BF16)]
    scratch += [pltpu.VMEM(*shape) for shape in kept_shapes(tokens)]
    scratch += [pltpu.SemaphoreType.DMA((6,))] + ring_scratch(tokens) + rows_in_scratch(FFN_COLS)
    operands = (x, vecs, bias, mask, wqkv, wm, *following)
    return collective(attn_forward_kernel, cid, outs, scratch, *operands, far_out=6)


def attn_backward_kernel(
    g_ref, x_ref, branch_ref, vec_ref, mask_ref, wqkv_ref, wm_ref, pending_left, pending_right, *refs
):
    ins, (out_ref, vecs_ref, bias_ref, dw_left, dw_right, summed) = refs[:6], refs[6:12]
    g16, g_all, joined, dk, dv, whole = refs[12:18]
    kept, move_sems, scratch = refs[18:24], refs[24], refs[25:]
    in_ref, q_ref, k_ref, v_ref, lse_ref, att_ref = kept
    tokens = x_ref.shape[0]
    ring = Ring(tokens, scratch[:9])
    rows_out = RowsOut(pending_left, pending_right, scratch[9:])
    moves = Moves(move_sems)
    peers = ring.peers() + rows_out.peers()
    greet(peers)
    for k in (1, 2, 3, 4, 5, 0):
        moves.start(k, ins[k], kept[k])
    g16[...] = (g_ref[...] * vec_ref[2:3]).astype(BF16)
    met(peers)
    ring.start_sums()

    def prepare():
        rows_out.start()
        dk[...] = jnp.zeros_like(dk)
        dv[...] = jnp.zeros_like(dv)
        moves.wait(1, 2, 3, 4)

    def visit(own, d):
        rows = ring.rows((ring.own if own else ring.other)[d])
        grad = dot_nn(g_all[rows, :], wm_ref[...]).astype(BF16)
        queries = []
        for h in range(2):
            part = grad[:, head_cols(h)]
            query = q_ref[h, rows, :]
            scores = dot_nt(query, k_ref[h]) * SCALE + mask_ref[...]
            probs = jnp.exp(scores - lse_ref[rows, h : h + 1])
            grad_probs = dot_nt(part, v_ref[h])
            weighted = jnp.sum(probs * grad_probs, axis=-1, keepdims=True)
            score_grad = (probs * (grad_probs - weighted)).astype(BF16)
            queries.append((dot_nn(score_grad, k_ref[h]) * SCALE).astype(BF16))
            dk[h] += dot_tn(score_grad, query)
            dv[h] += dot_tn(probs.astype(BF16), part)
        joined[rows, 0:HW] = jnp.concatenate(queries, axis=1)

    def back(own, d):
        rows = ring.rows((ring.own if own else ring.other)[d])
        ring.put(own, d, dot_nt(joined[rows, :], wqkv_ref[...]))

    ring.gather(g16, g_all, prepare, visit)
    later = [(dk[h] * SCALE).astype(BF16) for h in range(2)] + [dv[h].astype(BF16) for h in range(2)]
    joined[:, HW : 3 * HW] = jnp.concatenate(later, axis=1)
    back(False, 2)
    back(True, 2)
    ring.far()
    for d in (1, 3):
        back(False, d)
        back(True, d)
    ring.near()
    back(False, 0)
    back(True, 0)
    rows_out.middle()
    ring.relay()
    bias_ref[...] = sum_rows(joined[...].astype(F32))
    vecs_ref[2:3] = sum_rows(g_ref[...] * branch_ref[...])
    vecs_ref[3:4] = sum_rows(g16[...].astype(F32))
    vecs_ref[4:8] = jnp.zeros((4, D), F32)
    moves.finish()

    @pl.loop(0, D // 128)
    def _(k):
        at = pl.ds(pl.multiple_of(k * 128, 128), 128)
        whole[at, :] = jnp.concatenate(
            [
                dot_tn(in_ref[:, at], joined[...]),
                dot_tn(g_all[:, at], att_ref[...]),
                jnp.zeros((128, ATT_COLS - 4 * HW), F32),
            ],
            axis=1,
        )

    write_slabs(whole, dw_left, dw_right)
    rows_out.end(summed)
    input_grad = ring.total()
    normed, inv_std = layer_stats(x_ref[...])
    vecs_ref[0:1] = sum_rows(input_grad)
    vecs_ref[1:2] = sum_rows(input_grad * normed)
    out_ref[...] = g_ref[...] + layer_back(input_grad * (1.0 + vec_ref[1:2]), normed, inv_std)
    ring.leave()


def attn_backward(g, x, branch, vecs, mask, kept, wqkv, wm, pending, cid):
    tokens = x.shape[0]
    outs = (
        jax.ShapeDtypeStruct((tokens, D), F32),
        jax.ShapeDtypeStruct((8, D), F32),
        jax.ShapeDtypeStruct((1, 3 * HW), F32),
        *slab_shapes(ATT_COLS),
        jax.ShapeDtypeStruct((SLAB, FFN_COLS), BF16),
    )
    scratch = [
        pltpu.VMEM((tokens, D), BF16),
        pltpu.VMEM((8 * tokens, D), BF16),
        pltpu.VMEM((8 * tokens, 3 * HW), BF16),
        pltpu.VMEM((2, 8 * tokens, HEAD), F32),
        pltpu.VMEM((2, 8 * tokens, HEAD), F32),
        pltpu.VMEM((D, ATT_COLS), F32),
    ]
    scratch += [pltpu.VMEM(*shape) for shape in kept_shapes(tokens)]
    scratch += [pltpu.SemaphoreType.DMA((6,))] + ring_scratch(tokens) + rows_out_scratch(FFN_COLS)
    operands = (g, x, branch, vecs, mask, wqkv, wm, *pending, *kept)
    return collective(attn_backward_kernel, cid, outs, scratch, *operands, far_in=6)


def block_forward(x, mod, attn_w, biases, mask, next_ffn, next_attn, cid):
    attn_b, merge_b, expand_b, reduce_b = (b.astype(F32) for b in biases)
    group = own_group()
    zeros = jnp.zeros((4, D), F32)
    vec_one = jnp.concatenate([mod[0:3], merge_b[None], zeros])
    vec_two = jnp.concatenate([mod[3:6], reduce_b[None], zeros])
    bias = jnp.concatenate(
        [
            lax.dynamic_slice_in_dim(attn_b, group * HW, HW),
            jnp.zeros((HW,), F32),
            lax.dynamic_slice_in_dim(attn_b, D + group * HW, HW),
        ]
    )[None]
    middle, branch, we, wr, *kept = attn_forward(
        x, vec_one, bias, mask, *attn_w, next_ffn, cid
    )
    e_bias = lax.dynamic_slice_in_dim(expand_b, group * FW, FW)[None]
    output, mlp, *more = ffn_forward(middle, vec_two, e_bias, we, wr, next_attn, cid + 1)
    following, more = (more[:2], more[2:]) if next_attn else ((), more)
    params = (*attn_w, we, wr)
    return output, following, params, (x, vec_one, mask, middle, branch, kept, vec_two, mlp, more)


def block_backward(grad, saved, params, valid, pending, cid):
    x, vec_one, mask, middle, branch, kept, vec_two, mlp, more = saved
    wqkv, wm, we, wr = params
    group = own_group()
    grad, mod_two, bias_two, *dw_ffn = ffn_backward(
        grad, middle, mlp, vec_two, valid, *more, we, wr, pending, cid + 2
    )
    dw_ffn, earlier = dw_ffn[:2], dw_ffn[2:]
    grad, mod_one, bias_one, *dw_attn, ffn_rows = attn_backward(
        grad, x, branch, vec_one, mask, kept, wqkv, wm, slabs(dw_ffn), cid + 3
    )
    grad_expand_b = lax.dynamic_update_slice_in_dim(
        jnp.zeros((FF,), F32), bias_two[0], group * FW, 0
    )
    grad_attn_b = lax.dynamic_update_slice_in_dim(
        jnp.zeros((2 * D,), F32), bias_one[0, :HW], group * HW, 0
    )
    grad_attn_b = lax.dynamic_update_slice_in_dim(
        grad_attn_b, bias_one[0, 2 * HW :], D + group * HW, 0
    )
    mod_grad = jnp.concatenate([mod_one[0:3].reshape(-1), mod_two[0:3].reshape(-1)])
    biases = (grad_attn_b, mod_one[3], grad_expand_b, mod_two[3])
    return grad, mod_grad, dw_attn, ffn_rows, earlier, biases


def pack_weights(attention_weight, merge_weight, expand_weight, reduce_weight):
    def by_group(array):
        parts = array.reshape(*array.shape[:-1], 8, array.shape[-1] // 8)
        return jnp.moveaxis(parts, -2, 0)

    attn, merge = by_group(attention_weight), by_group(merge_weight)
    expand, reduce = by_group(expand_weight), by_group(reduce_weight)
    spare = jnp.zeros((8, 9, ATT_COLS - 4 * HW), BF16)
    columns = []
    for b in range(2):
        columns += [attn[:, b].reshape(8, 9, 3 * HW), merge[:, b], spare]
    for b in range(2):
        columns += [expand[:, b], reduce[:, b]]
    return pack_pieces(jnp.concatenate(columns, axis=2))


def pack_pieces(columns):
    pieces = columns.reshape(8, 9, PIECES, PIECE).swapaxes(1, 2)
    return jnp.pad(pieces.reshape(8, 9 * PIECES, PIECE), [(0, 0), (0, 1), (0, 0)])


def unpack_pieces(packed):
    pieces = packed[:, : 9 * PIECES].reshape(8, PIECES, 9, PIECE)
    return pieces.swapaxes(1, 2).reshape(8, 9, ALL_COLS)


def unpack_rows(packed):
    return unpack_pieces(packed).reshape(72, ALL_COLS)


def pack_grads(attn_one, attn_two, ffn_one, ffn_two):
    columns = jnp.concatenate([attn_one, attn_two, ffn_one, ffn_two], axis=1)
    return pack_pieces(columns[:72].reshape(8, 9, ALL_COLS))


def slab_pair(rows, start, cols):
    part = jnp.pad(rows[:, start : start + cols], [(0, SLAB - PART), (0, 0)])
    return part[:, : CUT[cols]], part[:, CUT[cols] :]


def unpack_grads(packed):
    columns = unpack_pieces(packed)

    def whole(at, width, inner):
        parts = columns[:, :, at : at + inner * width].reshape(8, 9, inner, width)
        return parts.transpose(1, 2, 0, 3).reshape(9, inner, 8 * width).astype(F32)

    starts = (0, ATT_COLS), (2 * ATT_COLS, 2 * ATT_COLS + FFN_COLS)
    return (
        jnp.stack([whole(at, HW, 3) for at in starts[0]]),
        jnp.stack([whole(at + 3 * HW, HW, 1)[:, 0] for at in starts[0]]),
        jnp.stack([whole(at, FW, 1)[:, 0] for at in starts[1]]),
        jnp.stack([whole(at + FW, FW, 1)[:, 0] for at in starts[1]]),
    )


def pack_small(parts):
    flat = jnp.concatenate([part.reshape(-1) for part in parts])
    return jnp.pad(flat, (0, 2048 - flat.shape[0])).reshape(16, 128)


def by_owner(array, dim):
    before, after = array.shape[:dim], array.shape[dim + 1 :]
    parts = array.reshape(*before, 128, array.shape[dim] // 128, *after)
    return jnp.moveaxis(parts, dim, 0).reshape(128, -1)


def from_owner(parts, shape, dim):
    split = parts.reshape(128, *shape[:dim], shape[dim] // 128, *shape[dim + 1 :])
    return jnp.moveaxis(split, 0, dim).reshape(shape)


def shards(
    latent,
    condition,
    routed_ids,
    embed_weight,
    embed_bias,
    modulation_weight,
    modulation_bias,
    attention_weight,
    attention_bias,
    merge_weight,
    merge_bias,
    expand_weight,
    expand_bias,
    reduce_weight,
    reduce_bias,
    final_modulation,
    final_offsets,
    unpatch_weight,
    unpatch_bias,
    pred_cotangent,
):
    count = latent.shape[0]
    tile_rows = latent.shape[1] // 2
    tile_cols = latent.shape[2] // 2
    tile_tokens = tile_rows * tile_cols
    rows_tiles = lax.axis_size("tx")
    cols_tiles = lax.axis_size("ty")
    tiles = rows_tiles * cols_tiles
    grid_side = tile_rows * rows_tiles
    row_index = lax.axis_index("tx") * tile_rows + jnp.arange(tile_rows, dtype=jnp.int32)
    col_index = lax.axis_index("ty") * tile_cols + jnp.arange(tile_cols, dtype=jnp.int32)
    token_index = (row_index[:, None] * grid_side + col_index[None, :]).reshape(tile_tokens)
    routed = jnp.sum(
        (routed_ids[:, :, None] == token_index[None, None, :]).astype(jnp.float32), axis=1
    )
    capacity = 7 * tile_tokens // 8
    id_tiles = (
        routed_ids // grid_side // tile_rows * cols_tiles + routed_ids % grid_side // tile_cols
    )
    tile_loads = jnp.sum(
        (id_tiles[:, :, None] == jnp.arange(tiles, dtype=jnp.int32)[None, None, :]).astype(
            jnp.int32
        ),
        axis=1,
    )
    routed_marks = jnp.arange(capacity, dtype=jnp.int32)[None, None, :] < tile_loads[:, :, None]
    routed_marks = routed_marks.astype(jnp.float32).reshape(count, tiles * capacity)
    everyone = jnp.ones((count, tile_tokens), jnp.float32)
    position, owner, valid = compact_plan(routed, capacity)
    width = D
    whole_index = lax.axis_index(DP_TX_TY)
    small_parts = (
        embed_weight,
        embed_bias,
        unpatch_weight,
        attention_bias,
        merge_bias,
        expand_bias,
        reduce_bias,
    )
    cond_rows = jax.nn.silu(condition.astype(F32)).astype(BF16)
    mod_cuts = (6 * D, 12 * D, 14 * D)
    mod_piece = modulation_bias.shape[1]
    final_piece = final_offsets.shape[0]
    placed_bias = jnp.zeros((MOD_ALL,), F32)
    for bias, at in (
        (modulation_bias[0], whole_index * mod_piece),
        (modulation_bias[1], 6 * D + whole_index * mod_piece),
        (final_offsets, 12 * D + whole_index * final_piece),
    ):
        placed_bias = lax.dynamic_update_slice_in_dim(placed_bias, bias.astype(F32), at, 0)
    mod_parts = jnp.concatenate(
        [
            jnp.dot(cond_rows, modulation_weight[0], preferred_element_type=F32),
            jnp.dot(cond_rows, modulation_weight[1], preferred_element_type=F32),
            jnp.dot(cond_rows, final_modulation, preferred_element_type=F32),
        ],
        axis=1,
    )
    mod_parts = jnp.pad(mod_parts + placed_bias[None], [(0, 0), (0, 16384 - MOD_ALL)])
    packed = pack_weights(attention_weight, merge_weight, expand_weight, reduce_weight)
    packed, mods, small = spread(packed, mod_parts.reshape(16, 128, 128), pack_small(small_parts))
    mods = mods.reshape(1, 16384)
    mod_one = mods[:, : 6 * D]
    mod_two = mods[:, 6 * D : 12 * D]
    head_mod = mods[:, 12 * D : 14 * D]
    small = small.transpose(1, 0, 2, 3).reshape(128, 2048)
    pieces = jnp.split(small, [sum(SMALL_IN[:k]) for k in range(1, 8)], axis=1)
    embed_w = from_owner(pieces[0], (16, D), 1)
    embed_b = from_owner(pieces[1], (D,), 0)
    unpatch_w = from_owner(pieces[2], (D, 32), 0)
    attn_b = from_owner(pieces[3], (2, 2 * D), 1)
    merge_b = from_owner(pieces[4], (2, D), 1)
    expand_b = from_owner(pieces[5], (2, FF), 1)
    reduce_b = from_owner(pieces[6], (2, D), 1)
    rows = unpack_rows(packed)
    first_attn = fetch_rows(slab_pair(rows, 0, ATT_COLS), ATT_COLS, 3)
    second_attn_rows = slab_pair(rows, ATT_COLS, ATT_COLS)
    first_ffn_rows = slab_pair(rows, 2 * ATT_COLS, FFN_COLS)
    second_ffn_rows = slab_pair(rows, 2 * ATT_COLS + FFN_COLS, FFN_COLS)
    placed = sincos_table(row_index.astype(jnp.float32), col_index.astype(jnp.float32), width)
    patches = to_patches(latent)
    initial_tokens = (
        jnp.einsum("btp,pd->btd", patches, embed_w, preferred_element_type=jnp.float32)
        + embed_b.astype(jnp.float32)
        + placed[None, :, :]
    )
    first_biases = (attn_b[0], merge_b[0], expand_b[0], reduce_b[0])
    second_biases = (attn_b[1], merge_b[1], expand_b[1], reduce_b[1])
    mask_one = jnp.zeros((1, tiles * tile_tokens), F32)
    mask_two = jnp.where(routed_marks > 0, 0.0, -1e30).astype(F32)
    middle_one, second_attn, first_params, saved_one = block_forward(
        initial_tokens[0],
        mod_one.reshape(6, D),
        first_attn,
        first_biases,
        mask_one,
        first_ffn_rows,
        second_attn_rows,
        10,
    )
    middle_one = middle_one[None]
    selected_rows = pick_rows(middle_one, owner)
    middle_two, _, second_params, saved_two = block_forward(
        selected_rows[0],
        mod_two.reshape(6, D),
        second_attn,
        second_biases,
        mask_two,
        second_ffn_rows,
        (),
        20,
    )
    middle_two = middle_two[None]
    keep_mask = routed[:, :, None] > 0
    ended = jnp.where(keep_mask, pick_rows(middle_two, position), middle_one)
    head_shift = head_mod[:, None, :width]
    head_scale = head_mod[:, None, width:]
    normed_end, inv_end = layer_stats(ended)
    final16 = (normed_end * (1.0 + head_scale) + head_shift).astype(jnp.bfloat16)
    outputs = jnp.einsum(
        "btd,do->bto", final16, unpatch_w, preferred_element_type=jnp.float32
    ) + unpatch_bias.astype(jnp.float32)
    predicted = from_patches(outputs.astype(jnp.bfloat16), tile_rows, tile_cols)
    cotangent = to_patches(pred_cotangent)
    grad_unpatch_w = jnp.einsum(
        "btd,bto->do", final16, cotangent, preferred_element_type=jnp.float32
    )
    grad_unpatch_b = jnp.sum(cotangent.astype(jnp.float32), axis=(0, 1))
    grad_final = jnp.einsum("bto,do->btd", cotangent, unpatch_w, preferred_element_type=jnp.float32)
    head_grad_mod = jnp.concatenate(
        [jnp.sum(grad_final, axis=1), jnp.sum(grad_final * normed_end, axis=1)], axis=-1
    )
    grad_ended = layer_back(grad_final * (1.0 + head_scale), normed_end, inv_end)
    grad_chosen = pick_rows(grad_ended, owner)
    grad_two, mod_grad_two, dw_attn_two, ffn_two, _, biases_two = block_backward(
        grad_chosen[0], saved_two, second_params, valid[0][:, None], (), 20
    )
    grad_middle = jnp.where(keep_mask, pick_rows(grad_two[None], position), grad_ended)
    grad_start, mod_grad_one, dw_attn_one, ffn_one, (attn_two,), biases_one = block_backward(
        grad_middle[0], saved_one, first_params, everyone[0][:, None], slabs(dw_attn_two), 10
    )
    grad_start = grad_start[None]
    attn_one = reduce_rows(dw_attn_one, ATT_COLS, 5)
    start_grad16 = grad_start.astype(jnp.bfloat16)
    grad_embed_w = jnp.einsum(
        "btp,btd->pd", patches, start_grad16, preferred_element_type=jnp.float32
    )
    grad_embed_b = jnp.sum(start_grad16.astype(jnp.float32), axis=(0, 1))
    latent_tokens = jnp.einsum(
        "btd,pd->btp", start_grad16, embed_w, preferred_element_type=jnp.float32
    )
    latent_grad = from_patches(latent_tokens, tile_rows, tile_cols)
    bias_grads = [jnp.stack([biases_one[member], biases_two[member]]) for member in range(4)]
    small_out = jnp.concatenate(
        [
            by_owner(grad_embed_w, 1),
            by_owner(grad_embed_b, 0),
            by_owner(grad_unpatch_w, 0),
            by_owner(bias_grads[0], 1),
            by_owner(bias_grads[1], 1),
            by_owner(bias_grads[2], 1),
            by_owner(bias_grads[3], 1),
            jnp.broadcast_to(grad_unpatch_b[None], (128, 32)),
        ],
        axis=1,
    )
    small_out = jnp.pad(small_out, [(0, 0), (0, 1024 - small_out.shape[1])])
    grad_mods = jnp.concatenate([mod_grad_one, mod_grad_two, head_grad_mod[0]])
    grad_mods = jnp.pad(grad_mods.reshape(8, MOD_ALL // 8), [(0, 0), (0, 2048 - MOD_ALL // 8)])
    packed_grads, mod_back, small_back = finish(
        pack_grads(attn_one, attn_two, ffn_one, ffn_two),
        grad_mods.reshape(8, 16, 128),
        small_out.reshape(16, 8, 8, 128),
    )
    small_back = small_back.reshape(1024)
    small_sizes = (*SMALL_IN, 32)
    small_sums = jnp.split(small_back, [sum(small_sizes[:k]) for k in range(1, 9)])
    mod_back = mod_back.reshape(8, 16, 2048)[:, :, : MOD_ALL // 8]
    mod_back = mod_back.transpose(1, 0, 2).reshape(16, MOD_ALL)
    one16 = mod_back[:, : mod_cuts[0]]
    two16 = mod_back[:, mod_cuts[0] : mod_cuts[1]]
    head16 = mod_back[:, mod_cuts[1] :]
    stacked = unpack_grads(packed_grads)
    mod_weight_grad = jnp.stack(
        [
            jnp.einsum("id,ie->de", cond_rows, one16, preferred_element_type=jnp.float32),
            jnp.einsum("id,ie->de", cond_rows, two16, preferred_element_type=jnp.float32),
        ]
    )
    mod_bias_grad = jnp.stack(
        [
            lax.dynamic_slice_in_dim(
                jnp.sum(one16.astype(jnp.float32), axis=0), whole_index * mod_piece, mod_piece
            ),
            lax.dynamic_slice_in_dim(
                jnp.sum(two16.astype(jnp.float32), axis=0), whole_index * mod_piece, mod_piece
            ),
        ]
    )
    final_mod_grad = jnp.einsum("id,ie->de", cond_rows, head16, preferred_element_type=jnp.float32)
    final_bias_grad = lax.dynamic_slice_in_dim(
        jnp.sum(head16.astype(jnp.float32), axis=0), whole_index * final_piece, final_piece
    )
    cond_terms = (
        jnp.einsum("ie,de->id", one16, modulation_weight[0], preferred_element_type=jnp.float32)
        + jnp.einsum("ie,de->id", two16, modulation_weight[1], preferred_element_type=jnp.float32)
        + jnp.einsum("ie,de->id", head16, final_modulation, preferred_element_type=jnp.float32)
    )
    silu_value, silu_pull = jax.vjp(jax.nn.silu, condition.astype(jnp.float32))
    condition_grad = silu_pull(cond_terms)[0]
    return (
        predicted,
        latent_grad,
        condition_grad,
        small_sums[0].reshape(16, 9),
        small_sums[1],
        mod_weight_grad,
        mod_bias_grad,
        stacked[0],
        small_sums[3].reshape(2, 18),
        stacked[1],
        small_sums[4].reshape(2, 9),
        stacked[2],
        small_sums[5].reshape(2, 36),
        stacked[3],
        small_sums[6].reshape(2, 9),
        final_mod_grad,
        final_bias_grad,
        small_sums[2].reshape(9, 32),
        small_sums[7],
    )


def solution(mesh):
    torus = Mesh(
        mesh.devices.reshape(4, 4, mesh.shape["tx"], mesh.shape["ty"]), ("dp_0", "dp_1", "tx", "ty")
    )
    return jax.shard_map(
        shards,
        mesh=torus,
        in_specs=(
            P(DP, "tx", "ty", None),
            P(None, DP_TX_TY),
            P(DP, None),
            P(None, DP_TX_TY),
            P(DP_TX_TY),
            P(None, DP_TX_TY, None),
            P(None, DP_TX_TY),
            P(None, DP_TX_TY, None, None),
            P(None, DP_TX_TY),
            P(None, DP_TX_TY, None),
            P(None, DP_TX_TY),
            P(None, DP_TX_TY, None),
            P(None, DP_TX_TY),
            P(None, DP_TX_TY, None),
            P(None, DP_TX_TY),
            P(DP_TX_TY, None),
            P(DP_TX_TY),
            P(DP_TX_TY, None),
            P(),
            P(DP, "tx", "ty", None),
        ),
        out_specs=(
            P(DP, "tx", "ty", None),
            P(DP, "tx", "ty", None),
            P(None, DP_TX_TY),
            P(None, DP_TX_TY),
            P(DP_TX_TY),
            P(None, DP_TX_TY, None),
            P(None, DP_TX_TY),
            P(None, DP_TX_TY, None, None),
            P(None, DP_TX_TY),
            P(None, DP_TX_TY, None),
            P(None, DP_TX_TY),
            P(None, DP_TX_TY, None),
            P(None, DP_TX_TY),
            P(None, DP_TX_TY, None),
            P(None, DP_TX_TY),
            P(DP_TX_TY, None),
            P(DP_TX_TY),
            P(DP_TX_TY, None),
            P(),
        ),
        check_vma=False,
    )
```

```python
import functools

import jax
import jax.numpy as jnp
import numpy as np
from jax import lax
from jax.experimental import pallas as pl
from jax.experimental.pallas import tpu as pltpu
from jax.sharding import Mesh
from jax.sharding import PartitionSpec as P

D = 1152
HEADS = 16
FF = 4608
HW = D // 8
FW = FF // 8
DP = ("dp_0", "dp_1")
DP_TX_TY = ("dp_0", "dp_1", "tx", "ty")
MESH = pl.DeviceIdType.MESH
VMEM = pl.BlockSpec(memory_space=pltpu.VMEM)
FAR = pl.BlockSpec(memory_space=pl.ANY)
F32 = jnp.float32
BF16 = jnp.bfloat16
ATT_COLS = 640
FFN_COLS = 2 * FW
ALL_COLS = 2 * (ATT_COLS + FFN_COLS)
PIECE = 512
PIECES = ALL_COLS // PIECE
MOD_ALL = 14 * D
SMALL_IN = (16 * 9, 9, 9 * 32, 2 * 18, 2 * 9, 2 * 36, 2 * 9)


def greet(peers):
    barrier = pltpu.get_barrier_semaphore()
    for peer in peers:
        pl.semaphore_signal(barrier, inc=1, device_id=peer, device_id_type=MESH)


def met(peers):
    pl.semaphore_wait(pltpu.get_barrier_semaphore(), len(peers))


def enter(peers):
    greet(peers)
    met(peers)


def send(src, dst, sems, k, peer):
    copy = pltpu.make_async_remote_copy(
        src_ref=src,
        dst_ref=dst,
        send_sem=sems[0].at[k],
        recv_sem=sems[1].at[k],
        device_id=peer,
        device_id_type=MESH,
    )
    copy.start()
    return copy


def group_peers():
    c, y = lax.axis_index("tx"), lax.axis_index("ty")
    found = []
    for dc in range(2):
        for dy in range(4):
            if dc or dy:
                oc, oy = lax.rem(c + dc, 2), lax.rem(y + dy, 4)
                found.append(({"tx": oc, "ty": oy}, oc * 4 + oy))
    return found


def image_peers():
    x, z = lax.axis_index("dp_0"), lax.axis_index("dp_1")
    found = []
    for dx in range(4):
        for dz in range(4):
            if dx or dz:
                ox, oz = lax.rem(x + dx, 4), lax.rem(z + dz, 4)
                found.append(({"dp_0": ox, "dp_1": oz}, ox * 4 + oz))
    return found


def own_group():
    return lax.axis_index("tx") * 4 + lax.axis_index("ty")


def own_image():
    return lax.axis_index("dp_0") * 4 + lax.axis_index("dp_1")


def dma_sems(n):
    return [pltpu.SemaphoreType.DMA((n,)), pltpu.SemaphoreType.DMA((n,))]


def collective(kernel, cid, outs, scratch, *operands, far_in=0, far_out=0, vmem=56 << 20):
    many = isinstance(outs, tuple)
    near_in = len(operands) - far_in
    near_out = (len(outs) if many else 1) - far_out
    out_specs = (VMEM,) * near_out + (FAR,) * far_out
    return pl.pallas_call(
        kernel,
        out_shape=outs,
        in_specs=[VMEM] * near_in + [FAR] * far_in,
        out_specs=out_specs if many else out_specs[0],
        scratch_shapes=scratch,
        compiler_params=pltpu.CompilerParams(
            collective_id=cid, has_side_effects=True, vmem_limit_bytes=vmem
        ),
    )(*operands)


class Moves:
    def __init__(self, sems):
        self.sems, self.copies = sems, {}

    def start(self, k, src, dst):
        self.copies[k] = pltpu.make_async_copy(src, dst, self.sems.at[k])
        self.copies[k].start()

    def wait(self, *which):
        for k in which:
            self.copies.pop(k).wait()

    def finish(self):
        self.wait(*list(self.copies))


def ring_peers():
    c, y = lax.axis_index("tx"), lax.axis_index("ty")
    return (
        {"tx": 1 - c},
        {"ty": lax.rem(y + 1, 4)},
        {"ty": lax.rem(y + 3, 4)},
        {"ty": lax.rem(y + 2, 4)},
    )


def layer_stats(value_rows):
    centered = value_rows - jnp.mean(value_rows, axis=-1, keepdims=True)
    inv_std = lax.rsqrt(jnp.mean(centered * centered, axis=-1, keepdims=True) + 1e-06)
    return (centered * inv_std, inv_std)


def layer_back(upstream, normed, inv_std):
    return inv_std * (
        upstream
        - jnp.mean(upstream, axis=-1, keepdims=True)
        - normed * jnp.mean(upstream * normed, axis=-1, keepdims=True)
    )


def sincos_table(row_pos, col_pos, width):
    quarter = width // 4
    freqs = jnp.power(10000.0, -jnp.arange(quarter, dtype=jnp.float32) / quarter)
    row_angle = row_pos[:, None] * freqs[None, :]
    col_angle = col_pos[:, None] * freqs[None, :]
    row_embed = jnp.concatenate([jnp.sin(row_angle), jnp.cos(row_angle)], axis=-1)
    col_embed = jnp.concatenate([jnp.sin(col_angle), jnp.cos(col_angle)], axis=-1)
    row_full = jnp.broadcast_to(
        row_embed[:, None, :], (row_pos.shape[0], col_pos.shape[0], width // 2)
    )
    col_full = jnp.broadcast_to(
        col_embed[None, :, :], (row_pos.shape[0], col_pos.shape[0], width // 2)
    )
    return jnp.concatenate([row_full, col_full], axis=-1).reshape(
        row_pos.shape[0] * col_pos.shape[0], width
    )


def to_patches(pixels):
    count, height, breadth, depth = pixels.shape
    shaped = pixels.reshape(count, height // 2, 2, breadth // 2, 2, depth)
    return shaped.transpose(0, 1, 3, 2, 4, 5).reshape(
        count, height // 2 * (breadth // 2), 4 * depth
    )


def from_patches(token_rows, tile_rows, tile_cols):
    count = token_rows.shape[0]
    depth = token_rows.shape[2] // 4
    shaped = token_rows.reshape(count, tile_rows, tile_cols, 2, 2, depth)
    return shaped.transpose(0, 1, 3, 2, 4, 5).reshape(count, 2 * tile_rows, 2 * tile_cols, depth)


def compact_plan(routed, capacity):
    count, tokens = routed.shape
    flags = routed > 0
    position = jnp.cumsum(flags.astype(jnp.int32), axis=1) - 1
    slots = jnp.where(flags, position, capacity)
    batch_index = jnp.broadcast_to(jnp.arange(count, dtype=jnp.int32)[:, None], (count, tokens))
    token_ids = jnp.arange(tokens, dtype=jnp.int32)[None, :]
    owner = (
        jnp.zeros((count, capacity), jnp.int32).at[batch_index, slots].set(token_ids, mode="drop")
    )
    filled = jnp.sum(flags.astype(jnp.int32), axis=1, keepdims=True)
    valid = (jnp.arange(capacity, dtype=jnp.int32)[None, :] < filled).astype(jnp.float32)
    return (jnp.where(flags, position, 0), owner, valid)


def pick_rows(value_rows, index):
    return jax.vmap(lambda table, where: jnp.take(table, where, axis=0))(value_rows, index)


def rows_at(index, tokens):
    return pl.ds(pl.multiple_of(index * tokens, 16), tokens)


def ring_scratch(tokens):
    half = (tokens // 2 + 15) // 16 * 16
    return [
        pltpu.VMEM((4, tokens, D), F32),
        pltpu.VMEM((4, tokens, D), BF16),
        pltpu.VMEM((4, tokens, D), BF16),
        pltpu.VMEM((3, tokens, D), BF16),
        pltpu.VMEM((2, tokens, D), BF16),
        pltpu.VMEM((half, D), BF16),
        pltpu.VMEM((tokens - half, D), BF16),
        pltpu.SemaphoreType.DMA((20,)),
        pltpu.SemaphoreType.DMA((20,)),
    ]


SLAB = 80
PART = D // 16
CUT = {ATT_COLS: 384, FFN_COLS: 640}


def line_peers():
    x, z = lax.axis_index("dp_0"), lax.axis_index("dp_1")
    along_x = [({"dp_0": lax.rem(x + d, 4)}, lax.rem(x + d, 4)) for d in (2, 1, 3)]
    along_z = [({"dp_1": lax.rem(z + d, 4)}, lax.rem(z + d, 4)) for d in (2, 1, 3)]
    return along_x, along_z


class RowsIn:
    def __init__(self, left_ref, right_ref, scratch):
        self.left, self.right = left_ref, right_ref
        self.all_left, self.all_right = scratch[:2]
        self.sems = tuple(scratch[2:4])
        self.x, self.z = lax.axis_index("dp_0"), lax.axis_index("dp_1")
        self.along_x, self.along_z = line_peers()

    def peers(self):
        return [peer for peer, _ in self.along_x + self.along_z]

    def start(self):
        x, z = self.x, self.z
        self.first = []
        for k, (peer, _) in enumerate(self.along_z):
            self.first.append(send(self.left, self.all_left.at[x, z], self.sems, k, peer))
        for k, (peer, _) in enumerate(self.along_x):
            self.first.append(send(self.right, self.all_right.at[x, z], self.sems, 3 + k, peer))
        self.all_left[x, z] = self.left[...]
        self.all_right[x, z] = self.right[...]

    def middle(self):
        left, right = self.all_left.at[self.x], self.all_right.at[:, self.z]
        self.second = []
        for copy in self.first[:3]:
            copy.wait_recv()
        for k, (peer, _) in enumerate(self.along_x):
            self.second.append(send(left, left, self.sems, 6 + k, peer))
        for copy in self.first[3:]:
            copy.wait_recv()
        for k, (peer, _) in enumerate(self.along_z):
            self.second.append(send(right, right, self.sems, 9 + k, peer))

    def end(self, one_ref, two_ref):
        for copy in self.second:
            copy.wait_recv()
        width, other = one_ref.shape[1], two_ref.shape[1]
        cut = self.left.shape[1]

        @pl.loop(0, 8)
        def _(pair):
            x, z = pair // 2, 2 * lax.rem(pair, 2)
            both = []
            for k in range(2):
                parts = [self.all_left[x, z + k], self.all_right[x, z + k]]
                both.append(jnp.concatenate(parts, axis=1).astype(F32)[:PART])
            value = jnp.concatenate(both, axis=0).astype(BF16)
            at = pl.ds(pl.multiple_of(pair * 2 * PART, 16), 2 * PART)
            one_ref[at, :] = value[:, :width]
            two_ref[at, :] = value[:, width : width + other]

        for copy in self.first + self.second:
            copy.wait_send()


def rows_in_scratch(cols):
    left = CUT[cols]
    return [
        pltpu.VMEM((4, 4, SLAB, left), BF16),
        pltpu.VMEM((4, 4, SLAB, cols - left), BF16),
    ] + dma_sems(12)


class RowsOut:
    def __init__(self, left_ref, right_ref, scratch):
        self.left, self.right = left_ref, right_ref
        self.got = scratch[0:2]
        self.mine = scratch[2:4]
        self.last = scratch[4:6]
        self.sems = tuple(scratch[6:8])
        self.x, self.z = lax.axis_index("dp_0"), lax.axis_index("dp_1")
        self.along_x, self.along_z = line_peers()

    def peers(self):
        return [peer for peer, _ in self.along_x + self.along_z]

    def start(self):
        self.first = []
        for k, (peer, at) in enumerate(self.along_x):
            part = self.left.at[at]
            self.first.append(send(part, self.got[0].at[k], self.sems, k, peer))
        for k, (peer, at) in enumerate(self.along_z):
            part = self.right.at[:, at]
            self.first.append(send(part, self.got[1].at[k], self.sems, 3 + k, peer))

    def middle(self):
        self.second = []
        for side, peers in ((0, self.along_z), (1, self.along_x)):
            for copy in self.first[3 * side : 3 * side + 3]:
                copy.wait_recv()
            got, mine = self.got[side], self.mine[side]

            @pl.loop(0, 4)
            def _(k):
                own = self.right[k, self.z] if side else self.left[self.x, k]
                total = own.astype(F32)
                for source in range(3):
                    total = total + got[source, k].astype(F32)
                mine[k] = total.astype(mine.dtype)

            for k, (peer, at) in enumerate(peers):
                part = mine.at[at]
                copy = send(part, self.last[side].at[k], self.sems, 6 + 3 * side + k, peer)
                self.second.append(copy)

    def end(self):
        for copy in self.second:
            copy.wait_recv()
        totals = []
        for side, own in ((0, self.z), (1, self.x)):
            total = self.mine[side][own].astype(F32)
            for source in range(3):
                total = total + self.last[side][source].astype(F32)
            totals.append(total)
        return totals

    def end_rows(self, out_ref):
        cut = self.left.shape[3]
        left, right = self.end()
        out_ref[:, :cut] = left.astype(BF16)
        out_ref[:, cut:] = right.astype(BF16)
        self.leave()

    def leave(self):
        for copy in self.first + self.second:
            copy.wait_send()


def rows_out_scratch(cols):
    return sum_scratch([(SLAB, CUT[cols]), (SLAB, cols - CUT[cols])], BF16)


def sum_scratch(shapes, dtype):
    return (
        [pltpu.VMEM((3, 4, *shape), dtype) for shape in shapes]
        + [pltpu.VMEM((4, *shape), dtype) for shape in shapes]
        + [pltpu.VMEM((3, *shape), dtype) for shape in shapes]
        + dma_sems(12)
    )


def slab_shapes(cols):
    widths = (CUT[cols], cols - CUT[cols])
    return tuple(jax.ShapeDtypeStruct((16, SLAB, w), BF16) for w in widths)


def slabs(pair):
    return [part.reshape(4, 4, *part.shape[1:]) for part in pair]


def write_slabs(whole, left_ref, right_ref):
    cut = left_ref.shape[2]

    @pl.loop(0, 16)
    def _(k):
        rows = whole[pl.ds(pl.multiple_of(k * PART, 8), PART), :]
        rows = jnp.concatenate([rows, jnp.zeros((SLAB - PART, rows.shape[1]), F32)], axis=0)
        rows = rows.astype(BF16)
        left_ref[k] = rows[:, :cut]
        right_ref[k] = rows[:, cut:]


def slab_views(rows_ref, start, cols):
    cut = start + CUT[cols]
    return rows_ref.at[:, start:cut], rows_ref.at[:, cut : start + cols]


def weight_shapes(cols):
    widths = (3 * HW, HW) if cols == ATT_COLS else (FW, FW)
    return tuple(jax.ShapeDtypeStruct((D, w), BF16) for w in widths)


class Ring:
    def __init__(self, tokens, scratch):
        self.tokens = tokens
        self.half = (tokens // 2 + 15) // 16 * 16
        self.kept, self.sib_out, self.sib_in, self.out, self.got = scratch[:5]
        self.far_low, self.far_high = scratch[5:7]
        self.sems = tuple(scratch[7:9])
        c, y = lax.axis_index("tx"), lax.axis_index("ty")
        self.sib, self.up, self.down, _ = ring_peers()
        self.own = [c * 4 + lax.rem(y + d, 4) for d in range(4)]
        self.other = [(1 - c) * 4 + lax.rem(y + d, 4) for d in range(4)]
        self.sent = []

    def peers(self):
        return [self.sib, self.up, self.down]

    def send(self, src, dst, k, peer):
        copy = send(src, dst, self.sems, k, peer)
        self.sent.append(copy)
        return copy

    def rows(self, index, start=0, stop=None):
        stop = self.tokens if stop is None else stop
        at = pl.multiple_of(index * self.tokens + start, 16)
        return pl.ds(at, stop - start)

    def gather(self, x_ref, all_ref, prepare, visit, between=None):
        half, tokens = self.half, self.tokens
        me, above, across, below = self.own
        first, last = slice(0, half), slice(half, tokens)

        def pass_on(index, k, peer, start=0, stop=None):
            part = all_ref.at[self.rows(index, start, stop)]
            return self.send(part, part, k, peer)

        def own_part(rows, k, peer):
            part = all_ref.at[self.rows(me, rows.start, rows.stop)]
            return self.send(x_ref.at[rows], part, k, peer)

        a1 = own_part(first, 0, self.up)
        b1 = own_part(last, 1, self.down)
        a2 = own_part(last, 2, self.up)
        b2 = own_part(first, 3, self.down)
        s0 = self.send(x_ref, all_ref.at[self.rows(me)], 4, self.sib)
        all_ref[self.rows(me), :] = x_ref[...]
        prepare()
        visit(True, 0)
        s0.wait_recv()
        visit(False, 0)
        a1.wait_recv()
        f1 = pass_on(below, 5, self.up, 0, half)
        b1.wait_recv()
        f2 = pass_on(above, 6, self.down, half, tokens)
        a2.wait_recv()
        s1 = pass_on(below, 7, self.sib)
        b2.wait_recv()
        s2 = pass_on(above, 8, self.sib)
        if between:
            between()
        visit(True, 3)
        visit(True, 1)
        s1.wait_recv()
        visit(False, 3)
        s2.wait_recv()
        visit(False, 1)
        f1.wait_recv()
        f2.wait_recv()
        s3 = pass_on(across, 9, self.sib)
        visit(True, 2)
        s3.wait_recv()
        visit(False, 2)

    def put(self, own, d, value):
        if own:
            self.kept[d] = value
        else:
            self.sib_out[d] = value.astype(BF16)
            self.swaps[d] = self.send(self.sib_out.at[d], self.sib_in.at[d], 10 + d, self.sib)

    def start_sums(self):
        self.swaps = {}

    def chip_sum(self, d):
        self.swaps[d].wait_recv()
        return self.kept[d] + self.sib_in[d].astype(F32)

    def near(self):
        half = self.half
        first, last = slice(0, half), slice(half, self.tokens)
        total = self.chip_sum(1)
        self.kept[1] = total
        self.out[0, last] = total[half:].astype(BF16)
        self.n1 = self.send(self.out.at[0, last], self.got.at[0, last], 14, self.up)
        total = self.chip_sum(3)
        self.kept[3] = total
        self.out[1, first] = total[:half].astype(BF16)
        self.n2 = self.send(self.out.at[1, first], self.got.at[1, first], 15, self.down)

    def far(self):
        half = self.half
        self.out[2] = self.chip_sum(2).astype(BF16)
        self.f1 = self.send(self.out.at[2, 0:half], self.far_low, 16, self.up)
        self.f2 = self.send(self.out.at[2, half : self.tokens], self.far_high, 17, self.down)

    def relay(self):
        half = self.half
        first, last = slice(0, half), slice(half, self.tokens)
        self.f1.wait_recv()
        self.out[0, first] = (self.kept[1, first] + self.far_low[...].astype(F32)).astype(BF16)
        self.r1 = self.send(self.out.at[0, first], self.got.at[0, first], 18, self.up)
        self.f2.wait_recv()
        self.out[1, last] = (self.kept[3, last] + self.far_high[...].astype(F32)).astype(BF16)
        self.r2 = self.send(self.out.at[1, last], self.got.at[1, last], 19, self.down)

    def total(self):
        value = self.chip_sum(0)
        for copy in (self.n1, self.n2, self.r1, self.r2):
            copy.wait_recv()
        return value + self.got[0].astype(F32) + self.got[1].astype(F32)

    def leave(self):
        for copy in self.sent:
            copy.wait_send()


def dot_nn(left, right):
    return lax.dot_general(left, right, (((1,), (0,)), ((), ())), preferred_element_type=F32)


def dot_nt(left, right):
    return lax.dot_general(left, right, (((1,), (1,)), ((), ())), preferred_element_type=F32)


def dot_tn(left, right):
    return lax.dot_general(left, right, (((0,), (0,)), ((), ())), preferred_element_type=F32)


def gelu_both(pre):
    root = 0.7978845608028654
    square = pre * pre
    bent = jnp.tanh(root * pre * (1.0 + 0.044715 * square))
    value = 0.5 * pre * (1.0 + bent)
    slope = 0.5 * (1.0 + bent) + 0.5 * pre * (1.0 - bent * bent) * root * (1.0 + 0.134145 * square)
    return value, slope


def sum_rows(value):
    return jnp.sum(value, axis=0, keepdims=True)


def ffn_forward_kernel(
    x_ref, vec_ref, bias_ref, we_ref, wr_ref, rows_ref,
    out_ref, mlp_ref, next_one, next_two, all_out, hid_out, slope_out,
    x16, all_ref, hid_ref, slope_ref, move_sems, *scratch
):
    tokens = x_ref.shape[0]
    ring = Ring(tokens, scratch[:9])
    rows_in = None
    if scratch[9:]:
        rows_in = RowsIn(*slab_views(rows_ref, ATT_COLS, ATT_COLS), scratch[9:])
    moves = Moves(move_sems)
    peers = ring.peers() + (rows_in.peers() if rows_in else [])
    greet(peers)
    normed, _ = layer_stats(x_ref[...])
    x16[...] = (normed * (1.0 + vec_ref[1:2]) + vec_ref[0:1]).astype(BF16)
    met(peers)
    ring.start_sums()

    def prepare():
        if rows_in:
            rows_in.start()

    def visit(own, d):
        rows = ring.rows((ring.own if own else ring.other)[d])
        pre = dot_nn(all_ref[rows, :], we_ref[...]) + bias_ref[...]
        value, slope = gelu_both(pre)
        hidden = value.astype(BF16)
        hid_ref[rows, :] = hidden
        slope_ref[rows, :] = slope.astype(BF16)
        ring.put(own, d, dot_nt(hidden, wr_ref[...]))
        if not own and d == 1:
            ring.near()

    ring.gather(x16, all_ref, prepare, visit, rows_in.middle if rows_in else None)
    ring.far()
    moves.start(0, all_ref, all_out)
    moves.start(1, hid_ref, hid_out)
    moves.start(2, slope_ref, slope_out)
    ring.relay()
    if rows_in:
        rows_in.end(next_one, next_two)
    mlp = ring.total() + vec_ref[3:4]
    mlp_ref[...] = mlp
    out_ref[...] = x_ref[...] + vec_ref[2:3] * mlp
    ring.leave()
    moves.finish()


def ffn_forward_last_kernel(
    x_ref, vec_ref, bias_ref, we_ref, wr_ref, out_ref, mlp_ref, all_out, hid_out, slope_out, *scratch
):
    ffn_forward_kernel(
        x_ref, vec_ref, bias_ref, we_ref, wr_ref, None,
        out_ref, mlp_ref, None, None, all_out, hid_out, slope_out, *scratch
    )


def ffn_forward(x, vecs, bias, we, wr, following, cid):
    tokens = x.shape[0]
    saved = [(8 * tokens, D), (8 * tokens, FW), (8 * tokens, FW)]
    outs = (
        jax.ShapeDtypeStruct((tokens, D), F32),
        jax.ShapeDtypeStruct((tokens, D), F32),
        *(weight_shapes(ATT_COLS) if following is not None else ()),
        *(jax.ShapeDtypeStruct(shape, BF16) for shape in saved),
    )
    scratch = [pltpu.VMEM((tokens, D), BF16)]
    scratch += [pltpu.VMEM(shape, BF16) for shape in saved]
    scratch += [pltpu.SemaphoreType.DMA((3,))] + ring_scratch(tokens)
    kernel = ffn_forward_last_kernel
    if following is not None:
        scratch += rows_in_scratch(ATT_COLS)
        kernel = ffn_forward_kernel
    operands = (x, vecs, bias, we, wr) + (() if following is None else (following,))
    return collective(kernel, cid, outs, scratch, *operands, far_out=3)


def ffn_backward_kernel(
    g_ref, x_ref, mlp_ref, vec_ref, valid_ref, we_ref, wr_ref, *refs
):
    tokens = x_ref.shape[0]
    refs = list(refs)
    pending = (refs.pop(0), refs.pop(0)) if len(refs) > 30 else None
    second_in, hid_in, slope_in, out_ref, vecs_ref, bias_ref, dw_left, dw_right = refs[:8]
    refs = refs[8:]
    summed = refs.pop(0) if pending else None
    g16, g_all, pre_all, second_ref, hid_ref, slope_ref, whole, move_sems = refs[:8]
    ring = Ring(tokens, refs[8:17])
    rows_out = RowsOut(*pending, refs[17:]) if pending else None
    moves = Moves(move_sems)
    peers = ring.peers() + (rows_out.peers() if rows_out else [])
    greet(peers)
    moves.start(0, slope_in, slope_ref)
    moves.start(1, hid_in, hid_ref)
    moves.start(2, second_in, second_ref)
    grad = g_ref[...] * valid_ref[...]
    g16[...] = (grad * vec_ref[2:3]).astype(BF16)
    met(peers)
    ring.start_sums()
    bias_ref[...] = jnp.zeros_like(bias_ref)

    def prepare():
        if rows_out:
            rows_out.start()
        moves.wait(0)

    def visit(own, d):
        rows = ring.rows((ring.own if own else ring.other)[d])
        pre_grad = (
            dot_nn(g_all[rows, :], wr_ref[...]) * slope_ref[rows, :].astype(F32)
        ).astype(BF16)
        pre_all[rows, :] = pre_grad
        bias_ref[...] += sum_rows(pre_grad.astype(F32))
        ring.put(own, d, dot_nt(pre_grad, we_ref[...]))
        if not own and d == 1:
            ring.near()

    ring.gather(g16, g_all, prepare, visit)
    ring.far()
    vecs_ref[2:3] = sum_rows(grad * mlp_ref[...])
    vecs_ref[3:4] = sum_rows(g16[...].astype(F32))
    vecs_ref[4:8] = jnp.zeros((4, D), F32)
    if rows_out:
        rows_out.middle()
    ring.relay()
    moves.finish()

    @pl.loop(0, D // 128)
    def _(k):
        at = pl.ds(pl.multiple_of(k * 128, 128), 128)
        whole[at, :] = jnp.concatenate(
            [
                dot_tn(second_ref[:, at], pre_all[...]),
                dot_tn(g_all[:, at], hid_ref[...]),
            ],
            axis=1,
        )

    write_slabs(whole, dw_left, dw_right)
    if rows_out:
        rows_out.end_rows(summed)
    second_grad = ring.total()
    normed, inv_std = layer_stats(x_ref[...])
    vecs_ref[0:1] = sum_rows(second_grad)
    vecs_ref[1:2] = sum_rows(second_grad * normed)
    out_ref[...] = grad + layer_back(second_grad * (1.0 + vec_ref[1:2]), normed, inv_std)
    ring.leave()


def ffn_backward(g, x, mlp, vecs, valid, second, hid, slope, we, wr, pending, cid):
    tokens = x.shape[0]
    outs = (
        jax.ShapeDtypeStruct((tokens, D), F32),
        jax.ShapeDtypeStruct((8, D), F32),
        jax.ShapeDtypeStruct((1, FW), F32),
        *slab_shapes(FFN_COLS),
        *((jax.ShapeDtypeStruct((SLAB, ATT_COLS), BF16),) if pending else ()),
    )
    scratch = [
        pltpu.VMEM((tokens, D), BF16),
        pltpu.VMEM((8 * tokens, D), BF16),
        pltpu.VMEM((8 * tokens, FW), BF16),
        pltpu.VMEM((8 * tokens, D), BF16),
        pltpu.VMEM((8 * tokens, FW), BF16),
        pltpu.VMEM((8 * tokens, FW), BF16),
        pltpu.VMEM((D, FFN_COLS), F32),
        pltpu.SemaphoreType.DMA((3,)),
    ] + ring_scratch(tokens)
    if pending:
        scratch += rows_out_scratch(ATT_COLS)
    operands = (g, x, mlp, vecs, valid, we, wr, *pending, second, hid, slope)
    return collective(ffn_backward_kernel, cid, outs, scratch, *operands, far_in=3)


def open_kernel(
    w_ref, pick_ref, m_ref, s_ref, rows_ref, one_ref, two_ref, m_out, s_out,
    w_got, m_got, m_sum, ss, rs, *scratch
):
    group = group_peers()
    sib, up, down, far = ring_peers()
    fetch = RowsIn(*slab_views(rows_ref, 0, ATT_COLS), scratch[:4])
    mods = RowsOut(m_ref.at[:, :, 0:64], m_ref.at[:, :, 64:128], scratch[4:])
    enter([peer for peer, _ in group] + fetch.peers())
    sems = (ss, rs)
    me, x, z = own_group(), lax.axis_index("dp_0"), lax.axis_index("dp_1")
    weights = [send(w_ref.at[at], w_got.at[me], sems, k, p) for k, (p, at) in enumerate(group)]
    small = s_out.at[me, x, z]
    first = [send(s_ref, small, sems, 7 + k, p) for k, (p, _) in enumerate(fetch.along_z)]
    mods.start()
    w_got[me] = w_ref[me]
    s_out[me, x, z] = s_ref[...]
    for copy in first:
        copy.wait_recv()
    small = s_out.at[me, x]
    second = [send(small, small, sems, 10 + k, p) for k, (p, _) in enumerate(fetch.along_x)]
    for copy in weights:
        copy.wait_recv()
    received = w_got[...].reshape(8 * w_got.shape[1], PIECE)
    for k in range(PIECES):
        cols = slice(k * PIECE, (k + 1) * PIECE)
        rows_ref[:, cols] = dot_nn(pick_ref[k], received).astype(BF16)
    fetch.start()
    for copy in second:
        copy.wait_recv()
    small = s_out.at[me]
    third = [send(small, small, sems, 13 + k, p) for k, p in enumerate((up, down, far, sib))]
    mods.middle()
    fetch.middle()
    left, right = mods.end()
    m_sum[0:64] = left
    m_sum[64:128] = right

    def chunk(ref, index):
        return ref.at[pl.ds(pl.multiple_of(index * 16, 16), 16)]

    m_first = [
        send(chunk(m_sum, at), m_got.at[me], sems, 20 + k, p) for k, (p, at) in enumerate(group)
    ]
    mine = pl.ds(pl.multiple_of(me * 16, 16), 16)
    m_got[me] = m_sum[mine, :]
    for copy in m_first:
        copy.wait_recv()
    total = m_got[0]
    for k in range(1, 8):
        total = total + m_got[k]
    m_out[mine, :] = total
    part = chunk(m_out, me)
    m_second = [send(part, part, sems, 27 + k, p) for k, (p, _) in enumerate(group)]
    c, y = lax.axis_index("tx"), lax.axis_index("ty")
    fourth = []
    for k, d in enumerate((3, 1, 2)):
        third[k].wait_recv()
        small = s_out.at[c * 4 + lax.rem(y + d, 4)]
        fourth.append(send(small, small, sems, 17 + k, sib))
    fetch.end(one_ref, two_ref)
    for copy in m_second + fourth + third[3:]:
        copy.wait_recv()
    for copy in weights + first + second + third + fourth + m_first + m_second:
        copy.wait_send()
    mods.leave()


def picking():
    picks = np.zeros((PIECES, SLAB, 8 * 64), np.float32)
    for k in range(PIECES):
        for row in range(72):
            picks[k, row, row // 9 * 64 + 9 * k + row % 9] = 1.0
    return picks


def open_up(weights, mods, small):
    outs = (
        jax.ShapeDtypeStruct((SLAB, ALL_COLS), BF16),
        *weight_shapes(ATT_COLS),
        jax.ShapeDtypeStruct((128, 128), F32),
        jax.ShapeDtypeStruct((8, 4, 4, *small.shape), BF16),
    )
    scratch = [
        pltpu.VMEM(weights.shape, BF16),
        pltpu.VMEM((8, 16, 128), F32),
        pltpu.VMEM((128, 128), F32),
    ] + dma_sems(34)
    scratch += rows_in_scratch(ATT_COLS) + sum_scratch([(64, 128), (64, 128)], F32)
    picks = jnp.asarray(picking(), BF16)
    return collective(open_kernel, 1, outs, scratch, weights, picks, mods, small)


EARLY = ATT_COLS + 2 * FFN_COLS
EARLY_PIECES = -(-EARLY // PIECE)
LATE_PIECES = -(-ATT_COLS // PIECE)
LATE_ROWS = 32


def packed_rows(picks_ref, parts, pieces):
    columns = jnp.concatenate(parts, axis=1)
    spare = pieces * PIECE - columns.shape[1]
    columns = jnp.concatenate([columns, jnp.zeros((SLAB, spare), BF16)], axis=1)
    total = jnp.zeros((8 * 64, PIECE), F32)
    for k in range(pieces):
        total = total + dot_tn(picks_ref[k], columns[:, k * PIECE : (k + 1) * PIECE])
    return total.astype(BF16).reshape(8, 64, PIECE)


def finish_kernel(
    left_ref, right_ref, attn_ref, ffn_one_ref, ffn_two_ref, picks_ref, m_ref, s_ref,
    early_out, late_out, m_out, s_out,
    early, late, m_got, s_mine, s_two, late_rows, ss, rs, *scratch
):
    group = group_peers()
    sib, up, down, far = ring_peers()
    rows = RowsOut(left_ref, right_ref, scratch[:8])
    small = RowsOut(s_ref.at[:, :, 0:32], s_ref.at[:, :, 32:64], scratch[8:])
    peers = [peer for peer, _ in group] + rows.peers()
    greet(peers)
    me, x, z = own_group(), lax.axis_index("dp_0"), lax.axis_index("dp_1")
    sems = (ss, rs)
    met(peers)
    rows.start()
    m_first = [send(m_ref.at[at], m_got.at[me], sems, k, p) for k, (p, at) in enumerate(group)]
    small.start()
    early[...] = packed_rows(
        picks_ref, [attn_ref[...], ffn_one_ref[...], ffn_two_ref[...]], EARLY_PIECES
    )
    sent = [send(early.at[at], early_out.at[me], sems, 7 + k, p) for k, (p, at) in enumerate(group)]
    early_out[me] = early[me]
    m_got[me] = m_ref[me]
    for copy in m_first:
        copy.wait_recv()
    total = m_got[0]
    for k in range(1, 8):
        total = total + m_got[k]
    m_out[me, x, z] = total.astype(BF16)
    part = m_out.at[me, x, z]
    m_second = [send(part, part, sems, 14 + k, p) for k, (p, _) in enumerate(rows.along_z)]
    small.middle()
    for copy in m_second:
        copy.wait_recv()
    part = m_out.at[me, x]
    m_third = [send(part, part, sems, 17 + k, p) for k, (p, _) in enumerate(rows.along_x)]
    left, right = small.end()
    s_mine[0:4] = left.reshape(4, 8, 128)
    s_mine[4:8] = right.reshape(4, 8, 128)
    s_last = [send(s_mine.at[at], s_two.at[me], sems, 20 + k, p) for k, (p, at) in enumerate(group)]
    s_two[me] = s_mine[me]
    for copy in m_third:
        copy.wait_recv()
    part = m_out.at[me]
    m_fourth = [send(part, part, sems, 27 + k, p) for k, p in enumerate((up, down, far, sib))]
    rows.middle()
    c, y = lax.axis_index("tx"), lax.axis_index("ty")
    m_fifth = []
    for k, d in enumerate((3, 1, 2)):
        m_fourth[k].wait_recv()
        part = m_out.at[c * 4 + lax.rem(y + d, 4)]
        m_fifth.append(send(part, part, sems, 31 + k, sib))
    for copy in s_last:
        copy.wait_recv()
    total = s_two[0]
    for k in range(1, 8):
        total = total + s_two[k]
    s_out[...] = total
    rows.end_rows(late_rows)
    late[...] = packed_rows(picks_ref, [late_rows[...]], LATE_PIECES)[:, :LATE_ROWS]
    later = [send(late.at[at], late_out.at[me], sems, 34 + k, p) for k, (p, at) in enumerate(group)]
    late_out[me] = late[me]
    for copy in sent + m_fourth[3:] + m_fifth + later:
        copy.wait_recv()
    small.leave()
    for copy in m_first + sent + m_second + m_third + s_last + m_fourth + m_fifth + later:
        copy.wait_send()


def finish(pair, attn, ffn_one, ffn_two, mods, small):
    outs = (
        jax.ShapeDtypeStruct((8, 64, PIECE), BF16),
        jax.ShapeDtypeStruct((8, LATE_ROWS, PIECE), BF16),
        jax.ShapeDtypeStruct((8, 4, 4, 16, 128), BF16),
        jax.ShapeDtypeStruct((8, 128), F32),
    )
    scratch = [
        pltpu.VMEM((8, 64, PIECE), BF16),
        pltpu.VMEM((8, LATE_ROWS, PIECE), BF16),
        pltpu.VMEM((8, 16, 128), F32),
        pltpu.VMEM((8, 8, 128), F32),
        pltpu.VMEM((8, 8, 128), F32),
        pltpu.VMEM((SLAB, ATT_COLS), BF16),
    ] + dma_sems(41)
    scratch += rows_out_scratch(ATT_COLS) + sum_scratch([(32, 128), (32, 128)], F32)
    picks = jnp.asarray(picking(), BF16)
    operands = (*slabs(pair), attn, ffn_one, ffn_two, picks, mods, small)
    return collective(finish_kernel, 2, outs, scratch, *operands)


def unpicking(pieces, height):
    picks = np.zeros((pieces, 128, 8 * height), np.float32)
    for k in range(pieces):
        for group in range(8):
            for row in range(9):
                picks[k, group * 16 + row, group * height + 9 * k + row] = 1.0
    return picks


def close_kernel(
    early_ref, late_ref, early_picks, late_picks, g_ref, cond_ref, mod_ref, final_ref,
    attn_ref, merge_ref, expand_ref, reduce_ref, mod_grad_ref, final_grad_ref, terms_ref, bias_ref,
    early, late
):
    received = early_ref[...].reshape(8 * 64, PIECE)
    for k in range(EARLY_PIECES):
        early[:, k * PIECE : (k + 1) * PIECE] = dot_nn(early_picks[k], received)
    received = late_ref[...].reshape(8 * LATE_ROWS, PIECE)
    for k in range(LATE_PIECES):
        late[:, k * PIECE : (k + 1) * PIECE] = dot_nn(late_picks[k], received)

    def whole(source, start, width):
        parts = [source[g * 16 : g * 16 + 16, start : start + width] for g in range(8)]
        return jnp.concatenate(parts, axis=1)[:9]

    for b, (source, start) in enumerate(((late, 0), (early, 0))):
        for j in range(3):
            attn_ref[b, j] = whole(source, start + j * HW, HW)
        merge_ref[b] = whole(source, start + 3 * HW, HW)
    for b, start in enumerate((ATT_COLS, ATT_COLS + FFN_COLS)):
        expand_ref[b] = whole(early, start, FW)
        reduce_ref[b] = whole(early, start + FW, FW)
    terms = jnp.zeros((16, 9), F32)
    for b in range(3):
        grads = g_ref[:, 6 * b * D : min(6 * b + 6, 14) * D]
        weights = mod_ref[b] if b < 2 else final_ref[...]
        product = dot_tn(cond_ref[...], grads)
        if b < 2:
            mod_grad_ref[b] = product
        else:
            final_grad_ref[...] = product
        terms = terms + dot_nt(grads, weights)
    terms_ref[...] = terms
    bias_ref[...] = sum_rows(g_ref[...].astype(F32))


def close(early, late, grads, cond, mod_weight, final_weight):
    outs = (
        jax.ShapeDtypeStruct((2, 3, 9, D), F32),
        jax.ShapeDtypeStruct((2, 9, D), F32),
        jax.ShapeDtypeStruct((2, 9, FF), F32),
        jax.ShapeDtypeStruct((2, 9, FF), F32),
        jax.ShapeDtypeStruct((2, 9, 6 * D), F32),
        jax.ShapeDtypeStruct((9, 2 * D), F32),
        jax.ShapeDtypeStruct((16, 9), F32),
        jax.ShapeDtypeStruct((1, 16384), F32),
    )
    operands = (
        early,
        late,
        jnp.asarray(unpicking(EARLY_PIECES, 64), BF16),
        jnp.asarray(unpicking(LATE_PIECES, LATE_ROWS), BF16),
        grads,
        cond,
        mod_weight,
        final_weight,
    )
    return pl.pallas_call(
        close_kernel,
        out_shape=outs,
        in_specs=[VMEM] * len(operands),
        out_specs=(VMEM,) * len(outs),
        scratch_shapes=[
            pltpu.VMEM((128, EARLY_PIECES * PIECE), F32),
            pltpu.VMEM((128, LATE_PIECES * PIECE), F32),
        ],
        compiler_params=pltpu.CompilerParams(vmem_limit_bytes=32 << 20),
    )(*operands)


HEAD = D // HEADS
SCALE = HEAD ** (-0.5)


def head_cols(h, start=0):
    return slice(start + h * HEAD, start + (h + 1) * HEAD)


def attn_forward_kernel(
    x_ref, vec_ref, bias_ref, mask_ref, wqkv_ref, wm_ref, rows_ref,
    out_ref, branch_ref, next_one, next_two, *refs, start
):
    outs, (x16, *kept, move_sems), scratch = refs[:6], refs[6:14], refs[14:]
    all_ref, q_ref, k_ref, v_ref, lse_ref, att_ref = kept
    tokens = x_ref.shape[0]
    ring = Ring(tokens, scratch[:9])
    rows_in = RowsIn(*slab_views(rows_ref, start, FFN_COLS), scratch[9:])
    moves = Moves(move_sems)
    peers = ring.peers() + rows_in.peers()
    greet(peers)
    normed, _ = layer_stats(x_ref[...])
    x16[...] = (normed * (1.0 + vec_ref[1:2]) + vec_ref[0:1]).astype(BF16)
    met(peers)
    ring.start_sums()

    def visit(own, d):
        rows = ring.rows((ring.own if own else ring.other)[d])
        joined = (dot_nn(all_ref[rows, :], wqkv_ref[...]) + bias_ref[...]).astype(BF16)
        for h in range(2):
            q_ref[h, rows, :] = joined[:, head_cols(h)]
            k_ref[h, rows, :] = joined[:, head_cols(h, HW)]
            v_ref[h, rows, :] = joined[:, head_cols(h, 2 * HW)]

    def attend(own, d):
        rows = ring.rows((ring.own if own else ring.other)[d])
        parts = []
        for h in range(2):
            scores = dot_nt(q_ref[h, rows, :], k_ref[h]) * SCALE + mask_ref[...]
            highest = jnp.max(scores, axis=-1, keepdims=True)
            shifted = jnp.exp(scores - highest)
            summed = jnp.sum(shifted, axis=-1, keepdims=True)
            probs = (shifted * (1.0 / summed)).astype(BF16)
            lse_ref[rows, h : h + 1] = highest + jnp.log(summed)
            parts.append(dot_nn(probs, v_ref[h]).astype(BF16))
        attended = jnp.concatenate(parts, axis=1)
        att_ref[rows, :] = attended
        ring.put(own, d, dot_nt(attended, wm_ref[...]))

    ring.gather(x16, all_ref, rows_in.start, visit, rows_in.middle)
    attend(False, 2)
    attend(True, 2)
    ring.far()
    for k in range(4):
        moves.start(k, kept[k], outs[k])
    for d in (1, 3):
        attend(False, d)
        attend(True, d)
    ring.near()
    ring.relay()
    attend(False, 0)
    attend(True, 0)
    for k in range(4, 6):
        moves.start(k, kept[k], outs[k])
    rows_in.end(next_one, next_two)
    branch = ring.total() + vec_ref[3:4]
    branch_ref[...] = branch
    out_ref[...] = x_ref[...] + vec_ref[2:3] * branch
    ring.leave()
    moves.finish()


def kept_shapes(tokens):
    heads = ((2, 8 * tokens, HEAD), BF16)
    return (
        ((8 * tokens, D), BF16),
        heads,
        heads,
        heads,
        ((8 * tokens, 2), F32),
        ((8 * tokens, HW), BF16),
    )


def attn_forward(x, vecs, bias, mask, wqkv, wm, rows, start, cid):
    tokens = x.shape[0]
    outs = (
        jax.ShapeDtypeStruct((tokens, D), F32),
        jax.ShapeDtypeStruct((tokens, D), F32),
        *weight_shapes(FFN_COLS),
        *(jax.ShapeDtypeStruct(*shape) for shape in kept_shapes(tokens)),
    )
    scratch = [pltpu.VMEM((tokens, D), BF16)]
    scratch += [pltpu.VMEM(*shape) for shape in kept_shapes(tokens)]
    scratch += [pltpu.SemaphoreType.DMA((6,))] + ring_scratch(tokens) + rows_in_scratch(FFN_COLS)
    operands = (x, vecs, bias, mask, wqkv, wm, rows)
    kernel = functools.partial(attn_forward_kernel, start=start)
    return collective(kernel, cid, outs, scratch, *operands, far_out=6)


def attn_backward_kernel(
    g_ref, x_ref, branch_ref, vec_ref, mask_ref, wqkv_ref, wm_ref, pending_left, pending_right, *refs
):
    ins, (out_ref, vecs_ref, bias_ref, dw_left, dw_right, summed) = refs[:6], refs[6:12]
    g16, g_all, joined, dk, dv, whole = refs[12:18]
    kept, move_sems, scratch = refs[18:24], refs[24], refs[25:]
    in_ref, q_ref, k_ref, v_ref, lse_ref, att_ref = kept
    tokens = x_ref.shape[0]
    ring = Ring(tokens, scratch[:9])
    rows_out = RowsOut(pending_left, pending_right, scratch[9:])
    moves = Moves(move_sems)
    peers = ring.peers() + rows_out.peers()
    greet(peers)
    for k in (1, 2, 3, 4, 5, 0):
        moves.start(k, ins[k], kept[k])
    g16[...] = (g_ref[...] * vec_ref[2:3]).astype(BF16)
    met(peers)
    ring.start_sums()

    def prepare():
        rows_out.start()
        dk[...] = jnp.zeros_like(dk)
        dv[...] = jnp.zeros_like(dv)
        moves.wait(1, 2, 3, 4)

    def visit(own, d):
        rows = ring.rows((ring.own if own else ring.other)[d])
        grad = dot_nn(g_all[rows, :], wm_ref[...]).astype(BF16)
        queries = []
        for h in range(2):
            part = grad[:, head_cols(h)]
            query = q_ref[h, rows, :]
            scores = dot_nt(query, k_ref[h]) * SCALE + mask_ref[...]
            probs = jnp.exp(scores - lse_ref[rows, h : h + 1])
            grad_probs = dot_nt(part, v_ref[h])
            weighted = jnp.sum(probs * grad_probs, axis=-1, keepdims=True)
            score_grad = (probs * (grad_probs - weighted)).astype(BF16)
            queries.append((dot_nn(score_grad, k_ref[h]) * SCALE).astype(BF16))
            dk[h] += dot_tn(score_grad, query)
            dv[h] += dot_tn(probs.astype(BF16), part)
        joined[rows, 0:HW] = jnp.concatenate(queries, axis=1)

    def back(own, d):
        rows = ring.rows((ring.own if own else ring.other)[d])
        ring.put(own, d, dot_nt(joined[rows, :], wqkv_ref[...]))

    ring.gather(g16, g_all, prepare, visit)
    later = [(dk[h] * SCALE).astype(BF16) for h in range(2)] + [dv[h].astype(BF16) for h in range(2)]
    joined[:, HW : 3 * HW] = jnp.concatenate(later, axis=1)
    back(False, 2)
    back(True, 2)
    ring.far()
    for d in (1, 3):
        back(False, d)
        back(True, d)
    ring.near()
    back(False, 0)
    back(True, 0)
    rows_out.middle()
    ring.relay()
    bias_ref[...] = sum_rows(joined[...].astype(F32))
    vecs_ref[2:3] = sum_rows(g_ref[...] * branch_ref[...])
    vecs_ref[3:4] = sum_rows(g16[...].astype(F32))
    vecs_ref[4:8] = jnp.zeros((4, D), F32)
    moves.finish()

    @pl.loop(0, D // 128)
    def _(k):
        at = pl.ds(pl.multiple_of(k * 128, 128), 128)
        whole[at, :] = jnp.concatenate(
            [
                dot_tn(in_ref[:, at], joined[...]),
                dot_tn(g_all[:, at], att_ref[...]),
                jnp.zeros((128, ATT_COLS - 4 * HW), F32),
            ],
            axis=1,
        )

    write_slabs(whole, dw_left, dw_right)
    rows_out.end_rows(summed)
    input_grad = ring.total()
    normed, inv_std = layer_stats(x_ref[...])
    vecs_ref[0:1] = sum_rows(input_grad)
    vecs_ref[1:2] = sum_rows(input_grad * normed)
    out_ref[...] = g_ref[...] + layer_back(input_grad * (1.0 + vec_ref[1:2]), normed, inv_std)
    ring.leave()


def attn_backward(g, x, branch, vecs, mask, kept, wqkv, wm, pending, cid):
    tokens = x.shape[0]
    outs = (
        jax.ShapeDtypeStruct((tokens, D), F32),
        jax.ShapeDtypeStruct((8, D), F32),
        jax.ShapeDtypeStruct((1, 3 * HW), F32),
        *slab_shapes(ATT_COLS),
        jax.ShapeDtypeStruct((SLAB, FFN_COLS), BF16),
    )
    scratch = [
        pltpu.VMEM((tokens, D), BF16),
        pltpu.VMEM((8 * tokens, D), BF16),
        pltpu.VMEM((8 * tokens, 3 * HW), BF16),
        pltpu.VMEM((2, 8 * tokens, HEAD), F32),
        pltpu.VMEM((2, 8 * tokens, HEAD), F32),
        pltpu.VMEM((D, ATT_COLS), F32),
    ]
    scratch += [pltpu.VMEM(*shape) for shape in kept_shapes(tokens)]
    scratch += [pltpu.SemaphoreType.DMA((6,))] + ring_scratch(tokens) + rows_out_scratch(FFN_COLS)
    operands = (g, x, branch, vecs, mask, wqkv, wm, *pending, *kept)
    return collective(attn_backward_kernel, cid, outs, scratch, *operands, far_in=6)


def block_forward(x, mod, attn_w, biases, mask, rows, start, more_blocks, cid):
    attn_b, merge_b, expand_b, reduce_b = (b.astype(F32) for b in biases)
    group = own_group()
    zeros = jnp.zeros((4, D), F32)
    vec_one = jnp.concatenate([mod[0:3], merge_b[None], zeros])
    vec_two = jnp.concatenate([mod[3:6], reduce_b[None], zeros])
    bias = jnp.concatenate(
        [
            lax.dynamic_slice_in_dim(attn_b, group * HW, HW),
            jnp.zeros((HW,), F32),
            lax.dynamic_slice_in_dim(attn_b, D + group * HW, HW),
        ]
    )[None]
    middle, branch, we, wr, *kept = attn_forward(
        x, vec_one, bias, mask, *attn_w, rows, start, cid
    )
    e_bias = lax.dynamic_slice_in_dim(expand_b, group * FW, FW)[None]
    next_rows = rows if more_blocks else None
    output, mlp, *more = ffn_forward(middle, vec_two, e_bias, we, wr, next_rows, cid + 1)
    following, more = (more[:2], more[2:]) if more_blocks else ((), more)
    params = (*attn_w, we, wr)
    return output, following, params, (x, vec_one, mask, middle, branch, kept, vec_two, mlp, more)


def block_backward(grad, saved, params, valid, pending, cid):
    x, vec_one, mask, middle, branch, kept, vec_two, mlp, more = saved
    wqkv, wm, we, wr = params
    group = own_group()
    grad, mod_two, bias_two, *dw_ffn = ffn_backward(
        grad, middle, mlp, vec_two, valid, *more, we, wr, pending, cid + 2
    )
    dw_ffn, earlier = dw_ffn[:2], dw_ffn[2:]
    grad, mod_one, bias_one, *dw_attn, ffn_rows = attn_backward(
        grad, x, branch, vec_one, mask, kept, wqkv, wm, slabs(dw_ffn), cid + 3
    )
    grad_expand_b = lax.dynamic_update_slice_in_dim(
        jnp.zeros((FF,), F32), bias_two[0], group * FW, 0
    )
    grad_attn_b = lax.dynamic_update_slice_in_dim(
        jnp.zeros((2 * D,), F32), bias_one[0, :HW], group * HW, 0
    )
    grad_attn_b = lax.dynamic_update_slice_in_dim(
        grad_attn_b, bias_one[0, 2 * HW :], D + group * HW, 0
    )
    mod_grad = jnp.concatenate([mod_one[0:3].reshape(-1), mod_two[0:3].reshape(-1)])
    biases = (grad_attn_b, mod_one[3], grad_expand_b, mod_two[3])
    return grad, mod_grad, dw_attn, ffn_rows, earlier, biases


def pack_weights(attention_weight, merge_weight, expand_weight, reduce_weight):
    def by_group(array):
        parts = array.reshape(*array.shape[:-1], 8, array.shape[-1] // 8)
        return jnp.moveaxis(parts, -2, 0)

    attn, merge = by_group(attention_weight), by_group(merge_weight)
    expand, reduce = by_group(expand_weight), by_group(reduce_weight)
    spare = jnp.zeros((8, 9, ATT_COLS - 4 * HW), BF16)
    columns = []
    for b in range(2):
        columns += [attn[:, b].reshape(8, 9, 3 * HW), merge[:, b], spare]
    for b in range(2):
        columns += [expand[:, b], reduce[:, b]]
    return pack_pieces(jnp.concatenate(columns, axis=2))


def pack_pieces(columns):
    pieces = columns.reshape(8, 9, PIECES, PIECE).swapaxes(1, 2)
    return jnp.pad(pieces.reshape(8, 9 * PIECES, PIECE), [(0, 0), (0, 1), (0, 0)])


def pack_small(parts):
    flat = jnp.concatenate([part.reshape(-1) for part in parts])
    return jnp.pad(flat, (0, 2048 - flat.shape[0])).reshape(16, 128)


def by_owner(array, dim):
    before, after = array.shape[:dim], array.shape[dim + 1 :]
    parts = array.reshape(*before, 128, array.shape[dim] // 128, *after)
    return jnp.moveaxis(parts, dim, 0).reshape(128, -1)


def from_owner(parts, shape, dim):
    split = parts.reshape(128, *shape[:dim], shape[dim] // 128, *shape[dim + 1 :])
    return jnp.moveaxis(split, 0, dim).reshape(shape)


def shards(
    latent,
    condition,
    routed_ids,
    embed_weight,
    embed_bias,
    modulation_weight,
    modulation_bias,
    attention_weight,
    attention_bias,
    merge_weight,
    merge_bias,
    expand_weight,
    expand_bias,
    reduce_weight,
    reduce_bias,
    final_modulation,
    final_offsets,
    unpatch_weight,
    unpatch_bias,
    pred_cotangent,
):
    count = latent.shape[0]
    tile_rows = latent.shape[1] // 2
    tile_cols = latent.shape[2] // 2
    tile_tokens = tile_rows * tile_cols
    rows_tiles = lax.axis_size("tx")
    cols_tiles = lax.axis_size("ty")
    tiles = rows_tiles * cols_tiles
    grid_side = tile_rows * rows_tiles
    row_index = lax.axis_index("tx") * tile_rows + jnp.arange(tile_rows, dtype=jnp.int32)
    col_index = lax.axis_index("ty") * tile_cols + jnp.arange(tile_cols, dtype=jnp.int32)
    token_index = (row_index[:, None] * grid_side + col_index[None, :]).reshape(tile_tokens)
    routed = jnp.sum(
        (routed_ids[:, :, None] == token_index[None, None, :]).astype(jnp.float32), axis=1
    )
    capacity = 7 * tile_tokens // 8
    id_tiles = (
        routed_ids // grid_side // tile_rows * cols_tiles + routed_ids % grid_side // tile_cols
    )
    tile_loads = jnp.sum(
        (id_tiles[:, :, None] == jnp.arange(tiles, dtype=jnp.int32)[None, None, :]).astype(
            jnp.int32
        ),
        axis=1,
    )
    routed_marks = jnp.arange(capacity, dtype=jnp.int32)[None, None, :] < tile_loads[:, :, None]
    routed_marks = routed_marks.astype(jnp.float32).reshape(count, tiles * capacity)
    everyone = jnp.ones((count, tile_tokens), jnp.float32)
    position, owner, valid = compact_plan(routed, capacity)
    width = D
    whole_index = lax.axis_index(DP_TX_TY)
    small_parts = (
        embed_weight,
        embed_bias,
        unpatch_weight,
        attention_bias,
        merge_bias,
        expand_bias,
        reduce_bias,
    )
    cond_rows = jax.nn.silu(condition.astype(F32)).astype(BF16)
    mod_piece = modulation_bias.shape[1]
    final_piece = final_offsets.shape[0]
    placed_bias = jnp.zeros((MOD_ALL,), F32)
    for bias, at in (
        (modulation_bias[0], whole_index * mod_piece),
        (modulation_bias[1], 6 * D + whole_index * mod_piece),
        (final_offsets, 12 * D + whole_index * final_piece),
    ):
        placed_bias = lax.dynamic_update_slice_in_dim(placed_bias, bias.astype(F32), at, 0)
    mod_parts = jnp.concatenate(
        [
            jnp.dot(cond_rows, modulation_weight[0], preferred_element_type=F32),
            jnp.dot(cond_rows, modulation_weight[1], preferred_element_type=F32),
            jnp.dot(cond_rows, final_modulation, preferred_element_type=F32),
        ],
        axis=1,
    )
    mod_parts = jnp.pad(mod_parts + placed_bias[None], [(0, 0), (0, 16384 - MOD_ALL)])
    packed = pack_weights(attention_weight, merge_weight, expand_weight, reduce_weight)
    rows, *first_attn, mods, small = open_up(
        packed, mod_parts.reshape(4, 4, 128, 128), pack_small(small_parts)
    )
    mods = mods.reshape(1, 16384)
    mod_one = mods[:, : 6 * D]
    mod_two = mods[:, 6 * D : 12 * D]
    head_mod = mods[:, 12 * D : 14 * D]
    small = small.reshape(8, 16, 2048).swapaxes(0, 1).reshape(128, 2048)
    pieces = jnp.split(small, [sum(SMALL_IN[:k]) for k in range(1, 8)], axis=1)
    embed_w = from_owner(pieces[0], (16, D), 1)
    embed_b = from_owner(pieces[1], (D,), 0)
    unpatch_w = from_owner(pieces[2], (D, 32), 0)
    attn_b = from_owner(pieces[3], (2, 2 * D), 1)
    merge_b = from_owner(pieces[4], (2, D), 1)
    expand_b = from_owner(pieces[5], (2, FF), 1)
    reduce_b = from_owner(pieces[6], (2, D), 1)
    placed = sincos_table(row_index.astype(jnp.float32), col_index.astype(jnp.float32), width)
    patches = to_patches(latent)
    initial_tokens = (
        jnp.einsum("btp,pd->btd", patches, embed_w, preferred_element_type=jnp.float32)
        + embed_b.astype(jnp.float32)
        + placed[None, :, :]
    )
    first_biases = (attn_b[0], merge_b[0], expand_b[0], reduce_b[0])
    second_biases = (attn_b[1], merge_b[1], expand_b[1], reduce_b[1])
    mask_one = jnp.zeros((1, tiles * tile_tokens), F32)
    mask_two = jnp.where(routed_marks > 0, 0.0, -1e30).astype(F32)
    middle_one, second_attn, first_params, saved_one = block_forward(
        initial_tokens[0],
        mod_one.reshape(6, D),
        first_attn,
        first_biases,
        mask_one,
        rows,
        2 * ATT_COLS,
        True,
        10,
    )
    middle_one = middle_one[None]
    selected_rows = pick_rows(middle_one, owner)
    middle_two, _, second_params, saved_two = block_forward(
        selected_rows[0],
        mod_two.reshape(6, D),
        second_attn,
        second_biases,
        mask_two,
        rows,
        2 * ATT_COLS + FFN_COLS,
        False,
        20,
    )
    middle_two = middle_two[None]
    keep_mask = routed[:, :, None] > 0
    ended = jnp.where(keep_mask, pick_rows(middle_two, position), middle_one)
    head_shift = head_mod[:, None, :width]
    head_scale = head_mod[:, None, width:]
    normed_end, inv_end = layer_stats(ended)
    final16 = (normed_end * (1.0 + head_scale) + head_shift).astype(jnp.bfloat16)
    outputs = jnp.einsum(
        "btd,do->bto", final16, unpatch_w, preferred_element_type=jnp.float32
    ) + unpatch_bias.astype(jnp.float32)
    predicted = from_patches(outputs.astype(jnp.bfloat16), tile_rows, tile_cols)
    cotangent = to_patches(pred_cotangent)
    grad_unpatch_w = jnp.einsum(
        "btd,bto->do", final16, cotangent, preferred_element_type=jnp.float32
    )
    grad_unpatch_b = jnp.sum(cotangent.astype(jnp.float32), axis=(0, 1))
    grad_final = jnp.einsum("bto,do->btd", cotangent, unpatch_w, preferred_element_type=jnp.float32)
    head_grad_mod = jnp.concatenate(
        [jnp.sum(grad_final, axis=1), jnp.sum(grad_final * normed_end, axis=1)], axis=-1
    )
    grad_ended = layer_back(grad_final * (1.0 + head_scale), normed_end, inv_end)
    grad_chosen = pick_rows(grad_ended, owner)
    grad_two, mod_grad_two, dw_attn_two, ffn_two, _, biases_two = block_backward(
        grad_chosen[0], saved_two, second_params, valid[0][:, None], (), 20
    )
    grad_middle = jnp.where(keep_mask, pick_rows(grad_two[None], position), grad_ended)
    grad_start, mod_grad_one, dw_attn_one, ffn_one, (attn_two,), biases_one = block_backward(
        grad_middle[0], saved_one, first_params, everyone[0][:, None], slabs(dw_attn_two), 10
    )
    grad_start = grad_start[None]
    start_grad16 = grad_start.astype(jnp.bfloat16)
    grad_embed_w = jnp.einsum(
        "btp,btd->pd", patches, start_grad16, preferred_element_type=jnp.float32
    )
    grad_embed_b = jnp.sum(start_grad16.astype(jnp.float32), axis=(0, 1))
    latent_tokens = jnp.einsum(
        "btd,pd->btp", start_grad16, embed_w, preferred_element_type=jnp.float32
    )
    latent_grad = from_patches(latent_tokens, tile_rows, tile_cols)
    bias_grads = [jnp.stack([biases_one[member], biases_two[member]]) for member in range(4)]
    small_out = jnp.concatenate(
        [
            by_owner(grad_embed_w, 1),
            by_owner(grad_embed_b, 0),
            by_owner(grad_unpatch_w, 0),
            by_owner(bias_grads[0], 1),
            by_owner(bias_grads[1], 1),
            by_owner(bias_grads[2], 1),
            by_owner(bias_grads[3], 1),
            jnp.broadcast_to(grad_unpatch_b[None], (128, 32)),
        ],
        axis=1,
    )
    small_out = jnp.pad(small_out, [(0, 0), (0, 1024 - small_out.shape[1])])
    grad_mods = jnp.concatenate([mod_grad_one, mod_grad_two, head_grad_mod[0]])
    grad_mods = jnp.pad(grad_mods, (0, 16384 - MOD_ALL))
    early, late, mod_back, small_back = finish(
        dw_attn_one,
        attn_two,
        ffn_one,
        ffn_two,
        grad_mods.reshape(8, 16, 128),
        small_out.reshape(4, 4, 64, 128),
    )
    mod_back = mod_back.reshape(8, 16, 2048).swapaxes(0, 1).reshape(16, 16384)
    attn_grad, *closed = close(
        early, late, mod_back, cond_rows, modulation_weight, final_modulation
    )
    merge_grad, expand_grad, reduce_grad, mod_weight_grad, final_mod_grad, cond_terms, bias_sum = closed
    small_back = small_back.reshape(1024)
    small_sizes = (*SMALL_IN, 32)
    small_sums = jnp.split(small_back, [sum(small_sizes[:k]) for k in range(1, 9)])
    mod_bias_grad = jnp.stack(
        [
            lax.dynamic_slice_in_dim(bias_sum[0], at + whole_index * mod_piece, mod_piece)
            for at in (0, 6 * D)
        ]
    )
    final_bias_grad = lax.dynamic_slice_in_dim(
        bias_sum[0], 12 * D + whole_index * final_piece, final_piece
    )
    silu_value, silu_pull = jax.vjp(jax.nn.silu, condition.astype(jnp.float32))
    condition_grad = silu_pull(cond_terms)[0]
    return (
        predicted,
        latent_grad,
        condition_grad,
        small_sums[0].reshape(16, 9),
        small_sums[1],
        mod_weight_grad,
        mod_bias_grad,
        attn_grad.swapaxes(1, 2),
        small_sums[3].reshape(2, 18),
        merge_grad,
        small_sums[4].reshape(2, 9),
        expand_grad,
        small_sums[5].reshape(2, 36),
        reduce_grad,
        small_sums[6].reshape(2, 9),
        final_mod_grad,
        final_bias_grad,
        small_sums[2].reshape(9, 32),
        small_sums[7],
    )


def solution(mesh):
    torus = Mesh(
        mesh.devices.reshape(4, 4, mesh.shape["tx"], mesh.shape["ty"]), ("dp_0", "dp_1", "tx", "ty")
    )
    return jax.shard_map(
        shards,
        mesh=torus,
        in_specs=(
            P(DP, "tx", "ty", None),
            P(None, DP_TX_TY),
            P(DP, None),
            P(None, DP_TX_TY),
            P(DP_TX_TY),
            P(None, DP_TX_TY, None),
            P(None, DP_TX_TY),
            P(None, DP_TX_TY, None, None),
            P(None, DP_TX_TY),
            P(None, DP_TX_TY, None),
            P(None, DP_TX_TY),
            P(None, DP_TX_TY, None),
            P(None, DP_TX_TY),
            P(None, DP_TX_TY, None),
            P(None, DP_TX_TY),
            P(DP_TX_TY, None),
            P(DP_TX_TY),
            P(DP_TX_TY, None),
            P(),
            P(DP, "tx", "ty", None),
        ),
        out_specs=(
            P(DP, "tx", "ty", None),
            P(DP, "tx", "ty", None),
            P(None, DP_TX_TY),
            P(None, DP_TX_TY),
            P(DP_TX_TY),
            P(None, DP_TX_TY, None),
            P(None, DP_TX_TY),
            P(None, DP_TX_TY, None, None),
            P(None, DP_TX_TY),
            P(None, DP_TX_TY, None),
            P(None, DP_TX_TY),
            P(None, DP_TX_TY, None),
            P(None, DP_TX_TY),
            P(None, DP_TX_TY, None),
            P(None, DP_TX_TY),
            P(DP_TX_TY, None),
            P(DP_TX_TY),
            P(DP_TX_TY, None),
            P(),
        ),
        check_vma=False,
    )
```

```python
import functools

import jax
import jax.numpy as jnp
import numpy as np
from jax import lax
from jax.experimental import pallas as pl
from jax.experimental.pallas import tpu as pltpu
from jax.sharding import Mesh
from jax.sharding import PartitionSpec as P

D = 1152
HEADS = 16
FF = 4608
HW = D // 8
FW = FF // 8
DP = ("dp_0", "dp_1")
DP_TX_TY = ("dp_0", "dp_1", "tx", "ty")
MESH = pl.DeviceIdType.MESH
VMEM = pl.BlockSpec(memory_space=pltpu.VMEM)
FAR = pl.BlockSpec(memory_space=pl.ANY)
F32 = jnp.float32
BF16 = jnp.bfloat16
ATT_COLS = 640
FFN_COLS = 2 * FW
ALL_COLS = 2 * (ATT_COLS + FFN_COLS)
PIECE = 512
PIECES = ALL_COLS // PIECE
MOD_ALL = 14 * D
SMALL_IN = (16 * 9, 9, 9 * 32, 2 * 18, 2 * 9, 2 * 36, 2 * 9)


def greet(peers):
    barrier = pltpu.get_barrier_semaphore()
    for peer in peers:
        pl.semaphore_signal(barrier, inc=1, device_id=peer, device_id_type=MESH)


def met(peers):
    pl.semaphore_wait(pltpu.get_barrier_semaphore(), len(peers))


def enter(peers):
    greet(peers)
    met(peers)


def send(src, dst, sems, k, peer):
    copy = pltpu.make_async_remote_copy(
        src_ref=src,
        dst_ref=dst,
        send_sem=sems[0].at[k],
        recv_sem=sems[1].at[k],
        device_id=peer,
        device_id_type=MESH,
    )
    copy.start()
    return copy


def group_peers():
    c, y = lax.axis_index("tx"), lax.axis_index("ty")
    found = []
    for dc in range(2):
        for dy in range(4):
            if dc or dy:
                oc, oy = lax.rem(c + dc, 2), lax.rem(y + dy, 4)
                found.append(({"tx": oc, "ty": oy}, oc * 4 + oy))
    return found


def own_group():
    return lax.axis_index("tx") * 4 + lax.axis_index("ty")


def dma_sems(n):
    return [pltpu.SemaphoreType.DMA((n,)), pltpu.SemaphoreType.DMA((n,))]


def collective(kernel, cid, outs, scratch, *operands, far_in=0, far_out=0, vmem=56 << 20):
    many = isinstance(outs, tuple)
    near_in = len(operands) - far_in
    near_out = (len(outs) if many else 1) - far_out
    out_specs = (VMEM,) * near_out + (FAR,) * far_out
    return pl.pallas_call(
        kernel,
        out_shape=outs,
        in_specs=[VMEM] * near_in + [FAR] * far_in,
        out_specs=out_specs if many else out_specs[0],
        scratch_shapes=scratch,
        compiler_params=pltpu.CompilerParams(
            collective_id=cid, has_side_effects=True, vmem_limit_bytes=vmem
        ),
    )(*operands)


def ring_peers():
    c, y = lax.axis_index("tx"), lax.axis_index("ty")
    return (
        {"tx": 1 - c},
        {"ty": lax.rem(y + 1, 4)},
        {"ty": lax.rem(y + 3, 4)},
        {"ty": lax.rem(y + 2, 4)},
    )


def layer_stats(value_rows):
    centered = value_rows - jnp.mean(value_rows, axis=-1, keepdims=True)
    inv_std = lax.rsqrt(jnp.mean(centered * centered, axis=-1, keepdims=True) + 1e-06)
    return (centered * inv_std, inv_std)


def layer_back(upstream, normed, inv_std):
    return inv_std * (
        upstream
        - jnp.mean(upstream, axis=-1, keepdims=True)
        - normed * jnp.mean(upstream * normed, axis=-1, keepdims=True)
    )


def sincos_table(row_pos, col_pos, width):
    quarter = width // 4
    freqs = jnp.power(10000.0, -jnp.arange(quarter, dtype=jnp.float32) / quarter)
    row_angle = row_pos[:, None] * freqs[None, :]
    col_angle = col_pos[:, None] * freqs[None, :]
    row_embed = jnp.concatenate([jnp.sin(row_angle), jnp.cos(row_angle)], axis=-1)
    col_embed = jnp.concatenate([jnp.sin(col_angle), jnp.cos(col_angle)], axis=-1)
    row_full = jnp.broadcast_to(
        row_embed[:, None, :], (row_pos.shape[0], col_pos.shape[0], width // 2)
    )
    col_full = jnp.broadcast_to(
        col_embed[None, :, :], (row_pos.shape[0], col_pos.shape[0], width // 2)
    )
    return jnp.concatenate([row_full, col_full], axis=-1).reshape(
        row_pos.shape[0] * col_pos.shape[0], width
    )


def to_patches(pixels):
    count, height, breadth, depth = pixels.shape
    shaped = pixels.reshape(count, height // 2, 2, breadth // 2, 2, depth)
    return shaped.transpose(0, 1, 3, 2, 4, 5).reshape(
        count, height // 2 * (breadth // 2), 4 * depth
    )


def from_patches(token_rows, tile_rows, tile_cols):
    count = token_rows.shape[0]
    depth = token_rows.shape[2] // 4
    shaped = token_rows.reshape(count, tile_rows, tile_cols, 2, 2, depth)
    return shaped.transpose(0, 1, 3, 2, 4, 5).reshape(count, 2 * tile_rows, 2 * tile_cols, depth)


def ring_local(tokens):
    return [
        pltpu.VMEM((4, tokens, D), F32),
        pltpu.VMEM((4, tokens, D), BF16),
        pltpu.VMEM((3, tokens, D), BF16),
    ]


def ring_remote(tokens):
    half = (tokens // 2 + 15) // 16 * 16
    return [
        pltpu.VMEM((4, tokens, D), BF16),
        pltpu.VMEM((2, tokens, D), BF16),
        pltpu.VMEM((half, D), BF16),
        pltpu.VMEM((tokens - half, D), BF16),
    ] + dma_sems(20)


SLAB = 80
PART = D // 16
CUT = {ATT_COLS: 384, FFN_COLS: 640}


def line_peers():
    x, z = lax.axis_index("dp_0"), lax.axis_index("dp_1")
    along_x = [({"dp_0": lax.rem(x + d, 4)}, lax.rem(x + d, 4)) for d in (2, 1, 3)]
    along_z = [({"dp_1": lax.rem(z + d, 4)}, lax.rem(z + d, 4)) for d in (2, 1, 3)]
    return along_x, along_z


class RowsIn:
    def __init__(self, left_ref, right_ref, scratch):
        self.left, self.right = left_ref, right_ref
        self.all_left, self.all_right = scratch[:2]
        self.sems = tuple(scratch[2:4])
        self.x, self.z = lax.axis_index("dp_0"), lax.axis_index("dp_1")
        self.along_x, self.along_z = line_peers()

    def peers(self):
        return [peer for peer, _ in self.along_x + self.along_z]

    def start(self):
        x, z = self.x, self.z
        self.first = []
        for k, (peer, _) in enumerate(self.along_z):
            self.first.append(send(self.left, self.all_left.at[x, z], self.sems, k, peer))
        for k, (peer, _) in enumerate(self.along_x):
            self.first.append(send(self.right, self.all_right.at[x, z], self.sems, 3 + k, peer))
        self.all_left[x, z] = self.left[...]
        self.all_right[x, z] = self.right[...]

    def middle(self):
        left, right = self.all_left.at[self.x], self.all_right.at[:, self.z]
        self.second = []
        for copy in self.first[:3]:
            copy.wait_recv()
        for k, (peer, _) in enumerate(self.along_x):
            self.second.append(send(left, left, self.sems, 6 + k, peer))
        for copy in self.first[3:]:
            copy.wait_recv()
        for k, (peer, _) in enumerate(self.along_z):
            self.second.append(send(right, right, self.sems, 9 + k, peer))

    def end(self, one_ref, two_ref):
        for copy in self.second:
            copy.wait_recv()
        width, other = one_ref.shape[1], two_ref.shape[1]
        cut = self.left.shape[1]

        @pl.loop(0, 8)
        def _(pair):
            x, z = pair // 2, 2 * lax.rem(pair, 2)
            both = []
            for k in range(2):
                parts = [self.all_left[x, z + k], self.all_right[x, z + k]]
                both.append(jnp.concatenate(parts, axis=1).astype(F32)[:PART])
            value = jnp.concatenate(both, axis=0).astype(BF16)
            at = pl.ds(pl.multiple_of(pair * 2 * PART, 16), 2 * PART)
            one_ref[at, :] = value[:, :width]
            two_ref[at, :] = value[:, width : width + other]

        for copy in self.first + self.second:
            copy.wait_send()


def rows_in_scratch(cols):
    left = CUT[cols]
    return [
        pltpu.VMEM((4, 4, SLAB, left), BF16),
        pltpu.VMEM((4, 4, SLAB, cols - left), BF16),
    ] + dma_sems(12)


class RowsOut:
    def __init__(self, left_ref, right_ref, scratch):
        self.left, self.right = left_ref, right_ref
        self.got = scratch[0:2]
        self.mine = scratch[2:4]
        self.last = scratch[4:6]
        self.sems = tuple(scratch[6:8])
        self.x, self.z = lax.axis_index("dp_0"), lax.axis_index("dp_1")
        self.along_x, self.along_z = line_peers()

    def peers(self):
        return [peer for peer, _ in self.along_x + self.along_z]

    def start(self):
        self.first = []
        for k, (peer, at) in enumerate(self.along_x):
            part = self.left.at[at]
            self.first.append(send(part, self.got[0].at[k], self.sems, k, peer))
        for k, (peer, at) in enumerate(self.along_z):
            part = self.right.at[:, at]
            self.first.append(send(part, self.got[1].at[k], self.sems, 3 + k, peer))

    def middle(self):
        self.second = []
        for side, peers in ((0, self.along_z), (1, self.along_x)):
            for copy in self.first[3 * side : 3 * side + 3]:
                copy.wait_recv()
            got, mine = self.got[side], self.mine[side]

            @pl.loop(0, 4)
            def _(k):
                own = self.right[k, self.z] if side else self.left[self.x, k]
                total = own.astype(F32)
                for source in range(3):
                    total = total + got[source, k].astype(F32)
                mine[k] = total.astype(mine.dtype)

            for k, (peer, at) in enumerate(peers):
                part = mine.at[at]
                copy = send(part, self.last[side].at[k], self.sems, 6 + 3 * side + k, peer)
                self.second.append(copy)

    def end(self):
        for copy in self.second:
            copy.wait_recv()
        totals = []
        for side, own in ((0, self.z), (1, self.x)):
            total = self.mine[side][own].astype(F32)
            for source in range(3):
                total = total + self.last[side][source].astype(F32)
            totals.append(total)
        return totals

    def end_rows(self, out_ref):
        cut = self.left.shape[3]
        left, right = self.end()
        out_ref[:, :cut] = left.astype(BF16)
        out_ref[:, cut:] = right.astype(BF16)
        self.leave()

    def leave(self):
        for copy in self.first + self.second:
            copy.wait_send()


def rows_out_scratch(cols):
    return sum_scratch([(SLAB, CUT[cols]), (SLAB, cols - CUT[cols])], BF16)


def sum_scratch(shapes, dtype):
    return (
        [pltpu.VMEM((3, 4, *shape), dtype) for shape in shapes]
        + [pltpu.VMEM((4, *shape), dtype) for shape in shapes]
        + [pltpu.VMEM((3, *shape), dtype) for shape in shapes]
        + dma_sems(12)
    )


def slab_views(rows_ref, start, cols):
    cut = start + CUT[cols]
    return rows_ref.at[:, start:cut], rows_ref.at[:, cut : start + cols]


def weight_shapes(cols):
    widths = (3 * HW, HW) if cols == ATT_COLS else (FW, FW)
    return tuple(jax.ShapeDtypeStruct((D, w), BF16) for w in widths)


class Ring:
    def __init__(self, tokens, local, remote):
        self.tokens = tokens
        self.half = (tokens // 2 + 15) // 16 * 16
        self.kept, self.sib_out, self.out = local
        self.sib_in, self.got, self.far_low, self.far_high = remote[:4]
        self.sems = tuple(remote[4:6])
        c, y = lax.axis_index("tx"), lax.axis_index("ty")
        self.sib, self.up, self.down, _ = ring_peers()
        self.own = [c * 4 + lax.rem(y + d, 4) for d in range(4)]
        self.other = [(1 - c) * 4 + lax.rem(y + d, 4) for d in range(4)]
        self.sent = []

    def peers(self):
        return [self.sib, self.up, self.down]

    def send(self, src, dst, k, peer):
        copy = send(src, dst, self.sems, k, peer)
        self.sent.append(copy)
        return copy

    def rows(self, index, start=0, stop=None):
        stop = self.tokens if stop is None else stop
        at = pl.multiple_of(index * self.tokens + start, 16)
        return pl.ds(at, stop - start)

    def gather(self, x_ref, all_ref, prepare, visit, between=None):
        half, tokens = self.half, self.tokens
        me, above, across, below = self.own
        first, last = slice(0, half), slice(half, tokens)

        def pass_on(index, k, peer, start=0, stop=None):
            part = all_ref.at[self.rows(index, start, stop)]
            return self.send(part, part, k, peer)

        def own_part(rows, k, peer):
            part = all_ref.at[self.rows(me, rows.start, rows.stop)]
            return self.send(x_ref.at[rows], part, k, peer)

        a1 = own_part(first, 0, self.up)
        b1 = own_part(last, 1, self.down)
        a2 = own_part(last, 2, self.up)
        b2 = own_part(first, 3, self.down)
        s0 = self.send(x_ref, all_ref.at[self.rows(me)], 4, self.sib)
        all_ref[self.rows(me), :] = x_ref[...]
        prepare()
        visit(True, 0)
        s0.wait_recv()
        visit(False, 0)
        a1.wait_recv()
        f1 = pass_on(below, 5, self.up, 0, half)
        b1.wait_recv()
        f2 = pass_on(above, 6, self.down, half, tokens)
        a2.wait_recv()
        s1 = pass_on(below, 7, self.sib)
        b2.wait_recv()
        s2 = pass_on(above, 8, self.sib)
        if between:
            between()
        visit(True, 3)
        visit(True, 1)
        s1.wait_recv()
        visit(False, 3)
        s2.wait_recv()
        visit(False, 1)
        f1.wait_recv()
        f2.wait_recv()
        s3 = pass_on(across, 9, self.sib)
        visit(True, 2)
        s3.wait_recv()
        visit(False, 2)

    def put(self, own, d, value):
        if own:
            self.kept[d] = value
        else:
            self.sib_out[d] = value.astype(BF16)
            self.swaps[d] = self.send(self.sib_out.at[d], self.sib_in.at[d], 10 + d, self.sib)

    def start_sums(self):
        self.swaps = {}

    def chip_sum(self, d):
        self.swaps[d].wait_recv()
        return self.kept[d] + self.sib_in[d].astype(F32)

    def near(self):
        half = self.half
        first, last = slice(0, half), slice(half, self.tokens)
        total = self.chip_sum(1)
        self.kept[1] = total
        self.out[0, last] = total[half:].astype(BF16)
        self.n1 = self.send(self.out.at[0, last], self.got.at[0, last], 14, self.up)
        total = self.chip_sum(3)
        self.kept[3] = total
        self.out[1, first] = total[:half].astype(BF16)
        self.n2 = self.send(self.out.at[1, first], self.got.at[1, first], 15, self.down)

    def far(self):
        half = self.half
        self.out[2] = self.chip_sum(2).astype(BF16)
        self.f1 = self.send(self.out.at[2, 0:half], self.far_low, 16, self.up)
        self.f2 = self.send(self.out.at[2, half : self.tokens], self.far_high, 17, self.down)

    def relay(self):
        half = self.half
        first, last = slice(0, half), slice(half, self.tokens)
        self.f1.wait_recv()
        self.out[0, first] = (self.kept[1, first] + self.far_low[...].astype(F32)).astype(BF16)
        self.r1 = self.send(self.out.at[0, first], self.got.at[0, first], 18, self.up)
        self.f2.wait_recv()
        self.out[1, last] = (self.kept[3, last] + self.far_high[...].astype(F32)).astype(BF16)
        self.r2 = self.send(self.out.at[1, last], self.got.at[1, last], 19, self.down)

    def total(self):
        value = self.chip_sum(0)
        for copy in (self.n1, self.n2, self.r1, self.r2):
            copy.wait_recv()
        return value + self.got[0].astype(F32) + self.got[1].astype(F32)

    def leave(self):
        for copy in self.sent:
            copy.wait_send()


def dot_nn(left, right):
    return lax.dot_general(left, right, (((1,), (0,)), ((), ())), preferred_element_type=F32)


def dot_nt(left, right):
    return lax.dot_general(left, right, (((1,), (1,)), ((), ())), preferred_element_type=F32)


def dot_tn(left, right):
    return lax.dot_general(left, right, (((0,), (0,)), ((), ())), preferred_element_type=F32)


def gelu_both(pre):
    root = 0.7978845608028654
    square = pre * pre
    bent = jnp.tanh(root * pre * (1.0 + 0.044715 * square))
    value = 0.5 * pre * (1.0 + bent)
    slope = 0.5 * (1.0 + bent) + 0.5 * pre * (1.0 - bent * bent) * root * (1.0 + 0.134145 * square)
    return value, slope


def sum_rows(value):
    return jnp.sum(value, axis=0, keepdims=True)


def open_kernel(
    w_ref, pick_ref, m_ref, s_ref, rows_ref, one_ref, two_ref, m_out, s_out,
    w_got, m_got, m_sum, ss, rs, *scratch
):
    group = group_peers()
    sib, up, down, far = ring_peers()
    fetch = RowsIn(*slab_views(rows_ref, 0, ATT_COLS), scratch[:4])
    mods = RowsOut(m_ref.at[:, :, 0:64], m_ref.at[:, :, 64:128], scratch[4:])
    enter([peer for peer, _ in group] + fetch.peers())
    sems = (ss, rs)
    me, x, z = own_group(), lax.axis_index("dp_0"), lax.axis_index("dp_1")
    weights = [send(w_ref.at[at], w_got.at[me], sems, k, p) for k, (p, at) in enumerate(group)]
    small = s_out.at[me, x, z]
    first = [send(s_ref, small, sems, 7 + k, p) for k, (p, _) in enumerate(fetch.along_z)]
    mods.start()
    w_got[me] = w_ref[me]
    s_out[me, x, z] = s_ref[...]
    for copy in first:
        copy.wait_recv()
    small = s_out.at[me, x]
    second = [send(small, small, sems, 10 + k, p) for k, (p, _) in enumerate(fetch.along_x)]
    for copy in weights:
        copy.wait_recv()
    received = w_got[...].reshape(8 * w_got.shape[1], PIECE)
    for k in range(PIECES):
        cols = slice(k * PIECE, (k + 1) * PIECE)
        rows_ref[:, cols] = dot_nn(pick_ref[k], received).astype(BF16)
    fetch.start()
    for copy in second:
        copy.wait_recv()
    small = s_out.at[me]
    third = [send(small, small, sems, 13 + k, p) for k, p in enumerate((up, down, far, sib))]
    mods.middle()
    fetch.middle()
    left, right = mods.end()
    m_sum[0:64] = left
    m_sum[64:128] = right

    def chunk(ref, index):
        return ref.at[pl.ds(pl.multiple_of(index * 16, 16), 16)]

    m_first = [
        send(chunk(m_sum, at), m_got.at[me], sems, 20 + k, p) for k, (p, at) in enumerate(group)
    ]
    mine = pl.ds(pl.multiple_of(me * 16, 16), 16)
    m_got[me] = m_sum[mine, :]
    for copy in m_first:
        copy.wait_recv()
    total = m_got[0]
    for k in range(1, 8):
        total = total + m_got[k]
    m_out[mine, :] = total
    part = chunk(m_out, me)
    m_second = [send(part, part, sems, 27 + k, p) for k, (p, _) in enumerate(group)]
    c, y = lax.axis_index("tx"), lax.axis_index("ty")
    fourth = []
    for k, d in enumerate((3, 1, 2)):
        third[k].wait_recv()
        small = s_out.at[c * 4 + lax.rem(y + d, 4)]
        fourth.append(send(small, small, sems, 17 + k, sib))
    fetch.end(one_ref, two_ref)
    for copy in m_second + fourth + third[3:]:
        copy.wait_recv()
    for copy in weights + first + second + third + fourth + m_first + m_second:
        copy.wait_send()
    mods.leave()


def picking():
    picks = np.zeros((PIECES, SLAB, 8 * 64), np.float32)
    for k in range(PIECES):
        for row in range(72):
            picks[k, row, row // 9 * 64 + 9 * k + row % 9] = 1.0
    return picks


def open_up(weights, mods, small):
    outs = (
        jax.ShapeDtypeStruct((SLAB, ALL_COLS), BF16),
        *weight_shapes(ATT_COLS),
        jax.ShapeDtypeStruct((128, 128), F32),
        jax.ShapeDtypeStruct((8, 4, 4, *small.shape), BF16),
    )
    scratch = [
        pltpu.VMEM(weights.shape, BF16),
        pltpu.VMEM((8, 16, 128), F32),
        pltpu.VMEM((128, 128), F32),
    ] + dma_sems(34)
    scratch += rows_in_scratch(ATT_COLS) + sum_scratch([(64, 128), (64, 128)], F32)
    picks = jnp.asarray(picking(), BF16)
    return collective(open_kernel, 1, outs, scratch, weights, picks, mods, small)


EARLY = ATT_COLS + 2 * FFN_COLS
EARLY_PIECES = -(-EARLY // PIECE)
LATE_PIECES = -(-ATT_COLS // PIECE)
LATE_ROWS = 32


def packed_rows(picks_ref, parts, pieces):
    columns = jnp.concatenate(parts, axis=1)
    spare = pieces * PIECE - columns.shape[1]
    columns = jnp.concatenate([columns, jnp.zeros((SLAB, spare), BF16)], axis=1)
    total = jnp.zeros((8 * 64, PIECE), F32)
    for k in range(pieces):
        total = total + dot_tn(picks_ref[k], columns[:, k * PIECE : (k + 1) * PIECE])
    return total.astype(BF16).reshape(8, 64, PIECE)


def finish_kernel(
    left_ref, right_ref, attn_ref, ffn_one_ref, ffn_two_ref, picks_ref, m_ref, s_ref,
    early_out, late_out, m_out, s_out,
    early, late, m_got, s_mine, s_two, late_rows, ss, rs, *scratch
):
    group = group_peers()
    sib, up, down, far = ring_peers()
    rows = RowsOut(left_ref, right_ref, scratch[:8])
    small = RowsOut(s_ref.at[:, :, 0:32], s_ref.at[:, :, 32:64], scratch[8:])
    peers = [peer for peer, _ in group] + rows.peers()
    greet(peers)
    me, x, z = own_group(), lax.axis_index("dp_0"), lax.axis_index("dp_1")
    sems = (ss, rs)
    met(peers)
    rows.start()
    m_first = [send(m_ref.at[at], m_got.at[me], sems, k, p) for k, (p, at) in enumerate(group)]
    small.start()
    early[...] = packed_rows(
        picks_ref, [attn_ref[...], ffn_one_ref[...], ffn_two_ref[...]], EARLY_PIECES
    )
    sent = [send(early.at[at], early_out.at[me], sems, 7 + k, p) for k, (p, at) in enumerate(group)]
    early_out[me] = early[me]
    m_got[me] = m_ref[me]
    for copy in m_first:
        copy.wait_recv()
    total = m_got[0]
    for k in range(1, 8):
        total = total + m_got[k]
    m_out[me, x, z] = total.astype(BF16)
    part = m_out.at[me, x, z]
    m_second = [send(part, part, sems, 14 + k, p) for k, (p, _) in enumerate(rows.along_z)]
    small.middle()
    for copy in m_second:
        copy.wait_recv()
    part = m_out.at[me, x]
    m_third = [send(part, part, sems, 17 + k, p) for k, (p, _) in enumerate(rows.along_x)]
    left, right = small.end()
    s_mine[0:4] = left.reshape(4, 8, 128)
    s_mine[4:8] = right.reshape(4, 8, 128)
    s_last = [send(s_mine.at[at], s_two.at[me], sems, 20 + k, p) for k, (p, at) in enumerate(group)]
    s_two[me] = s_mine[me]
    for copy in m_third:
        copy.wait_recv()
    part = m_out.at[me]
    m_fourth = [send(part, part, sems, 27 + k, p) for k, p in enumerate((up, down, far, sib))]
    rows.middle()
    c, y = lax.axis_index("tx"), lax.axis_index("ty")
    m_fifth = []
    for k, d in enumerate((3, 1, 2)):
        m_fourth[k].wait_recv()
        part = m_out.at[c * 4 + lax.rem(y + d, 4)]
        m_fifth.append(send(part, part, sems, 31 + k, sib))
    for copy in s_last:
        copy.wait_recv()
    total = s_two[0]
    for k in range(1, 8):
        total = total + s_two[k]
    s_out[...] = total
    rows.end_rows(late_rows)
    late[...] = packed_rows(picks_ref, [late_rows[...]], LATE_PIECES)[:, :LATE_ROWS]
    later = [send(late.at[at], late_out.at[me], sems, 34 + k, p) for k, (p, at) in enumerate(group)]
    late_out[me] = late[me]
    for copy in sent + m_fourth[3:] + m_fifth + later:
        copy.wait_recv()
    small.leave()
    for copy in m_first + sent + m_second + m_third + s_last + m_fourth + m_fifth + later:
        copy.wait_send()


def finish(pair, attn, ffn_one, ffn_two, mods, small):
    outs = (
        jax.ShapeDtypeStruct((8, 64, PIECE), BF16),
        jax.ShapeDtypeStruct((8, LATE_ROWS, PIECE), BF16),
        jax.ShapeDtypeStruct((8, 4, 4, 16, 128), BF16),
        jax.ShapeDtypeStruct((8, 128), F32),
    )
    scratch = [
        pltpu.VMEM((8, 64, PIECE), BF16),
        pltpu.VMEM((8, LATE_ROWS, PIECE), BF16),
        pltpu.VMEM((8, 16, 128), F32),
        pltpu.VMEM((8, 8, 128), F32),
        pltpu.VMEM((8, 8, 128), F32),
        pltpu.VMEM((SLAB, ATT_COLS), BF16),
    ] + dma_sems(41)
    scratch += rows_out_scratch(ATT_COLS) + sum_scratch([(32, 128), (32, 128)], F32)
    picks = jnp.asarray(picking(), BF16)
    operands = (*pair, attn, ffn_one, ffn_two, picks, mods, small)
    return collective(finish_kernel, 2, outs, scratch, *operands)


def unpicking(pieces, height):
    picks = np.zeros((pieces, 128, 8 * height), np.float32)
    for k in range(pieces):
        for group in range(8):
            for row in range(9):
                picks[k, group * 16 + row, group * height + 9 * k + row] = 1.0
    return picks


def close_kernel(
    early_ref, late_ref, early_picks, late_picks, g_ref, cond_ref, mod_ref, final_ref,
    attn_ref, merge_ref, expand_ref, reduce_ref, mod_grad_ref, final_grad_ref, terms_ref, bias_ref,
    early, late
):
    received = early_ref[...].reshape(8 * 64, PIECE)
    for k in range(EARLY_PIECES):
        early[:, k * PIECE : (k + 1) * PIECE] = dot_nn(early_picks[k], received)
    received = late_ref[...].reshape(8 * LATE_ROWS, PIECE)
    for k in range(LATE_PIECES):
        late[:, k * PIECE : (k + 1) * PIECE] = dot_nn(late_picks[k], received)

    def whole(source, start, width):
        parts = [source[g * 16 : g * 16 + 16, start : start + width] for g in range(8)]
        return jnp.concatenate(parts, axis=1)[:9]

    for b, (source, start) in enumerate(((late, 0), (early, 0))):
        for j in range(3):
            attn_ref[b, j] = whole(source, start + j * HW, HW)
        merge_ref[b] = whole(source, start + 3 * HW, HW)
    for b, start in enumerate((ATT_COLS, ATT_COLS + FFN_COLS)):
        expand_ref[b] = whole(early, start, FW)
        reduce_ref[b] = whole(early, start + FW, FW)
    terms = jnp.zeros((16, 9), F32)
    for b in range(3):
        grads = g_ref[:, 6 * b * D : min(6 * b + 6, 14) * D]
        weights = mod_ref[b] if b < 2 else final_ref[...]
        product = dot_tn(cond_ref[...], grads)
        if b < 2:
            mod_grad_ref[b] = product
        else:
            final_grad_ref[...] = product
        terms = terms + dot_nt(grads, weights)
    terms_ref[...] = terms
    bias_ref[...] = sum_rows(g_ref[...].astype(F32))


def close(early, late, grads, cond, mod_weight, final_weight):
    outs = (
        jax.ShapeDtypeStruct((2, 3, 9, D), F32),
        jax.ShapeDtypeStruct((2, 9, D), F32),
        jax.ShapeDtypeStruct((2, 9, FF), F32),
        jax.ShapeDtypeStruct((2, 9, FF), F32),
        jax.ShapeDtypeStruct((2, 9, 6 * D), F32),
        jax.ShapeDtypeStruct((9, 2 * D), F32),
        jax.ShapeDtypeStruct((16, 9), F32),
        jax.ShapeDtypeStruct((1, 16384), F32),
    )
    operands = (
        early,
        late,
        jnp.asarray(unpicking(EARLY_PIECES, 64), BF16),
        jnp.asarray(unpicking(LATE_PIECES, LATE_ROWS), BF16),
        grads,
        cond,
        mod_weight,
        final_weight,
    )
    return pl.pallas_call(
        close_kernel,
        out_shape=outs,
        in_specs=[VMEM] * len(operands),
        out_specs=(VMEM,) * len(outs),
        scratch_shapes=[
            pltpu.VMEM((128, EARLY_PIECES * PIECE), F32),
            pltpu.VMEM((128, LATE_PIECES * PIECE), F32),
        ],
        compiler_params=pltpu.CompilerParams(vmem_limit_bytes=32 << 20),
    )(*operands)


HEAD = D // HEADS
SCALE = HEAD ** (-0.5)


def head_cols(h, start=0):
    return slice(start + h * HEAD, start + (h + 1) * HEAD)


class Refs:
    pass


def make_specs(entry):
    return list(entry) if isinstance(entry, list) else [entry]


def launch(body, cid, near, far, outs, kept, scratch, vmem=60 << 20):
    twins = {name: (value.shape, value.dtype) for name, value in far.items()}
    twins.update(kept)
    groups = {name: make_specs(entry) for name, entry in scratch.items()}

    def kernel(*refs):
        refs = iter(refs)
        r = Refs()
        r.hbm = {}
        for name in near:
            setattr(r, name, next(refs))
        for name in far:
            r.hbm[name] = next(refs)
        for name in outs:
            setattr(r, name, next(refs))
        for name in kept:
            r.hbm[name] = next(refs)
        for name in twins:
            setattr(r, name, next(refs))
        r.move_sems = next(refs)
        for name, specs in groups.items():
            found = [next(refs) for _ in specs]
            setattr(r, name, found if isinstance(scratch[name], list) else found[0])
        r.index = {name: k for k, name in enumerate(twins)}
        r.moving = {}
        body(r)

    shapes = [jax.ShapeDtypeStruct(*spec) for spec in (*outs.values(), *kept.values())]
    results = pl.pallas_call(
        kernel,
        out_shape=tuple(shapes),
        in_specs=[VMEM] * len(near) + [FAR] * len(far),
        out_specs=(VMEM,) * len(outs) + (FAR,) * len(kept),
        scratch_shapes=[pltpu.VMEM(*spec) for spec in twins.values()]
        + [pltpu.SemaphoreType.DMA((len(twins),))]
        + [spec for specs in groups.values() for spec in specs],
        compiler_params=pltpu.CompilerParams(
            collective_id=cid, has_side_effects=True, vmem_limit_bytes=vmem
        ),
    )(*near.values(), *far.values())
    return dict(zip((*outs, *kept), results))


def load(r, *names):
    for name in names:
        copy = pltpu.make_async_copy(r.hbm[name], getattr(r, name), r.move_sems.at[r.index[name]])
        copy.start()
        r.moving[name] = copy


def load_into(r, name, ref):
    copy = pltpu.make_async_copy(r.hbm[name], ref, r.move_sems.at[r.index[name]])
    copy.start()
    r.moving[name] = copy


def save(r, *names):
    for name in names:
        copy = pltpu.make_async_copy(getattr(r, name), r.hbm[name], r.move_sems.at[r.index[name]])
        copy.start()
        r.moving[name] = copy


def settle(r, *names):
    for name in names or tuple(r.moving):
        r.moving.pop(name).wait()


def exact(left, right, dims):
    return lax.dot_general(
        left,
        right,
        ((dims[:1], dims[1:]), ((), ())),
        precision=lax.Precision.HIGHEST,
        preferred_element_type=F32,
    )


def choice(place_ref, capacity):
    tokens = place_ref.shape[1]
    slots = lax.broadcasted_iota(jnp.int32, (capacity, tokens), 0)
    return jnp.where(slots == place_ref[...], 1.0, 0.0).astype(F32)


def spread_back(picks, chosen, others):
    used = exact(picks, jnp.ones((picks.shape[0], 128), F32), (0, 0))[:, :1]
    return exact(picks, chosen, (0, 0)) + others * (1.0 - used)


def modulated(x, vec_ref):
    normed, _ = layer_stats(x)
    return (normed * (1.0 + vec_ref[1:2]) + vec_ref[0:1]).astype(BF16)


def forward_body(r, tokens, start, last):
    ring = Ring(tokens, r.ring_local, r.ring_one)
    fetch = RowsIn(*slab_views(r.rows, start, FFN_COLS), r.fetch_one)
    peers = ring.peers() + fetch.peers()
    greet(peers)
    if last:
        r.x[...] = exact(choice(r.place, tokens), r.first[...], (1, 0))
    else:
        r.x[...] = dot_nn(r.patches[...], r.embed_w[...]) + r.embed_b[...] + r.placed[...]
    r.x16[...] = modulated(r.x[...], r.vec_one)
    met(peers)
    save(r, "x")
    ring.start_sums()

    def visit(own, d):
        rows = ring.rows((ring.own if own else ring.other)[d])
        joined = (dot_nn(r.in_all[rows, :], r.wqkv[...]) + r.bias_one[...]).astype(BF16)
        for h in range(2):
            r.q[h, rows, :] = joined[:, head_cols(h)]
            r.k[h, rows, :] = joined[:, head_cols(h, HW)]
            r.v[h, rows, :] = joined[:, head_cols(h, 2 * HW)]

    def attend(own, d):
        rows = ring.rows((ring.own if own else ring.other)[d])
        parts = []
        for h in range(2):
            scores = dot_nt(r.q[h, rows, :], r.k[h]) * SCALE + r.mask[...]
            highest = jnp.max(scores, axis=-1, keepdims=True)
            shifted = jnp.exp(scores - highest)
            summed = jnp.sum(shifted, axis=-1, keepdims=True)
            probs = (shifted * (1.0 / summed)).astype(BF16)
            r.lse[rows, h : h + 1] = highest + jnp.log(summed)
            parts.append(dot_nn(probs, r.v[h]).astype(BF16))
        attended = jnp.concatenate(parts, axis=1)
        r.att[rows, :] = attended
        ring.put(own, d, dot_nt(attended, r.wm[...]))

    ring.gather(r.x16, r.in_all, fetch.start, visit, fetch.middle)
    attend(False, 2)
    attend(True, 2)
    ring.far()
    save(r, "in_all", "q", "k", "v")
    for d in (1, 3):
        attend(False, d)
        attend(True, d)
    ring.near()
    ring.relay()
    attend(False, 0)
    attend(True, 0)
    save(r, "lse", "att")
    fetch.end(r.we, r.wr)
    save(r, "we", "wr")
    branch = ring.total() + r.vec_one[3:4]
    r.branch[...] = branch
    middle = r.x[...] + r.vec_one[2:3] * branch
    r.middle[...] = middle
    save(r, "branch", "middle")
    ring.leave()

    ring = Ring(tokens, r.ring_local, r.ring_two)
    fetch = None
    if not last:
        fetch = RowsIn(*slab_views(r.rows, ATT_COLS, ATT_COLS), r.fetch_two)
    r.x16[...] = modulated(middle, r.vec_two)
    ring.start_sums()

    def prepare():
        if fetch:
            fetch.start()

    def expand(own, d):
        rows = ring.rows((ring.own if own else ring.other)[d])
        pre = dot_nn(r.second[rows, :], r.we[...]) + r.bias_two[...]
        value, slope = gelu_both(pre)
        hidden = value.astype(BF16)
        r.hid[rows, :] = hidden
        r.slope[rows, :] = slope.astype(BF16)
        ring.put(own, d, dot_nt(hidden, r.wr[...]))
        if not own and d == 1:
            ring.near()

    ring.gather(r.x16, r.second, prepare, expand, fetch.middle if fetch else None)
    ring.far()
    save(r, "second", "hid", "slope")
    ring.relay()
    if fetch:
        fetch.end(r.next_wqkv, r.next_wm)
    mlp = ring.total() + r.vec_two[3:4]
    r.mlp[...] = mlp
    save(r, "mlp")
    r.out[...] = r.middle[...] + r.vec_two[2:3] * mlp
    ring.leave()
    settle(r)


def kept_shapes(tokens):
    heads = ((2, 8 * tokens, HEAD), BF16)
    wide, tile = ((8 * tokens, D), BF16), ((tokens, D), F32)
    hidden = ((8 * tokens, FW), BF16)
    return {
        "x": tile,
        "in_all": wide,
        "q": heads,
        "k": heads,
        "v": heads,
        "lse": ((8 * tokens, 2), F32),
        "att": ((8 * tokens, HW), BF16),
        "branch": tile,
        "middle": tile,
        "second": wide,
        "hid": hidden,
        "slope": hidden,
        "mlp": tile,
        "we": ((D, FW), BF16),
        "wr": ((D, FW), BF16),
    }


def block_forward(near, tokens, start, last, cid):
    outs = {"out": ((tokens, D), F32)}
    scratch = {
        "x16": pltpu.VMEM((tokens, D), BF16),
        "ring_local": ring_local(tokens),
        "ring_one": ring_remote(tokens),
        "ring_two": ring_remote(tokens),
        "fetch_one": rows_in_scratch(FFN_COLS),
    }
    if not last:
        outs["next_wqkv"] = ((D, 3 * HW), BF16)
        outs["next_wm"] = ((D, HW), BF16)
        scratch["fetch_two"] = rows_in_scratch(ATT_COLS)
    body = functools.partial(forward_body, tokens=tokens, start=start, last=last)
    return launch(body, cid, near, {}, outs, kept_shapes(tokens), scratch)


def backward_body(r, tokens, last):
    ring = Ring(tokens, r.ring_local, r.ring_one)
    sums = None if last else RowsOut(r.pending_left, r.pending_right, r.sums_one)
    peers = ring.peers() + line_only(line_peers())
    greet(peers)
    load(r, "slope", "wr", "we", "hid", "second", "mlp", "middle")
    load(r, "q", "k", "v", "lse", "att", "x", "branch")
    if not last:
        picks = choice(r.place, r.grad_two.shape[0])
        r.g[...] = spread_back(picks, r.grad_two[...], r.grad_ended[...])
    else:
        r.g[...] = r.grad_in[...]
    r.g16[...] = (r.g[...] * r.vec_two[2:3]).astype(BF16)
    met(peers)
    ring.start_sums()
    r.bias_two[...] = jnp.zeros_like(r.bias_two)

    def prepare():
        if sums:
            sums.start()
        settle(r, "slope", "wr", "we")

    def visit(own, d):
        rows = ring.rows((ring.own if own else ring.other)[d])
        pre_grad = (
            dot_nn(r.g_one[rows, :], r.wr[...]) * r.slope[rows, :].astype(F32)
        ).astype(BF16)
        r.pre_all[rows, :] = pre_grad
        r.bias_two[...] += sum_rows(pre_grad.astype(F32))
        ring.put(own, d, dot_nt(pre_grad, r.we[...]))
        if not own and d == 1:
            ring.near()

    ring.gather(r.g16, r.g_one, prepare, visit)
    ring.far()
    settle(r, "hid", "second", "mlp", "middle")
    weight_grads(r.g_one, r.hid, r.whole_two, FW)
    ring.relay()
    if sums:
        sums.middle()
    r.vecs_two[2:3] = sum_rows(r.g[...] * r.mlp[...])
    r.vecs_two[3:4] = sum_rows(r.g16[...].astype(F32))
    r.vecs_two[4:8] = jnp.zeros((4, D), F32)
    weight_grads(r.second, r.pre_all, r.whole_one, FW)
    load_into(r, "in_all", r.second)
    write_slabs((r.whole_one, FW), (r.whole_two, FW), r.ffn_left, r.ffn_right)
    if sums:
        sums.end_rows(r.attn_rows)
    second_grad = ring.total()
    normed, inv_std = layer_stats(r.middle[...])
    r.vecs_two[0:1] = sum_rows(second_grad)
    r.vecs_two[1:2] = sum_rows(second_grad * normed)
    r.g[...] += layer_back(second_grad * (1.0 + r.vec_two[1:2]), normed, inv_std)
    ring.leave()

    ring = Ring(tokens, r.ring_local, r.ring_two)
    sums = RowsOut(r.ffn_left, r.ffn_right, r.sums_two)
    r.g16[...] = (r.g[...] * r.vec_one[2:3]).astype(BF16)
    ring.start_sums()

    def prepare_attention():
        sums.start()
        r.dk[...] = jnp.zeros_like(r.dk)
        r.dv[...] = jnp.zeros_like(r.dv)
        settle(r, "q", "k", "v", "lse")

    def attend(own, d):
        rows = ring.rows((ring.own if own else ring.other)[d])
        grad = dot_nn(r.g_two[rows, :], r.wm[...]).astype(BF16)
        queries = []
        for h in range(2):
            part = grad[:, head_cols(h)]
            query = r.q[h, rows, :]
            scores = dot_nt(query, r.k[h]) * SCALE + r.mask[...]
            probs = jnp.exp(scores - r.lse[rows, h : h + 1])
            grad_probs = dot_nt(part, r.v[h])
            weighted = jnp.sum(probs * grad_probs, axis=-1, keepdims=True)
            score_grad = (probs * (grad_probs - weighted)).astype(BF16)
            queries.append((dot_nn(score_grad, r.k[h]) * SCALE).astype(BF16))
            r.dk[h] += dot_tn(score_grad, query)
            r.dv[h] += dot_tn(probs.astype(BF16), part)
        r.joined[rows, 0:HW] = jnp.concatenate(queries, axis=1)

    def back(own, d):
        rows = ring.rows((ring.own if own else ring.other)[d])
        ring.put(own, d, dot_nt(r.joined[rows, :], r.wqkv[...]))

    ring.gather(r.g16, r.g_two, prepare_attention, attend)
    later = [(r.dk[h] * SCALE).astype(BF16) for h in range(2)]
    later += [r.dv[h].astype(BF16) for h in range(2)]
    r.joined[:, HW : 3 * HW] = jnp.concatenate(later, axis=1)
    back(False, 2)
    back(True, 2)
    ring.far()
    for d in (1, 3):
        back(False, d)
        back(True, d)
    ring.near()
    back(False, 0)
    back(True, 0)
    settle(r)
    weight_grads(r.g_two, r.att, r.whole_two, HW)
    ring.relay()
    sums.middle()
    r.bias_one[...] = sum_rows(r.joined[...].astype(F32))
    r.vecs_one[2:3] = sum_rows(r.g[...] * r.branch[...])
    r.vecs_one[3:4] = sum_rows(r.g16[...].astype(F32))
    r.vecs_one[4:8] = jnp.zeros((4, D), F32)
    weight_grads(r.second, r.joined, r.whole_one, 3 * HW)
    write_slabs((r.whole_one, 3 * HW), (r.whole_two, HW), r.attn_left, r.attn_right)
    sums.end_rows(r.ffn_rows)
    input_grad = ring.total()
    normed, inv_std = layer_stats(r.x[...])
    r.vecs_one[0:1] = sum_rows(input_grad)
    r.vecs_one[1:2] = sum_rows(input_grad * normed)
    grad = r.g[...] + layer_back(input_grad * (1.0 + r.vec_one[1:2]), normed, inv_std)
    if last:
        r.out[...] = grad
    else:
        grad16 = grad.astype(BF16)
        r.embed_w_grad[...] = dot_tn(r.patches[...], grad16)
        r.embed_b_grad[...] = sum_rows(grad16.astype(F32))
        r.latent[...] = dot_nt(grad16, r.embed_w[...])
    ring.leave()


def weight_grads(left_ref, right_ref, whole_ref, width):
    @pl.loop(0, D // 128)
    def _(k):
        at = pl.ds(pl.multiple_of(k * 128, 128), 128)
        whole_ref[at, :width] = dot_tn(left_ref[:, at], right_ref[...])


def write_slabs(one, two, left_ref, right_ref):
    cut = left_ref.shape[3]
    cols = cut + right_ref.shape[3]

    @pl.loop(0, 16)
    def _(k):
        at = pl.ds(pl.multiple_of(k * PART, 8), PART)
        parts = [ref[at, :width] for ref, width in (one, two)]
        spare = cols - one[1] - two[1]
        if spare:
            parts.append(jnp.zeros((PART, spare), F32))
        rows = jnp.concatenate(parts, axis=1)
        rows = jnp.concatenate([rows, jnp.zeros((SLAB - PART, cols), F32)], axis=0).astype(BF16)
        x, z = k // 4, lax.rem(k, 4)
        left_ref[x, z] = rows[:, :cut]
        right_ref[x, z] = rows[:, cut:]


def line_only(lines):
    return [peer for peer, _ in lines[0] + lines[1]]


def slab_specs(cols):
    widths = (CUT[cols], cols - CUT[cols])
    return [((4, 4, SLAB, width), BF16) for width in widths]


def block_backward(near, far, tokens, last, cid):
    vecs = ((8, D), F32)
    attn_left, attn_right = slab_specs(ATT_COLS)
    outs = {
        "vecs_one": vecs,
        "vecs_two": vecs,
        "bias_one": ((1, 3 * HW), F32),
        "bias_two": ((1, FW), F32),
        "attn_left": attn_left,
        "attn_right": attn_right,
        "ffn_rows": ((SLAB, FFN_COLS), BF16),
    }
    wide, tile = (8 * tokens, D), (tokens, D)
    scratch = {
        "g16": pltpu.VMEM(tile, BF16),
        "g_one": pltpu.VMEM(wide, BF16),
        "g_two": pltpu.VMEM(wide, BF16),
        "pre_all": pltpu.VMEM((8 * tokens, FW), BF16),
        "joined": pltpu.VMEM((8 * tokens, 3 * HW), BF16),
        "dk": pltpu.VMEM((2, 8 * tokens, HEAD), F32),
        "dv": pltpu.VMEM((2, 8 * tokens, HEAD), F32),
        "whole_one": pltpu.VMEM((D, FW), F32),
        "whole_two": pltpu.VMEM((D, FW), F32),
        "ffn_left": pltpu.VMEM(*slab_specs(FFN_COLS)[0]),
        "ffn_right": pltpu.VMEM(*slab_specs(FFN_COLS)[1]),
        "ring_local": ring_local(tokens),
        "ring_one": ring_remote(tokens),
        "ring_two": ring_remote(tokens),
        "sums_two": rows_out_scratch(FFN_COLS),
    }
    if last:
        outs["out"] = (tile, F32)
        scratch["g"] = pltpu.VMEM(tile, F32)
    else:
        outs["attn_rows"] = ((SLAB, ATT_COLS), BF16)
        outs["embed_w_grad"] = ((16, D), F32)
        outs["embed_b_grad"] = ((1, D), F32)
        outs["latent"] = ((tokens, 16), F32)
        scratch["g"] = pltpu.VMEM(tile, F32)
        scratch["sums_one"] = rows_out_scratch(ATT_COLS)
    body = functools.partial(backward_body, tokens=tokens, last=last)
    return launch(body, cid, near, far, outs, {}, scratch, vmem=62 << 20)


def head_kernel(
    first_ref, two_ref, place_ref, vec_ref, unpatch_ref, bias_ref, cot_ref,
    out_ref, unpatch_grad_ref, vecs_ref, ended_ref, chosen_ref
):
    picks = choice(place_ref, two_ref.shape[0])
    ended = spread_back(picks, two_ref[...], first_ref[...])
    normed, inv_std = layer_stats(ended)
    final16 = (normed * (1.0 + vec_ref[1:2]) + vec_ref[0:1]).astype(BF16)
    out_ref[...] = (dot_nn(final16, unpatch_ref[...]) + bias_ref[...]).astype(BF16)
    unpatch_grad_ref[...] = dot_tn(final16, cot_ref[...])
    grad = dot_nt(cot_ref[...], unpatch_ref[...])
    vecs_ref[0:1] = sum_rows(grad)
    vecs_ref[1:2] = sum_rows(grad * normed)
    grad = layer_back(grad * (1.0 + vec_ref[1:2]), normed, inv_std)
    ended_ref[...] = grad
    chosen_ref[...] = exact(picks, grad, (1, 0))


def head(first, two, place, vecs, unpatch, bias, cotangent):
    tokens, capacity = first.shape[0], two.shape[0]
    outs = (
        jax.ShapeDtypeStruct((tokens, 32), BF16),
        jax.ShapeDtypeStruct((D, 32), F32),
        jax.ShapeDtypeStruct((2, D), F32),
        jax.ShapeDtypeStruct((tokens, D), F32),
        jax.ShapeDtypeStruct((capacity, D), F32),
    )
    return pl.pallas_call(
        head_kernel,
        out_shape=outs,
        in_specs=[VMEM] * 7,
        out_specs=(VMEM,) * 5,
        compiler_params=pltpu.CompilerParams(vmem_limit_bytes=32 << 20),
    )(first, two, place, vecs, unpatch, bias, cotangent)


def pack_weights(attention_weight, merge_weight, expand_weight, reduce_weight):
    def by_group(array):
        parts = array.reshape(*array.shape[:-1], 8, array.shape[-1] // 8)
        return jnp.moveaxis(parts, -2, 0)

    attn, merge = by_group(attention_weight), by_group(merge_weight)
    expand, reduce = by_group(expand_weight), by_group(reduce_weight)
    spare = jnp.zeros((8, 9, ATT_COLS - 4 * HW), BF16)
    columns = []
    for b in range(2):
        columns += [attn[:, b].reshape(8, 9, 3 * HW), merge[:, b], spare]
    for b in range(2):
        columns += [expand[:, b], reduce[:, b]]
    return pack_pieces(jnp.concatenate(columns, axis=2))


def pack_pieces(columns):
    pieces = columns.reshape(8, 9, PIECES, PIECE).swapaxes(1, 2)
    return jnp.pad(pieces.reshape(8, 9 * PIECES, PIECE), [(0, 0), (0, 1), (0, 0)])


def pack_small(parts):
    flat = jnp.concatenate([part.reshape(-1) for part in parts])
    return jnp.pad(flat, (0, 2048 - flat.shape[0])).reshape(16, 128)


def by_owner(array, dim):
    before, after = array.shape[:dim], array.shape[dim + 1 :]
    parts = array.reshape(*before, 128, array.shape[dim] // 128, *after)
    return jnp.moveaxis(parts, dim, 0).reshape(128, -1)


def from_owner(parts, shape, dim):
    split = parts.reshape(128, *shape[:dim], shape[dim] // 128, *shape[dim + 1 :])
    return jnp.moveaxis(split, 0, dim).reshape(shape)


def shards(
    latent,
    condition,
    routed_ids,
    embed_weight,
    embed_bias,
    modulation_weight,
    modulation_bias,
    attention_weight,
    attention_bias,
    merge_weight,
    merge_bias,
    expand_weight,
    expand_bias,
    reduce_weight,
    reduce_bias,
    final_modulation,
    final_offsets,
    unpatch_weight,
    unpatch_bias,
    pred_cotangent,
):
    count = latent.shape[0]
    tile_rows = latent.shape[1] // 2
    tile_cols = latent.shape[2] // 2
    tile_tokens = tile_rows * tile_cols
    rows_tiles = lax.axis_size("tx")
    cols_tiles = lax.axis_size("ty")
    tiles = rows_tiles * cols_tiles
    grid_side = tile_rows * rows_tiles
    row_index = lax.axis_index("tx") * tile_rows + jnp.arange(tile_rows, dtype=jnp.int32)
    col_index = lax.axis_index("ty") * tile_cols + jnp.arange(tile_cols, dtype=jnp.int32)
    token_index = (row_index[:, None] * grid_side + col_index[None, :]).reshape(tile_tokens)
    routed = jnp.sum(
        (routed_ids[:, :, None] == token_index[None, None, :]).astype(jnp.float32), axis=1
    )
    capacity = 7 * tile_tokens // 8
    id_tiles = (
        routed_ids // grid_side // tile_rows * cols_tiles + routed_ids % grid_side // tile_cols
    )
    tile_loads = jnp.sum(
        (id_tiles[:, :, None] == jnp.arange(tiles, dtype=jnp.int32)[None, None, :]).astype(
            jnp.int32
        ),
        axis=1,
    )
    routed_marks = jnp.arange(capacity, dtype=jnp.int32)[None, None, :] < tile_loads[:, :, None]
    routed_marks = routed_marks.astype(jnp.float32).reshape(count, tiles * capacity)
    flags = routed[0] > 0
    place = jnp.where(flags, jnp.cumsum(flags.astype(jnp.int32)) - 1, -1)[None]
    whole_index = lax.axis_index(DP_TX_TY)
    small_parts = (
        embed_weight,
        embed_bias,
        unpatch_weight,
        attention_bias,
        merge_bias,
        expand_bias,
        reduce_bias,
    )
    cond_rows = jax.nn.silu(condition.astype(F32)).astype(BF16)
    mod_piece = modulation_bias.shape[1]
    final_piece = final_offsets.shape[0]
    placed_bias = jnp.zeros((MOD_ALL,), F32)
    for bias, at in (
        (modulation_bias[0], whole_index * mod_piece),
        (modulation_bias[1], 6 * D + whole_index * mod_piece),
        (final_offsets, 12 * D + whole_index * final_piece),
    ):
        placed_bias = lax.dynamic_update_slice_in_dim(placed_bias, bias.astype(F32), at, 0)
    mod_parts = jnp.concatenate(
        [
            jnp.dot(cond_rows, modulation_weight[0], preferred_element_type=F32),
            jnp.dot(cond_rows, modulation_weight[1], preferred_element_type=F32),
            jnp.dot(cond_rows, final_modulation, preferred_element_type=F32),
        ],
        axis=1,
    )
    mod_parts = jnp.pad(mod_parts + placed_bias[None], [(0, 0), (0, 16384 - MOD_ALL)])
    packed = pack_weights(attention_weight, merge_weight, expand_weight, reduce_weight)
    rows, *first_attn, mods, small = open_up(
        packed, mod_parts.reshape(4, 4, 128, 128), pack_small(small_parts)
    )
    mods = mods.reshape(1, 16384)
    mod_one = mods[:, : 6 * D]
    mod_two = mods[:, 6 * D : 12 * D]
    head_mod = mods[:, 12 * D : 14 * D]
    small = small.reshape(8, 16, 2048).swapaxes(0, 1).reshape(128, 2048)
    pieces = jnp.split(small, [sum(SMALL_IN[:k]) for k in range(1, 8)], axis=1)
    embed_w = from_owner(pieces[0], (16, D), 1)
    embed_b = from_owner(pieces[1], (D,), 0)
    unpatch_w = from_owner(pieces[2], (D, 32), 0)
    attn_b = from_owner(pieces[3], (2, 2 * D), 1)
    merge_b = from_owner(pieces[4], (2, D), 1)
    expand_b = from_owner(pieces[5], (2, FF), 1)
    reduce_b = from_owner(pieces[6], (2, D), 1)
    placed = sincos_table(row_index.astype(F32), col_index.astype(F32), D)
    patches = to_patches(latent)[0]
    mask_one = jnp.zeros((1, tiles * tile_tokens), F32)
    mask_two = jnp.where(routed_marks > 0, 0.0, -1e30).astype(F32)
    group = own_group()
    zeros = jnp.zeros((4, D), F32)

    def own_cols(bias, start, cols):
        return lax.dynamic_slice_in_dim(bias, start + group * cols, cols).astype(F32)

    def block_near(b, mod, wqkv, wm, mask):
        vecs = mod.reshape(6, D)
        bias = [own_cols(attn_b[b], 0, HW), jnp.zeros((HW,), F32), own_cols(attn_b[b], D, HW)]
        return {
            "vec_one": jnp.concatenate([vecs[0:3], merge_b[b].astype(F32)[None], zeros]),
            "vec_two": jnp.concatenate([vecs[3:6], reduce_b[b].astype(F32)[None], zeros]),
            "mask": mask,
            "wqkv": wqkv,
            "wm": wm,
        }, {
            "bias_one": jnp.concatenate(bias)[None],
            "bias_two": own_cols(expand_b[b], 0, FW)[None],
            "rows": rows,
        }

    near_one, more_one = block_near(0, mod_one, *first_attn, mask_one)
    start_one = {"patches": patches, "embed_w": embed_w, "embed_b": embed_b.astype(F32)[None]}
    kept_one = block_forward(
        {**near_one, **more_one, **start_one, "placed": placed}, tile_tokens, 2 * ATT_COLS, False, 10
    )
    near_two, more_two = block_near(
        1, mod_two, kept_one.pop("next_wqkv"), kept_one.pop("next_wm"), mask_two
    )
    first = kept_one.pop("out")
    kept_two = block_forward(
        {**near_two, **more_two, "first": first, "place": place},
        capacity,
        2 * ATT_COLS + FFN_COLS,
        True,
        11,
    )
    cotangent = to_patches(pred_cotangent)[0]
    outputs, grad_unpatch_w, head_grad_mod, grad_ended, grad_chosen = head(
        first,
        kept_two.pop("out"),
        place,
        head_mod.reshape(2, D),
        unpatch_w,
        unpatch_bias.astype(F32)[None],
        cotangent,
    )
    predicted = from_patches(outputs[None], tile_rows, tile_cols)
    grad_unpatch_b = jnp.sum(cotangent.astype(F32), axis=0)
    back_two = block_backward({**near_two, "grad_in": grad_chosen}, kept_two, capacity, True, 12)
    later = {
        "pending_left": back_two["attn_left"],
        "pending_right": back_two["attn_right"],
        "grad_two": back_two["out"],
        "grad_ended": grad_ended,
        "place": place,
        "patches": patches,
        "embed_w": embed_w,
    }
    back_one = block_backward({**near_one, **later}, kept_one, tile_tokens, False, 13)
    latent_grad = from_patches(back_one["latent"][None], tile_rows, tile_cols)
    grad_embed_w, grad_embed_b = back_one["embed_w_grad"], back_one["embed_b_grad"][0]

    def placed_cols(parts, length):
        whole = jnp.zeros((length,), F32)
        for part, at in parts:
            whole = lax.dynamic_update_slice_in_dim(whole, part, at, 0)
        return whole

    def bias_parts(back):
        one, two = back["bias_one"][0], back["bias_two"][0]
        return (
            placed_cols([(one[:HW], group * HW), (one[2 * HW :], D + group * HW)], 2 * D),
            back["vecs_one"][3],
            placed_cols([(two, group * FW)], FF),
            back["vecs_two"][3],
        )

    biases_one, biases_two = bias_parts(back_one), bias_parts(back_two)
    mod_grads = [back[name][0:3].reshape(-1) for back in (back_one, back_two) for name in ("vecs_one", "vecs_two")]
    bias_grads = [jnp.stack([biases_one[member], biases_two[member]]) for member in range(4)]
    small_out = jnp.concatenate(
        [
            by_owner(grad_embed_w, 1),
            by_owner(grad_embed_b, 0),
            by_owner(grad_unpatch_w, 0),
            by_owner(bias_grads[0], 1),
            by_owner(bias_grads[1], 1),
            by_owner(bias_grads[2], 1),
            by_owner(bias_grads[3], 1),
            jnp.broadcast_to(grad_unpatch_b[None], (128, 32)),
        ],
        axis=1,
    )
    small_out = jnp.pad(small_out, [(0, 0), (0, 1024 - small_out.shape[1])])
    grad_mods = jnp.concatenate([*mod_grads, head_grad_mod.reshape(-1)])
    grad_mods = jnp.pad(grad_mods, (0, 16384 - MOD_ALL))
    early, late, mod_back, small_back = finish(
        (back_one["attn_left"], back_one["attn_right"]),
        back_one["attn_rows"],
        back_one["ffn_rows"],
        back_two["ffn_rows"],
        grad_mods.reshape(8, 16, 128),
        small_out.reshape(4, 4, 64, 128),
    )
    mod_back = mod_back.reshape(8, 16, 2048).swapaxes(0, 1).reshape(16, 16384)
    attn_grad, *closed = close(
        early, late, mod_back, cond_rows, modulation_weight, final_modulation
    )
    merge_grad, expand_grad, reduce_grad, mod_weight_grad, final_mod_grad, cond_terms, bias_sum = closed
    small_back = small_back.reshape(1024)
    small_sizes = (*SMALL_IN, 32)
    small_sums = jnp.split(small_back, [sum(small_sizes[:k]) for k in range(1, 9)])
    mod_bias_grad = jnp.stack(
        [
            lax.dynamic_slice_in_dim(bias_sum[0], at + whole_index * mod_piece, mod_piece)
            for at in (0, 6 * D)
        ]
    )
    final_bias_grad = lax.dynamic_slice_in_dim(
        bias_sum[0], 12 * D + whole_index * final_piece, final_piece
    )
    silu_value, silu_pull = jax.vjp(jax.nn.silu, condition.astype(jnp.float32))
    condition_grad = silu_pull(cond_terms)[0]
    return (
        predicted,
        latent_grad,
        condition_grad,
        small_sums[0].reshape(16, 9),
        small_sums[1],
        mod_weight_grad,
        mod_bias_grad,
        attn_grad.swapaxes(1, 2),
        small_sums[3].reshape(2, 18),
        merge_grad,
        small_sums[4].reshape(2, 9),
        expand_grad,
        small_sums[5].reshape(2, 36),
        reduce_grad,
        small_sums[6].reshape(2, 9),
        final_mod_grad,
        final_bias_grad,
        small_sums[2].reshape(9, 32),
        small_sums[7],
    )


def solution(mesh):
    torus = Mesh(
        mesh.devices.reshape(4, 4, mesh.shape["tx"], mesh.shape["ty"]), ("dp_0", "dp_1", "tx", "ty")
    )
    return jax.shard_map(
        shards,
        mesh=torus,
        in_specs=(
            P(DP, "tx", "ty", None),
            P(None, DP_TX_TY),
            P(DP, None),
            P(None, DP_TX_TY),
            P(DP_TX_TY),
            P(None, DP_TX_TY, None),
            P(None, DP_TX_TY),
            P(None, DP_TX_TY, None, None),
            P(None, DP_TX_TY),
            P(None, DP_TX_TY, None),
            P(None, DP_TX_TY),
            P(None, DP_TX_TY, None),
            P(None, DP_TX_TY),
            P(None, DP_TX_TY, None),
            P(None, DP_TX_TY),
            P(DP_TX_TY, None),
            P(DP_TX_TY),
            P(DP_TX_TY, None),
            P(),
            P(DP, "tx", "ty", None),
        ),
        out_specs=(
            P(DP, "tx", "ty", None),
            P(DP, "tx", "ty", None),
            P(None, DP_TX_TY),
            P(None, DP_TX_TY),
            P(DP_TX_TY),
            P(None, DP_TX_TY, None),
            P(None, DP_TX_TY),
            P(None, DP_TX_TY, None, None),
            P(None, DP_TX_TY),
            P(None, DP_TX_TY, None),
            P(None, DP_TX_TY),
            P(None, DP_TX_TY, None),
            P(None, DP_TX_TY),
            P(None, DP_TX_TY, None),
            P(None, DP_TX_TY),
            P(DP_TX_TY, None),
            P(DP_TX_TY),
            P(DP_TX_TY, None),
            P(),
        ),
        check_vma=False,
    )
```

```python
import functools

import jax
import jax.numpy as jnp
import numpy as np
from jax import lax
from jax.experimental import pallas as pl
from jax.experimental.pallas import tpu as pltpu
from jax.sharding import Mesh
from jax.sharding import PartitionSpec as P

D = 1152
HEADS = 16
FF = 4608
HW = D // 8
FW = FF // 8
DP = ("dp_0", "dp_1")
DP_TX_TY = ("dp_0", "dp_1", "tx", "ty")
MESH = pl.DeviceIdType.MESH
VMEM = pl.BlockSpec(memory_space=pltpu.VMEM)
FAR = pl.BlockSpec(memory_space=pl.ANY)
F32 = jnp.float32
BF16 = jnp.bfloat16
ATT_COLS = 640
FFN_COLS = 2 * FW
ALL_COLS = 2 * (ATT_COLS + FFN_COLS)
PIECE = 512
PIECES = ALL_COLS // PIECE


def greet(peers):
    barrier = pltpu.get_barrier_semaphore()
    for peer in peers:
        pl.semaphore_signal(barrier, inc=1, device_id=peer, device_id_type=MESH)


def met(peers):
    pl.semaphore_wait(pltpu.get_barrier_semaphore(), len(peers))


def enter(peers):
    greet(peers)
    met(peers)


def send(src, dst, sems, k, peer):
    copy = pltpu.make_async_remote_copy(
        src_ref=src,
        dst_ref=dst,
        send_sem=sems[0].at[k],
        recv_sem=sems[1].at[k],
        device_id=peer,
        device_id_type=MESH,
    )
    copy.start()
    return copy


def group_peers():
    c, y = lax.axis_index("tx"), lax.axis_index("ty")
    found = []
    for dc in range(2):
        for dy in range(4):
            if dc or dy:
                oc, oy = lax.rem(c + dc, 2), lax.rem(y + dy, 4)
                found.append(({"tx": oc, "ty": oy}, oc * 4 + oy))
    return found


def own_group():
    return lax.axis_index("tx") * 4 + lax.axis_index("ty")


def dma_sems(n):
    return [pltpu.SemaphoreType.DMA((n,)), pltpu.SemaphoreType.DMA((n,))]


def ring_peers():
    c, y = lax.axis_index("tx"), lax.axis_index("ty")
    return (
        {"tx": 1 - c},
        {"ty": lax.rem(y + 1, 4)},
        {"ty": lax.rem(y + 3, 4)},
        {"ty": lax.rem(y + 2, 4)},
    )


def layer_stats(value_rows):
    centered = value_rows - jnp.mean(value_rows, axis=-1, keepdims=True)
    inv_std = lax.rsqrt(jnp.mean(centered * centered, axis=-1, keepdims=True) + 1e-06)
    return (centered * inv_std, inv_std)


def layer_back(upstream, normed, inv_std):
    return inv_std * (
        upstream
        - jnp.mean(upstream, axis=-1, keepdims=True)
        - normed * jnp.mean(upstream * normed, axis=-1, keepdims=True)
    )


def sincos_table(row_pos, col_pos, width):
    quarter = width // 4
    freqs = jnp.power(10000.0, -jnp.arange(quarter, dtype=jnp.float32) / quarter)
    row_angle = row_pos[:, None] * freqs[None, :]
    col_angle = col_pos[:, None] * freqs[None, :]
    row_embed = jnp.concatenate([jnp.sin(row_angle), jnp.cos(row_angle)], axis=-1)
    col_embed = jnp.concatenate([jnp.sin(col_angle), jnp.cos(col_angle)], axis=-1)
    row_full = jnp.broadcast_to(
        row_embed[:, None, :], (row_pos.shape[0], col_pos.shape[0], width // 2)
    )
    col_full = jnp.broadcast_to(
        col_embed[None, :, :], (row_pos.shape[0], col_pos.shape[0], width // 2)
    )
    return jnp.concatenate([row_full, col_full], axis=-1).reshape(
        row_pos.shape[0] * col_pos.shape[0], width
    )


def ring_local(tokens):
    return [
        pltpu.VMEM((4, tokens, D), F32),
        pltpu.VMEM((4, tokens, D), BF16),
        pltpu.VMEM((3, tokens, D), BF16),
    ]


def ring_remote(tokens):
    half = (tokens // 2 + 15) // 16 * 16
    return [
        pltpu.VMEM((4, tokens, D), BF16),
        pltpu.VMEM((2, tokens, D), BF16),
        pltpu.VMEM((half, D), BF16),
        pltpu.VMEM((tokens - half, D), BF16),
    ] + dma_sems(24)


SLAB = 80
PART = D // 16
CUT = {ATT_COLS: 384, FFN_COLS: 640}


def line_peers():
    x, z = lax.axis_index("dp_0"), lax.axis_index("dp_1")
    along_x = [({"dp_0": lax.rem(x + d, 4)}, lax.rem(x + d, 4)) for d in (2, 1, 3)]
    along_z = [({"dp_1": lax.rem(z + d, 4)}, lax.rem(z + d, 4)) for d in (2, 1, 3)]
    return along_x, along_z


class RowsIn:
    def __init__(self, left_ref, right_ref, scratch):
        self.left, self.right = left_ref, right_ref
        self.all_left, self.all_right = scratch[:2]
        self.sems = tuple(scratch[2:4])
        self.x, self.z = lax.axis_index("dp_0"), lax.axis_index("dp_1")
        self.along_x, self.along_z = line_peers()

    def peers(self):
        return [peer for peer, _ in self.along_x + self.along_z]

    def start(self):
        x, z = self.x, self.z
        self.first = []
        for k, (peer, _) in enumerate(self.along_z):
            self.first.append(send(self.left, self.all_left.at[x, z], self.sems, k, peer))
        for k, (peer, _) in enumerate(self.along_x):
            self.first.append(send(self.right, self.all_right.at[x, z], self.sems, 3 + k, peer))
        self.all_left[x, z] = self.left[...]
        self.all_right[x, z] = self.right[...]

    def middle(self):
        left, right = self.all_left.at[self.x], self.all_right.at[:, self.z]
        self.second = []
        for copy in self.first[:3]:
            copy.wait_recv()
        for k, (peer, _) in enumerate(self.along_x):
            self.second.append(send(left, left, self.sems, 6 + k, peer))
        for copy in self.first[3:]:
            copy.wait_recv()
        for k, (peer, _) in enumerate(self.along_z):
            self.second.append(send(right, right, self.sems, 9 + k, peer))

    def end(self, one_ref, two_ref):
        for copy in self.second:
            copy.wait_recv()
        width, other = one_ref.shape[1], two_ref.shape[1]
        cut = self.left.shape[1]

        @pl.loop(0, 8)
        def _(pair):
            x, z = pair // 2, 2 * lax.rem(pair, 2)
            both = []
            for k in range(2):
                parts = [self.all_left[x, z + k], self.all_right[x, z + k]]
                both.append(jnp.concatenate(parts, axis=1).astype(F32)[:PART])
            value = jnp.concatenate(both, axis=0).astype(BF16)
            at = pl.ds(pl.multiple_of(pair * 2 * PART, 16), 2 * PART)
            one_ref[at, :] = value[:, :width]
            two_ref[at, :] = value[:, width : width + other]

        for copy in self.first + self.second:
            copy.wait_send()


def rows_in_scratch(cols):
    left = CUT[cols]
    return [
        pltpu.VMEM((4, 4, SLAB, left), BF16),
        pltpu.VMEM((4, 4, SLAB, cols - left), BF16),
    ] + dma_sems(12)


class RowsOut:
    def __init__(self, left_ref, right_ref, scratch):
        self.left, self.right = left_ref, right_ref
        self.got = scratch[0:2]
        self.mine = scratch[2:4]
        self.last = scratch[4:6]
        self.sems = tuple(scratch[6:8])
        self.x, self.z = lax.axis_index("dp_0"), lax.axis_index("dp_1")
        self.along_x, self.along_z = line_peers()

    def peers(self):
        return [peer for peer, _ in self.along_x + self.along_z]

    def start(self):
        self.first = []
        for k, (peer, at) in enumerate(self.along_x):
            part = self.left.at[at]
            self.first.append(send(part, self.got[0].at[k], self.sems, k, peer))
        for k, (peer, at) in enumerate(self.along_z):
            part = self.right.at[:, at]
            self.first.append(send(part, self.got[1].at[k], self.sems, 3 + k, peer))

    def middle(self):
        self.second = []
        for side, peers in ((0, self.along_z), (1, self.along_x)):
            for copy in self.first[3 * side : 3 * side + 3]:
                copy.wait_recv()
            got, mine = self.got[side], self.mine[side]

            @pl.loop(0, 4)
            def _(k):
                own = self.right[k, self.z] if side else self.left[self.x, k]
                across, below, above = (got[source, k].astype(F32) for source in range(3))
                total = (own.astype(F32) + across) + (below + above)
                mine[k] = total.astype(mine.dtype)

            for k, (peer, at) in enumerate(peers):
                part = mine.at[at]
                copy = send(part, self.last[side].at[k], self.sems, 6 + 3 * side + k, peer)
                self.second.append(copy)

    def end(self):
        for copy in self.second:
            copy.wait_recv()
        totals = []
        for side, own in ((0, self.z), (1, self.x)):
            across, below, above = (self.last[side][source].astype(F32) for source in range(3))
            totals.append((self.mine[side][own].astype(F32) + across) + (below + above))
        return totals

    def end_rows(self, out_ref):
        cut = self.left.shape[3]
        left, right = self.end()
        out_ref[:, :cut] = left.astype(BF16)
        out_ref[:, cut:] = right.astype(BF16)
        self.leave()

    def leave(self):
        for copy in self.first + self.second:
            copy.wait_send()


def rows_out_scratch(cols):
    return sum_scratch([(SLAB, CUT[cols]), (SLAB, cols - CUT[cols])], BF16)


def sum_scratch(shapes, dtype):
    return (
        [pltpu.VMEM((3, 4, *shape), dtype) for shape in shapes]
        + [pltpu.VMEM((4, *shape), dtype) for shape in shapes]
        + [pltpu.VMEM((3, *shape), dtype) for shape in shapes]
        + dma_sems(12)
    )


def slab_views(rows_ref, start, cols):
    cut = start + CUT[cols]
    return rows_ref.at[:, start:cut], rows_ref.at[:, cut : start + cols]


def weight_shapes(cols):
    widths = (3 * HW, HW) if cols == ATT_COLS else (FW, FW)
    return tuple(jax.ShapeDtypeStruct((D, w), BF16) for w in widths)


class Ring:
    def __init__(self, tokens, local, remote):
        self.tokens = tokens
        self.half = (tokens // 2 + 15) // 16 * 16
        self.kept, self.sib_out, self.out = local
        self.sib_in, self.got, self.far_low, self.far_high = remote[:4]
        self.sems = tuple(remote[4:6])
        c, y = lax.axis_index("tx"), lax.axis_index("ty")
        self.sib, self.up, self.down, _ = ring_peers()
        self.own = [c * 4 + lax.rem(y + d, 4) for d in range(4)]
        self.other = [(1 - c) * 4 + lax.rem(y + d, 4) for d in range(4)]
        self.sent = []

    def peers(self):
        return [self.sib, self.up, self.down]

    def send(self, src, dst, k, peer):
        copy = send(src, dst, self.sems, k, peer)
        self.sent.append(copy)
        return copy

    def rows(self, index, start=0, stop=None):
        stop = self.tokens if stop is None else stop
        at = pl.multiple_of(index * self.tokens + start, 16)
        return pl.ds(at, stop - start)

    def gather(self, x_ref, all_ref, prepare, visit, between=None):
        half, tokens = self.half, self.tokens
        me, above, across, below = self.own
        first, last = slice(0, half), slice(half, tokens)

        def pass_on(index, k, peer, start=0, stop=None):
            part = all_ref.at[self.rows(index, start, stop)]
            return self.send(part, part, k, peer)

        def own_part(rows, k, peer):
            part = all_ref.at[self.rows(me, rows.start, rows.stop)]
            return self.send(x_ref.at[rows], part, k, peer)

        a1 = own_part(first, 0, self.up)
        b1 = own_part(last, 1, self.down)
        a2 = own_part(last, 2, self.up)
        b2 = own_part(first, 3, self.down)
        s0 = self.send(x_ref, all_ref.at[self.rows(me)], 4, self.sib)
        all_ref[self.rows(me), :] = x_ref[...]
        prepare()
        visit(True, 0)
        s0.wait_recv()
        visit(False, 0)
        a1.wait_recv()
        f1 = pass_on(below, 5, self.up, 0, half)
        b1.wait_recv()
        f2 = pass_on(above, 6, self.down, half, tokens)
        a2.wait_recv()
        s1 = pass_on(below, 7, self.sib)
        b2.wait_recv()
        s2 = pass_on(above, 8, self.sib)
        if between:
            between()
        visit(True, 3)
        visit(True, 1)
        s1.wait_recv()
        visit(False, 3)
        s2.wait_recv()
        visit(False, 1)
        f1.wait_recv()
        f2.wait_recv()
        s3 = pass_on(across, 9, self.sib)
        visit(True, 2)
        s3.wait_recv()
        visit(False, 2)

    def put(self, own, d, value):
        if own:
            self.kept[d] = value
        else:
            self.sib_out[d] = value.astype(BF16)
            self.swaps[d] = self.send(self.sib_out.at[d], self.sib_in.at[d], 10 + d, self.sib)

    def start_sums(self):
        self.swaps = {}

    def chip_sum(self, d):
        self.swaps[d].wait_recv()
        return self.kept[d] + self.sib_in[d].astype(F32)

    def near(self):
        half = self.half
        first, last = slice(0, half), slice(half, self.tokens)
        total = self.chip_sum(1)
        self.kept[1] = total
        self.out[0, last] = total[half:].astype(BF16)
        self.n1 = self.send(self.out.at[0, last], self.got.at[0, last], 14, self.up)
        total = self.chip_sum(3)
        self.kept[3] = total
        self.out[1, first] = total[:half].astype(BF16)
        self.n2 = self.send(self.out.at[1, first], self.got.at[1, first], 15, self.down)

    def far(self):
        half = self.half
        self.out[2] = self.chip_sum(2).astype(BF16)
        self.low, self.high = [], []
        for k, (start, stop) in enumerate(((0, 32), (32, half))):
            part = self.out.at[2, start:stop]
            self.low.append(self.send(part, self.far_low.at[start:stop], 16 + k, self.up))
        for k, (start, stop) in enumerate(((half, half + 32), (half + 32, self.tokens))):
            part = self.out.at[2, start:stop]
            landing = self.far_high.at[start - half : stop - half]
            self.high.append(self.send(part, landing, 18 + k, self.down))

    def relay(self):
        half, self.last = self.half, []
        for k in range(2):
            rows = slice(0, 32) if k == 0 else slice(32, half)
            self.low[k].wait_recv()
            value = self.kept[1, rows] + self.far_low[rows].astype(F32)
            self.out[0, rows] = value.astype(BF16)
            part = self.out.at[0, rows]
            self.last.append(self.send(part, self.got.at[0, rows], 20 + k, self.up))
            rows = slice(half, half + 32) if k == 0 else slice(half + 32, self.tokens)
            self.high[k].wait_recv()
            landed = self.far_high[rows.start - half : rows.stop - half]
            self.out[1, rows] = (self.kept[3, rows] + landed.astype(F32)).astype(BF16)
            part = self.out.at[1, rows]
            self.last.append(self.send(part, self.got.at[1, rows], 22 + k, self.down))

    def total(self):
        value = self.chip_sum(0)
        for copy in [self.n1, self.n2] + self.last:
            copy.wait_recv()
        return value + self.got[0].astype(F32) + self.got[1].astype(F32)

    def leave(self):
        for copy in self.sent:
            copy.wait_send()


def dot_nn(left, right):
    return lax.dot_general(left, right, (((1,), (0,)), ((), ())), preferred_element_type=F32)


def dot_nt(left, right):
    return lax.dot_general(left, right, (((1,), (1,)), ((), ())), preferred_element_type=F32)


def dot_tn(left, right):
    return lax.dot_general(left, right, (((0,), (0,)), ((), ())), preferred_element_type=F32)


def gelu_both(pre):
    root = 0.7978845608028654
    square = pre * pre
    bent = jnp.tanh(root * pre * (1.0 + 0.044715 * square))
    value = 0.5 * pre * (1.0 + bent)
    slope = 0.5 * (1.0 + bent) + 0.5 * pre * (1.0 - bent * bent) * root * (1.0 + 0.134145 * square)
    return value, slope


def sum_rows(value):
    return jnp.sum(value, axis=0, keepdims=True)


HEAD = D // HEADS
SCALE = HEAD ** (-0.5)


def head_cols(h, start=0):
    return slice(start + h * HEAD, start + (h + 1) * HEAD)


class Refs:
    pass


class Results(dict):
    __getattr__ = dict.__getitem__


def make_specs(entry):
    return list(entry) if isinstance(entry, list) else [entry]


def launch(body, cid, near, far, outs, kept, scratch, vmem=60 << 20):
    twins = {name: (value.shape, value.dtype) for name, value in far.items()}
    twins.update(kept)
    groups = {name: make_specs(entry) for name, entry in scratch.items()}

    def kernel(*refs):
        refs = iter(refs)
        r, hbm = Refs(), {}
        for name in near:
            setattr(r, name, next(refs))
        for name in far:
            hbm[name] = next(refs)
        for name in outs:
            setattr(r, name, next(refs))
        for name in kept:
            hbm[name] = next(refs)
        r.moves, r.moving = {}, {}
        for k, name in enumerate(twins):
            ref = next(refs)
            setattr(r, name, ref)
            r.moves[id(ref)] = (hbm[name], k)
        if twins:
            r.move_sems = next(refs)
        for name, specs in groups.items():
            found = [next(refs) for _ in specs]
            setattr(r, name, found if isinstance(scratch[name], list) else found[0])
        body(r)

    shapes = [jax.ShapeDtypeStruct(*spec) for spec in (*outs.values(), *kept.values())]
    results = pl.pallas_call(
        kernel,
        out_shape=tuple(shapes),
        in_specs=[VMEM] * len(near) + [FAR] * len(far),
        out_specs=(VMEM,) * len(outs) + (FAR,) * len(kept),
        scratch_shapes=[pltpu.VMEM(*spec) for spec in twins.values()]
        + ([pltpu.SemaphoreType.DMA((len(twins),))] if twins else [])
        + [spec for specs in groups.values() for spec in specs],
        compiler_params=pltpu.CompilerParams(
            collective_id=cid, has_side_effects=cid is not None, vmem_limit_bytes=vmem
        ),
    )(*near.values(), *far.values())
    return Results(zip(outs, results)), Results(zip(kept, results[len(outs) :]))


def load_into(r, ref, target):
    source, k = r.moves[id(ref)]
    r.moving[id(ref)] = pltpu.make_async_copy(source, target, r.move_sems.at[k])
    r.moving[id(ref)].start()


def load(r, *refs):
    for ref in refs:
        load_into(r, ref, ref)


def save(r, *refs):
    for ref in refs:
        target, k = r.moves[id(ref)]
        r.moving[id(ref)] = pltpu.make_async_copy(ref, target, r.move_sems.at[k])
        r.moving[id(ref)].start()


def settle(r, *refs):
    for key in [id(ref) for ref in refs] or list(r.moving):
        r.moving.pop(key).wait()


def exact(left, right, dims):
    return lax.dot_general(
        left,
        right,
        ((dims[:1], dims[1:]), ((), ())),
        precision=lax.Precision.HIGHEST,
        preferred_element_type=F32,
    )


def choice(place_ref, capacity):
    tokens = place_ref.shape[1]
    slots = lax.broadcasted_iota(jnp.int32, (capacity, tokens), 0)
    return jnp.where(slots == place_ref[...], 1.0, 0.0).astype(F32)


def spread_back(picks, chosen, others):
    used = exact(picks, jnp.ones((picks.shape[0], 128), F32), (0, 0))[:, :1]
    return exact(picks, chosen, (0, 0)) + others * (1.0 - used)


def modulated(x, vec_ref):
    normed, _ = layer_stats(x)
    return (normed * (1.0 + vec_ref[1:2]) + vec_ref[0:1]).astype(BF16)


def full_width(parts, at):
    height = parts[0].shape[0]
    used = at + sum(part.shape[1] for part in parts)
    if at:
        parts = [jnp.zeros((height, at), F32), *parts]
    if used < 128:
        parts = [*parts, jnp.zeros((height, 128 - used), F32)]
    return jnp.concatenate(parts, axis=1)


def to_tokens(pixels_ref, square, tokens_ref, at):
    wide, depth, high = pixels_ref.shape
    square[...] = jnp.zeros_like(square)
    square[: wide * depth, :high] = pixels_ref[...].astype(F32).reshape(wide * depth, high)
    square[...] = jnp.transpose(square[...])
    size = 2 * depth
    lines = [square[pl.ds(line, high // 2, stride=2), :] for line in range(2)]
    for c in range(wide // 2):
        parts = [value[:, c * size : (c + 1) * size] for value in lines]
        tokens_ref[pl.ds(c, high // 2, stride=wide // 2), :] = full_width(parts, at)


def to_pixels(tokens_ref, square, pixels_ref, at):
    wide, depth, high = pixels_ref.shape
    square[...] = jnp.zeros_like(square)
    size = 2 * depth
    columns = [tokens_ref[pl.ds(c, high // 2, stride=wide // 2), :] for c in range(wide // 2)]
    for line in range(2):
        start = at + line * size
        parts = [value[:, start : start + size] for value in columns]
        square[pl.ds(line, high // 2, stride=2), :] = full_width(parts, 0)
    value = jnp.transpose(square[...])[: wide * depth, :high].reshape(wide, depth, high)
    pixels_ref[...] = value.astype(pixels_ref.dtype)


UNPATCH, EMBED, BLOCKS, EMBED_BIAS = 0, 32, 48, 64
WHOLE = 16384


def own_targets():
    group = own_group()
    return group * (D // 16), group * (D // 8)


def bias_table():
    table = np.zeros((8, 1024), np.int32)
    for col in range(3 * HW):
        part, e = divmod(col, HW)
        table[0, col] = (e // 18 + (64 if part == 2 else 0)) * 9 + e % 9 if part != 1 else -(1 << 20)
        table[1, col] = e % 18 // 9
    for e in range(FW):
        table[0, 3 * HW + e] = e // 36 * 9 + e % 9
        table[1, 3 * HW + e] = e % 36 // 9
    return table


def bias_picks(table_ref, cols, shift):
    rows = lax.broadcasted_iota(jnp.int32, (D, cols.stop - cols.start), 0)
    return jnp.where(rows == table_ref[0:1, cols] + shift, 1.0, 0.0).astype(F32)


ATT_BIAS = slice(0, 3 * HW)
FFN_BIAS = slice(3 * HW, 3 * HW + FW)


def mod_places(index):
    e = lax.broadcasted_iota(jnp.int32, (1, 128), 1)
    at = jnp.where(e < 108, 6 * D - 54 + index * 54 + e, 12 * D - 108 + index * 18 + e)
    at = jnp.where(e < 54, index * 54 + e, at)
    at = jnp.where(e < 126, at, -1)
    lines = lax.broadcasted_iota(jnp.int32, (128, 128), 0)
    return lines == lax.shift_right_arithmetic(at, 7), lines == jnp.bitwise_and(at, 127)


def whole_index():
    x, z = lax.axis_index("dp_0"), lax.axis_index("dp_1")
    return (x * 4 + z) * 8 + own_group()


def route(r):
    token = lax.broadcasted_iota(jnp.int32, (128, 512), 0)
    row = lax.axis_index("tx") * 16 + token // 8
    col = lax.axis_index("ty") * 8 + lax.rem(token, 8)
    hits = jnp.where(row * 32 + col == r.ids[...], 1.0, 0.0).astype(BF16)
    flags = dot_nt(jnp.ones((8, 512), BF16), hits)
    lines = lax.broadcasted_iota(jnp.int32, (128, 128), 0)
    lanes = lax.broadcasted_iota(jnp.int32, (128, 128), 1)
    before = dot_nn(flags.astype(BF16), jnp.where(lines <= lanes, 1.0, 0.0).astype(BF16))
    r.place[...] = jnp.where(flags > 0, before - 1.0, -1.0)[0:1].astype(jnp.int32)
    tile = r.ids[...] // 512 * 4 + lax.rem(r.ids[...], 32) // 8
    slot = lax.broadcasted_iota(jnp.int32, r.mask.shape, 1)
    capacity = r.mask.shape[1] // 8
    used = slot < 0
    for k in range(8):
        load_k = jnp.sum(jnp.where(tile == k, 1.0, 0.0), axis=1, keepdims=True).astype(jnp.int32)
        at = slot - k * capacity
        used = used | ((at >= 0) & (at < capacity) & (at < load_k))
    r.mask[...] = jnp.where(used, 0.0, -1e30)


def open_body(r):
    group = group_peers()
    sib, up, down, far = ring_peers()
    fetch = RowsIn(*slab_views(r.rows, 0, ATT_COLS), r.fetch)
    mods = RowsOut(r.m_mine.at[:, :, 0:64], r.m_mine.at[:, :, 64:128], r.mods)
    peers = [peer for peer, _ in group] + fetch.peers()
    greet(peers)
    r.pack[...] = jnp.zeros_like(r.pack)
    attn = [[r.attn_w[:, j, b, :] for j in range(3)] for b in range(2)]
    merge = [r.merge_w[:, b, :] for b in range(2)]
    expand = [r.expand_w[:, b, :] for b in range(2)]
    reduce = [r.reduce_w[:, b, :] for b in range(2)]
    spare = jnp.zeros((9, ATT_COLS - 4 * HW), BF16)
    for p in range(8):
        narrow, wide = slice(p * HW, (p + 1) * HW), slice(p * FW, (p + 1) * FW)
        parts = []
        for b in range(2):
            parts += [attn[b][j][:, narrow] for j in range(3)] + [merge[b][:, narrow], spare]
        for b in range(2):
            parts += [expand[b][:, wide], reduce[b][:, wide]]
        r.pack[p * 16 : p * 16 + 9, :] = jnp.concatenate(parts, axis=1)
    packed = jnp.zeros((8 * 64, PIECE), F32)
    for k in range(PIECES):
        packed = packed + dot_tn(r.unpicks[k], r.pack[:, k * PIECE : (k + 1) * PIECE])
    r.w_mine[...] = packed.astype(BF16).reshape(8, 64, PIECE)
    r.lines[...] = jnp.zeros_like(r.lines)
    r.lines[EMBED : EMBED + 16, 0:9] = r.embed_w[...].astype(F32)
    for b in range(2):
        at = BLOCKS + 8 * b
        for j in range(2):
            r.lines[at + j : at + j + 1, 0:9] = r.attn_b[b : b + 1, 9 * j : 9 * j + 9].astype(F32)
        for j in range(4):
            value = r.expand_b[b : b + 1, 9 * j : 9 * j + 9].astype(F32)
            r.lines[at + 2 + j : at + 3 + j, 0:9] = value
        r.lines[at + 6 : at + 7, 0:9] = r.merge_b[b : b + 1].astype(F32)
        r.lines[at + 7 : at + 8, 0:9] = r.reduce_b[b : b + 1].astype(F32)
    r.lines[EMBED_BIAS : EMBED_BIAS + 1, 0:9] = r.embed_b[...].astype(F32)
    r.block[...] = jnp.transpose(r.lines[...])[0:16]
    r.block[0:9, UNPATCH : UNPATCH + 32] = r.unpatch_w[...].astype(F32)
    me, x, z = own_group(), lax.axis_index("dp_0"), lax.axis_index("dp_1")
    r.small[x, z, me] = r.block[...].astype(BF16)
    met(peers)
    sems = (r.ss, r.rs)
    weights = [
        send(r.w_mine.at[at], r.w_got.at[me], sems, k, p) for k, (p, at) in enumerate(group)
    ]
    small = r.small.at[x, z, me]
    first = [send(small, small, sems, 7 + k, p) for k, (p, _) in enumerate(fetch.along_z)]
    r.w_got[me] = r.w_mine[me]

    condition = r.condition[...].astype(F32)
    cond16 = (condition / (1.0 + jnp.exp(-condition))).astype(BF16)
    on_line, on_lane = mod_places(whole_index())
    r.places[...] = jnp.zeros_like(r.places)
    r.places[0:1, 0:54] = r.mod_b[0:1].astype(F32)
    r.places[0:1, 54:108] = r.mod_b[1:2].astype(F32)
    r.places[0:1, 108:126] = r.final_b[...].astype(F32)
    left = jnp.where(on_line, r.places[0:1], 0.0).astype(BF16)
    right = jnp.where(on_lane, 1.0, 0.0).astype(BF16)
    r.placed_bias[...] = dot_nt(left, right)
    r.m_mine[:, :, 126:128] = jnp.zeros((4, 4, 2, 128), F32)
    for b in range(3):
        weight = r.mod_w[:, b, :] if b < 2 else r.final_w[...]
        part = dot_nn(cond16, weight)
        for k in range(part.shape[1] // 128):
            line = 54 * b + k
            value = part[:, k * 128 : (k + 1) * 128] + r.placed_bias[line : line + 1]
            r.m_mine[:, :, line, :] = value.reshape(4, 4, 128)
    mods.start()
    for copy in first:
        copy.wait_recv()
    small = r.small.at[x, :, me]
    second = [send(small, small, sems, 10 + k, p) for k, (p, _) in enumerate(fetch.along_x)]
    for copy in weights:
        copy.wait_recv()
    received = r.w_got[...].reshape(8 * 64, PIECE)
    for k in range(PIECES):
        r.rows[:, k * PIECE : (k + 1) * PIECE] = dot_nn(r.picks[k], received).astype(BF16)
    fetch.start()
    for copy in second:
        copy.wait_recv()
    small = r.small.at[:, :, me]
    third = [send(small, small, sems, 13 + k, p) for k, p in enumerate((up, down, far, sib))]
    mods.middle()
    fetch.middle()
    route(r)
    r.m_sum[0:64], r.m_sum[64:128] = mods.end()

    def chunk(ref, index):
        return ref.at[pl.ds(pl.multiple_of(index * 16, 16), 16)]

    m_first = [
        send(chunk(r.m_sum, at), r.m_got.at[me], sems, 20 + k, p) for k, (p, at) in enumerate(group)
    ]
    mine = pl.ds(pl.multiple_of(me * 16, 16), 16)
    r.m_got[me] = r.m_sum[mine, :]
    for copy in m_first:
        copy.wait_recv()
    total = r.m_got[0]
    for k in range(1, 8):
        total = total + r.m_got[k]
    r.m_all[mine, :] = total
    part = chunk(r.m_all, me)
    m_second = [send(part, part, sems, 27 + k, p) for k, (p, _) in enumerate(group)]
    c, y = lax.axis_index("tx"), lax.axis_index("ty")
    fourth = []
    for k, d in enumerate((3, 1, 2)):
        third[k].wait_recv()
        small = r.small.at[:, :, c * 4 + lax.rem(y + d, 4)]
        fourth.append(send(small, small, sems, 17 + k, sib))
    for copy in fourth + third[3:]:
        copy.wait_recv()

    @pl.loop(0, 16)
    def _(k):
        got = r.small[k // 4, lax.rem(k, 4)].reshape(128, 128)
        at = pl.ds(pl.multiple_of(k * PART, 8), PART)
        r.feat32[at, :] = dot_nn(r.pick_small[...], got)[:PART]

    r.feat[...] = r.feat32[...].astype(BF16)
    for k in range(9):
        cols = slice(k * 128, (k + 1) * 128)
        r.turned[:, cols] = jnp.transpose(r.feat32[cols, :])
    attn_at, ffn_at = own_targets()
    picks = bias_picks(r.table, ATT_BIAS, attn_at).astype(BF16)
    blocks = r.turned[BLOCKS : BLOCKS + 16].astype(BF16)
    narrow = dot_nn(blocks, picks)
    wide = dot_nn(blocks, bias_picks(r.table, FFN_BIAS, ffn_at).astype(BF16))
    for b, (one, two) in enumerate(((r.bias_one_0, r.bias_two_0), (r.bias_one_1, r.bias_two_1))):
        at, which = 8 * b, r.table[1:2, ATT_BIAS]
        one[...] = jnp.where(which == 0, narrow[at : at + 1], narrow[at + 1 : at + 2])
        value, which = wide[at + 2 : at + 3], r.table[1:2, FFN_BIAS]
        for j in range(1, 4):
            value = jnp.where(which == j, wide[at + 2 + j : at + 3 + j], value)
        two[...] = value
    for copy in m_second:
        copy.wait_recv()

    def mod_line(k):
        return jnp.concatenate([r.m_all[9 * k + i : 9 * k + i + 1] for i in range(9)], axis=1)

    vecs = (r.vec_one_0, r.vec_two_0, r.vec_one_1, r.vec_two_1)
    for k, ref in enumerate(vecs):
        for i in range(3):
            ref[i : i + 1] = mod_line(3 * k + i)
        at = BLOCKS + 8 * (k // 2) + 6 + k % 2
        ref[3:4] = r.turned[at : at + 1]
        ref[4:5] = r.turned[EMBED_BIAS : EMBED_BIAS + 1]
        ref[5:8] = jnp.zeros((3, D), F32)
    r.head_vec[0:1] = mod_line(12)
    r.head_vec[1:2] = mod_line(13)
    fetch.end(r.wqkv, r.wm)
    for copy in weights + first + second + third + fourth + m_first + m_second:
        copy.wait_send()
    mods.leave()


def picking():
    picks = np.zeros((PIECES, SLAB, 8 * 64), np.float32)
    for k in range(PIECES):
        for row in range(72):
            picks[k, row, row // 9 * 64 + 9 * k + row % 9] = 1.0
    return picks


def picking_small():
    picks = np.zeros((SLAB, 128), np.float32)
    for row in range(72):
        picks[row, row // 9 * 16 + row % 9] = 1.0
    return picks


def open_up(arguments):
    near = dict(
        **arguments,
        unpicks=jnp.asarray(unpicking(PIECES, 64), BF16),
        picks=jnp.asarray(picking(), BF16),
        pick_small=jnp.asarray(picking_small(), BF16),
        table=jnp.asarray(bias_table()),
    )
    vec = ((8, D), F32)
    outs = dict(
        rows=((SLAB, ALL_COLS), BF16),
        wqkv=((D, 3 * HW), BF16),
        wm=((D, HW), BF16),
        feat=((D, 128), BF16),
        vec_one_0=vec,
        vec_two_0=vec,
        vec_one_1=vec,
        vec_two_1=vec,
        head_vec=((2, D), F32),
        place=((1, 128), jnp.int32),
        mask=((1, 8 * 112), F32),
        bias_one_0=((1, 3 * HW), F32),
        bias_one_1=((1, 3 * HW), F32),
        bias_two_0=((1, FW), F32),
        bias_two_1=((1, FW), F32),
    )
    scratch = dict(
        pack=pltpu.VMEM((128, ALL_COLS), BF16),
        w_mine=pltpu.VMEM((8, 64, PIECE), BF16),
        w_got=pltpu.VMEM((8, 64, PIECE), BF16),
        lines=pltpu.VMEM((128, 128), F32),
        block=pltpu.VMEM((16, 128), F32),
        small=pltpu.VMEM((4, 4, 8, 16, 128), BF16),
        places=pltpu.VMEM((8, 128), F32),
        placed_bias=pltpu.VMEM((128, 128), F32),
        m_mine=pltpu.VMEM((4, 4, 128, 128), F32),
        m_sum=pltpu.VMEM((128, 128), F32),
        m_got=pltpu.VMEM((8, 16, 128), F32),
        m_all=pltpu.VMEM((128, 128), F32),
        feat32=pltpu.VMEM((D, 128), F32),
        turned=pltpu.VMEM((128, D), F32),
        ss=dma_sems(34)[0],
        rs=dma_sems(34)[1],
        fetch=rows_in_scratch(ATT_COLS),
        mods=sum_scratch([(64, 128), (64, 128)], F32),
    )
    return launch(open_body, 1, near, {}, outs, {}, scratch)[0]


EARLY = ATT_COLS + 2 * FFN_COLS
EARLY_PIECES = -(-EARLY // PIECE)
LATE_PIECES = -(-ATT_COLS // PIECE)
LATE_ROWS = 32


def packed_rows(picks_ref, parts, pieces):
    columns = jnp.concatenate(parts, axis=1)
    spare = pieces * PIECE - columns.shape[1]
    columns = jnp.concatenate([columns, jnp.zeros((SLAB, spare), BF16)], axis=1)
    total = jnp.zeros((8 * 64, PIECE), F32)
    for k in range(pieces):
        total = total + dot_tn(picks_ref[k], columns[:, k * PIECE : (k + 1) * PIECE])
    return total.astype(BF16).reshape(8, 64, PIECE)


def bias_lines(table_ref, cols, shift, biases, count):
    which = table_ref[1:2, cols]
    parts = []
    for bias in biases:
        rest = jnp.concatenate(
            [jnp.where(which == j, bias, 0.0) for j in range(count)]
            + [jnp.zeros((8 - count, bias.shape[1]), F32)],
            axis=0,
        )
        for _ in range(3):
            part = rest.astype(BF16).astype(F32)
            parts.append(part)
            rest = rest - part
    parts = jnp.concatenate(parts, axis=0).astype(BF16)
    found = dot_nt(parts, bias_picks(table_ref, cols, shift).astype(BF16))
    sums = [found[24 * k : 24 * k + 8] for k in range(2)]
    return [
        (sums[k] + found[24 * k + 8 : 24 * k + 16] + found[24 * k + 16 : 24 * k + 24])[:count]
        for k in range(2)
    ]


def finish_body(r):
    group = group_peers()
    sib, up, down, far = ring_peers()
    rows = RowsOut(r.left, r.right, r.rows_sums)
    small = RowsOut(r.small.at[:, :, 0:40], r.small.at[:, :, 40:80], r.small_sums)
    peers = [peer for peer, _ in group] + rows.peers()
    greet(peers)
    me, x, z = own_group(), lax.axis_index("dp_0"), lax.axis_index("dp_1")
    sems = (r.ss, r.rs)
    r.m_mine[...] = jnp.zeros_like(r.m_mine)
    vecs = (r.vecs_one_0, r.vecs_two_0, r.vecs_one_1, r.vecs_two_1, r.head_vecs)
    for k, ref in enumerate(vecs):
        for i in range(3 if k < 4 else 2):
            for j in range(9):
                line = 27 * k + 9 * i + j
                r.m_mine[line // 16, line % 16 : line % 16 + 1] = ref[
                    i : i + 1, j * 128 : (j + 1) * 128
                ]
    met(peers)
    rows.start()
    m_first = [send(r.m_mine.at[at], r.m_got.at[me], sems, k, p) for k, (p, at) in enumerate(group)]
    r.m_got[me] = r.m_mine[me]
    attn_at, ffn_at = own_targets()
    biases = (r.bias_one_0[...], r.bias_one_1[...])
    narrow = bias_lines(r.table, ATT_BIAS, attn_at, biases, 2)
    biases = (r.bias_two_0[...], r.bias_two_1[...])
    wide = bias_lines(r.table, FFN_BIAS, ffn_at, biases, 4)
    vecs = ((r.vecs_one_0, r.vecs_two_0), (r.vecs_one_1, r.vecs_two_1))
    for k in range(2):
        r.bias_rows[k, 0:2] = narrow[k]
        r.bias_rows[k, 2:6] = wide[k]
        r.bias_rows[k, 6:7] = vecs[k][0][3:4]
        r.bias_rows[k, 7:8] = vecs[k][1][3:4]
    r.turned[...] = jnp.zeros_like(r.turned)
    for k in range(9):
        cols = slice(k * 128, (k + 1) * 128)
        r.lines[...] = jnp.zeros_like(r.lines)
        r.lines[0:32] = r.unpatch_rows[:, cols]
        r.lines[32:48] = r.embed_rows[0:16, cols]
        r.lines[48:56] = r.bias_rows[0, :, cols]
        r.lines[56:64] = r.bias_rows[1, :, cols]
        r.lines[64:72] = r.embed_rows[16:24, cols]
        r.turned[cols, :] = jnp.transpose(r.lines[...])
    for k in range(16):
        r.small[k // 4, k % 4, 0:72] = r.turned[k * PART : (k + 1) * PART, :]
        r.small[k // 4, k % 4, 72:80] = r.unpatch_bias[...]
    small.start()
    r.early[...] = packed_rows(
        r.picks, [r.attn_rows[...], r.ffn_rows_0[...], r.ffn_rows_1[...]], EARLY_PIECES
    )
    sent = [
        send(r.early.at[at], r.early_out.at[me], sems, 7 + k, p) for k, (p, at) in enumerate(group)
    ]
    r.early_out[me] = r.early[me]
    for copy in m_first:
        copy.wait_recv()
    total = r.m_got[0]
    for k in range(1, 8):
        total = total + r.m_got[k]
    r.m_out[me, x, z] = total.astype(BF16)
    part = r.m_out.at[me, x, z]
    m_second = [send(part, part, sems, 14 + k, p) for k, (p, _) in enumerate(rows.along_z)]
    small.middle()
    for copy in m_second:
        copy.wait_recv()
    part = r.m_out.at[me, x]
    m_third = [send(part, part, sems, 17 + k, p) for k, (p, _) in enumerate(rows.along_x)]
    r.s_total[0:40], r.s_total[40:80] = small.end()
    for g in range(8):
        r.s_mine[g, 0:9] = r.s_total[9 * g : 9 * g + 9]
        r.s_mine[g, 9:16] = r.s_total[72:79]
    s_last = [
        send(r.s_mine.at[at], r.s_two.at[me], sems, 20 + k, p) for k, (p, at) in enumerate(group)
    ]
    r.s_two[me] = r.s_mine[me]
    for copy in m_third:
        copy.wait_recv()
    part = r.m_out.at[me]
    m_fourth = [send(part, part, sems, 27 + k, p) for k, p in enumerate((up, down, far, sib))]
    rows.middle()
    c, y = lax.axis_index("tx"), lax.axis_index("ty")
    m_fifth = []
    for k, d in enumerate((3, 1, 2)):
        m_fourth[k].wait_recv()
        part = r.m_out.at[c * 4 + lax.rem(y + d, 4)]
        m_fifth.append(send(part, part, sems, 31 + k, sib))
    for copy in s_last:
        copy.wait_recv()
    total = r.s_two[0]
    for k in range(1, 8):
        total = total + r.s_two[k]
    r.s_out[...] = total
    rows.end_rows(r.late_rows)
    r.late[...] = packed_rows(r.picks, [r.late_rows[...]], LATE_PIECES)[:, :LATE_ROWS]
    later = [
        send(r.late.at[at], r.late_out.at[me], sems, 34 + k, p) for k, (p, at) in enumerate(group)
    ]
    r.late_out[me] = r.late[me]
    for copy in sent + m_fourth[3:] + m_fifth + later:
        copy.wait_recv()
    small.leave()
    for copy in m_first + sent + m_second + m_third + s_last + m_fourth + m_fifth + later:
        copy.wait_send()


def finish(near):
    near = dict(near, picks=jnp.asarray(picking(), BF16))
    outs = dict(
        early_out=((8, 64, PIECE), BF16),
        late_out=((8, LATE_ROWS, PIECE), BF16),
        m_out=((8, 4, 4, 16, 128), BF16),
        s_out=((16, 128), F32),
    )
    scratch = dict(
        early=pltpu.VMEM((8, 64, PIECE), BF16),
        late=pltpu.VMEM((8, LATE_ROWS, PIECE), BF16),
        m_mine=pltpu.VMEM((8, 16, 128), F32),
        m_got=pltpu.VMEM((8, 16, 128), F32),
        lines=pltpu.VMEM((128, 128), F32),
        bias_rows=pltpu.VMEM((2, 8, D), F32),
        turned=pltpu.VMEM((D, 128), F32),
        small=pltpu.VMEM((4, 4, 80, 128), F32),
        s_total=pltpu.VMEM((80, 128), F32),
        s_mine=pltpu.VMEM((8, 16, 128), F32),
        s_two=pltpu.VMEM((8, 16, 128), F32),
        late_rows=pltpu.VMEM((SLAB, ATT_COLS), BF16),
        ss=dma_sems(41)[0],
        rs=dma_sems(41)[1],
        rows_sums=rows_out_scratch(ATT_COLS),
        small_sums=sum_scratch([(40, 128), (40, 128)], F32),
    )
    return launch(finish_body, 2, near, {}, outs, {}, scratch)[0]


def unpicking(pieces, height):
    picks = np.zeros((pieces, 128, 8 * height), np.float32)
    for k in range(pieces):
        for group in range(8):
            for row in range(9):
                picks[k, group * 16 + row, group * height + 9 * k + row] = 1.0
    return picks


def close_body(r):
    load(r, r.early_in, r.late_in, r.m_in)
    settle(r, r.early_in, r.late_in)
    received = r.early_in[...].reshape(8 * 64, PIECE)
    for k in range(EARLY_PIECES):
        r.early[:, k * PIECE : (k + 1) * PIECE] = dot_nn(r.early_picks[k], received)
    received = r.late_in[...].reshape(8 * LATE_ROWS, PIECE)
    for k in range(LATE_PIECES):
        r.late[:, k * PIECE : (k + 1) * PIECE] = dot_nn(r.late_picks[k], received)

    def whole(source, start, width):
        parts = [source[g * 16 : g * 16 + 16, start : start + width] for g in range(8)]
        return jnp.concatenate(parts, axis=1)[:9]

    for b, (source, start) in enumerate(((r.late, 0), (r.early, 0))):
        for j in range(3):
            r.attn[:, j, b, :] = whole(source, start + j * HW, HW)
        r.merge[:, b, :] = whole(source, start + 3 * HW, HW)
    for b, start in enumerate((ATT_COLS, ATT_COLS + FFN_COLS)):
        r.expand[:, b, :] = whole(r.early, start, FW)
        r.reduce[:, b, :] = whole(r.early, start + FW, FW)
    settle(r, r.m_in)
    for k in range(128):
        value = r.m_in[k // 16, :, :, k % 16, :]
        r.grads[:, k * 128 : (k + 1) * 128] = value.reshape(16, 128)
        r.sums[k : k + 1] = sum_rows(value.reshape(16, 128).astype(F32))
    condition = r.condition[...].astype(F32)
    gate = 1.0 / (1.0 + jnp.exp(-condition))
    cond16 = (condition / (1.0 + jnp.exp(-condition))).astype(BF16)
    terms = jnp.zeros((16, 9), F32)
    for b in range(3):
        grads = r.grads[:, 6 * b * D : min(6 * b + 6, 14) * D]
        weights = r.mod_w[:, b, :] if b < 2 else r.final_w[...]
        product = dot_tn(cond16, grads)
        if b < 2:
            r.mod_grad[:, b, :] = product
        else:
            r.final_grad[...] = product
        terms = terms + dot_nt(grads, weights)
    r.condition_grad[...] = terms * (gate * (1.0 + condition * (1.0 - gate)))
    on_line, on_lane = mod_places(whole_index())
    found = exact(r.sums[...], jnp.where(on_lane, 1.0, 0.0).astype(F32), (1, 0))
    found = sum_rows(jnp.where(on_line, found, 0.0))
    r.mod_b[0:1] = found[:, 0:54]
    r.mod_b[1:2] = found[:, 54:108]
    r.final_b[...] = found[:, 108:126]
    r.square[...] = jnp.zeros_like(r.square)
    r.square[0:16] = r.s_in[...]
    turned = jnp.transpose(r.square[...])
    r.unpatch_w[...] = r.s_in[0:9, 0:32]
    r.unpatch_b[...] = r.s_in[9:10, 0:32]
    r.embed_w[...] = turned[32:48, 0:9]
    r.embed_b[...] = turned[64:65, 0:9]
    for b in range(2):
        at = BLOCKS + 8 * b
        for j in range(2):
            r.attn_b[b : b + 1, 9 * j : 9 * j + 9] = turned[at + j : at + j + 1, 0:9]
        for j in range(4):
            r.expand_b[b : b + 1, 9 * j : 9 * j + 9] = turned[at + 2 + j : at + 3 + j, 0:9]
        r.merge_b[b : b + 1] = turned[at + 6 : at + 7, 0:9]
        r.reduce_b[b : b + 1] = turned[at + 7 : at + 8, 0:9]


def close(near, far):
    near = dict(
        **near,
        early_picks=jnp.asarray(unpicking(EARLY_PIECES, 64), BF16),
        late_picks=jnp.asarray(unpicking(LATE_PIECES, LATE_ROWS), BF16),
    )
    outs = dict(
        attn=((9, 3, 2, D), F32),
        merge=((9, 2, D), F32),
        expand=((9, 2, FF), F32),
        reduce=((9, 2, FF), F32),
        mod_grad=((9, 2, 6 * D), F32),
        final_grad=((9, 2 * D), F32),
        condition_grad=((16, 9), F32),
        mod_b=((2, 54), F32),
        final_b=((1, 18), F32),
        unpatch_w=((9, 32), F32),
        unpatch_b=((1, 32), F32),
        embed_w=((16, 9), F32),
        embed_b=((1, 9), F32),
        attn_b=((2, 18), F32),
        expand_b=((2, 36), F32),
        merge_b=((2, 9), F32),
        reduce_b=((2, 9), F32),
    )
    scratch = dict(
        early=pltpu.VMEM((128, EARLY_PIECES * PIECE), F32),
        late=pltpu.VMEM((128, LATE_PIECES * PIECE), F32),
        grads=pltpu.VMEM((16, WHOLE), BF16),
        sums=pltpu.VMEM((128, 128), F32),
        square=pltpu.VMEM((128, 128), F32),
    )
    return launch(close_body, None, near, far, outs, {}, scratch, vmem=40 << 20)[0]


def forward_body(r, tokens, start, last):
    ring = Ring(tokens, r.ring_local, r.ring_one)
    fetch = RowsIn(*slab_views(r.rows, start, FFN_COLS), r.fetch_one)
    peers = ring.peers() + fetch.peers()
    greet(peers)
    if last:
        r.x[...] = exact(choice(r.place, tokens), r.first[...], (1, 0))
    else:
        r.token_cols[...] = jnp.zeros_like(r.token_cols)
        to_tokens(r.pixels, r.square, r.token_cols, EMBED)
        r.patches[...] = r.token_cols[...].astype(BF16)
        r.x[...] = dot_nt(r.patches[...], r.feat[...]) + r.vec_one[4:5] + r.placed[...]
    r.x16[...] = modulated(r.x[...], r.vec_one)
    met(peers)
    save(r, r.x)
    ring.start_sums()

    def visit(own, d):
        rows = ring.rows((ring.own if own else ring.other)[d])
        joined = (dot_nn(r.in_all[rows, :], r.wqkv[...]) + r.bias_one[...]).astype(BF16)
        for h in range(2):
            r.q[h, rows, :] = joined[:, head_cols(h)]
            r.k[h, rows, :] = joined[:, head_cols(h, HW)]
            r.v[h, rows, :] = joined[:, head_cols(h, 2 * HW)]

    def attend(own, d):
        rows = ring.rows((ring.own if own else ring.other)[d])
        parts = []
        for h in range(2):
            scores = dot_nt(r.q[h, rows, :], r.k[h]) * SCALE
            if last:
                scores = scores + r.mask[...]
            highest = jnp.max(scores, axis=-1, keepdims=True)
            shifted = jnp.exp(scores - highest)
            summed = jnp.sum(shifted, axis=-1, keepdims=True)
            probs = (shifted * (1.0 / summed)).astype(BF16)
            r.lse[rows, h : h + 1] = highest + jnp.log(summed)
            parts.append(dot_nn(probs, r.v[h]).astype(BF16))
        attended = jnp.concatenate(parts, axis=1)
        r.att[rows, :] = attended
        ring.put(own, d, dot_nt(attended, r.wm[...]))

    ring.gather(r.x16, r.in_all, fetch.start, visit, fetch.middle)
    attend(False, 2)
    attend(True, 2)
    ring.far()
    save(r, r.in_all, r.q, r.k, r.v)
    for d in (1, 3):
        attend(False, d)
        attend(True, d)
    ring.near()
    ring.relay()
    attend(False, 0)
    attend(True, 0)
    save(r, r.lse, r.att)
    fetch.end(r.we, r.wr)
    save(r, r.we, r.wr)
    branch = ring.total() + r.vec_one[3:4]
    r.branch[...] = branch
    middle = r.x[...] + r.vec_one[2:3] * branch
    r.middle[...] = middle
    save(r, r.branch, r.middle)
    ring.leave()

    ring = Ring(tokens, r.ring_local, r.ring_two)
    fetch = None
    if not last:
        fetch = RowsIn(*slab_views(r.rows, ATT_COLS, ATT_COLS), r.fetch_two)
    r.x16[...] = modulated(middle, r.vec_two)
    ring.start_sums()

    def prepare():
        if fetch:
            fetch.start()

    def expand(own, d):
        rows = ring.rows((ring.own if own else ring.other)[d])
        pre = dot_nn(r.second[rows, :], r.we[...]) + r.bias_two[...]
        value, slope = gelu_both(pre)
        hidden = value.astype(BF16)
        r.hid[rows, :] = hidden
        r.slope[rows, :] = slope.astype(BF16)
        ring.put(own, d, dot_nt(hidden, r.wr[...]))
        if not own and d == 1:
            ring.near()

    ring.gather(r.x16, r.second, prepare, expand, fetch.middle if fetch else None)
    ring.far()
    save(r, r.second, r.hid, r.slope)
    ring.relay()
    if fetch:
        fetch.end(r.next_wqkv, r.next_wm)
    mlp = ring.total() + r.vec_two[3:4]
    r.mlp[...] = mlp
    save(r, r.mlp)
    r.out[...] = r.middle[...] + r.vec_two[2:3] * mlp
    ring.leave()
    settle(r)


def kept_shapes(tokens):
    heads = ((2, 8 * tokens, HEAD), BF16)
    wide, tile = ((8 * tokens, D), BF16), ((tokens, D), F32)
    hidden = ((8 * tokens, FW), BF16)
    return dict(
        x=tile,
        in_all=wide,
        q=heads,
        k=heads,
        v=heads,
        lse=((8 * tokens, 2), F32),
        att=((8 * tokens, HW), BF16),
        branch=tile,
        middle=tile,
        second=wide,
        hid=hidden,
        slope=hidden,
        mlp=tile,
        we=((D, FW), BF16),
        wr=((D, FW), BF16),
    )


def block_forward(near, tokens, start, last, cid):
    outs = dict(out=((tokens, D), F32))
    scratch = dict(
        x16=pltpu.VMEM((tokens, D), BF16),
        ring_local=ring_local(tokens),
        ring_one=ring_remote(tokens),
        ring_two=ring_remote(tokens),
        fetch_one=rows_in_scratch(FFN_COLS),
    )
    if not last:
        outs.update(next_wqkv=((D, 3 * HW), BF16))
        outs.update(next_wm=((D, HW), BF16))
        outs.update(patches=((128, 128), BF16))
        scratch.update(square=pltpu.VMEM((128, 128), F32), token_cols=pltpu.VMEM((128, 128), F32))
        scratch.update(fetch_two=rows_in_scratch(ATT_COLS))
    body = functools.partial(forward_body, tokens=tokens, start=start, last=last)
    return launch(body, cid, near, {}, outs, kept_shapes(tokens), scratch)


def head(r):
    picks = choice(r.place, r.two.shape[0])
    ended = spread_back(picks, r.two[...], r.first[...])
    normed, inv_std = layer_stats(ended)
    final16 = (normed * (1.0 + r.head_vec[1:2]) + r.head_vec[0:1]).astype(BF16)
    unpatch = r.feat[:, UNPATCH : UNPATCH + 32]
    r.token_cols[...] = jnp.zeros_like(r.token_cols)
    r.token_cols[:, 0:32] = dot_nn(final16, unpatch) + r.unpatch_b[...].astype(F32)
    to_pixels(r.token_cols, r.square, r.predicted, 0)
    to_tokens(r.cotangent_pixels, r.square, r.token_cols, 0)
    r.cotangent[...] = r.token_cols[:, 0:32].astype(BF16)
    r.unpatch_rows[...] = dot_tn(r.cotangent[...], final16)
    r.unpatch_bias[...] = jnp.zeros_like(r.unpatch_bias)
    r.unpatch_bias[0:1, 0:32] = sum_rows(r.cotangent[...].astype(F32))
    grad = dot_nt(r.cotangent[...], unpatch)
    r.head_vecs[0:1] = sum_rows(grad)
    r.head_vecs[1:2] = sum_rows(grad * normed)
    grad = layer_back(grad * (1.0 + r.head_vec[1:2]), normed, inv_std)
    r.grad_ended[...] = grad
    r.g[...] = exact(picks, grad, (1, 0))


def backward_body(r, tokens, last):
    ring = Ring(tokens, r.ring_local, r.ring_one)
    sums = None if last else RowsOut(r.pending_left, r.pending_right, r.sums_one)
    peers = ring.peers() + line_only(line_peers())
    greet(peers)
    if last:
        load(r, r.first, r.two, r.slope, r.wr, r.we)
    else:
        load(r, r.grad_two, r.grad_ended, r.slope, r.wr, r.we, r.pending_left, r.pending_right)
    load(r, r.hid, r.second, r.mlp, r.middle)
    load(r, r.q, r.k, r.v, r.lse, r.wm, r.wqkv, r.att, r.x, r.branch)
    if last:
        settle(r, r.first, r.two)
        head(r)
    else:
        settle(r, r.grad_two, r.grad_ended)
        picks = choice(r.place, r.grad_two.shape[0])
        r.g[...] = spread_back(picks, r.grad_two[...], r.grad_ended[...])
    r.g16[...] = (r.g[...] * r.vec_two[2:3]).astype(BF16)
    met(peers)
    ring.start_sums()
    r.bias_two[...] = jnp.zeros_like(r.bias_two)

    def prepare():
        if sums:
            settle(r, r.pending_left, r.pending_right)
            sums.start()
        settle(r, r.slope, r.wr, r.we)

    def visit(own, d):
        rows = ring.rows((ring.own if own else ring.other)[d])
        pre_grad = (
            dot_nn(r.g_one[rows, :], r.wr[...]) * r.slope[rows, :].astype(F32)
        ).astype(BF16)
        r.pre_all[rows, :] = pre_grad
        r.bias_two[...] += sum_rows(pre_grad.astype(F32))
        ring.put(own, d, dot_nt(pre_grad, r.we[...]))
        if not own and d == 1:
            ring.near()

    ring.gather(r.g16, r.g_one, prepare, visit)
    ring.far()
    settle(r, r.hid, r.second, r.mlp, r.middle)
    weight_grads(r.g_one, r.hid, r.whole_two, FW)
    ring.relay()
    if sums:
        sums.middle()
    r.vecs_two[2:3] = sum_rows(r.g[...] * r.mlp[...])
    r.vecs_two[3:4] = sum_rows(r.g16[...].astype(F32))
    r.vecs_two[4:8] = jnp.zeros((4, D), F32)
    weight_grads(r.second, r.pre_all, r.whole_one, FW)
    load_into(r, r.in_all, r.second)
    write_slabs((r.whole_one, FW), (r.whole_two, FW), r.ffn_left, r.ffn_right)
    if sums:
        sums.end_rows(r.attn_rows)
    second_grad = ring.total()
    normed, inv_std = layer_stats(r.middle[...])
    r.vecs_two[0:1] = sum_rows(second_grad)
    r.vecs_two[1:2] = sum_rows(second_grad * normed)
    r.g[...] += layer_back(second_grad * (1.0 + r.vec_two[1:2]), normed, inv_std)
    ring.leave()

    ring = Ring(tokens, r.ring_local, r.ring_two)
    sums = RowsOut(r.ffn_left, r.ffn_right, r.sums_two)
    r.g16[...] = (r.g[...] * r.vec_one[2:3]).astype(BF16)
    ring.start_sums()

    def prepare_attention():
        sums.start()
        r.dk[...] = jnp.zeros_like(r.dk)
        r.dv[...] = jnp.zeros_like(r.dv)
        settle(r, r.q, r.k, r.v, r.lse, r.wm)

    def attend(own, d):
        rows = ring.rows((ring.own if own else ring.other)[d])
        grad = dot_nn(r.g_two[rows, :], r.wm[...]).astype(BF16)
        queries = []
        for h in range(2):
            part = grad[:, head_cols(h)]
            query = r.q[h, rows, :]
            scores = dot_nt(query, r.k[h]) * SCALE
            if last:
                scores = scores + r.mask[...]
            probs = jnp.exp(scores - r.lse[rows, h : h + 1])
            grad_probs = dot_nt(part, r.v[h])
            weighted = jnp.sum(probs * grad_probs, axis=-1, keepdims=True)
            score_grad = (probs * (grad_probs - weighted)).astype(BF16)
            queries.append((dot_nn(score_grad, r.k[h]) * SCALE).astype(BF16))
            r.dk[h] += dot_tn(score_grad, query)
            r.dv[h] += dot_tn(probs.astype(BF16), part)
        r.joined[rows, 0:HW] = jnp.concatenate(queries, axis=1)

    def back(own, d):
        rows = ring.rows((ring.own if own else ring.other)[d])
        ring.put(own, d, dot_nt(r.joined[rows, :], r.wqkv[...]))

    ring.gather(r.g16, r.g_two, prepare_attention, attend)
    settle(r, r.wqkv)
    later = [(r.dk[h] * SCALE).astype(BF16) for h in range(2)]
    later += [r.dv[h].astype(BF16) for h in range(2)]
    r.joined[:, HW : 3 * HW] = jnp.concatenate(later, axis=1)
    back(False, 2)
    back(True, 2)
    ring.far()
    for d in (1, 3):
        back(False, d)
        back(True, d)
    ring.near()
    back(False, 0)
    back(True, 0)
    settle(r)
    weight_grads(r.g_two, r.att, r.whole_two, HW)
    ring.relay()
    sums.middle()
    r.bias_one[...] = sum_rows(r.joined[...].astype(F32))
    r.vecs_one[2:3] = sum_rows(r.g[...] * r.branch[...])
    r.vecs_one[3:4] = sum_rows(r.g16[...].astype(F32))
    r.vecs_one[4:8] = jnp.zeros((4, D), F32)
    weight_grads(r.second, r.joined, r.whole_one, 3 * HW)
    write_slabs((r.whole_one, 3 * HW), (r.whole_two, HW), r.attn_left, r.attn_right)
    sums.end_rows(r.ffn_rows)
    input_grad = ring.total()
    normed, inv_std = layer_stats(r.x[...])
    r.vecs_one[0:1] = sum_rows(input_grad)
    r.vecs_one[1:2] = sum_rows(input_grad * normed)
    grad = r.g[...] + layer_back(input_grad * (1.0 + r.vec_one[1:2]), normed, inv_std)
    if last:
        r.out[...] = grad
    else:
        grad16 = grad.astype(BF16)
        r.embed_rows[0:16] = dot_tn(r.patches[...], grad16)[EMBED : EMBED + 16]
        r.embed_rows[16:17] = sum_rows(grad16.astype(F32))
        r.embed_rows[17:24] = jnp.zeros((7, D), F32)
        r.token_cols[...] = dot_nn(grad16, r.feat[...])
        to_pixels(r.token_cols, r.square, r.latent, EMBED)
    ring.leave()


def weight_grads(left_ref, right_ref, whole_ref, width):
    @pl.loop(0, D // 128)
    def _(k):
        at = pl.ds(pl.multiple_of(k * 128, 128), 128)
        whole_ref[at, :width] = dot_tn(left_ref[:, at], right_ref[...])


def write_slabs(one, two, left_ref, right_ref):
    cut = left_ref.shape[3]
    cols = cut + right_ref.shape[3]

    @pl.loop(0, 16)
    def _(k):
        at = pl.ds(pl.multiple_of(k * PART, 8), PART)
        parts = [ref[at, :width] for ref, width in (one, two)]
        spare = cols - one[1] - two[1]
        if spare:
            parts.append(jnp.zeros((PART, spare), F32))
        rows = jnp.concatenate(parts, axis=1)
        rows = jnp.concatenate([rows, jnp.zeros((SLAB - PART, cols), F32)], axis=0).astype(BF16)
        x, z = k // 4, lax.rem(k, 4)
        left_ref[x, z] = rows[:, :cut]
        right_ref[x, z] = rows[:, cut:]


def line_only(lines):
    return [peer for peer, _ in lines[0] + lines[1]]


def slab_specs(cols):
    widths = (CUT[cols], cols - CUT[cols])
    return [((4, 4, SLAB, width), BF16) for width in widths]


def block_backward(near, far, tokens, last, cid):
    vecs = ((8, D), F32)
    attn_left, attn_right = slab_specs(ATT_COLS)
    outs = dict(
        vecs_one=vecs,
        vecs_two=vecs,
        bias_one=((1, 3 * HW), F32),
        bias_two=((1, FW), F32),
        attn_left=attn_left,
        attn_right=attn_right,
        ffn_rows=((SLAB, FFN_COLS), BF16),
    )
    wide, tile = (8 * tokens, D), (tokens, D)
    scratch = dict(
        g16=pltpu.VMEM(tile, BF16),
        square=pltpu.VMEM((128, 128), F32),
        token_cols=pltpu.VMEM((128, 128), F32),
        g_one=pltpu.VMEM(wide, BF16),
        g_two=pltpu.VMEM(wide, BF16),
        pre_all=pltpu.VMEM((8 * tokens, FW), BF16),
        joined=pltpu.VMEM((8 * tokens, 3 * HW), BF16),
        dk=pltpu.VMEM((2, 8 * tokens, HEAD), F32),
        dv=pltpu.VMEM((2, 8 * tokens, HEAD), F32),
        whole_one=pltpu.VMEM((D, FW), F32),
        whole_two=pltpu.VMEM((D, FW), F32),
        ffn_left=pltpu.VMEM(*slab_specs(FFN_COLS)[0]),
        ffn_right=pltpu.VMEM(*slab_specs(FFN_COLS)[1]),
        ring_local=ring_local(tokens),
        ring_one=ring_remote(tokens),
        ring_two=ring_remote(tokens),
        sums_two=rows_out_scratch(FFN_COLS),
    )
    if last:
        outs.update(out=(tile, F32))
        outs.update(predicted=((16, 8, 32), BF16))
        outs.update(unpatch_rows=((32, D), F32))
        outs.update(unpatch_bias=((8, 128), F32))
        outs.update(head_vecs=((2, D), F32))
        scratch.update(cotangent=pltpu.VMEM((128, 32), BF16))
        outs.update(grad_ended=((128, D), F32))
        scratch.update(g=pltpu.VMEM(tile, F32))
    else:
        outs.update(attn_rows=((SLAB, ATT_COLS), BF16))
        outs.update(embed_rows=((24, D), F32))
        outs.update(latent=((16, 4, 32), F32))
        scratch.update(g=pltpu.VMEM(tile, F32))
        scratch.update(sums_one=rows_out_scratch(ATT_COLS))
    body = functools.partial(backward_body, tokens=tokens, last=last)
    return launch(body, cid, near, far, outs, {}, scratch, vmem=62 << 20)[0]


def shards(
    latent,
    condition,
    routed_ids,
    embed_weight,
    embed_bias,
    modulation_weight,
    modulation_bias,
    attention_weight,
    attention_bias,
    merge_weight,
    merge_bias,
    expand_weight,
    expand_bias,
    reduce_weight,
    reduce_bias,
    final_modulation,
    final_offsets,
    unpatch_weight,
    unpatch_bias,
    pred_cotangent,
):
    tile_rows = latent.shape[1] // 2
    tile_cols = latent.shape[2] // 2
    tile_tokens = tile_rows * tile_cols
    capacity = 7 * tile_tokens // 8
    row_index = lax.axis_index("tx") * tile_rows + jnp.arange(tile_rows, dtype=jnp.int32)
    col_index = lax.axis_index("ty") * tile_cols + jnp.arange(tile_cols, dtype=jnp.int32)
    placed = sincos_table(row_index.astype(F32), col_index.astype(F32), D)
    mod_w = modulation_weight.swapaxes(0, 1)
    got = open_up(
        dict(
            condition=condition,
            ids=routed_ids,
            mod_w=mod_w,
            final_w=final_modulation,
            attn_w=attention_weight.transpose(1, 2, 0, 3),
            merge_w=merge_weight.swapaxes(0, 1),
            expand_w=expand_weight.swapaxes(0, 1),
            reduce_w=reduce_weight.swapaxes(0, 1),
            embed_w=embed_weight,
            embed_b=embed_bias[None],
            unpatch_w=unpatch_weight,
            attn_b=attention_bias,
            merge_b=merge_bias,
            expand_b=expand_bias,
            reduce_b=reduce_bias,
            mod_b=modulation_bias,
            final_b=final_offsets[None],
        )
    )
    vecs_one = dict(vec_one=got.vec_one_0, vec_two=got.vec_two_0)
    vecs_two = dict(vec_one=got.vec_one_1, vec_two=got.vec_two_1, mask=got.mask)
    outs_one, kept_one = block_forward(
        dict(
            vecs_one,
            bias_one=got.bias_one_0,
            bias_two=got.bias_two_0,
            rows=got.rows,
            wqkv=got.wqkv,
            wm=got.wm,
            pixels=latent.transpose(0, 2, 3, 1)[0],
            feat=got.feat,
            placed=placed,
        ),
        tile_tokens,
        2 * ATT_COLS,
        False,
        10,
    )
    outs_two, kept_two = block_forward(
        dict(
            vecs_two,
            bias_one=got.bias_one_1,
            bias_two=got.bias_two_1,
            rows=got.rows,
            wqkv=outs_one.next_wqkv,
            wm=outs_one.next_wm,
            first=outs_one.out,
            place=got.place,
        ),
        capacity,
        2 * ATT_COLS + FFN_COLS,
        True,
        11,
    )
    back_two = block_backward(
        dict(
            vecs_two,
            place=got.place,
            head_vec=got.head_vec,
            feat=got.feat,
            unpatch_b=unpatch_bias[None],
            cotangent_pixels=pred_cotangent.transpose(0, 2, 3, 1)[0],
        ),
        dict(
            kept_two,
            first=outs_one.out,
            two=outs_two.out,
            wqkv=outs_one.next_wqkv,
            wm=outs_one.next_wm,
        ),
        capacity,
        True,
        12,
    )
    back_one = block_backward(
        dict(vecs_one, place=got.place, patches=outs_one.patches, feat=got.feat),
        dict(
            kept_one,
            wqkv=got.wqkv,
            wm=got.wm,
            pending_left=back_two.attn_left,
            pending_right=back_two.attn_right,
            grad_two=back_two.out,
            grad_ended=back_two.grad_ended,
        ),
        tile_tokens,
        False,
        13,
    )
    ended = finish(
        dict(
            left=back_one.attn_left,
            right=back_one.attn_right,
            attn_rows=back_one.attn_rows,
            ffn_rows_0=back_one.ffn_rows,
            ffn_rows_1=back_two.ffn_rows,
            vecs_one_0=back_one.vecs_one,
            vecs_two_0=back_one.vecs_two,
            vecs_one_1=back_two.vecs_one,
            vecs_two_1=back_two.vecs_two,
            head_vecs=back_two.head_vecs,
            unpatch_rows=back_two.unpatch_rows,
            embed_rows=back_one.embed_rows,
            bias_one_0=back_one.bias_one,
            bias_two_0=back_one.bias_two,
            bias_one_1=back_two.bias_one,
            bias_two_1=back_two.bias_two,
            table=jnp.asarray(bias_table()),
            unpatch_bias=back_two.unpatch_bias,
        )
    )
    last = close(
        dict(s_in=ended.s_out, condition=condition, mod_w=mod_w, final_w=final_modulation),
        dict(early_in=ended.early_out, late_in=ended.late_out, m_in=ended.m_out),
    )
    return (
        back_two.predicted.transpose(2, 0, 1)[None],
        back_one.latent.transpose(2, 0, 1)[None],
        last.condition_grad,
        last.embed_w,
        last.embed_b[0],
        last.mod_grad.swapaxes(0, 1),
        last.mod_b,
        last.attn.transpose(2, 0, 1, 3),
        last.attn_b,
        last.merge.swapaxes(0, 1),
        last.merge_b,
        last.expand.swapaxes(0, 1),
        last.expand_b,
        last.reduce.swapaxes(0, 1),
        last.reduce_b,
        last.final_grad,
        last.final_b[0],
        last.unpatch_w,
        last.unpatch_b[0],
    )


def solution(mesh):
    torus = Mesh(
        mesh.devices.reshape(4, 4, mesh.shape["tx"], mesh.shape["ty"]), ("dp_0", "dp_1", "tx", "ty")
    )
    return jax.shard_map(
        shards,
        mesh=torus,
        in_specs=(
            P(DP, "tx", "ty", None),
            P(None, DP_TX_TY),
            P(DP, None),
            P(None, DP_TX_TY),
            P(DP_TX_TY),
            P(None, DP_TX_TY, None),
            P(None, DP_TX_TY),
            P(None, DP_TX_TY, None, None),
            P(None, DP_TX_TY),
            P(None, DP_TX_TY, None),
            P(None, DP_TX_TY),
            P(None, DP_TX_TY, None),
            P(None, DP_TX_TY),
            P(None, DP_TX_TY, None),
            P(None, DP_TX_TY),
            P(DP_TX_TY, None),
            P(DP_TX_TY),
            P(DP_TX_TY, None),
            P(),
            P(DP, "tx", "ty", None),
        ),
        out_specs=(
            P(DP, "tx", "ty", None),
            P(DP, "tx", "ty", None),
            P(None, DP_TX_TY),
            P(None, DP_TX_TY),
            P(DP_TX_TY),
            P(None, DP_TX_TY, None),
            P(None, DP_TX_TY),
            P(None, DP_TX_TY, None, None),
            P(None, DP_TX_TY),
            P(None, DP_TX_TY, None),
            P(None, DP_TX_TY),
            P(None, DP_TX_TY, None),
            P(None, DP_TX_TY),
            P(None, DP_TX_TY, None),
            P(None, DP_TX_TY),
            P(DP_TX_TY, None),
            P(DP_TX_TY),
            P(DP_TX_TY, None),
            P(),
        ),
        check_vma=False,
    )
```

```python
import functools

import jax
import jax.numpy as jnp
import numpy as np
from jax import lax
from jax.experimental import pallas as pl
from jax.experimental.pallas import tpu as pltpu
from jax.sharding import Mesh
from jax.sharding import PartitionSpec as P

D = 1152
HEADS = 16
FF = 4608
HW = D // 8
FW = FF // 8
DP = ("dp_0", "dp_1")
DP_TX_TY = ("dp_0", "dp_1", "tx", "ty")
MESH = pl.DeviceIdType.MESH
VMEM = pl.BlockSpec(memory_space=pltpu.VMEM)
FAR = pl.BlockSpec(memory_space=pl.ANY)
F32 = jnp.float32
BF16 = jnp.bfloat16
ATT_COLS = 640
FFN_COLS = 2 * FW
ALL_COLS = 2 * (ATT_COLS + FFN_COLS)
PIECE = 512
PIECES = ALL_COLS // PIECE


def greet(peers):
    barrier = pltpu.get_barrier_semaphore()
    for peer in peers:
        pl.semaphore_signal(barrier, inc=1, device_id=peer, device_id_type=MESH)


def met(peers):
    pl.semaphore_wait(pltpu.get_barrier_semaphore(), len(peers))


def enter(peers):
    greet(peers)
    met(peers)


def send(src, dst, sems, k, peer):
    copy = pltpu.make_async_remote_copy(
        src_ref=src,
        dst_ref=dst,
        send_sem=sems[0].at[k],
        recv_sem=sems[1].at[k],
        device_id=peer,
        device_id_type=MESH,
    )
    copy.start()
    return copy


def group_peers():
    c, y = lax.axis_index("tx"), lax.axis_index("ty")
    found = []
    for dc in range(2):
        for dy in range(4):
            if dc or dy:
                oc, oy = lax.rem(c + dc, 2), lax.rem(y + dy, 4)
                found.append(({"tx": oc, "ty": oy}, oc * 4 + oy))
    return found


def own_group():
    return lax.axis_index("tx") * 4 + lax.axis_index("ty")


def dma_sems(n):
    return [pltpu.SemaphoreType.DMA((n,)), pltpu.SemaphoreType.DMA((n,))]


def ring_peers():
    c, y = lax.axis_index("tx"), lax.axis_index("ty")
    return (
        {"tx": 1 - c},
        {"ty": lax.rem(y + 1, 4)},
        {"ty": lax.rem(y + 3, 4)},
        {"ty": lax.rem(y + 2, 4)},
    )


def layer_stats(value_rows):
    centered = value_rows - jnp.mean(value_rows, axis=-1, keepdims=True)
    inv_std = lax.rsqrt(jnp.mean(centered * centered, axis=-1, keepdims=True) + 1e-06)
    return (centered * inv_std, inv_std)


def layer_back(upstream, normed, inv_std):
    return inv_std * (
        upstream
        - jnp.mean(upstream, axis=-1, keepdims=True)
        - normed * jnp.mean(upstream * normed, axis=-1, keepdims=True)
    )


def sincos_table(row_pos, col_pos, width):
    quarter = width // 4
    freqs = jnp.power(10000.0, -jnp.arange(quarter, dtype=jnp.float32) / quarter)
    row_angle = row_pos[:, None] * freqs[None, :]
    col_angle = col_pos[:, None] * freqs[None, :]
    row_embed = jnp.concatenate([jnp.sin(row_angle), jnp.cos(row_angle)], axis=-1)
    col_embed = jnp.concatenate([jnp.sin(col_angle), jnp.cos(col_angle)], axis=-1)
    row_full = jnp.broadcast_to(
        row_embed[:, None, :], (row_pos.shape[0], col_pos.shape[0], width // 2)
    )
    col_full = jnp.broadcast_to(
        col_embed[None, :, :], (row_pos.shape[0], col_pos.shape[0], width // 2)
    )
    return jnp.concatenate([row_full, col_full], axis=-1).reshape(
        row_pos.shape[0] * col_pos.shape[0], width
    )


SLAB = 80
PART = D // 16
CUT = {ATT_COLS: 384, FFN_COLS: 640}


def line_peers():
    x, z = lax.axis_index("dp_0"), lax.axis_index("dp_1")
    along_x = [({"dp_0": lax.rem(x + d, 4)}, lax.rem(x + d, 4)) for d in (2, 1, 3)]
    along_z = [({"dp_1": lax.rem(z + d, 4)}, lax.rem(z + d, 4)) for d in (2, 1, 3)]
    return along_x, along_z


class RowsIn:
    def __init__(self, left_ref, right_ref, scratch):
        self.left, self.right = left_ref, right_ref
        self.all_left, self.all_right = scratch[:2]
        self.sems = tuple(scratch[2:4])
        self.x, self.z = lax.axis_index("dp_0"), lax.axis_index("dp_1")
        self.along_x, self.along_z = line_peers()

    def peers(self):
        return [peer for peer, _ in self.along_x + self.along_z]

    def start(self):
        x, z = self.x, self.z
        self.first = []
        for k, (peer, _) in enumerate(self.along_z):
            self.first.append(send(self.left, self.all_left.at[x, z], self.sems, k, peer))
        for k, (peer, _) in enumerate(self.along_x):
            self.first.append(send(self.right, self.all_right.at[x, z], self.sems, 3 + k, peer))
        self.all_left[x, z] = self.left[...]
        self.all_right[x, z] = self.right[...]

    def middle(self):
        left, right = self.all_left.at[self.x], self.all_right.at[:, self.z]
        self.second = []
        for copy in self.first[:3]:
            copy.wait_recv()
        for k, (peer, _) in enumerate(self.along_x):
            self.second.append(send(left, left, self.sems, 6 + k, peer))
        for copy in self.first[3:]:
            copy.wait_recv()
        for k, (peer, _) in enumerate(self.along_z):
            self.second.append(send(right, right, self.sems, 9 + k, peer))

    def end(self, one_ref, two_ref):
        for copy in self.second:
            copy.wait_recv()
        width, other = one_ref.shape[1], two_ref.shape[1]
        cut = self.left.shape[1]

        @pl.loop(0, 8)
        def _(pair):
            x, z = pair // 2, 2 * lax.rem(pair, 2)
            both = []
            for k in range(2):
                parts = [self.all_left[x, z + k], self.all_right[x, z + k]]
                both.append(jnp.concatenate(parts, axis=1).astype(F32)[:PART])
            value = jnp.concatenate(both, axis=0).astype(BF16)
            at = pl.ds(pl.multiple_of(pair * 2 * PART, 16), 2 * PART)
            one_ref[at, :] = value[:, :width]
            two_ref[at, :] = value[:, width : width + other]

        for copy in self.first + self.second:
            copy.wait_send()


def rows_in_scratch(cols):
    left = CUT[cols]
    return [
        pltpu.VMEM((4, 4, SLAB, left), BF16),
        pltpu.VMEM((4, 4, SLAB, cols - left), BF16),
    ] + dma_sems(12)


class RowsOut:
    def __init__(self, left_ref, right_ref, scratch):
        self.left, self.right = left_ref, right_ref
        self.got = scratch[0:2]
        self.mine = scratch[2:4]
        self.last = scratch[4:6]
        self.sems = tuple(scratch[6:8])
        self.x, self.z = lax.axis_index("dp_0"), lax.axis_index("dp_1")
        self.along_x, self.along_z = line_peers()

    def peers(self):
        return [peer for peer, _ in self.along_x + self.along_z]

    def start(self):
        self.first = []
        for k, (peer, at) in enumerate(self.along_x):
            part = self.left.at[at]
            self.first.append(send(part, self.got[0].at[k], self.sems, k, peer))
        for k, (peer, at) in enumerate(self.along_z):
            part = self.right.at[:, at]
            self.first.append(send(part, self.got[1].at[k], self.sems, 3 + k, peer))

    def middle(self):
        self.second = []
        for side, peers in ((0, self.along_z), (1, self.along_x)):
            for copy in self.first[3 * side : 3 * side + 3]:
                copy.wait_recv()
            got, mine = self.got[side], self.mine[side]

            @pl.loop(0, 4)
            def _(k):
                own = self.right[k, self.z] if side else self.left[self.x, k]
                across, below, above = (got[source, k].astype(F32) for source in range(3))
                total = (own.astype(F32) + across) + (below + above)
                mine[k] = total.astype(mine.dtype)

            for k, (peer, at) in enumerate(peers):
                part = mine.at[at]
                copy = send(part, self.last[side].at[k], self.sems, 6 + 3 * side + k, peer)
                self.second.append(copy)

    def end(self):
        for copy in self.second:
            copy.wait_recv()
        totals = []
        for side, own in ((0, self.z), (1, self.x)):
            across, below, above = (self.last[side][source].astype(F32) for source in range(3))
            totals.append((self.mine[side][own].astype(F32) + across) + (below + above))
        return totals

    def end_rows(self, out_ref):
        cut = self.left.shape[3]
        left, right = self.end()
        out_ref[:, :cut] = left.astype(BF16)
        out_ref[:, cut:] = right.astype(BF16)
        self.leave()

    def leave(self):
        for copy in self.first + self.second:
            copy.wait_send()


def rows_out_scratch(cols):
    return sum_scratch([(SLAB, CUT[cols]), (SLAB, cols - CUT[cols])], BF16)


def sum_scratch(shapes, dtype):
    return (
        [pltpu.VMEM((3, 4, *shape), dtype) for shape in shapes]
        + [pltpu.VMEM((4, *shape), dtype) for shape in shapes]
        + [pltpu.VMEM((3, *shape), dtype) for shape in shapes]
        + dma_sems(12)
    )


def slab_views(rows_ref, start, cols):
    cut = start + CUT[cols]
    return rows_ref.at[:, start:cut], rows_ref.at[:, cut : start + cols]


def weight_shapes(cols):
    widths = (3 * HW, HW) if cols == ATT_COLS else (FW, FW)
    return tuple(jax.ShapeDtypeStruct((D, w), BF16) for w in widths)


def dot_nn(left, right):
    return lax.dot_general(left, right, (((1,), (0,)), ((), ())), preferred_element_type=F32)


def dot_nt(left, right):
    return lax.dot_general(left, right, (((1,), (1,)), ((), ())), preferred_element_type=F32)


def dot_tn(left, right):
    return lax.dot_general(left, right, (((0,), (0,)), ((), ())), preferred_element_type=F32)


def gelu_both(pre):
    root = 0.7978845608028654
    square = pre * pre
    bent = jnp.tanh(root * pre * (1.0 + 0.044715 * square))
    value = 0.5 * pre * (1.0 + bent)
    slope = 0.5 * (1.0 + bent) + 0.5 * pre * (1.0 - bent * bent) * root * (1.0 + 0.134145 * square)
    return value, slope


def sum_rows(value):
    return jnp.sum(value, axis=0, keepdims=True)


HEAD = D // HEADS
SCALE = HEAD ** (-0.5)


def head_cols(h, start=0):
    return slice(start + h * HEAD, start + (h + 1) * HEAD)


class Refs:
    pass


class Results(dict):
    __getattr__ = dict.__getitem__


def launch(body, cid, near, far, outs, kept, scratch, vmem=60 << 20):
    twins = {name: (value.shape, value.dtype) for name, value in far.items()}
    twins.update(kept)
    groups, tree = jax.tree.flatten(scratch, is_leaf=lambda entry: not isinstance(entry, (dict, list)))

    def kernel(*refs):
        refs = iter(refs)
        r, hbm = Refs(), {}
        for name in near:
            setattr(r, name, next(refs))
        for name in far:
            hbm[name] = next(refs)
        for name in outs:
            setattr(r, name, next(refs))
        for name in kept:
            hbm[name] = next(refs)
        r.moves, r.moving = {}, {}
        for k, name in enumerate(twins):
            ref = next(refs)
            setattr(r, name, ref)
            r.moves[id(ref)] = (hbm[name], k)
        if twins:
            r.move_sems = next(refs)
        for name, entry in jax.tree.unflatten(tree, list(refs)).items():
            setattr(r, name, entry)
        body(r)

    shapes = [jax.ShapeDtypeStruct(*spec) for spec in (*outs.values(), *kept.values())]
    results = pl.pallas_call(
        kernel,
        out_shape=tuple(shapes),
        in_specs=[VMEM] * len(near) + [FAR] * len(far),
        out_specs=(VMEM,) * len(outs) + (FAR,) * len(kept),
        scratch_shapes=[pltpu.VMEM(*spec) for spec in twins.values()]
        + ([pltpu.SemaphoreType.DMA((len(twins),))] if twins else [])
        + groups,
        compiler_params=pltpu.CompilerParams(
            collective_id=cid, has_side_effects=cid is not None, vmem_limit_bytes=vmem
        ),
    )(*near.values(), *far.values())
    return Results(zip(outs, results)), Results(zip(kept, results[len(outs) :]))


def load_into(r, ref, target):
    source, k = r.moves[id(ref)]
    r.moving[id(ref)] = pltpu.make_async_copy(source, target, r.move_sems.at[k])
    r.moving[id(ref)].start()


def load(r, *refs):
    for ref in refs:
        load_into(r, ref, ref)


def save(r, *refs):
    for ref in refs:
        target, k = r.moves[id(ref)]
        r.moving[id(ref)] = pltpu.make_async_copy(ref, target, r.move_sems.at[k])
        r.moving[id(ref)].start()


def settle(r, *refs):
    for key in [id(ref) for ref in refs] or list(r.moving):
        r.moving.pop(key).wait()


def exact(left, right, dims):
    return lax.dot_general(
        left,
        right,
        ((dims[:1], dims[1:]), ((), ())),
        precision=lax.Precision.HIGHEST,
        preferred_element_type=F32,
    )


def choice(place_ref, capacity):
    tokens = place_ref.shape[1]
    slots = lax.broadcasted_iota(jnp.int32, (capacity, tokens), 0)
    return jnp.where(slots == place_ref[...], 1.0, 0.0).astype(F32)


def spread_back(picks, chosen, others):
    used = exact(picks, jnp.ones((picks.shape[0], 128), F32), (0, 0))[:, :1]
    return exact(picks, chosen, (0, 0)) + others * (1.0 - used)


def modulated(x, vec_ref):
    normed, _ = layer_stats(x)
    return (normed * (1.0 + vec_ref[1:2]) + vec_ref[0:1]).astype(BF16)


def full_width(parts, at):
    height = parts[0].shape[0]
    used = at + sum(part.shape[1] for part in parts)
    if at:
        parts = [jnp.zeros((height, at), F32), *parts]
    if used < 128:
        parts = [*parts, jnp.zeros((height, 128 - used), F32)]
    return jnp.concatenate(parts, axis=1)


def to_tokens(pixels_ref, square, tokens_ref, at):
    wide, depth, high = pixels_ref.shape
    square[...] = jnp.zeros_like(square)
    square[: wide * depth, :high] = pixels_ref[...].astype(F32).reshape(wide * depth, high)
    square[...] = jnp.transpose(square[...])
    size = 2 * depth
    lines = [square[pl.ds(line, high // 2, stride=2), :] for line in range(2)]
    for c in range(wide // 2):
        parts = [value[:, c * size : (c + 1) * size] for value in lines]
        tokens_ref[pl.ds(c, high // 2, stride=wide // 2), :] = full_width(parts, at)


def to_pixels(tokens_ref, square, pixels_ref, at):
    wide, depth, high = pixels_ref.shape
    square[...] = jnp.zeros_like(square)
    size = 2 * depth
    columns = [tokens_ref[pl.ds(c, high // 2, stride=wide // 2), :] for c in range(wide // 2)]
    for line in range(2):
        start = at + line * size
        parts = [value[:, start : start + size] for value in columns]
        square[pl.ds(line, high // 2, stride=2), :] = full_width(parts, 0)
    value = jnp.transpose(square[...])[: wide * depth, :high].reshape(wide, depth, high)
    pixels_ref[...] = value.astype(pixels_ref.dtype)


FIRST = 64
PIECE_ROWS = 32


def half_sizes(tokens):
    return FIRST, tokens - FIRST


def half_local(size):
    return [
        pltpu.VMEM((4, size, D), F32),
        pltpu.VMEM((4, size, D), BF16),
        pltpu.VMEM((3, size, D), BF16),
    ]


def half_remote(size):
    return [
        pltpu.VMEM((4, size, D), BF16),
        pltpu.VMEM((2, size, D), BF16),
        pltpu.VMEM((PIECE_ROWS, D), BF16),
        pltpu.VMEM((size - PIECE_ROWS, D), BF16),
    ] + dma_sems(20)


class Half:
    def __init__(self, which, tokens, x_ref, all_ref, local, remote):
        sizes = half_sizes(tokens)
        self.size = sizes[which]
        self.own = slice(which * FIRST, which * FIRST + self.size)
        self.base = which * 8 * FIRST
        self.x, self.all = x_ref, all_ref
        self.kept, self.sib_out, self.out = local
        self.sib_in, self.got, self.far_low, self.far_high = remote[:4]
        self.sems = tuple(remote[4:6])
        self.sib, self.up, self.down, _ = ring_peers()
        self.low, self.high = slice(0, PIECE_ROWS), slice(PIECE_ROWS, self.size)
        self.sent, self.swaps = [], {}

    def peers(self):
        return [self.sib, self.up, self.down]

    def send(self, src, dst, k, peer):
        copy = send(src, dst, self.sems, k, peer)
        self.sent.append(copy)
        return copy

    def pair(self, d):
        start = self.base + 2 * d * self.size
        return slice(start, start + 2 * self.size)

    def slot(self, d, other, rows=None):
        start = self.base + (2 * d + other) * self.size
        rows = slice(0, self.size) if rows is None else rows
        return self.all.at[start + rows.start : start + rows.stop]

    def source(self, rows):
        return self.x.at[self.own.start + rows.start : self.own.start + rows.stop]

    def issue(self):
        low, high = self.low, self.high
        self.a1 = self.send(self.source(low), self.slot(3, 0, low), 0, self.up)
        self.b1 = self.send(self.source(high), self.slot(1, 0, high), 1, self.down)
        whole = slice(0, self.size)
        self.arrive = {0: self.send(self.source(whole), self.slot(0, 1), 4, self.sib)}
        start = self.base
        self.all[start : start + self.size, :] = self.x[self.own, :]

    def issue_rest(self):
        low, high = self.low, self.high
        self.a2 = self.send(self.source(high), self.slot(3, 0, high), 2, self.up)
        self.b2 = self.send(self.source(low), self.slot(1, 0, low), 3, self.down)

    def forward(self):
        low, high = self.low, self.high
        self.a1.wait_recv()
        self.f1 = self.send(self.slot(3, 0, low), self.slot(2, 0, low), 5, self.up)
        self.b1.wait_recv()
        self.f2 = self.send(self.slot(1, 0, high), self.slot(2, 0, high), 6, self.down)

    def near_arrive(self):
        self.a2.wait_recv()
        self.arrive[3] = self.send(self.slot(3, 0), self.slot(3, 1), 7, self.sib)
        self.b2.wait_recv()
        self.arrive[1] = self.send(self.slot(1, 0), self.slot(1, 1), 8, self.sib)

    def far_arrive(self):
        self.f1.wait_recv()
        self.f2.wait_recv()
        self.arrive[2] = self.send(self.slot(2, 0), self.slot(2, 1), 9, self.sib)

    def ready(self, d):
        self.arrive[d].wait_recv()

    def put(self, d, value):
        self.kept[d] = value[: self.size]
        self.sib_out[d] = value[self.size :].astype(BF16)
        self.swaps[d] = self.send(self.sib_out.at[d], self.sib_in.at[d], 10 + d, self.sib)

    def chip_sum(self, d):
        self.swaps[d].wait_recv()
        return self.kept[d] + self.sib_in[d].astype(F32)

    def near(self):
        low, high = self.low, self.high
        total = self.chip_sum(1)
        self.kept[1] = total
        self.out[0, high] = total[high].astype(BF16)
        self.n1 = self.send(self.out.at[0, high], self.got.at[0, high], 14, self.up)
        total = self.chip_sum(3)
        self.kept[3] = total
        self.out[1, low] = total[low].astype(BF16)
        self.n2 = self.send(self.out.at[1, low], self.got.at[1, low], 15, self.down)

    def far(self):
        self.out[2] = self.chip_sum(2).astype(BF16)
        self.low_sent = self.send(self.out.at[2, self.low], self.far_low, 16, self.up)
        self.high_sent = self.send(self.out.at[2, self.high], self.far_high, 17, self.down)

    def relay(self):
        low, high = self.low, self.high
        self.low_sent.wait_recv()
        self.out[0, low] = (self.kept[1, low] + self.far_low[...].astype(F32)).astype(BF16)
        self.r1 = self.send(self.out.at[0, low], self.got.at[0, low], 18, self.up)
        self.high_sent.wait_recv()
        self.out[1, high] = (self.kept[3, high] + self.far_high[...].astype(F32)).astype(BF16)
        self.r2 = self.send(self.out.at[1, high], self.got.at[1, high], 19, self.down)

    def total(self):
        value = self.chip_sum(0)
        for copy in (self.n1, self.n2, self.r1, self.r2):
            copy.wait_recv()
        value = value + self.got[0].astype(F32) + self.got[1].astype(F32)
        for copy in self.sent:
            copy.wait_send()
        return value


def gather_both(a, b, prepare, visit, between):
    prepare()
    a.ready(0)
    visit(a, 0)
    a.forward()
    b.issue_rest()
    b.ready(0)
    visit(b, 0)
    a.near_arrive()
    b.forward()
    between()
    a.ready(3)
    visit(a, 3)
    a.ready(1)
    visit(a, 1)
    a.far_arrive()
    b.near_arrive()
    b.ready(3)
    visit(b, 3)
    a.ready(2)
    visit(a, 2)
    b.ready(1)
    visit(b, 1)
    b.far_arrive()
    b.ready(2)
    visit(b, 2)


def gather_and_sum(a, b, prepare, visit, between):
    prepare()
    a.ready(0)
    visit(a, 0)
    a.forward()
    b.issue_rest()
    b.ready(0)
    visit(b, 0)
    a.near_arrive()
    b.forward()
    between()
    a.ready(3)
    visit(a, 3)
    a.ready(1)
    visit(a, 1)
    a.far_arrive()
    b.near_arrive()
    a.near()
    b.ready(3)
    visit(b, 3)
    a.ready(2)
    visit(a, 2)
    b.ready(1)
    visit(b, 1)
    a.far()
    b.far_arrive()
    b.near()
    b.ready(2)
    visit(b, 2)
    a.relay()
    b.far()


def sum_both(a, b, make):
    make(a, 2)
    make(b, 2)
    a.far()
    make(a, 1)
    b.far()
    make(a, 3)
    make(a, 0)
    a.near()
    make(b, 1)
    a.relay()
    make(b, 3)
    make(b, 0)
    b.near()
    b.relay()


def nothing():
    pass


def halves(r, tokens, x_ref, all_ref, remote):
    return [Half(k, tokens, x_ref, all_ref, r.local[k], remote[k]) for k in range(2)]


UNPATCH, EMBED, BLOCKS, EMBED_BIAS = 0, 32, 48, 64
WHOLE = 16384


def own_targets():
    group = own_group()
    return group * (D // 16), group * (D // 8)


def bias_table():
    table = np.zeros((8, 1024), np.int32)
    for col in range(3 * HW):
        part, e = divmod(col, HW)
        table[0, col] = (e // 18 + (64 if part == 2 else 0)) * 9 + e % 9 if part != 1 else -(1 << 20)
        table[1, col] = e % 18 // 9
    for e in range(FW):
        table[0, 3 * HW + e] = e // 36 * 9 + e % 9
        table[1, 3 * HW + e] = e % 36 // 9
    return table


def bias_picks(table_ref, cols, shift):
    rows = lax.broadcasted_iota(jnp.int32, (D, cols.stop - cols.start), 0)
    return jnp.where(rows == table_ref[0:1, cols] + shift, 1.0, 0.0).astype(F32)


ATT_BIAS = slice(0, 3 * HW)
FFN_BIAS = slice(3 * HW, 3 * HW + FW)


def mod_places(index):
    e = lax.broadcasted_iota(jnp.int32, (1, 128), 1)
    at = jnp.where(e < 108, 6 * D - 54 + index * 54 + e, 12 * D - 108 + index * 18 + e)
    at = jnp.where(e < 54, index * 54 + e, at)
    at = jnp.where(e < 126, at, -1)
    lines = lax.broadcasted_iota(jnp.int32, (128, 128), 0)
    return lines == lax.shift_right_arithmetic(at, 7), lines == jnp.bitwise_and(at, 127)


def whole_index():
    x, z = lax.axis_index("dp_0"), lax.axis_index("dp_1")
    return (x * 4 + z) * 8 + own_group()


def route(r):
    token = lax.broadcasted_iota(jnp.int32, (128, 512), 0)
    row = lax.axis_index("tx") * 16 + token // 8
    col = lax.axis_index("ty") * 8 + lax.rem(token, 8)
    hits = jnp.where(row * 32 + col == r.ids[...], 1.0, 0.0).astype(BF16)
    flags = dot_nt(jnp.ones((8, 512), BF16), hits)
    lines = lax.broadcasted_iota(jnp.int32, (128, 128), 0)
    lanes = lax.broadcasted_iota(jnp.int32, (128, 128), 1)
    before = dot_nn(flags.astype(BF16), jnp.where(lines <= lanes, 1.0, 0.0).astype(BF16))
    r.place[...] = jnp.where(flags > 0, before - 1.0, -1.0)[0:1].astype(jnp.int32)
    row, col = r.ids[...] // 512, lax.rem(r.ids[...], 32) // 8
    chip = lax.rem(col - lax.axis_index("ty") + 4, 4)
    other = jnp.where(row == lax.axis_index("tx"), 0, 1)
    tile = chip * 2 + other
    slot = lax.broadcasted_iota(jnp.int32, r.mask.shape, 1)
    used = slot < 0
    for k in range(8):
        count = jnp.sum(jnp.where(tile == k, 1.0, 0.0), axis=1, keepdims=True).astype(jnp.int32)
        for which, size in enumerate(half_sizes(r.mask.shape[1] // 8)):
            at = slot - which * 8 * FIRST - k * size
            used = used | ((at >= 0) & (at < size) & (at + which * FIRST < count))
    r.mask[...] = jnp.where(used, 0.0, -1e30)


def open_body(r):
    group = group_peers()
    sib, up, down, far = ring_peers()
    fetch = RowsIn(*slab_views(r.rows, 0, ATT_COLS), r.fetch)
    mods = RowsOut(r.m_mine.at[:, :, 0:64], r.m_mine.at[:, :, 64:128], r.mods)
    peers = [peer for peer, _ in group] + fetch.peers()
    greet(peers)
    load(r, r.attn_w, r.merge_w, r.expand_w, r.reduce_w, r.unpicks)
    load(r, r.mod_w, r.final_w, r.picks, r.table)
    r.pack[...] = jnp.zeros_like(r.pack)
    settle(r, r.attn_w, r.merge_w, r.expand_w, r.reduce_w)
    attn = [[r.attn_w[:, j, b, :] for j in range(3)] for b in range(2)]
    merge = [r.merge_w[:, b, :] for b in range(2)]
    expand = [r.expand_w[:, b, :] for b in range(2)]
    reduce = [r.reduce_w[:, b, :] for b in range(2)]
    spare = jnp.zeros((9, ATT_COLS - 4 * HW), BF16)
    for p in range(8):
        narrow, wide = slice(p * HW, (p + 1) * HW), slice(p * FW, (p + 1) * FW)
        parts = []
        for b in range(2):
            parts += [attn[b][j][:, narrow] for j in range(3)] + [merge[b][:, narrow], spare]
        for b in range(2):
            parts += [expand[b][:, wide], reduce[b][:, wide]]
        r.pack[p * 16 : p * 16 + 9, :] = jnp.concatenate(parts, axis=1)
    settle(r, r.unpicks)
    packed = jnp.zeros((8 * 64, PIECE), F32)
    for k in range(PIECES):
        packed = packed + dot_tn(r.unpicks[k], r.pack[:, k * PIECE : (k + 1) * PIECE])
    r.w_mine[...] = packed.astype(BF16).reshape(8, 64, PIECE)
    r.lines[...] = jnp.zeros_like(r.lines)
    r.lines[EMBED : EMBED + 16, 0:9] = r.embed_w[...].astype(F32)
    for b in range(2):
        at = BLOCKS + 8 * b
        for j in range(2):
            r.lines[at + j : at + j + 1, 0:9] = r.attn_b[b : b + 1, 9 * j : 9 * j + 9].astype(F32)
        for j in range(4):
            value = r.expand_b[b : b + 1, 9 * j : 9 * j + 9].astype(F32)
            r.lines[at + 2 + j : at + 3 + j, 0:9] = value
        r.lines[at + 6 : at + 7, 0:9] = r.merge_b[b : b + 1].astype(F32)
        r.lines[at + 7 : at + 8, 0:9] = r.reduce_b[b : b + 1].astype(F32)
    r.lines[EMBED_BIAS : EMBED_BIAS + 1, 0:9] = r.embed_b[...].astype(F32)
    r.block[...] = jnp.transpose(r.lines[...])[0:16]
    r.block[0:9, UNPATCH : UNPATCH + 32] = r.unpatch_w[...].astype(F32)
    me, x, z = own_group(), lax.axis_index("dp_0"), lax.axis_index("dp_1")
    r.small[x, z, me] = r.block[...].astype(BF16)
    met(peers)
    sems = (r.ss, r.rs)
    weights = [
        send(r.w_mine.at[at], r.w_got.at[me], sems, k, p) for k, (p, at) in enumerate(group)
    ]
    small = r.small.at[x, z, me]
    first = [send(small, small, sems, 7 + k, p) for k, (p, _) in enumerate(fetch.along_z)]
    r.w_got[me] = r.w_mine[me]

    condition = r.condition[...].astype(F32)
    cond16 = (condition / (1.0 + jnp.exp(-condition))).astype(BF16)
    on_line, on_lane = mod_places(whole_index())
    r.places[...] = jnp.zeros_like(r.places)
    r.places[0:1, 0:54] = r.mod_b[0:1].astype(F32)
    r.places[0:1, 54:108] = r.mod_b[1:2].astype(F32)
    r.places[0:1, 108:126] = r.final_b[...].astype(F32)
    left = jnp.where(on_line, r.places[0:1], 0.0).astype(BF16)
    right = jnp.where(on_lane, 1.0, 0.0).astype(BF16)
    r.placed_bias[...] = dot_nt(left, right)
    r.m_mine[:, :, 126:128] = jnp.zeros((4, 4, 2, 128), F32)
    settle(r, r.mod_w, r.final_w)
    for b in range(3):
        weight = r.mod_w[:, b, :] if b < 2 else r.final_w[...]
        part = dot_nn(cond16, weight)
        for k in range(part.shape[1] // 128):
            line = 54 * b + k
            value = part[:, k * 128 : (k + 1) * 128] + r.placed_bias[line : line + 1]
            r.m_mine[:, :, line, :] = value.reshape(4, 4, 128)
    mods.start()
    for copy in first:
        copy.wait_recv()
    small = r.small.at[x, :, me]
    second = [send(small, small, sems, 10 + k, p) for k, (p, _) in enumerate(fetch.along_x)]
    for copy in weights:
        copy.wait_recv()
    settle(r, r.picks, r.table)
    received = r.w_got[...].reshape(8 * 64, PIECE)
    for k in range(PIECES):
        r.rows[:, k * PIECE : (k + 1) * PIECE] = dot_nn(r.picks[k], received).astype(BF16)
    fetch.start()
    save(r, r.rows)
    for copy in second:
        copy.wait_recv()
    small = r.small.at[:, :, me]
    third = [send(small, small, sems, 13 + k, p) for k, p in enumerate((up, down, far, sib))]
    mods.middle()
    fetch.middle()
    route(r)
    r.m_sum[0:64], r.m_sum[64:128] = mods.end()

    def chunk(ref, index):
        return ref.at[pl.ds(pl.multiple_of(index * 16, 16), 16)]

    m_first = [
        send(chunk(r.m_sum, at), r.m_got.at[me], sems, 20 + k, p) for k, (p, at) in enumerate(group)
    ]
    mine = pl.ds(pl.multiple_of(me * 16, 16), 16)
    r.m_got[me] = r.m_sum[mine, :]
    for copy in m_first:
        copy.wait_recv()
    total = r.m_got[0]
    for k in range(1, 8):
        total = total + r.m_got[k]
    r.m_all[mine, :] = total
    part = chunk(r.m_all, me)
    m_second = [send(part, part, sems, 27 + k, p) for k, (p, _) in enumerate(group)]
    c, y = lax.axis_index("tx"), lax.axis_index("ty")
    fourth = []
    for k, d in enumerate((3, 1, 2)):
        third[k].wait_recv()
        small = r.small.at[:, :, c * 4 + lax.rem(y + d, 4)]
        fourth.append(send(small, small, sems, 17 + k, sib))
    for copy in fourth + third[3:]:
        copy.wait_recv()

    @pl.loop(0, 16)
    def _(k):
        got = r.small[k // 4, lax.rem(k, 4)].reshape(128, 128)
        at = pl.ds(pl.multiple_of(k * PART, 8), PART)
        r.feat32[at, :] = dot_nn(r.pick_small[...], got)[:PART]

    r.feat[...] = r.feat32[...].astype(BF16)
    save(r, r.feat)
    for k in range(9):
        cols = slice(k * 128, (k + 1) * 128)
        r.turned[:, cols] = jnp.transpose(r.feat32[cols, :])
    attn_at, ffn_at = own_targets()
    picks = bias_picks(r.table, ATT_BIAS, attn_at).astype(BF16)
    blocks = r.turned[BLOCKS : BLOCKS + 16].astype(BF16)
    narrow = dot_nn(blocks, picks)
    wide = dot_nn(blocks, bias_picks(r.table, FFN_BIAS, ffn_at).astype(BF16))
    for b, (one, two) in enumerate(((r.bias_one_0, r.bias_two_0), (r.bias_one_1, r.bias_two_1))):
        at, which = 8 * b, r.table[1:2, ATT_BIAS]
        one[...] = jnp.where(which == 0, narrow[at : at + 1], narrow[at + 1 : at + 2])
        value, which = wide[at + 2 : at + 3], r.table[1:2, FFN_BIAS]
        for j in range(1, 4):
            value = jnp.where(which == j, wide[at + 2 + j : at + 3 + j], value)
        two[...] = value
    for copy in m_second:
        copy.wait_recv()

    def mod_line(k):
        return jnp.concatenate([r.m_all[9 * k + i : 9 * k + i + 1] for i in range(9)], axis=1)

    vecs = (r.vec_one_0, r.vec_two_0, r.vec_one_1, r.vec_two_1)
    for k, ref in enumerate(vecs):
        for i in range(3):
            ref[i : i + 1] = mod_line(3 * k + i)
        at = BLOCKS + 8 * (k // 2) + 6 + k % 2
        ref[3:4] = r.turned[at : at + 1]
        ref[4:5] = r.turned[EMBED_BIAS : EMBED_BIAS + 1]
        ref[5:8] = jnp.zeros((3, D), F32)
    r.head_vec[0:1] = mod_line(12)
    r.head_vec[1:2] = mod_line(13)
    fetch.end(r.wqkv, r.wm)
    save(r, r.wqkv, r.wm)
    for copy in weights + first + second + third + fourth + m_first + m_second:
        copy.wait_send()
    mods.leave()
    settle(r)


def picking():
    picks = np.zeros((PIECES, SLAB, 8 * 64), np.float32)
    for k in range(PIECES):
        for row in range(72):
            picks[k, row, row // 9 * 64 + 9 * k + row % 9] = 1.0
    return picks


def picking_small():
    picks = np.zeros((SLAB, 128), np.float32)
    for row in range(72):
        picks[row, row // 9 * 16 + row % 9] = 1.0
    return picks


def open_up(near, far):
    near = dict(near, pick_small=jnp.asarray(picking_small(), BF16))
    far = dict(
        far,
        unpicks=jnp.asarray(unpicking(PIECES, 64), BF16),
        picks=jnp.asarray(picking(), BF16),
        table=jnp.asarray(bias_table()),
    )
    vec = ((8, D), F32)
    outs = dict(
        vec_one_0=vec,
        vec_two_0=vec,
        vec_one_1=vec,
        vec_two_1=vec,
        head_vec=((2, D), F32),
        place=((1, 128), jnp.int32),
        mask=((1, 8 * 112), F32),
        bias_one_0=((1, 3 * HW), F32),
        bias_one_1=((1, 3 * HW), F32),
        bias_two_0=((1, FW), F32),
        bias_two_1=((1, FW), F32),
    )
    kept = dict(
        rows=((SLAB, ALL_COLS), BF16),
        wqkv=((D, 3 * HW), BF16),
        wm=((D, HW), BF16),
        feat=((D, 128), BF16),
    )
    scratch = dict(
        pack=pltpu.VMEM((128, ALL_COLS), BF16),
        w_mine=pltpu.VMEM((8, 64, PIECE), BF16),
        w_got=pltpu.VMEM((8, 64, PIECE), BF16),
        lines=pltpu.VMEM((128, 128), F32),
        block=pltpu.VMEM((16, 128), F32),
        small=pltpu.VMEM((4, 4, 8, 16, 128), BF16),
        places=pltpu.VMEM((8, 128), F32),
        placed_bias=pltpu.VMEM((128, 128), F32),
        m_mine=pltpu.VMEM((4, 4, 128, 128), F32),
        m_sum=pltpu.VMEM((128, 128), F32),
        m_got=pltpu.VMEM((8, 16, 128), F32),
        m_all=pltpu.VMEM((128, 128), F32),
        feat32=pltpu.VMEM((D, 128), F32),
        turned=pltpu.VMEM((128, D), F32),
        ss=dma_sems(34)[0],
        rs=dma_sems(34)[1],
        fetch=rows_in_scratch(ATT_COLS),
        mods=sum_scratch([(64, 128), (64, 128)], F32),
    )
    near_outs, far_outs = launch(open_body, 1, near, far, outs, kept, scratch)
    return Results(near_outs, **far_outs)


EARLY = ATT_COLS + 2 * FFN_COLS
EARLY_PIECES = -(-EARLY // PIECE)
LATE_PIECES = -(-ATT_COLS // PIECE)
LATE_ROWS = 32


def packed_rows(picks_ref, parts, pieces):
    columns = jnp.concatenate(parts, axis=1)
    spare = pieces * PIECE - columns.shape[1]
    columns = jnp.concatenate([columns, jnp.zeros((SLAB, spare), BF16)], axis=1)
    total = jnp.zeros((8 * 64, PIECE), F32)
    for k in range(pieces):
        total = total + dot_tn(picks_ref[k], columns[:, k * PIECE : (k + 1) * PIECE])
    return total.astype(BF16).reshape(8, 64, PIECE)


def bias_lines(table_ref, cols, shift, biases, count):
    which = table_ref[1:2, cols]
    parts = []
    for bias in biases:
        rest = jnp.concatenate(
            [jnp.where(which == j, bias, 0.0) for j in range(count)]
            + [jnp.zeros((8 - count, bias.shape[1]), F32)],
            axis=0,
        )
        for _ in range(3):
            part = rest.astype(BF16).astype(F32)
            parts.append(part)
            rest = rest - part
    parts = jnp.concatenate(parts, axis=0).astype(BF16)
    found = dot_nt(parts, bias_picks(table_ref, cols, shift).astype(BF16))
    sums = [found[24 * k : 24 * k + 8] for k in range(2)]
    return [
        (sums[k] + found[24 * k + 8 : 24 * k + 16] + found[24 * k + 16 : 24 * k + 24])[:count]
        for k in range(2)
    ]


def finish_body(r):
    group = group_peers()
    sib, up, down, far = ring_peers()
    rows = RowsOut(r.left, r.right, r.rows_sums)
    small = RowsOut(r.small.at[:, :, 0:40], r.small.at[:, :, 40:80], r.small_sums)
    peers = [peer for peer, _ in group] + rows.peers()
    greet(peers)
    me, x, z = own_group(), lax.axis_index("dp_0"), lax.axis_index("dp_1")
    sems = (r.ss, r.rs)
    load(r, r.left, r.right, r.picks, r.attn_rows, r.ffn_rows_0, r.ffn_rows_1)
    load(r, r.unpatch_rows, r.embed_rows, r.table)
    r.m_mine[...] = jnp.zeros_like(r.m_mine)
    vecs = (r.vecs_one_0, r.vecs_two_0, r.vecs_one_1, r.vecs_two_1, r.head_vecs)
    for k, ref in enumerate(vecs):
        for i in range(3 if k < 4 else 2):
            for j in range(9):
                line = 27 * k + 9 * i + j
                r.m_mine[line // 16, line % 16 : line % 16 + 1] = ref[
                    i : i + 1, j * 128 : (j + 1) * 128
                ]
    met(peers)
    settle(r, r.left, r.right)
    rows.start()
    m_first = [send(r.m_mine.at[at], r.m_got.at[me], sems, k, p) for k, (p, at) in enumerate(group)]
    r.m_got[me] = r.m_mine[me]
    settle(r)
    attn_at, ffn_at = own_targets()
    biases = (r.bias_one_0[...], r.bias_one_1[...])
    narrow = bias_lines(r.table, ATT_BIAS, attn_at, biases, 2)
    biases = (r.bias_two_0[...], r.bias_two_1[...])
    wide = bias_lines(r.table, FFN_BIAS, ffn_at, biases, 4)
    vecs = ((r.vecs_one_0, r.vecs_two_0), (r.vecs_one_1, r.vecs_two_1))
    for k in range(2):
        r.bias_rows[k, 0:2] = narrow[k]
        r.bias_rows[k, 2:6] = wide[k]
        r.bias_rows[k, 6:7] = vecs[k][0][3:4]
        r.bias_rows[k, 7:8] = vecs[k][1][3:4]
    r.turned[...] = jnp.zeros_like(r.turned)
    for k in range(9):
        cols = slice(k * 128, (k + 1) * 128)
        r.lines[...] = jnp.zeros_like(r.lines)
        r.lines[0:32] = r.unpatch_rows[:, cols]
        r.lines[32:48] = r.embed_rows[0:16, cols]
        r.lines[48:56] = r.bias_rows[0, :, cols]
        r.lines[56:64] = r.bias_rows[1, :, cols]
        r.lines[64:72] = r.embed_rows[16:24, cols]
        r.turned[cols, :] = jnp.transpose(r.lines[...])
    for k in range(16):
        r.small[k // 4, k % 4, 0:72] = r.turned[k * PART : (k + 1) * PART, :]
        r.small[k // 4, k % 4, 72:80] = r.unpatch_bias[...]
    small.start()
    r.early[...] = packed_rows(
        r.picks, [r.attn_rows[...], r.ffn_rows_0[...], r.ffn_rows_1[...]], EARLY_PIECES
    )
    sent = [
        send(r.early.at[at], r.early_out.at[me], sems, 7 + k, p) for k, (p, at) in enumerate(group)
    ]
    r.early_out[me] = r.early[me]
    for copy in m_first:
        copy.wait_recv()
    total = r.m_got[0]
    for k in range(1, 8):
        total = total + r.m_got[k]
    r.m_out[me, x, z] = total.astype(BF16)
    part = r.m_out.at[me, x, z]
    m_second = [send(part, part, sems, 14 + k, p) for k, (p, _) in enumerate(rows.along_z)]
    small.middle()
    for copy in m_second:
        copy.wait_recv()
    part = r.m_out.at[me, x]
    m_third = [send(part, part, sems, 17 + k, p) for k, (p, _) in enumerate(rows.along_x)]
    r.s_total[0:40], r.s_total[40:80] = small.end()
    for g in range(8):
        r.s_mine[g, 0:9] = r.s_total[9 * g : 9 * g + 9]
        r.s_mine[g, 9:16] = r.s_total[72:79]
    s_last = [
        send(r.s_mine.at[at], r.s_two.at[me], sems, 20 + k, p) for k, (p, at) in enumerate(group)
    ]
    r.s_two[me] = r.s_mine[me]
    for copy in m_third:
        copy.wait_recv()
    part = r.m_out.at[me]
    m_fourth = [send(part, part, sems, 27 + k, p) for k, p in enumerate((up, down, far, sib))]
    rows.middle()
    c, y = lax.axis_index("tx"), lax.axis_index("ty")
    m_fifth = []
    for k, d in enumerate((3, 1, 2)):
        m_fourth[k].wait_recv()
        part = r.m_out.at[c * 4 + lax.rem(y + d, 4)]
        m_fifth.append(send(part, part, sems, 31 + k, sib))
    for copy in s_last:
        copy.wait_recv()
    total = r.s_two[0]
    for k in range(1, 8):
        total = total + r.s_two[k]
    r.s_out[...] = total
    rows.end_rows(r.late_rows)
    r.late[...] = packed_rows(r.picks, [r.late_rows[...]], LATE_PIECES)[:, :LATE_ROWS]
    later = [
        send(r.late.at[at], r.late_out.at[me], sems, 34 + k, p) for k, (p, at) in enumerate(group)
    ]
    r.late_out[me] = r.late[me]
    for copy in sent + m_fourth[3:] + m_fifth + later:
        copy.wait_recv()
    small.leave()
    for copy in m_first + sent + m_second + m_third + s_last + m_fourth + m_fifth + later:
        copy.wait_send()


def finish(near, far):
    far = dict(far, picks=jnp.asarray(picking(), BF16), table=jnp.asarray(bias_table()))
    outs = dict(
        early_out=((8, 64, PIECE), BF16),
        late_out=((8, LATE_ROWS, PIECE), BF16),
        m_out=((8, 4, 4, 16, 128), BF16),
        s_out=((16, 128), F32),
    )
    scratch = dict(
        early=pltpu.VMEM((8, 64, PIECE), BF16),
        late=pltpu.VMEM((8, LATE_ROWS, PIECE), BF16),
        m_mine=pltpu.VMEM((8, 16, 128), F32),
        m_got=pltpu.VMEM((8, 16, 128), F32),
        lines=pltpu.VMEM((128, 128), F32),
        bias_rows=pltpu.VMEM((2, 8, D), F32),
        turned=pltpu.VMEM((D, 128), F32),
        small=pltpu.VMEM((4, 4, 80, 128), F32),
        s_total=pltpu.VMEM((80, 128), F32),
        s_mine=pltpu.VMEM((8, 16, 128), F32),
        s_two=pltpu.VMEM((8, 16, 128), F32),
        late_rows=pltpu.VMEM((SLAB, ATT_COLS), BF16),
        ss=dma_sems(41)[0],
        rs=dma_sems(41)[1],
        rows_sums=rows_out_scratch(ATT_COLS),
        small_sums=sum_scratch([(40, 128), (40, 128)], F32),
    )
    return launch(finish_body, 2, near, far, outs, {}, scratch)[0]


def unpicking(pieces, height):
    picks = np.zeros((pieces, 128, 8 * height), np.float32)
    for k in range(pieces):
        for group in range(8):
            for row in range(9):
                picks[k, group * 16 + row, group * height + 9 * k + row] = 1.0
    return picks


def close_body(r):
    load(r, r.early_in, r.early_picks, r.late_in, r.late_picks, r.m_in, r.mod_w, r.final_w)
    settle(r, r.early_in, r.late_in, r.early_picks, r.late_picks)
    received = r.early_in[...].reshape(8 * 64, PIECE)
    for k in range(EARLY_PIECES):
        r.early[:, k * PIECE : (k + 1) * PIECE] = dot_nn(r.early_picks[k], received)
    received = r.late_in[...].reshape(8 * LATE_ROWS, PIECE)
    for k in range(LATE_PIECES):
        r.late[:, k * PIECE : (k + 1) * PIECE] = dot_nn(r.late_picks[k], received)

    def whole(source, start, width):
        parts = [source[g * 16 : g * 16 + 16, start : start + width] for g in range(8)]
        return jnp.concatenate(parts, axis=1)[:9]

    for b, (source, start) in enumerate(((r.late, 0), (r.early, 0))):
        for j in range(3):
            r.attn[:, j, b, :] = whole(source, start + j * HW, HW)
        r.merge[:, b, :] = whole(source, start + 3 * HW, HW)
    for b, start in enumerate((ATT_COLS, ATT_COLS + FFN_COLS)):
        r.expand[:, b, :] = whole(r.early, start, FW)
        r.reduce[:, b, :] = whole(r.early, start + FW, FW)
    save(r, r.attn, r.merge, r.expand, r.reduce)
    settle(r, r.m_in, r.mod_w, r.final_w)
    for k in range(128):
        value = r.m_in[k // 16, :, :, k % 16, :]
        r.grads[:, k * 128 : (k + 1) * 128] = value.reshape(16, 128)
        r.sums[k : k + 1] = sum_rows(value.reshape(16, 128).astype(F32))
    condition = r.condition[...].astype(F32)
    gate = 1.0 / (1.0 + jnp.exp(-condition))
    cond16 = (condition / (1.0 + jnp.exp(-condition))).astype(BF16)
    terms = jnp.zeros((16, 9), F32)
    for b in range(3):
        grads = r.grads[:, 6 * b * D : min(6 * b + 6, 14) * D]
        weights = r.mod_w[:, b, :] if b < 2 else r.final_w[...]
        product = dot_tn(cond16, grads)
        if b < 2:
            r.mod_grad[:, b, :] = product
        else:
            r.final_grad[...] = product
        terms = terms + dot_nt(grads, weights)
    save(r, r.mod_grad, r.final_grad)
    r.predicted[...] = r.predicted_in[...]
    r.latent[...] = r.latent_in[...]
    r.condition_grad[...] = terms * (gate * (1.0 + condition * (1.0 - gate)))
    on_line, on_lane = mod_places(whole_index())
    found = exact(r.sums[...], jnp.where(on_lane, 1.0, 0.0).astype(F32), (1, 0))
    found = sum_rows(jnp.where(on_line, found, 0.0))
    r.mod_b[0:1] = found[:, 0:54]
    r.mod_b[1:2] = found[:, 54:108]
    r.final_b[...] = found[:, 108:126]
    r.square[...] = jnp.zeros_like(r.square)
    r.square[0:16] = r.s_in[...]
    turned = jnp.transpose(r.square[...])
    r.unpatch_w[...] = r.s_in[0:9, 0:32]
    r.unpatch_b[...] = r.s_in[9:10, 0:32]
    r.embed_w[...] = turned[32:48, 0:9]
    r.embed_b[...] = turned[64:65, 0:9]
    for b in range(2):
        at = BLOCKS + 8 * b
        for j in range(2):
            r.attn_b[b : b + 1, 9 * j : 9 * j + 9] = turned[at + j : at + j + 1, 0:9]
        for j in range(4):
            r.expand_b[b : b + 1, 9 * j : 9 * j + 9] = turned[at + 2 + j : at + 3 + j, 0:9]
        r.merge_b[b : b + 1] = turned[at + 6 : at + 7, 0:9]
        r.reduce_b[b : b + 1] = turned[at + 7 : at + 8, 0:9]
    settle(r)


def close(near, far):
    far = dict(
        far,
        early_picks=jnp.asarray(unpicking(EARLY_PIECES, 64), BF16),
        late_picks=jnp.asarray(unpicking(LATE_PIECES, LATE_ROWS), BF16),
    )
    kept = dict(
        attn=((9, 3, 2, D), F32),
        merge=((9, 2, D), F32),
        expand=((9, 2, FF), F32),
        reduce=((9, 2, FF), F32),
        mod_grad=((9, 2, 6 * D), F32),
        final_grad=((9, 2 * D), F32),
    )
    outs = dict(
        predicted=((16, 8, 32), BF16),
        latent=((16, 4, 32), F32),
        condition_grad=((16, 9), F32),
        mod_b=((2, 54), F32),
        final_b=((1, 18), F32),
        unpatch_w=((9, 32), F32),
        unpatch_b=((1, 32), F32),
        embed_w=((16, 9), F32),
        embed_b=((1, 9), F32),
        attn_b=((2, 18), F32),
        expand_b=((2, 36), F32),
        merge_b=((2, 9), F32),
        reduce_b=((2, 9), F32),
    )
    scratch = dict(
        early=pltpu.VMEM((128, EARLY_PIECES * PIECE), F32),
        late=pltpu.VMEM((128, LATE_PIECES * PIECE), F32),
        grads=pltpu.VMEM((16, WHOLE), BF16),
        sums=pltpu.VMEM((128, 128), F32),
        square=pltpu.VMEM((128, 128), F32),
    )
    near_outs, far_outs = launch(close_body, None, near, far, outs, kept, scratch)
    return Results(near_outs, **far_outs)


def forward_body(r, tokens, start, last):
    a, b = halves(r, tokens, r.x16, r.in_all, r.remote_one)
    fetch = RowsIn(*slab_views(r.rows, start, FFN_COLS), r.fetch_one)
    peers = a.peers() + fetch.peers()
    greet(peers)
    if last:
        load(r, r.first, r.wqkv, r.rows, r.wm)
        settle(r, r.first)
        r.x[...] = exact(choice(r.place, tokens), r.first[...], (1, 0))
    else:
        load(r, r.feat, r.placed, r.wqkv, r.rows, r.wm)
        settle(r, r.feat, r.placed)
        r.token_cols[...] = jnp.zeros_like(r.token_cols)
        to_tokens(r.pixels, r.square, r.token_cols, EMBED)
        r.patches[...] = r.token_cols[...].astype(BF16)
        r.x[...] = dot_nt(r.patches[...], r.feat[...]) + r.vec_one[4:5] + r.placed[...]
    r.x16[...] = modulated(r.x[...], r.vec_one)
    met(peers)
    a.issue()
    a.issue_rest()
    b.issue()
    save(r, r.x)
    if not last:
        save(r, r.patches)

    def prepare():
        settle(r, r.wqkv, r.rows)
        fetch.start()

    def visit(half, d):
        rows = half.pair(d)
        joined = (dot_nn(r.in_all[rows, :], r.wqkv[...]) + r.bias_one[...]).astype(BF16)
        for h in range(2):
            r.q[h, rows, :] = joined[:, head_cols(h)]
            r.k[h, rows, :] = joined[:, head_cols(h, HW)]
            r.v[h, rows, :] = joined[:, head_cols(h, 2 * HW)]

    def attend(half, d):
        rows = half.pair(d)
        parts = []
        for h in range(2):
            scores = dot_nt(r.q[h, rows, :], r.k[h]) * SCALE
            if last:
                scores = scores + r.mask[...]
            highest = jnp.max(scores, axis=-1, keepdims=True)
            shifted = jnp.exp(scores - highest)
            summed = jnp.sum(shifted, axis=-1, keepdims=True)
            probs = (shifted * (1.0 / summed)).astype(BF16)
            r.lse[rows, h : h + 1] = highest + jnp.log(summed)
            parts.append(dot_nn(probs, r.v[h]).astype(BF16))
        attended = jnp.concatenate(parts, axis=1)
        r.att[rows, :] = attended
        half.put(d, dot_nt(attended, r.wm[...]))

    gather_both(a, b, prepare, visit, fetch.middle)
    settle(r, r.wm)
    save(r, r.in_all, r.q, r.k, r.v)
    sum_both(a, b, attend)
    save(r, r.lse, r.att)
    fetch.end(r.we, r.wr)
    save(r, r.we, r.wr)
    follow = halves(r, tokens, r.x16, r.second, r.remote_two)

    def finish_half(half, after):
        branch = half.total() + r.vec_one[3:4]
        middle = r.x[half.own, :] + r.vec_one[2:3] * branch
        r.x16[half.own, :] = modulated(middle, r.vec_two)
        after.issue()
        r.branch[half.own, :] = branch
        r.middle[half.own, :] = middle

    finish_half(a, follow[0])
    follow[0].issue_rest()
    finish_half(b, follow[1])
    save(r, r.branch, r.middle)
    a, b = follow
    fetch = None
    if not last:
        fetch = RowsIn(*slab_views(r.rows, ATT_COLS, ATT_COLS), r.fetch_two)

    def expand(half, d):
        rows = half.pair(d)
        pre = dot_nn(r.second[rows, :], r.we[...]) + r.bias_two[...]
        value, slope = gelu_both(pre)
        hidden = value.astype(BF16)
        r.hid[rows, :] = hidden
        r.slope[rows, :] = slope.astype(BF16)
        half.put(d, dot_nt(hidden, r.wr[...]))

    if fetch:
        gather_and_sum(a, b, fetch.start, expand, fetch.middle)
    else:
        gather_and_sum(a, b, nothing, expand, nothing)
    save(r, r.second, r.hid, r.slope)
    b.relay()
    if fetch:
        fetch.end(r.next_wqkv, r.next_wm)
        save(r, r.next_wqkv, r.next_wm)
    for half in (a, b):
        mlp = half.total() + r.vec_two[3:4]
        r.mlp[half.own, :] = mlp
        r.out[half.own, :] = r.middle[half.own, :] + r.vec_two[2:3] * mlp
    save(r, r.mlp, r.out)
    settle(r)


def ring_scratch(tokens):
    sizes = half_sizes(tokens)
    remote = [half_remote(size) for size in sizes]
    return dict(local=[half_local(size) for size in sizes], remote_one=remote, remote_two=remote)


def kept_shapes(tokens):
    heads = ((2, 8 * tokens, HEAD), BF16)
    wide, tile = ((8 * tokens, D), BF16), ((tokens, D), F32)
    hidden = ((8 * tokens, FW), BF16)
    return dict(
        x=tile,
        in_all=wide,
        q=heads,
        k=heads,
        v=heads,
        lse=((8 * tokens, 2), F32),
        att=((8 * tokens, HW), BF16),
        branch=tile,
        middle=tile,
        second=wide,
        hid=hidden,
        slope=hidden,
        mlp=tile,
        we=((D, FW), BF16),
        wr=((D, FW), BF16),
    )


def block_forward(near, far, tokens, start, last, cid):
    kept = dict(kept_shapes(tokens), out=((tokens, D), F32))
    scratch = dict(
        x16=pltpu.VMEM((tokens, D), BF16),
        **ring_scratch(tokens),
        fetch_one=rows_in_scratch(FFN_COLS),
    )
    if not last:
        kept.update(
            next_wqkv=((D, 3 * HW), BF16), next_wm=((D, HW), BF16), patches=((128, 128), BF16)
        )
        scratch.update(
            square=pltpu.VMEM((128, 128), F32),
            token_cols=pltpu.VMEM((128, 128), F32),
            fetch_two=rows_in_scratch(ATT_COLS),
        )
    body = functools.partial(forward_body, tokens=tokens, start=start, last=last)
    return launch(body, cid, near, far, {}, kept, scratch)[1]


def head(r):
    picks = choice(r.place, r.two.shape[0])
    ended = spread_back(picks, r.two[...], r.first[...])
    normed, inv_std = layer_stats(ended)
    final16 = (normed * (1.0 + r.head_vec[1:2]) + r.head_vec[0:1]).astype(BF16)
    unpatch = r.feat[:, UNPATCH : UNPATCH + 32]
    r.token_cols[...] = jnp.zeros_like(r.token_cols)
    r.token_cols[:, 0:32] = dot_nn(final16, unpatch) + r.unpatch_b[...].astype(F32)
    to_pixels(r.token_cols, r.square, r.predicted, 0)
    to_tokens(r.cotangent_pixels, r.square, r.token_cols, 0)
    r.cotangent[...] = r.token_cols[:, 0:32].astype(BF16)
    r.unpatch_rows[...] = dot_tn(r.cotangent[...], final16)
    r.unpatch_bias[...] = jnp.zeros_like(r.unpatch_bias)
    r.unpatch_bias[0:1, 0:32] = sum_rows(r.cotangent[...].astype(F32))
    grad = dot_nt(r.cotangent[...], unpatch)
    r.head_vecs[0:1] = sum_rows(grad)
    r.head_vecs[1:2] = sum_rows(grad * normed)
    grad = layer_back(grad * (1.0 + r.head_vec[1:2]), normed, inv_std)
    r.grad_ended[...] = grad
    r.g[...] = exact(picks, grad, (1, 0))


def backward_body(r, tokens, last):
    a, b = halves(r, tokens, r.g16, r.g_one, r.remote_one)
    sums = None if last else RowsOut(r.pending_left, r.pending_right, r.sums_one)
    peers = a.peers() + line_only(line_peers())
    greet(peers)
    if last:
        load(r, r.first, r.two, r.feat, r.slope, r.wr, r.we)
    else:
        load(r, r.grad_two, r.grad_ended, r.slope, r.wr, r.we, r.pending_left, r.pending_right)
        load(r, r.feat, r.patches)
    load(r, r.hid, r.second, r.mlp, r.middle)
    load(r, r.q, r.k, r.v, r.lse, r.wm, r.wqkv, r.att, r.x, r.branch)
    if last:
        settle(r, r.first, r.two, r.feat)
        head(r)
    else:
        settle(r, r.grad_two, r.grad_ended)
        picks = choice(r.place, r.grad_two.shape[0])
        r.g[...] = spread_back(picks, r.grad_two[...], r.grad_ended[...])
    r.g16[...] = (r.g[...] * r.vec_two[2:3]).astype(BF16)
    met(peers)
    a.issue()
    a.issue_rest()
    b.issue()
    r.bias_two[...] = jnp.zeros_like(r.bias_two)

    def prepare():
        if sums:
            settle(r, r.pending_left, r.pending_right)
            sums.start()
        settle(r, r.slope, r.wr, r.we)

    def visit(half, d):
        rows = half.pair(d)
        pre_grad = (
            dot_nn(r.g_one[rows, :], r.wr[...]) * r.slope[rows, :].astype(F32)
        ).astype(BF16)
        r.pre_all[rows, :] = pre_grad
        r.bias_two[...] += sum_rows(pre_grad.astype(F32))
        half.put(d, dot_nt(pre_grad, r.we[...]))

    if last:
        save(r, r.grad_ended, r.unpatch_rows)
    gather_and_sum(a, b, prepare, visit, nothing)
    settle(r, r.hid, r.second, r.mlp, r.middle)
    r.vecs_two[2:3] = sum_rows(r.g[...] * r.mlp[...])
    r.vecs_two[3:4] = sum_rows(r.g16[...].astype(F32))
    r.vecs_two[4:8] = jnp.zeros((4, D), F32)
    if sums:
        sums.middle()
    b.relay()
    weight_grads(r.g_one, r.hid, r.whole_two, FW)
    follow = halves(r, tokens, r.g16, r.g_two, r.remote_two)

    def finish_half(half, after):
        second_grad = half.total()
        normed, inv_std = layer_stats(r.middle[half.own, :])
        grad = r.g[half.own, :] + layer_back(
            second_grad * (1.0 + r.vec_two[1:2]), normed, inv_std
        )
        r.g[half.own, :] = grad
        r.g16[half.own, :] = (grad * r.vec_one[2:3]).astype(BF16)
        after.issue()
        return sum_rows(second_grad), sum_rows(second_grad * normed)

    shift_a, scale_a = finish_half(a, follow[0])
    follow[0].issue_rest()
    shift_b, scale_b = finish_half(b, follow[1])
    r.vecs_two[0:1] = shift_a + shift_b
    r.vecs_two[1:2] = scale_a + scale_b
    weight_grads(r.second, r.pre_all, r.whole_one, FW)
    load_into(r, r.in_all, r.second)
    write_slabs((r.whole_one, FW), (r.whole_two, FW), r.ffn_left, r.ffn_right)
    if sums:
        sums.end_rows(r.attn_rows)
        save(r, r.attn_rows)
    a, b = follow
    sums = RowsOut(r.ffn_left, r.ffn_right, r.sums_two)

    def prepare_attention():
        sums.start()
        r.dk[...] = jnp.zeros_like(r.dk)
        r.dv[...] = jnp.zeros_like(r.dv)
        settle(r, r.q, r.k, r.v, r.lse, r.wm)

    def attend(half, d):
        rows = half.pair(d)
        grad = dot_nn(r.g_two[rows, :], r.wm[...]).astype(BF16)
        queries = []
        for h in range(2):
            part = grad[:, head_cols(h)]
            query = r.q[h, rows, :]
            scores = dot_nt(query, r.k[h]) * SCALE
            if last:
                scores = scores + r.mask[...]
            probs = jnp.exp(scores - r.lse[rows, h : h + 1])
            grad_probs = dot_nt(part, r.v[h])
            weighted = jnp.sum(probs * grad_probs, axis=-1, keepdims=True)
            score_grad = (probs * (grad_probs - weighted)).astype(BF16)
            queries.append((dot_nn(score_grad, r.k[h]) * SCALE).astype(BF16))
            r.dk[h] += dot_tn(score_grad, query)
            r.dv[h] += dot_tn(probs.astype(BF16), part)
        r.joined[rows, 0:HW] = jnp.concatenate(queries, axis=1)

    def back(half, d):
        half.put(d, dot_nt(r.joined[half.pair(d), :], r.wqkv[...]))

    gather_both(a, b, prepare_attention, attend, nothing)
    settle(r, r.wqkv)
    later = [(r.dk[h] * SCALE).astype(BF16) for h in range(2)]
    later += [r.dv[h].astype(BF16) for h in range(2)]
    r.joined[:, HW : 3 * HW] = jnp.concatenate(later, axis=1)
    sum_both(a, b, back)
    settle(r)
    sums.middle()
    r.bias_one[...] = sum_rows(r.joined[...].astype(F32))
    r.vecs_one[2:3] = sum_rows(r.g[...] * r.branch[...])
    r.vecs_one[3:4] = sum_rows(r.g16[...].astype(F32))
    r.vecs_one[4:8] = jnp.zeros((4, D), F32)
    weight_grads(r.g_two, r.att, r.whole_two, HW)
    weight_grads(r.second, r.joined, r.whole_one, 3 * HW)
    write_slabs((r.whole_one, 3 * HW), (r.whole_two, HW), r.attn_left, r.attn_right)
    save(r, r.attn_left, r.attn_right)
    sums.end_rows(r.ffn_rows)
    save(r, r.ffn_rows)
    shift, scale = 0.0, 0.0
    for half in (a, b):
        input_grad = half.total()
        normed, inv_std = layer_stats(r.x[half.own, :])
        shift = shift + sum_rows(input_grad)
        scale = scale + sum_rows(input_grad * normed)
        scaled = input_grad * (1.0 + r.vec_one[1:2])
        r.g[half.own, :] = r.g[half.own, :] + layer_back(scaled, normed, inv_std)
    r.vecs_one[0:1] = shift
    r.vecs_one[1:2] = scale
    if last:
        r.out[...] = r.g[...]
        save(r, r.out)
    else:
        grad16 = r.g[...].astype(BF16)
        r.embed_rows[0:16] = dot_tn(r.patches[...], grad16)[EMBED : EMBED + 16]
        r.embed_rows[16:17] = sum_rows(grad16.astype(F32))
        r.embed_rows[17:24] = jnp.zeros((7, D), F32)
        save(r, r.embed_rows)
        r.token_cols[...] = dot_nn(grad16, r.feat[...])
        to_pixels(r.token_cols, r.square, r.latent, EMBED)
    settle(r)


def weight_grads(left_ref, right_ref, whole_ref, width):
    @pl.loop(0, D // 384)
    def _(k):
        at = pl.ds(pl.multiple_of(k * 384, 128), 384)
        whole_ref[at, :width] = dot_tn(left_ref[:, at], right_ref[...])


def write_slabs(one, two, left_ref, right_ref):
    cut = left_ref.shape[3]
    cols = cut + right_ref.shape[3]

    @pl.loop(0, 16)
    def _(k):
        at = pl.ds(pl.multiple_of(k * PART, 8), PART)
        parts = [ref[at, :width] for ref, width in (one, two)]
        spare = cols - one[1] - two[1]
        if spare:
            parts.append(jnp.zeros((PART, spare), F32))
        rows = jnp.concatenate(parts, axis=1)
        rows = jnp.concatenate([rows, jnp.zeros((SLAB - PART, cols), F32)], axis=0).astype(BF16)
        x, z = k // 4, lax.rem(k, 4)
        left_ref[x, z] = rows[:, :cut]
        right_ref[x, z] = rows[:, cut:]


def line_only(lines):
    return [peer for peer, _ in lines[0] + lines[1]]


def slab_specs(cols):
    widths = (CUT[cols], cols - CUT[cols])
    return [((4, 4, SLAB, width), BF16) for width in widths]


def block_backward(near, far, tokens, last, cid):
    vecs = ((8, D), F32)
    attn_left, attn_right = slab_specs(ATT_COLS)
    wide, tile = (8 * tokens, D), (tokens, D)
    outs = dict(vecs_one=vecs, vecs_two=vecs)
    outs.update(bias_one=((1, 3 * HW), F32), bias_two=((1, FW), F32))
    kept = dict(attn_left=attn_left, attn_right=attn_right, ffn_rows=((SLAB, FFN_COLS), BF16))
    scratch = dict(
        g=pltpu.VMEM(tile, F32),
        g16=pltpu.VMEM(tile, BF16),
        square=pltpu.VMEM((128, 128), F32),
        token_cols=pltpu.VMEM((128, 128), F32),
        g_one=pltpu.VMEM(wide, BF16),
        g_two=pltpu.VMEM(wide, BF16),
        pre_all=pltpu.VMEM((8 * tokens, FW), BF16),
        joined=pltpu.VMEM((8 * tokens, 3 * HW), BF16),
        dk=pltpu.VMEM((2, 8 * tokens, HEAD), F32),
        dv=pltpu.VMEM((2, 8 * tokens, HEAD), F32),
        whole_one=pltpu.VMEM((D, FW), F32),
        whole_two=pltpu.VMEM((D, FW), F32),
        ffn_left=pltpu.VMEM(*slab_specs(FFN_COLS)[0]),
        ffn_right=pltpu.VMEM(*slab_specs(FFN_COLS)[1]),
        **ring_scratch(tokens),
        sums_two=rows_out_scratch(FFN_COLS),
    )
    if last:
        outs.update(
            predicted=((16, 8, 32), BF16), unpatch_bias=((8, 128), F32), head_vecs=((2, D), F32)
        )
        kept.update(out=(tile, F32), unpatch_rows=((32, D), F32), grad_ended=((128, D), F32))
        scratch.update(cotangent=pltpu.VMEM((128, 32), BF16))
    else:
        outs.update(latent=((16, 4, 32), F32))
        kept.update(attn_rows=((SLAB, ATT_COLS), BF16), embed_rows=((24, D), F32))
        scratch.update(sums_one=rows_out_scratch(ATT_COLS))
    body = functools.partial(backward_body, tokens=tokens, last=last)
    near_outs, far_outs = launch(body, cid, near, far, outs, kept, scratch, vmem=62 << 20)
    return Results(near_outs, **far_outs)


def shards(
    latent,
    condition,
    routed_ids,
    embed_weight,
    embed_bias,
    modulation_weight,
    modulation_bias,
    attention_weight,
    attention_bias,
    merge_weight,
    merge_bias,
    expand_weight,
    expand_bias,
    reduce_weight,
    reduce_bias,
    final_modulation,
    final_offsets,
    unpatch_weight,
    unpatch_bias,
    pred_cotangent,
):
    tile_rows = latent.shape[1] // 2
    tile_cols = latent.shape[2] // 2
    tile_tokens = tile_rows * tile_cols
    capacity = 7 * tile_tokens // 8
    row_index = lax.axis_index("tx") * tile_rows + jnp.arange(tile_rows, dtype=jnp.int32)
    col_index = lax.axis_index("ty") * tile_cols + jnp.arange(tile_cols, dtype=jnp.int32)
    placed = sincos_table(row_index.astype(F32), col_index.astype(F32), D)
    mod_w = modulation_weight.swapaxes(0, 1)
    got = open_up(
        dict(
            condition=condition,
            ids=routed_ids,
            embed_w=embed_weight,
            embed_b=embed_bias[None],
            unpatch_w=unpatch_weight,
            attn_b=attention_bias,
            merge_b=merge_bias,
            expand_b=expand_bias,
            reduce_b=reduce_bias,
            mod_b=modulation_bias,
            final_b=final_offsets[None],
        ),
        dict(
            mod_w=mod_w,
            final_w=final_modulation,
            attn_w=attention_weight.transpose(1, 2, 0, 3),
            merge_w=merge_weight.swapaxes(0, 1),
            expand_w=expand_weight.swapaxes(0, 1),
            reduce_w=reduce_weight.swapaxes(0, 1),
        ),
    )
    vecs_one = dict(vec_one=got.vec_one_0, vec_two=got.vec_two_0)
    vecs_two = dict(vec_one=got.vec_one_1, vec_two=got.vec_two_1, mask=got.mask)
    kept_one = block_forward(
        dict(
            vecs_one,
            bias_one=got.bias_one_0,
            bias_two=got.bias_two_0,
            pixels=latent.transpose(0, 2, 3, 1)[0],
        ),
        dict(feat=got.feat, placed=placed, rows=got.rows, wqkv=got.wqkv, wm=got.wm),
        tile_tokens,
        2 * ATT_COLS,
        False,
        10,
    )
    weights_two = dict(wqkv=kept_one.next_wqkv, wm=kept_one.next_wm)
    kept_two = block_forward(
        dict(vecs_two, bias_one=got.bias_one_1, bias_two=got.bias_two_1, place=got.place),
        dict(weights_two, rows=got.rows, first=kept_one.out),
        capacity,
        2 * ATT_COLS + FFN_COLS,
        True,
        11,
    )

    def saved(kept, tokens):
        return {name: kept[name] for name in kept_shapes(tokens)}

    back_two = block_backward(
        dict(
            vecs_two,
            place=got.place,
            head_vec=got.head_vec,
            unpatch_b=unpatch_bias[None],
            cotangent_pixels=pred_cotangent.transpose(0, 2, 3, 1)[0],
        ),
        dict(
            saved(kept_two, capacity),
            **weights_two,
            feat=got.feat,
            first=kept_one.out,
            two=kept_two.out,
        ),
        capacity,
        True,
        12,
    )
    back_one = block_backward(
        dict(vecs_one, place=got.place),
        dict(
            saved(kept_one, tile_tokens),
            wqkv=got.wqkv,
            wm=got.wm,
            feat=got.feat,
            patches=kept_one.patches,
            pending_left=back_two.attn_left,
            pending_right=back_two.attn_right,
            grad_two=back_two.out,
            grad_ended=back_two.grad_ended,
        ),
        tile_tokens,
        False,
        13,
    )
    ended = finish(
        dict(
            vecs_one_0=back_one.vecs_one,
            vecs_two_0=back_one.vecs_two,
            vecs_one_1=back_two.vecs_one,
            vecs_two_1=back_two.vecs_two,
            head_vecs=back_two.head_vecs,
            bias_one_0=back_one.bias_one,
            bias_two_0=back_one.bias_two,
            bias_one_1=back_two.bias_one,
            bias_two_1=back_two.bias_two,
            unpatch_bias=back_two.unpatch_bias,
        ),
        dict(
            left=back_one.attn_left,
            right=back_one.attn_right,
            attn_rows=back_one.attn_rows,
            ffn_rows_0=back_one.ffn_rows,
            ffn_rows_1=back_two.ffn_rows,
            unpatch_rows=back_two.unpatch_rows,
            embed_rows=back_one.embed_rows,
        ),
    )
    last = close(
        dict(
            s_in=ended.s_out,
            condition=condition,
            predicted_in=back_two.predicted,
            latent_in=back_one.latent,
        ),
        dict(
            early_in=ended.early_out,
            late_in=ended.late_out,
            m_in=ended.m_out,
            mod_w=mod_w,
            final_w=final_modulation,
        ),
    )
    return (
        last.predicted.transpose(2, 0, 1)[None],
        last.latent.transpose(2, 0, 1)[None],
        last.condition_grad,
        last.embed_w,
        last.embed_b[0],
        last.mod_grad.swapaxes(0, 1),
        last.mod_b,
        last.attn.transpose(2, 0, 1, 3),
        last.attn_b,
        last.merge.swapaxes(0, 1),
        last.merge_b,
        last.expand.swapaxes(0, 1),
        last.expand_b,
        last.reduce.swapaxes(0, 1),
        last.reduce_b,
        last.final_grad,
        last.final_b[0],
        last.unpatch_w,
        last.unpatch_b[0],
    )


def solution(mesh):
    torus = Mesh(
        mesh.devices.reshape(4, 4, mesh.shape["tx"], mesh.shape["ty"]), ("dp_0", "dp_1", "tx", "ty")
    )
    return jax.shard_map(
        shards,
        mesh=torus,
        in_specs=(
            P(DP, "tx", "ty", None),
            P(None, DP_TX_TY),
            P(DP, None),
            P(None, DP_TX_TY),
            P(DP_TX_TY),
            P(None, DP_TX_TY, None),
            P(None, DP_TX_TY),
            P(None, DP_TX_TY, None, None),
            P(None, DP_TX_TY),
            P(None, DP_TX_TY, None),
            P(None, DP_TX_TY),
            P(None, DP_TX_TY, None),
            P(None, DP_TX_TY),
            P(None, DP_TX_TY, None),
            P(None, DP_TX_TY),
            P(DP_TX_TY, None),
            P(DP_TX_TY),
            P(DP_TX_TY, None),
            P(),
            P(DP, "tx", "ty", None),
        ),
        out_specs=(
            P(DP, "tx", "ty", None),
            P(DP, "tx", "ty", None),
            P(None, DP_TX_TY),
            P(None, DP_TX_TY),
            P(DP_TX_TY),
            P(None, DP_TX_TY, None),
            P(None, DP_TX_TY),
            P(None, DP_TX_TY, None, None),
            P(None, DP_TX_TY),
            P(None, DP_TX_TY, None),
            P(None, DP_TX_TY),
            P(None, DP_TX_TY, None),
            P(None, DP_TX_TY),
            P(None, DP_TX_TY, None),
            P(None, DP_TX_TY),
            P(DP_TX_TY, None),
            P(DP_TX_TY),
            P(DP_TX_TY, None),
            P(),
        ),
        check_vma=False,
    )
```

```python
import functools

import jax
import jax.numpy as jnp
import numpy as np
from jax import lax
from jax.experimental import pallas as pl
from jax.experimental.pallas import tpu as pltpu
from jax.sharding import Mesh
from jax.sharding import PartitionSpec as P

D = 1152
HEADS = 16
FF = 4608
HW = D // 8
FW = FF // 8
DP = ("dp_0", "dp_1")
DP_TX_TY = ("dp_0", "dp_1", "tx", "ty")
MESH = pl.DeviceIdType.MESH
VMEM = pl.BlockSpec(memory_space=pltpu.VMEM)
FAR = pl.BlockSpec(memory_space=pl.ANY)
F32 = jnp.float32
BF16 = jnp.bfloat16
ATT_COLS = 640
FFN_COLS = 2 * FW
ALL_COLS = 2 * (ATT_COLS + FFN_COLS)
PIECE = 512
PIECES = ALL_COLS // PIECE


def greet(peers):
    barrier = pltpu.get_barrier_semaphore()
    for peer in peers:
        pl.semaphore_signal(barrier, inc=1, device_id=peer, device_id_type=MESH)


def met(peers):
    pl.semaphore_wait(pltpu.get_barrier_semaphore(), len(peers))


def enter(peers):
    greet(peers)
    met(peers)


def send(src, dst, sems, k, peer):
    copy = pltpu.make_async_remote_copy(
        src_ref=src,
        dst_ref=dst,
        send_sem=sems[0].at[k],
        recv_sem=sems[1].at[k],
        device_id=peer,
        device_id_type=MESH,
    )
    copy.start()
    return copy


def group_peers():
    c, y = lax.axis_index("tx"), lax.axis_index("ty")
    found = []
    for dc in range(2):
        for dy in range(4):
            if dc or dy:
                oc, oy = lax.rem(c + dc, 2), lax.rem(y + dy, 4)
                found.append(({"tx": oc, "ty": oy}, oc * 4 + oy))
    return found


def own_group():
    return lax.axis_index("tx") * 4 + lax.axis_index("ty")


def dma_sems(n):
    return [pltpu.SemaphoreType.DMA((n,)), pltpu.SemaphoreType.DMA((n,))]


def ring_peers():
    c, y = lax.axis_index("tx"), lax.axis_index("ty")
    return (
        {"tx": 1 - c},
        {"ty": lax.rem(y + 1, 4)},
        {"ty": lax.rem(y + 3, 4)},
        {"ty": lax.rem(y + 2, 4)},
    )


def layer_stats(value_rows):
    centered = value_rows - jnp.mean(value_rows, axis=-1, keepdims=True)
    inv_std = lax.rsqrt(jnp.mean(centered * centered, axis=-1, keepdims=True) + 1e-06)
    return (centered * inv_std, inv_std)


def layer_back(upstream, normed, inv_std):
    return inv_std * (
        upstream
        - jnp.mean(upstream, axis=-1, keepdims=True)
        - normed * jnp.mean(upstream * normed, axis=-1, keepdims=True)
    )


def sincos_table(row_pos, col_pos, width):
    quarter = width // 4
    freqs = jnp.power(10000.0, -jnp.arange(quarter, dtype=jnp.float32) / quarter)
    row_angle = row_pos[:, None] * freqs[None, :]
    col_angle = col_pos[:, None] * freqs[None, :]
    row_embed = jnp.concatenate([jnp.sin(row_angle), jnp.cos(row_angle)], axis=-1)
    col_embed = jnp.concatenate([jnp.sin(col_angle), jnp.cos(col_angle)], axis=-1)
    row_full = jnp.broadcast_to(
        row_embed[:, None, :], (row_pos.shape[0], col_pos.shape[0], width // 2)
    )
    col_full = jnp.broadcast_to(
        col_embed[None, :, :], (row_pos.shape[0], col_pos.shape[0], width // 2)
    )
    return jnp.concatenate([row_full, col_full], axis=-1).reshape(
        row_pos.shape[0] * col_pos.shape[0], width
    )


SLAB = 80
PART = D // 16
CUT = {ATT_COLS: 384, FFN_COLS: 640}


def line_peers():
    x, z = lax.axis_index("dp_0"), lax.axis_index("dp_1")
    along_x = [({"dp_0": lax.rem(x + d, 4)}, lax.rem(x + d, 4)) for d in (2, 1, 3)]
    along_z = [({"dp_1": lax.rem(z + d, 4)}, lax.rem(z + d, 4)) for d in (2, 1, 3)]
    return along_x, along_z


class RowsIn:
    def __init__(self, left_ref, right_ref, scratch):
        self.left, self.right = left_ref, right_ref
        self.all_left, self.all_right = scratch[:2]
        self.sems = tuple(scratch[2:4])
        self.x, self.z = lax.axis_index("dp_0"), lax.axis_index("dp_1")
        self.along_x, self.along_z = line_peers()

    def peers(self):
        return [peer for peer, _ in self.along_x + self.along_z]

    def start(self):
        x, z = self.x, self.z
        self.first = []
        for k, (peer, _) in enumerate(self.along_z):
            self.first.append(send(self.left, self.all_left.at[x, z], self.sems, k, peer))
        for k, (peer, _) in enumerate(self.along_x):
            self.first.append(send(self.right, self.all_right.at[x, z], self.sems, 3 + k, peer))
        self.all_left[x, z] = self.left[...]
        self.all_right[x, z] = self.right[...]

    def middle(self):
        left, right = self.all_left.at[self.x], self.all_right.at[:, self.z]
        self.second = []
        for copy in self.first[:3]:
            copy.wait_recv()
        for k, (peer, _) in enumerate(self.along_x):
            self.second.append(send(left, left, self.sems, 6 + k, peer))
        for copy in self.first[3:]:
            copy.wait_recv()
        for k, (peer, _) in enumerate(self.along_z):
            self.second.append(send(right, right, self.sems, 9 + k, peer))

    def end(self, one_ref, two_ref):
        for copy in self.second:
            copy.wait_recv()
        width, other = one_ref.shape[1], two_ref.shape[1]
        cut = self.left.shape[1]

        @pl.loop(0, 8)
        def _(pair):
            x, z = pair // 2, 2 * lax.rem(pair, 2)
            both = []
            for k in range(2):
                parts = [self.all_left[x, z + k], self.all_right[x, z + k]]
                both.append(jnp.concatenate(parts, axis=1).astype(F32)[:PART])
            value = jnp.concatenate(both, axis=0).astype(BF16)
            at = pl.ds(pl.multiple_of(pair * 2 * PART, 16), 2 * PART)
            one_ref[at, :] = value[:, :width]
            two_ref[at, :] = value[:, width : width + other]

        for copy in self.first + self.second:
            copy.wait_send()


def rows_in_scratch(cols):
    left = CUT[cols]
    return [
        pltpu.VMEM((4, 4, SLAB, left), BF16),
        pltpu.VMEM((4, 4, SLAB, cols - left), BF16),
    ] + dma_sems(12)


class RowsOut:
    def __init__(self, left_ref, right_ref, scratch):
        self.left, self.right = left_ref, right_ref
        self.got = scratch[0:2]
        self.mine = scratch[2:4]
        self.last = scratch[4:6]
        self.sems = tuple(scratch[6:8])
        self.x, self.z = lax.axis_index("dp_0"), lax.axis_index("dp_1")
        self.along_x, self.along_z = line_peers()

    def peers(self):
        return [peer for peer, _ in self.along_x + self.along_z]

    def start(self):
        self.first = []
        for k, (peer, at) in enumerate(self.along_x):
            part = self.left.at[at]
            self.first.append(send(part, self.got[0].at[k], self.sems, k, peer))
        for k, (peer, at) in enumerate(self.along_z):
            part = self.right.at[:, at]
            self.first.append(send(part, self.got[1].at[k], self.sems, 3 + k, peer))

    def middle(self):
        self.second = []
        for side, peers in ((0, self.along_z), (1, self.along_x)):
            for copy in self.first[3 * side : 3 * side + 3]:
                copy.wait_recv()
            got, mine = self.got[side], self.mine[side]

            @pl.loop(0, 4)
            def _(k):
                own = self.right[k, self.z] if side else self.left[self.x, k]
                across, below, above = (got[source, k].astype(F32) for source in range(3))
                total = (own.astype(F32) + across) + (below + above)
                mine[k] = total.astype(mine.dtype)

            for k, (peer, at) in enumerate(peers):
                part = mine.at[at]
                copy = send(part, self.last[side].at[k], self.sems, 6 + 3 * side + k, peer)
                self.second.append(copy)

    def end(self):
        for copy in self.second:
            copy.wait_recv()
        totals = []
        for side, own in ((0, self.z), (1, self.x)):
            across, below, above = (self.last[side][source].astype(F32) for source in range(3))
            totals.append((self.mine[side][own].astype(F32) + across) + (below + above))
        return totals

    def end_rows(self, out_ref):
        cut = self.left.shape[3]
        left, right = self.end()
        out_ref[:, :cut] = left.astype(BF16)
        out_ref[:, cut:] = right.astype(BF16)
        self.leave()

    def leave(self):
        for copy in self.first + self.second:
            copy.wait_send()


def rows_out_scratch(cols):
    return sum_scratch([(SLAB, CUT[cols]), (SLAB, cols - CUT[cols])], BF16)


def sum_scratch(shapes, dtype):
    return (
        [pltpu.VMEM((3, 4, *shape), dtype) for shape in shapes]
        + [pltpu.VMEM((4, *shape), dtype) for shape in shapes]
        + [pltpu.VMEM((3, *shape), dtype) for shape in shapes]
        + dma_sems(12)
    )


def slab_views(rows_ref, start, cols):
    cut = start + CUT[cols]
    return rows_ref.at[:, start:cut], rows_ref.at[:, cut : start + cols]


def weight_shapes(cols):
    widths = (3 * HW, HW) if cols == ATT_COLS else (FW, FW)
    return tuple(jax.ShapeDtypeStruct((D, w), BF16) for w in widths)


def dot_nn(left, right):
    return lax.dot_general(left, right, (((1,), (0,)), ((), ())), preferred_element_type=F32)


def dot_nt(left, right):
    return lax.dot_general(left, right, (((1,), (1,)), ((), ())), preferred_element_type=F32)


def dot_tn(left, right):
    return lax.dot_general(left, right, (((0,), (0,)), ((), ())), preferred_element_type=F32)


def gelu_both(pre):
    root = 0.7978845608028654
    square = pre * pre
    bent = jnp.tanh(root * pre * (1.0 + 0.044715 * square))
    value = 0.5 * pre * (1.0 + bent)
    slope = 0.5 * (1.0 + bent) + 0.5 * pre * (1.0 - bent * bent) * root * (1.0 + 0.134145 * square)
    return value, slope


def sum_rows(value):
    return jnp.sum(value, axis=0, keepdims=True)


HEAD = D // HEADS
SCALE = HEAD ** (-0.5)


def head_cols(h, start=0):
    return slice(start + h * HEAD, start + (h + 1) * HEAD)


class Refs:
    pass


class Results(dict):
    __getattr__ = dict.__getitem__


def launch(body, cid, near, far, outs, kept, scratch, vmem=60 << 20):
    twins = {name: (value.shape, value.dtype) for name, value in far.items()}
    twins.update(kept)
    groups, tree = jax.tree.flatten(scratch, is_leaf=lambda entry: not isinstance(entry, (dict, list)))

    def kernel(*refs):
        refs = iter(refs)
        r, hbm = Refs(), {}
        for name in near:
            setattr(r, name, next(refs))
        for name in far:
            hbm[name] = next(refs)
        for name in outs:
            setattr(r, name, next(refs))
        for name in kept:
            hbm[name] = next(refs)
        r.moves, r.moving = {}, {}
        for k, name in enumerate(twins):
            ref = next(refs)
            setattr(r, name, ref)
            r.moves[id(ref)] = (hbm[name], k)
        if twins:
            r.move_sems = next(refs)
        for name, entry in jax.tree.unflatten(tree, list(refs)).items():
            setattr(r, name, entry)
        body(r)

    shapes = [jax.ShapeDtypeStruct(*spec) for spec in (*outs.values(), *kept.values())]
    results = pl.pallas_call(
        kernel,
        out_shape=tuple(shapes),
        in_specs=[VMEM] * len(near) + [FAR] * len(far),
        out_specs=(VMEM,) * len(outs) + (FAR,) * len(kept),
        scratch_shapes=[pltpu.VMEM(*spec) for spec in twins.values()]
        + ([pltpu.SemaphoreType.DMA((len(twins),))] if twins else [])
        + groups,
        compiler_params=pltpu.CompilerParams(
            collective_id=cid, has_side_effects=cid is not None, vmem_limit_bytes=vmem
        ),
    )(*near.values(), *far.values())
    return Results(zip(outs, results)), Results(zip(kept, results[len(outs) :]))


def load_into(r, ref, target):
    source, k = r.moves[id(ref)]
    r.moving[id(ref)] = pltpu.make_async_copy(source, target, r.move_sems.at[k])
    r.moving[id(ref)].start()


def load(r, *refs):
    for ref in refs:
        load_into(r, ref, ref)


def save(r, *refs):
    for ref in refs:
        target, k = r.moves[id(ref)]
        r.moving[id(ref)] = pltpu.make_async_copy(ref, target, r.move_sems.at[k])
        r.moving[id(ref)].start()


def settle(r, *refs):
    for key in [id(ref) for ref in refs] or list(r.moving):
        r.moving.pop(key).wait()


def exact(left, right, dims):
    return lax.dot_general(
        left,
        right,
        ((dims[:1], dims[1:]), ((), ())),
        precision=lax.Precision.HIGHEST,
        preferred_element_type=F32,
    )


def choice(place_ref, capacity):
    tokens = place_ref.shape[1]
    slots = lax.broadcasted_iota(jnp.int32, (capacity, tokens), 0)
    return jnp.where(slots == place_ref[...], 1.0, 0.0).astype(F32)


def spread_back(picks, chosen, others):
    used = exact(picks, jnp.ones((picks.shape[0], 128), F32), (0, 0))[:, :1]
    return exact(picks, chosen, (0, 0)) + others * (1.0 - used)


def modulated(x, vec_ref):
    normed, _ = layer_stats(x)
    return (normed * (1.0 + vec_ref[1:2]) + vec_ref[0:1]).astype(BF16)


def full_width(parts, at):
    height = parts[0].shape[0]
    used = at + sum(part.shape[1] for part in parts)
    if at:
        parts = [jnp.zeros((height, at), F32), *parts]
    if used < 128:
        parts = [*parts, jnp.zeros((height, 128 - used), F32)]
    return jnp.concatenate(parts, axis=1)


def to_tokens(pixels_ref, square, tokens_ref, at):
    wide, depth, high = pixels_ref.shape
    square[...] = jnp.zeros_like(square)
    square[: wide * depth, :high] = pixels_ref[...].astype(F32).reshape(wide * depth, high)
    square[...] = jnp.transpose(square[...])
    size = 2 * depth
    lines = [square[pl.ds(line, high // 2, stride=2), :] for line in range(2)]
    for c in range(wide // 2):
        parts = [value[:, c * size : (c + 1) * size] for value in lines]
        tokens_ref[pl.ds(c, high // 2, stride=wide // 2), :] = full_width(parts, at)


def to_pixels(tokens_ref, square, pixels_ref, at):
    wide, depth, high = pixels_ref.shape
    square[...] = jnp.zeros_like(square)
    size = 2 * depth
    columns = [tokens_ref[pl.ds(c, high // 2, stride=wide // 2), :] for c in range(wide // 2)]
    for line in range(2):
        start = at + line * size
        parts = [value[:, start : start + size] for value in columns]
        square[pl.ds(line, high // 2, stride=2), :] = full_width(parts, 0)
    value = jnp.transpose(square[...])[: wide * depth, :high].reshape(wide, depth, high)
    pixels_ref[...] = value.astype(pixels_ref.dtype)


FIRST = 64
PIECE_ROWS = 32


def half_sizes(tokens):
    return FIRST, tokens - FIRST


def half_local(size):
    return [
        pltpu.VMEM((4, size, D), F32),
        pltpu.VMEM((4, size, D), BF16),
        pltpu.VMEM((3, size, D), BF16),
    ]


def half_remote(size):
    return [
        pltpu.VMEM((4, size, D), BF16),
        pltpu.VMEM((2, size, D), BF16),
        pltpu.VMEM((PIECE_ROWS, D), BF16),
        pltpu.VMEM((size - PIECE_ROWS, D), BF16),
    ] + dma_sems(20)


class Half:
    def __init__(self, which, tokens, x_ref, all_ref, local, remote):
        sizes = half_sizes(tokens)
        self.size = sizes[which]
        self.own = slice(which * FIRST, which * FIRST + self.size)
        self.base = which * 8 * FIRST
        self.x, self.all = x_ref, all_ref
        self.kept, self.sib_out, self.out = local
        self.sib_in, self.got, self.far_low, self.far_high = remote[:4]
        self.sems = tuple(remote[4:6])
        self.sib, self.up, self.down, _ = ring_peers()
        self.low, self.high = slice(0, PIECE_ROWS), slice(PIECE_ROWS, self.size)
        self.sent, self.swaps = [], {}

    def peers(self):
        return [self.sib, self.up, self.down]

    def send(self, src, dst, k, peer):
        copy = send(src, dst, self.sems, k, peer)
        self.sent.append(copy)
        return copy

    def pair(self, d):
        start = self.base + 2 * d * self.size
        return slice(start, start + 2 * self.size)

    def slot(self, d, other, rows=None):
        start = self.base + (2 * d + other) * self.size
        rows = slice(0, self.size) if rows is None else rows
        return self.all.at[start + rows.start : start + rows.stop]

    def source(self, rows):
        return self.x.at[self.own.start + rows.start : self.own.start + rows.stop]

    def issue(self):
        low, high = self.low, self.high
        self.a1 = self.send(self.source(low), self.slot(3, 0, low), 0, self.up)
        self.b1 = self.send(self.source(high), self.slot(1, 0, high), 1, self.down)
        whole = slice(0, self.size)
        self.arrive = {0: self.send(self.source(whole), self.slot(0, 1), 4, self.sib)}
        start = self.base
        self.all[start : start + self.size, :] = self.x[self.own, :]

    def issue_rest(self):
        low, high = self.low, self.high
        self.a2 = self.send(self.source(high), self.slot(3, 0, high), 2, self.up)
        self.b2 = self.send(self.source(low), self.slot(1, 0, low), 3, self.down)

    def forward(self):
        low, high = self.low, self.high
        self.a1.wait_recv()
        self.f1 = self.send(self.slot(3, 0, low), self.slot(2, 0, low), 5, self.up)
        self.b1.wait_recv()
        self.f2 = self.send(self.slot(1, 0, high), self.slot(2, 0, high), 6, self.down)

    def near_arrive(self):
        self.a2.wait_recv()
        self.arrive[3] = self.send(self.slot(3, 0), self.slot(3, 1), 7, self.sib)
        self.b2.wait_recv()
        self.arrive[1] = self.send(self.slot(1, 0), self.slot(1, 1), 8, self.sib)

    def far_arrive(self):
        self.f1.wait_recv()
        self.f2.wait_recv()
        self.arrive[2] = self.send(self.slot(2, 0), self.slot(2, 1), 9, self.sib)

    def ready(self, d):
        self.arrive[d].wait_recv()

    def put(self, d, value):
        self.kept[d] = value[: self.size]
        self.sib_out[d] = value[self.size :].astype(BF16)
        self.swaps[d] = self.send(self.sib_out.at[d], self.sib_in.at[d], 10 + d, self.sib)

    def chip_sum(self, d):
        self.swaps[d].wait_recv()
        return self.kept[d] + self.sib_in[d].astype(F32)

    def near(self):
        low, high = self.low, self.high
        total = self.chip_sum(1)
        self.kept[1] = total
        self.out[0, high] = total[high].astype(BF16)
        self.n1 = self.send(self.out.at[0, high], self.got.at[0, high], 14, self.up)
        total = self.chip_sum(3)
        self.kept[3] = total
        self.out[1, low] = total[low].astype(BF16)
        self.n2 = self.send(self.out.at[1, low], self.got.at[1, low], 15, self.down)

    def far(self):
        self.out[2] = self.chip_sum(2).astype(BF16)
        self.low_sent = self.send(self.out.at[2, self.low], self.far_low, 16, self.up)
        self.high_sent = self.send(self.out.at[2, self.high], self.far_high, 17, self.down)

    def relay(self):
        low, high = self.low, self.high
        self.low_sent.wait_recv()
        self.out[0, low] = (self.kept[1, low] + self.far_low[...].astype(F32)).astype(BF16)
        self.r1 = self.send(self.out.at[0, low], self.got.at[0, low], 18, self.up)
        self.high_sent.wait_recv()
        self.out[1, high] = (self.kept[3, high] + self.far_high[...].astype(F32)).astype(BF16)
        self.r2 = self.send(self.out.at[1, high], self.got.at[1, high], 19, self.down)

    def total(self):
        value = self.chip_sum(0)
        for copy in (self.n1, self.n2, self.r1, self.r2):
            copy.wait_recv()
        value = value + self.got[0].astype(F32) + self.got[1].astype(F32)
        for copy in self.sent:
            copy.wait_send()
        return value


def gather_both(a, b, prepare, visit, between):
    prepare()
    a.ready(0)
    visit(a, 0)
    a.forward()
    b.issue_rest()
    b.ready(0)
    visit(b, 0)
    a.near_arrive()
    b.forward()
    between()
    a.ready(3)
    visit(a, 3)
    a.ready(1)
    visit(a, 1)
    a.far_arrive()
    b.near_arrive()
    b.ready(3)
    visit(b, 3)
    a.ready(2)
    visit(a, 2)
    b.ready(1)
    visit(b, 1)
    b.far_arrive()
    b.ready(2)
    visit(b, 2)


def gather_and_sum(a, b, prepare, visit, between):
    prepare()
    a.ready(0)
    visit(a, 0)
    a.forward()
    b.issue_rest()
    b.ready(0)
    visit(b, 0)
    a.near_arrive()
    b.forward()
    between()
    a.ready(3)
    visit(a, 3)
    a.ready(1)
    visit(a, 1)
    a.far_arrive()
    b.near_arrive()
    a.near()
    b.ready(3)
    visit(b, 3)
    a.ready(2)
    visit(a, 2)
    b.ready(1)
    visit(b, 1)
    a.far()
    b.far_arrive()
    b.near()
    b.ready(2)
    visit(b, 2)
    a.relay()
    b.far()


def sum_both(a, b, make):
    make(a, 2)
    make(b, 2)
    a.far()
    make(a, 1)
    b.far()
    make(a, 3)
    make(a, 0)
    a.near()
    make(b, 1)
    a.relay()
    make(b, 3)
    make(b, 0)
    b.near()
    b.relay()


def nothing():
    pass


def halves(r, tokens, x_ref, all_ref, remote):
    return [Half(k, tokens, x_ref, all_ref, r.local[k], remote[k]) for k in range(2)]


UNPATCH, EMBED, BLOCKS, EMBED_BIAS = 0, 32, 48, 64
WHOLE = 16384


def own_targets():
    group = own_group()
    return group * (D // 16), group * (D // 8)


def bias_table():
    table = np.zeros((8, 1024), np.int32)
    for col in range(3 * HW):
        part, e = divmod(col, HW)
        table[0, col] = (e // 18 + (64 if part == 2 else 0)) * 9 + e % 9 if part != 1 else -(1 << 20)
        table[1, col] = e % 18 // 9
    for e in range(FW):
        table[0, 3 * HW + e] = e // 36 * 9 + e % 9
        table[1, 3 * HW + e] = e % 36 // 9
    return table


def bias_picks(table_ref, cols, shift):
    rows = lax.broadcasted_iota(jnp.int32, (D, cols.stop - cols.start), 0)
    return jnp.where(rows == table_ref[0:1, cols] + shift, 1.0, 0.0).astype(F32)


ATT_BIAS = slice(0, 3 * HW)
FFN_BIAS = slice(3 * HW, 3 * HW + FW)


def mod_places(index):
    e = lax.broadcasted_iota(jnp.int32, (1, 128), 1)
    at = jnp.where(e < 108, 6 * D - 54 + index * 54 + e, 12 * D - 108 + index * 18 + e)
    at = jnp.where(e < 54, index * 54 + e, at)
    at = jnp.where(e < 126, at, -1)
    lines = lax.broadcasted_iota(jnp.int32, (128, 128), 0)
    return lines == lax.shift_right_arithmetic(at, 7), lines == jnp.bitwise_and(at, 127)


def whole_index():
    x, z = lax.axis_index("dp_0"), lax.axis_index("dp_1")
    return (x * 4 + z) * 8 + own_group()


def route(r):
    token = lax.broadcasted_iota(jnp.int32, (128, 512), 0)
    row = lax.axis_index("tx") * 16 + token // 8
    col = lax.axis_index("ty") * 8 + lax.rem(token, 8)
    hits = jnp.where(row * 32 + col == r.ids[...], 1.0, 0.0).astype(BF16)
    flags = dot_nt(jnp.ones((8, 512), BF16), hits)
    lines = lax.broadcasted_iota(jnp.int32, (128, 128), 0)
    lanes = lax.broadcasted_iota(jnp.int32, (128, 128), 1)
    before = dot_nn(flags.astype(BF16), jnp.where(lines <= lanes, 1.0, 0.0).astype(BF16))
    r.place[...] = jnp.where(flags > 0, before - 1.0, -1.0)[0:1].astype(jnp.int32)
    row, col = r.ids[...] // 512, lax.rem(r.ids[...], 32) // 8
    chip = lax.rem(col - lax.axis_index("ty") + 4, 4)
    other = jnp.where(row == lax.axis_index("tx"), 0, 1)
    tile = chip * 2 + other
    slot = lax.broadcasted_iota(jnp.int32, r.mask.shape, 1)
    used = slot < 0
    for k in range(8):
        count = jnp.sum(jnp.where(tile == k, 1.0, 0.0), axis=1, keepdims=True).astype(jnp.int32)
        for which, size in enumerate(half_sizes(r.mask.shape[1] // 8)):
            at = slot - which * 8 * FIRST - k * size
            used = used | ((at >= 0) & (at < size) & (at + which * FIRST < count))
    r.mask[...] = jnp.where(used, 0.0, -1e30)


def open_body(r):
    group = group_peers()
    sib, up, down, far = ring_peers()
    fetch = RowsIn(*slab_views(r.rows, 0, ATT_COLS), r.fetch)
    mods = RowsOut(r.m_mine.at[:, :, 0:64], r.m_mine.at[:, :, 64:128], r.mods)
    peers = [peer for peer, _ in group] + fetch.peers()
    greet(peers)
    load(r, r.attn_w, r.merge_w, r.expand_w, r.reduce_w, r.unpicks)
    load(r, r.mod_w, r.final_w, r.picks, r.table)
    r.pack[...] = jnp.zeros_like(r.pack)
    settle(r, r.attn_w, r.merge_w, r.expand_w, r.reduce_w)
    attn = [[r.attn_w[:, j, b, :] for j in range(3)] for b in range(2)]
    merge = [r.merge_w[:, b, :] for b in range(2)]
    expand = [r.expand_w[:, b, :] for b in range(2)]
    reduce = [r.reduce_w[:, b, :] for b in range(2)]
    spare = jnp.zeros((9, ATT_COLS - 4 * HW), BF16)
    for p in range(8):
        narrow, wide = slice(p * HW, (p + 1) * HW), slice(p * FW, (p + 1) * FW)
        parts = []
        for b in range(2):
            parts += [attn[b][j][:, narrow] for j in range(3)] + [merge[b][:, narrow], spare]
        for b in range(2):
            parts += [expand[b][:, wide], reduce[b][:, wide]]
        r.pack[p * 16 : p * 16 + 9, :] = jnp.concatenate(parts, axis=1)
    settle(r, r.unpicks)
    packed = jnp.zeros((8 * 64, PIECE), F32)
    for k in range(PIECES):
        packed = packed + dot_tn(r.unpicks[k], r.pack[:, k * PIECE : (k + 1) * PIECE])
    r.w_mine[...] = packed.astype(BF16).reshape(8, 64, PIECE)
    r.lines[...] = jnp.zeros_like(r.lines)
    r.lines[EMBED : EMBED + 16, 0:9] = r.embed_w[...].astype(F32)
    for b in range(2):
        at = BLOCKS + 8 * b
        for j in range(2):
            r.lines[at + j : at + j + 1, 0:9] = r.attn_b[b : b + 1, 9 * j : 9 * j + 9].astype(F32)
        for j in range(4):
            value = r.expand_b[b : b + 1, 9 * j : 9 * j + 9].astype(F32)
            r.lines[at + 2 + j : at + 3 + j, 0:9] = value
        r.lines[at + 6 : at + 7, 0:9] = r.merge_b[b : b + 1].astype(F32)
        r.lines[at + 7 : at + 8, 0:9] = r.reduce_b[b : b + 1].astype(F32)
    r.lines[EMBED_BIAS : EMBED_BIAS + 1, 0:9] = r.embed_b[...].astype(F32)
    r.block[...] = jnp.transpose(r.lines[...])[0:16]
    r.block[0:9, UNPATCH : UNPATCH + 32] = r.unpatch_w[...].astype(F32)
    me, x, z = own_group(), lax.axis_index("dp_0"), lax.axis_index("dp_1")
    r.small[x, z, me] = r.block[...].astype(BF16)
    met(peers)
    sems = (r.ss, r.rs)
    weights = [
        send(r.w_mine.at[at], r.w_got.at[me], sems, k, p) for k, (p, at) in enumerate(group)
    ]
    small = r.small.at[x, z, me]
    first = [send(small, small, sems, 7 + k, p) for k, (p, _) in enumerate(fetch.along_z)]
    r.w_got[me] = r.w_mine[me]

    condition = r.condition[...].astype(F32)
    cond16 = (condition / (1.0 + jnp.exp(-condition))).astype(BF16)
    on_line, on_lane = mod_places(whole_index())
    r.places[...] = jnp.zeros_like(r.places)
    r.places[0:1, 0:54] = r.mod_b[0:1].astype(F32)
    r.places[0:1, 54:108] = r.mod_b[1:2].astype(F32)
    r.places[0:1, 108:126] = r.final_b[...].astype(F32)
    left = jnp.where(on_line, r.places[0:1], 0.0).astype(BF16)
    right = jnp.where(on_lane, 1.0, 0.0).astype(BF16)
    r.placed_bias[...] = dot_nt(left, right)
    r.m_mine[:, :, 126:128] = jnp.zeros((4, 4, 2, 128), F32)
    settle(r, r.mod_w, r.final_w)
    for b in range(3):
        weight = r.mod_w[:, b, :] if b < 2 else r.final_w[...]
        part = dot_nn(cond16, weight)
        for k in range(part.shape[1] // 128):
            line = 54 * b + k
            value = part[:, k * 128 : (k + 1) * 128] + r.placed_bias[line : line + 1]
            r.m_mine[:, :, line, :] = value.reshape(4, 4, 128)
    mods.start()
    for copy in first:
        copy.wait_recv()
    small = r.small.at[x, :, me]
    second = [send(small, small, sems, 10 + k, p) for k, (p, _) in enumerate(fetch.along_x)]
    for copy in weights:
        copy.wait_recv()
    settle(r, r.picks, r.table)
    received = r.w_got[...].reshape(8 * 64, PIECE)
    for k in range(PIECES):
        r.rows[:, k * PIECE : (k + 1) * PIECE] = dot_nn(r.picks[k], received).astype(BF16)
    fetch.start()
    save(r, r.rows)
    for copy in second:
        copy.wait_recv()
    small = r.small.at[:, :, me]
    third = [send(small, small, sems, 13 + k, p) for k, p in enumerate((up, down, far, sib))]
    mods.middle()
    fetch.middle()
    route(r)
    r.m_sum[0:64], r.m_sum[64:128] = mods.end()

    def chunk(ref, index):
        return ref.at[pl.ds(pl.multiple_of(index * 16, 16), 16)]

    m_first = [
        send(chunk(r.m_sum, at), r.m_got.at[me], sems, 20 + k, p) for k, (p, at) in enumerate(group)
    ]
    mine = pl.ds(pl.multiple_of(me * 16, 16), 16)
    r.m_got[me] = r.m_sum[mine, :]
    for copy in m_first:
        copy.wait_recv()
    total = r.m_got[0]
    for k in range(1, 8):
        total = total + r.m_got[k]
    r.m_all[mine, :] = total
    part = chunk(r.m_all, me)
    m_second = [send(part, part, sems, 27 + k, p) for k, (p, _) in enumerate(group)]
    c, y = lax.axis_index("tx"), lax.axis_index("ty")
    fourth = []
    for k, d in enumerate((3, 1, 2)):
        third[k].wait_recv()
        small = r.small.at[:, :, c * 4 + lax.rem(y + d, 4)]
        fourth.append(send(small, small, sems, 17 + k, sib))
    for copy in fourth + third[3:]:
        copy.wait_recv()

    @pl.loop(0, 16)
    def _(k):
        got = r.small[k // 4, lax.rem(k, 4)].reshape(128, 128)
        at = pl.ds(pl.multiple_of(k * PART, 8), PART)
        r.feat32[at, :] = dot_nn(r.pick_small[...], got)[:PART]

    r.feat[...] = r.feat32[...].astype(BF16)
    save(r, r.feat)
    for k in range(9):
        cols = slice(k * 128, (k + 1) * 128)
        r.turned[:, cols] = jnp.transpose(r.feat32[cols, :])
    attn_at, ffn_at = own_targets()
    picks = bias_picks(r.table, ATT_BIAS, attn_at).astype(BF16)
    blocks = r.turned[BLOCKS : BLOCKS + 16].astype(BF16)
    narrow = dot_nn(blocks, picks)
    wide = dot_nn(blocks, bias_picks(r.table, FFN_BIAS, ffn_at).astype(BF16))
    for b, (one, two) in enumerate(((r.bias_one_0, r.bias_two_0), (r.bias_one_1, r.bias_two_1))):
        at, which = 8 * b, r.table[1:2, ATT_BIAS]
        one[...] = jnp.where(which == 0, narrow[at : at + 1], narrow[at + 1 : at + 2])
        value, which = wide[at + 2 : at + 3], r.table[1:2, FFN_BIAS]
        for j in range(1, 4):
            value = jnp.where(which == j, wide[at + 2 + j : at + 3 + j], value)
        two[...] = value
    for copy in m_second:
        copy.wait_recv()

    def mod_line(k):
        return jnp.concatenate([r.m_all[9 * k + i : 9 * k + i + 1] for i in range(9)], axis=1)

    vecs = (r.vec_one_0, r.vec_two_0, r.vec_one_1, r.vec_two_1)
    for k, ref in enumerate(vecs):
        for i in range(3):
            ref[i : i + 1] = mod_line(3 * k + i)
        at = BLOCKS + 8 * (k // 2) + 6 + k % 2
        ref[3:4] = r.turned[at : at + 1]
        ref[4:5] = r.turned[EMBED_BIAS : EMBED_BIAS + 1]
        ref[5:8] = jnp.zeros((3, D), F32)
    r.head_vec[0:1] = mod_line(12)
    r.head_vec[1:2] = mod_line(13)
    fetch.end(r.wqkv, r.wm)
    save(r, r.wqkv, r.wm)
    for copy in weights + first + second + third + fourth + m_first + m_second:
        copy.wait_send()
    mods.leave()
    settle(r)


def picking(pieces, height):
    picks = np.zeros((pieces, SLAB, 8 * height), np.float32)
    for k in range(pieces):
        for row in range(72):
            picks[k, row, row // 9 * height + 9 * k + row % 9] = 1.0
    return picks


def picking_small():
    picks = np.zeros((SLAB, 128), np.float32)
    for row in range(72):
        picks[row, row // 9 * 16 + row % 9] = 1.0
    return picks


def open_up(near, far):
    near = dict(near, pick_small=jnp.asarray(picking_small(), BF16))
    far = dict(
        far,
        unpicks=jnp.asarray(unpicking(PIECES, 64), BF16),
        picks=jnp.asarray(picking(PIECES, 64), BF16),
        table=jnp.asarray(bias_table()),
    )
    vec = ((8, D), F32)
    outs = dict(
        vec_one_0=vec,
        vec_two_0=vec,
        vec_one_1=vec,
        vec_two_1=vec,
        head_vec=((2, D), F32),
        place=((1, 128), jnp.int32),
        mask=((1, 8 * 112), F32),
        bias_one_0=((1, 3 * HW), F32),
        bias_one_1=((1, 3 * HW), F32),
        bias_two_0=((1, FW), F32),
        bias_two_1=((1, FW), F32),
    )
    kept = dict(
        rows=((SLAB, ALL_COLS), BF16),
        wqkv=((D, 3 * HW), BF16),
        wm=((D, HW), BF16),
        feat=((D, 128), BF16),
    )
    scratch = dict(
        pack=pltpu.VMEM((128, ALL_COLS), BF16),
        w_mine=pltpu.VMEM((8, 64, PIECE), BF16),
        w_got=pltpu.VMEM((8, 64, PIECE), BF16),
        lines=pltpu.VMEM((128, 128), F32),
        block=pltpu.VMEM((16, 128), F32),
        small=pltpu.VMEM((4, 4, 8, 16, 128), BF16),
        places=pltpu.VMEM((8, 128), F32),
        placed_bias=pltpu.VMEM((128, 128), F32),
        m_mine=pltpu.VMEM((4, 4, 128, 128), F32),
        m_sum=pltpu.VMEM((128, 128), F32),
        m_got=pltpu.VMEM((8, 16, 128), F32),
        m_all=pltpu.VMEM((128, 128), F32),
        feat32=pltpu.VMEM((D, 128), F32),
        turned=pltpu.VMEM((128, D), F32),
        ss=dma_sems(34)[0],
        rs=dma_sems(34)[1],
        fetch=rows_in_scratch(ATT_COLS),
        mods=sum_scratch([(64, 128), (64, 128)], F32),
    )
    near_outs, far_outs = launch(open_body, 1, near, far, outs, kept, scratch)
    return Results(near_outs, **far_outs)


EARLY = ATT_COLS + 2 * FFN_COLS
EARLY_PIECES = -(-EARLY // PIECE)
LATE_PIECE = 128
LATE_PIECES = ATT_COLS // LATE_PIECE
LATE_ROWS = 48


def packed_rows(picks_ref, parts, piece):
    pieces, _, height = picks_ref.shape
    columns = jnp.concatenate(parts, axis=1)
    spare = pieces * piece - columns.shape[1]
    if spare:
        columns = jnp.concatenate([columns, jnp.zeros((SLAB, spare), BF16)], axis=1)
    total = jnp.zeros((height, piece), F32)
    for k in range(pieces):
        total = total + dot_tn(picks_ref[k], columns[:, k * piece : (k + 1) * piece])
    return total.astype(BF16).reshape(8, height // 8, piece)


def bias_lines(table_ref, cols, shift, biases, count):
    which = table_ref[1:2, cols]
    parts = []
    for bias in biases:
        rest = jnp.concatenate(
            [jnp.where(which == j, bias, 0.0) for j in range(count)]
            + [jnp.zeros((8 - count, bias.shape[1]), F32)],
            axis=0,
        )
        for _ in range(3):
            part = rest.astype(BF16).astype(F32)
            parts.append(part)
            rest = rest - part
    parts = jnp.concatenate(parts, axis=0).astype(BF16)
    found = dot_nt(parts, bias_picks(table_ref, cols, shift).astype(BF16))
    sums = [found[24 * k : 24 * k + 8] for k in range(2)]
    return [
        (sums[k] + found[24 * k + 8 : 24 * k + 16] + found[24 * k + 16 : 24 * k + 24])[:count]
        for k in range(2)
    ]


def finish_body(r):
    group = group_peers()
    sib, up, down, far = ring_peers()
    rows = RowsOut(r.left, r.right, r.rows_sums)
    small = RowsOut(r.small.at[:, :, 0:40], r.small.at[:, :, 40:80], r.small_sums)
    peers = [peer for peer, _ in group] + rows.peers()
    greet(peers)
    me, x, z = own_group(), lax.axis_index("dp_0"), lax.axis_index("dp_1")
    sems = (r.ss, r.rs)
    load(r, r.left, r.right, r.picks, r.late_picks, r.attn_rows, r.ffn_rows_0, r.ffn_rows_1)
    load(r, r.unpatch_rows, r.embed_rows, r.table)
    r.m_mine[...] = jnp.zeros_like(r.m_mine)
    vecs = (r.vecs_one_0, r.vecs_two_0, r.vecs_one_1, r.vecs_two_1, r.head_vecs)
    for k, ref in enumerate(vecs):
        for i in range(3 if k < 4 else 2):
            for j in range(9):
                line = 27 * k + 9 * i + j
                r.m_mine[line // 16, line % 16 : line % 16 + 1] = ref[
                    i : i + 1, j * 128 : (j + 1) * 128
                ]
    met(peers)
    settle(r, r.left, r.right)
    rows.start()
    m_first = [send(r.m_mine.at[at], r.m_got.at[me], sems, k, p) for k, (p, at) in enumerate(group)]
    r.m_got[me] = r.m_mine[me]
    settle(r)
    attn_at, ffn_at = own_targets()
    biases = (r.bias_one_0[...], r.bias_one_1[...])
    narrow = bias_lines(r.table, ATT_BIAS, attn_at, biases, 2)
    biases = (r.bias_two_0[...], r.bias_two_1[...])
    wide = bias_lines(r.table, FFN_BIAS, ffn_at, biases, 4)
    vecs = ((r.vecs_one_0, r.vecs_two_0), (r.vecs_one_1, r.vecs_two_1))
    for k in range(2):
        r.bias_rows[k, 0:2] = narrow[k]
        r.bias_rows[k, 2:6] = wide[k]
        r.bias_rows[k, 6:7] = vecs[k][0][3:4]
        r.bias_rows[k, 7:8] = vecs[k][1][3:4]
    r.turned[...] = jnp.zeros_like(r.turned)
    for k in range(9):
        cols = slice(k * 128, (k + 1) * 128)
        r.lines[...] = jnp.zeros_like(r.lines)
        r.lines[0:32] = r.unpatch_rows[:, cols]
        r.lines[32:48] = r.embed_rows[0:16, cols]
        r.lines[48:56] = r.bias_rows[0, :, cols]
        r.lines[56:64] = r.bias_rows[1, :, cols]
        r.lines[64:72] = r.embed_rows[16:24, cols]
        r.turned[cols, :] = jnp.transpose(r.lines[...])
    for k in range(16):
        r.small[k // 4, k % 4, 0:72] = r.turned[k * PART : (k + 1) * PART, :]
        r.small[k // 4, k % 4, 72:80] = r.unpatch_bias[...]
    small.start()
    r.early[...] = packed_rows(
        r.picks, [r.attn_rows[...], r.ffn_rows_0[...], r.ffn_rows_1[...]], PIECE
    )
    sent = [
        send(r.early.at[at], r.early_out.at[me], sems, 7 + k, p) for k, (p, at) in enumerate(group)
    ]
    r.early_out[me] = r.early[me]
    for copy in m_first:
        copy.wait_recv()
    total = r.m_got[0]
    for k in range(1, 8):
        total = total + r.m_got[k]
    r.m_out[me, x, z] = total.astype(BF16)
    part = r.m_out.at[me, x, z]
    m_second = [send(part, part, sems, 14 + k, p) for k, (p, _) in enumerate(rows.along_z)]
    rows.middle()
    small.middle()
    for copy in m_second:
        copy.wait_recv()
    part = r.m_out.at[me, x]
    m_third = [send(part, part, sems, 17 + k, p) for k, (p, _) in enumerate(rows.along_x)]
    r.s_total[0:40], r.s_total[40:80] = small.end()
    for g in range(8):
        r.s_mine[g, 0:9] = r.s_total[9 * g : 9 * g + 9]
        r.s_mine[g, 9:16] = r.s_total[72:79]
    s_last = [
        send(r.s_mine.at[at], r.s_two.at[me], sems, 20 + k, p) for k, (p, at) in enumerate(group)
    ]
    r.s_two[me] = r.s_mine[me]
    for copy in m_third:
        copy.wait_recv()
    part = r.m_out.at[me]
    m_fourth = [send(part, part, sems, 27 + k, p) for k, p in enumerate((up, down, far, sib))]
    rows.end_rows(r.late_rows)
    r.late[...] = packed_rows(r.late_picks, [r.late_rows[...]], LATE_PIECE)
    later = [
        send(r.late.at[at], r.late_out.at[me], sems, 34 + k, p) for k, (p, at) in enumerate(group)
    ]
    r.late_out[me] = r.late[me]
    c, y = lax.axis_index("tx"), lax.axis_index("ty")
    m_fifth = []
    for k, d in enumerate((3, 1, 2)):
        m_fourth[k].wait_recv()
        part = r.m_out.at[c * 4 + lax.rem(y + d, 4)]
        m_fifth.append(send(part, part, sems, 31 + k, sib))
    for copy in s_last:
        copy.wait_recv()
    total = r.s_two[0]
    for k in range(1, 8):
        total = total + r.s_two[k]
    r.s_out[...] = total
    for copy in sent + m_fourth[3:] + m_fifth + later:
        copy.wait_recv()
    small.leave()
    for copy in m_first + sent + m_second + m_third + s_last + m_fourth + m_fifth + later:
        copy.wait_send()


def finish(near, far):
    far = dict(
        far,
        picks=jnp.asarray(picking(EARLY_PIECES, 64), BF16),
        late_picks=jnp.asarray(picking(LATE_PIECES, LATE_ROWS), BF16),
        table=jnp.asarray(bias_table()),
    )
    outs = dict(
        early_out=((8, 64, PIECE), BF16),
        late_out=((8, LATE_ROWS, LATE_PIECE), BF16),
        m_out=((8, 4, 4, 16, 128), BF16),
        s_out=((16, 128), F32),
    )
    scratch = dict(
        early=pltpu.VMEM((8, 64, PIECE), BF16),
        late=pltpu.VMEM((8, LATE_ROWS, LATE_PIECE), BF16),
        m_mine=pltpu.VMEM((8, 16, 128), F32),
        m_got=pltpu.VMEM((8, 16, 128), F32),
        lines=pltpu.VMEM((128, 128), F32),
        bias_rows=pltpu.VMEM((2, 8, D), F32),
        turned=pltpu.VMEM((D, 128), F32),
        small=pltpu.VMEM((4, 4, 80, 128), F32),
        s_total=pltpu.VMEM((80, 128), F32),
        s_mine=pltpu.VMEM((8, 16, 128), F32),
        s_two=pltpu.VMEM((8, 16, 128), F32),
        late_rows=pltpu.VMEM((SLAB, ATT_COLS), BF16),
        ss=dma_sems(41)[0],
        rs=dma_sems(41)[1],
        rows_sums=rows_out_scratch(ATT_COLS),
        small_sums=sum_scratch([(40, 128), (40, 128)], F32),
    )
    return launch(finish_body, 2, near, far, outs, {}, scratch)[0]


def unpicking(pieces, height):
    picks = np.zeros((pieces, 128, 8 * height), np.float32)
    for k in range(pieces):
        for group in range(8):
            for row in range(9):
                picks[k, group * 16 + row, group * height + 9 * k + row] = 1.0
    return picks


def close_body(r):
    load(r, r.early_in, r.early_picks, r.late_in, r.late_picks, r.m_in, r.mod_w, r.final_w)
    settle(r, r.early_in, r.late_in, r.early_picks, r.late_picks)
    received = r.early_in[...].reshape(8 * 64, PIECE)
    for k in range(EARLY_PIECES):
        r.early[:, k * PIECE : (k + 1) * PIECE] = dot_nn(r.early_picks[k], received)
    received = r.late_in[...].reshape(8 * LATE_ROWS, LATE_PIECE)
    for k in range(LATE_PIECES):
        r.late[:, k * LATE_PIECE : (k + 1) * LATE_PIECE] = dot_nn(r.late_picks[k], received)

    def whole(source, start, width):
        parts = [source[g * 16 : g * 16 + 16, start : start + width] for g in range(8)]
        return jnp.concatenate(parts, axis=1)[:9]

    for b, (source, start) in enumerate(((r.late, 0), (r.early, 0))):
        for j in range(3):
            r.attn[:, j, b, :] = whole(source, start + j * HW, HW)
        r.merge[:, b, :] = whole(source, start + 3 * HW, HW)
    for b, start in enumerate((ATT_COLS, ATT_COLS + FFN_COLS)):
        r.expand[:, b, :] = whole(r.early, start, FW)
        r.reduce[:, b, :] = whole(r.early, start + FW, FW)
    save(r, r.attn, r.merge, r.expand, r.reduce)
    settle(r, r.m_in, r.mod_w, r.final_w)
    for k in range(128):
        value = r.m_in[k // 16, :, :, k % 16, :]
        r.grads[:, k * 128 : (k + 1) * 128] = value.reshape(16, 128)
        r.sums[k : k + 1] = sum_rows(value.reshape(16, 128).astype(F32))
    condition = r.condition[...].astype(F32)
    gate = 1.0 / (1.0 + jnp.exp(-condition))
    cond16 = (condition / (1.0 + jnp.exp(-condition))).astype(BF16)
    terms = jnp.zeros((16, 9), F32)
    for b in range(3):
        grads = r.grads[:, 6 * b * D : min(6 * b + 6, 14) * D]
        weights = r.mod_w[:, b, :] if b < 2 else r.final_w[...]
        product = dot_tn(cond16, grads)
        if b < 2:
            r.mod_grad[:, b, :] = product
        else:
            r.final_grad[...] = product
        terms = terms + dot_nt(grads, weights)
    save(r, r.mod_grad, r.final_grad)
    r.predicted[...] = r.predicted_in[...]
    r.latent[...] = r.latent_in[...]
    r.condition_grad[...] = terms * (gate * (1.0 + condition * (1.0 - gate)))
    on_line, on_lane = mod_places(whole_index())
    found = exact(r.sums[...], jnp.where(on_lane, 1.0, 0.0).astype(F32), (1, 0))
    found = sum_rows(jnp.where(on_line, found, 0.0))
    r.mod_b[0:1] = found[:, 0:54]
    r.mod_b[1:2] = found[:, 54:108]
    r.final_b[...] = found[:, 108:126]
    r.square[...] = jnp.zeros_like(r.square)
    r.square[0:16] = r.s_in[...]
    turned = jnp.transpose(r.square[...])
    r.unpatch_w[...] = r.s_in[0:9, 0:32]
    r.unpatch_b[...] = r.s_in[9:10, 0:32]
    r.embed_w[...] = turned[32:48, 0:9]
    r.embed_b[...] = turned[64:65, 0:9]
    for b in range(2):
        at = BLOCKS + 8 * b
        for j in range(2):
            r.attn_b[b : b + 1, 9 * j : 9 * j + 9] = turned[at + j : at + j + 1, 0:9]
        for j in range(4):
            r.expand_b[b : b + 1, 9 * j : 9 * j + 9] = turned[at + 2 + j : at + 3 + j, 0:9]
        r.merge_b[b : b + 1] = turned[at + 6 : at + 7, 0:9]
        r.reduce_b[b : b + 1] = turned[at + 7 : at + 8, 0:9]
    settle(r)


def close(near, far):
    far = dict(
        far,
        early_picks=jnp.asarray(unpicking(EARLY_PIECES, 64), BF16),
        late_picks=jnp.asarray(unpicking(LATE_PIECES, LATE_ROWS), BF16),
    )
    kept = dict(
        attn=((9, 3, 2, D), F32),
        merge=((9, 2, D), F32),
        expand=((9, 2, FF), F32),
        reduce=((9, 2, FF), F32),
        mod_grad=((9, 2, 6 * D), F32),
        final_grad=((9, 2 * D), F32),
    )
    outs = dict(
        predicted=((16, 8, 32), BF16),
        latent=((16, 4, 32), F32),
        condition_grad=((16, 9), F32),
        mod_b=((2, 54), F32),
        final_b=((1, 18), F32),
        unpatch_w=((9, 32), F32),
        unpatch_b=((1, 32), F32),
        embed_w=((16, 9), F32),
        embed_b=((1, 9), F32),
        attn_b=((2, 18), F32),
        expand_b=((2, 36), F32),
        merge_b=((2, 9), F32),
        reduce_b=((2, 9), F32),
    )
    scratch = dict(
        early=pltpu.VMEM((128, EARLY_PIECES * PIECE), F32),
        late=pltpu.VMEM((128, ATT_COLS), F32),
        grads=pltpu.VMEM((16, WHOLE), BF16),
        sums=pltpu.VMEM((128, 128), F32),
        square=pltpu.VMEM((128, 128), F32),
    )
    near_outs, far_outs = launch(close_body, None, near, far, outs, kept, scratch)
    return Results(near_outs, **far_outs)


def forward_body(r, tokens, start, last):
    a, b = halves(r, tokens, r.x16, r.in_all, r.remote_one)
    fetch = RowsIn(*slab_views(r.rows, start, FFN_COLS), r.fetch_one)
    peers = a.peers() + fetch.peers()
    greet(peers)
    if last:
        load(r, r.first, r.wqkv, r.rows, r.wm)
        settle(r, r.first)
        r.x[...] = exact(choice(r.place, tokens), r.first[...], (1, 0))
    else:
        load(r, r.feat, r.placed, r.wqkv, r.rows, r.wm)
        settle(r, r.feat, r.placed)
        r.token_cols[...] = jnp.zeros_like(r.token_cols)
        to_tokens(r.pixels, r.square, r.token_cols, EMBED)
        r.patches[...] = r.token_cols[...].astype(BF16)
        r.x[...] = dot_nt(r.patches[...], r.feat[...]) + r.vec_one[4:5] + r.placed[...]
    r.x16[...] = modulated(r.x[...], r.vec_one)
    met(peers)
    a.issue()
    a.issue_rest()
    b.issue()
    save(r, r.x)
    if not last:
        save(r, r.patches)

    def prepare():
        settle(r, r.wqkv, r.rows)
        fetch.start()

    def visit(half, d):
        rows = half.pair(d)
        joined = (dot_nn(r.in_all[rows, :], r.wqkv[...]) + r.bias_one[...]).astype(BF16)
        for h in range(2):
            r.q[h, rows, :] = joined[:, head_cols(h)]
            r.k[h, rows, :] = joined[:, head_cols(h, HW)]
            r.v[h, rows, :] = joined[:, head_cols(h, 2 * HW)]

    def attend(half, d):
        rows = half.pair(d)
        parts = []
        for h in range(2):
            scores = dot_nt(r.q[h, rows, :], r.k[h]) * SCALE
            if last:
                scores = scores + r.mask[...]
            highest = jnp.max(scores, axis=-1, keepdims=True)
            shifted = jnp.exp(scores - highest)
            summed = jnp.sum(shifted, axis=-1, keepdims=True)
            probs = (shifted * (1.0 / summed)).astype(BF16)
            r.lse[rows, h : h + 1] = highest + jnp.log(summed)
            parts.append(dot_nn(probs, r.v[h]).astype(BF16))
        attended = jnp.concatenate(parts, axis=1)
        r.att[rows, :] = attended
        half.put(d, dot_nt(attended, r.wm[...]))

    gather_both(a, b, prepare, visit, fetch.middle)
    settle(r, r.wm)
    save(r, r.in_all, r.q, r.k, r.v)
    sum_both(a, b, attend)
    save(r, r.lse, r.att)
    fetch.end(r.we, r.wr)
    save(r, r.we, r.wr)
    follow = halves(r, tokens, r.x16, r.second, r.remote_two)

    def finish_half(half, after):
        branch = half.total() + r.vec_one[3:4]
        middle = r.x[half.own, :] + r.vec_one[2:3] * branch
        r.x16[half.own, :] = modulated(middle, r.vec_two)
        after.issue()
        r.branch[half.own, :] = branch
        r.middle[half.own, :] = middle

    finish_half(a, follow[0])
    follow[0].issue_rest()
    finish_half(b, follow[1])
    save(r, r.branch, r.middle)
    a, b = follow
    fetch = None
    if not last:
        fetch = RowsIn(*slab_views(r.rows, ATT_COLS, ATT_COLS), r.fetch_two)

    def expand(half, d):
        rows = half.pair(d)
        pre = dot_nn(r.second[rows, :], r.we[...]) + r.bias_two[...]
        value, slope = gelu_both(pre)
        hidden = value.astype(BF16)
        r.hid[rows, :] = hidden
        r.slope[rows, :] = slope.astype(BF16)
        half.put(d, dot_nt(hidden, r.wr[...]))

    if fetch:
        gather_and_sum(a, b, fetch.start, expand, fetch.middle)
    else:
        gather_and_sum(a, b, nothing, expand, nothing)
    save(r, r.second, r.hid, r.slope)
    b.relay()
    if fetch:
        fetch.end(r.next_wqkv, r.next_wm)
        save(r, r.next_wqkv, r.next_wm)
    for half in (a, b):
        mlp = half.total() + r.vec_two[3:4]
        r.mlp[half.own, :] = mlp
        r.out[half.own, :] = r.middle[half.own, :] + r.vec_two[2:3] * mlp
    save(r, r.mlp, r.out)
    settle(r)


def ring_scratch(tokens):
    sizes = half_sizes(tokens)
    remote = [half_remote(size) for size in sizes]
    return dict(local=[half_local(size) for size in sizes], remote_one=remote, remote_two=remote)


def kept_shapes(tokens):
    heads = ((2, 8 * tokens, HEAD), BF16)
    wide, tile = ((8 * tokens, D), BF16), ((tokens, D), F32)
    hidden = ((8 * tokens, FW), BF16)
    return dict(
        x=tile,
        in_all=wide,
        q=heads,
        k=heads,
        v=heads,
        lse=((8 * tokens, 2), F32),
        att=((8 * tokens, HW), BF16),
        branch=tile,
        middle=tile,
        second=wide,
        hid=hidden,
        slope=hidden,
        mlp=tile,
        we=((D, FW), BF16),
        wr=((D, FW), BF16),
    )


def block_forward(near, far, tokens, start, last, cid):
    kept = dict(kept_shapes(tokens), out=((tokens, D), F32))
    scratch = dict(
        x16=pltpu.VMEM((tokens, D), BF16),
        **ring_scratch(tokens),
        fetch_one=rows_in_scratch(FFN_COLS),
    )
    if not last:
        kept.update(
            next_wqkv=((D, 3 * HW), BF16), next_wm=((D, HW), BF16), patches=((128, 128), BF16)
        )
        scratch.update(
            square=pltpu.VMEM((128, 128), F32),
            token_cols=pltpu.VMEM((128, 128), F32),
            fetch_two=rows_in_scratch(ATT_COLS),
        )
    body = functools.partial(forward_body, tokens=tokens, start=start, last=last)
    return launch(body, cid, near, far, {}, kept, scratch)[1]


def head(r):
    picks = choice(r.place, r.two.shape[0])
    ended = spread_back(picks, r.two[...], r.first[...])
    normed, inv_std = layer_stats(ended)
    final16 = (normed * (1.0 + r.head_vec[1:2]) + r.head_vec[0:1]).astype(BF16)
    unpatch = r.feat[:, UNPATCH : UNPATCH + 32]
    r.token_cols[...] = jnp.zeros_like(r.token_cols)
    r.token_cols[:, 0:32] = dot_nn(final16, unpatch) + r.unpatch_b[...].astype(F32)
    to_pixels(r.token_cols, r.square, r.predicted, 0)
    to_tokens(r.cotangent_pixels, r.square, r.token_cols, 0)
    r.cotangent[...] = r.token_cols[:, 0:32].astype(BF16)
    r.unpatch_rows[...] = dot_tn(r.cotangent[...], final16)
    r.unpatch_bias[...] = jnp.zeros_like(r.unpatch_bias)
    r.unpatch_bias[0:1, 0:32] = sum_rows(r.cotangent[...].astype(F32))
    grad = dot_nt(r.cotangent[...], unpatch)
    r.head_vecs[0:1] = sum_rows(grad)
    r.head_vecs[1:2] = sum_rows(grad * normed)
    grad = layer_back(grad * (1.0 + r.head_vec[1:2]), normed, inv_std)
    r.grad_ended[...] = grad
    r.g[...] = exact(picks, grad, (1, 0))


def backward_body(r, tokens, last):
    a, b = halves(r, tokens, r.g16, r.g_one, r.remote_one)
    sums = None if last else RowsOut(r.pending_left, r.pending_right, r.sums_one)
    peers = a.peers() + line_only(line_peers())
    greet(peers)
    if last:
        load(r, r.first, r.two, r.feat, r.slope, r.wr, r.we)
    else:
        load(r, r.grad_two, r.grad_ended, r.slope, r.wr, r.we, r.pending_left, r.pending_right)
        load(r, r.feat, r.patches)
    load(r, r.hid, r.second, r.mlp, r.middle)
    load(r, r.q, r.k, r.v, r.lse, r.wm, r.wqkv, r.att, r.x, r.branch)
    if last:
        settle(r, r.first, r.two, r.feat)
        head(r)
    else:
        settle(r, r.grad_two, r.grad_ended)
        picks = choice(r.place, r.grad_two.shape[0])
        r.g[...] = spread_back(picks, r.grad_two[...], r.grad_ended[...])
    r.g16[...] = (r.g[...] * r.vec_two[2:3]).astype(BF16)
    met(peers)
    a.issue()
    a.issue_rest()
    b.issue()
    r.bias_two[...] = jnp.zeros_like(r.bias_two)

    def prepare():
        if sums:
            settle(r, r.pending_left, r.pending_right)
            sums.start()
        settle(r, r.slope, r.wr, r.we)

    def visit(half, d):
        rows = half.pair(d)
        pre_grad = (
            dot_nn(r.g_one[rows, :], r.wr[...]) * r.slope[rows, :].astype(F32)
        ).astype(BF16)
        r.pre_all[rows, :] = pre_grad
        r.bias_two[...] += sum_rows(pre_grad.astype(F32))
        half.put(d, dot_nt(pre_grad, r.we[...]))

    if last:
        save(r, r.grad_ended, r.unpatch_rows)
    gather_and_sum(a, b, prepare, visit, nothing)
    settle(r, r.hid, r.second, r.mlp, r.middle)
    r.vecs_two[2:3] = sum_rows(r.g[...] * r.mlp[...])
    r.vecs_two[3:4] = sum_rows(r.g16[...].astype(F32))
    r.vecs_two[4:8] = jnp.zeros((4, D), F32)
    weight_grads(r.g_one, r.hid, r.whole_two, FW)
    b.relay()
    follow = halves(r, tokens, r.g16, r.g_two, r.remote_two)

    def finish_half(half, after):
        second_grad = half.total()
        normed, inv_std = layer_stats(r.middle[half.own, :])
        grad = r.g[half.own, :] + layer_back(
            second_grad * (1.0 + r.vec_two[1:2]), normed, inv_std
        )
        r.g[half.own, :] = grad
        r.g16[half.own, :] = (grad * r.vec_one[2:3]).astype(BF16)
        after.issue()
        return sum_rows(second_grad), sum_rows(second_grad * normed)

    shift_a, scale_a = finish_half(a, follow[0])
    follow[0].issue_rest()
    if sums:
        sums.middle()
    weight_grads(r.second, r.pre_all, r.whole_one, FW)
    shift_b, scale_b = finish_half(b, follow[1])
    r.vecs_two[0:1] = shift_a + shift_b
    r.vecs_two[1:2] = scale_a + scale_b
    load_into(r, r.in_all, r.second)
    write_slabs((r.whole_one, FW), (r.whole_two, FW), r.ffn_left, r.ffn_right)
    if sums:
        sums.end_rows(r.attn_rows)
        save(r, r.attn_rows)
    a, b = follow
    sums = RowsOut(r.ffn_left, r.ffn_right, r.sums_two)

    def prepare_attention():
        sums.start()
        r.dk[...] = jnp.zeros_like(r.dk)
        r.dv[...] = jnp.zeros_like(r.dv)
        settle(r, r.q, r.k, r.v, r.lse, r.wm)

    def attend(half, d):
        rows = half.pair(d)
        grad = dot_nn(r.g_two[rows, :], r.wm[...]).astype(BF16)
        queries = []
        for h in range(2):
            part = grad[:, head_cols(h)]
            query = r.q[h, rows, :]
            scores = dot_nt(query, r.k[h]) * SCALE
            if last:
                scores = scores + r.mask[...]
            probs = jnp.exp(scores - r.lse[rows, h : h + 1])
            grad_probs = dot_nt(part, r.v[h])
            weighted = jnp.sum(probs * grad_probs, axis=-1, keepdims=True)
            score_grad = (probs * (grad_probs - weighted)).astype(BF16)
            queries.append((dot_nn(score_grad, r.k[h]) * SCALE).astype(BF16))
            r.dk[h] += dot_tn(score_grad, query)
            r.dv[h] += dot_tn(probs.astype(BF16), part)
        r.joined[rows, 0:HW] = jnp.concatenate(queries, axis=1)

    def back(half, d):
        half.put(d, dot_nt(r.joined[half.pair(d), :], r.wqkv[...]))

    gather_both(a, b, prepare_attention, attend, nothing)
    settle(r, r.wqkv)
    later = [(r.dk[h] * SCALE).astype(BF16) for h in range(2)]
    later += [r.dv[h].astype(BF16) for h in range(2)]
    r.joined[:, HW : 3 * HW] = jnp.concatenate(later, axis=1)
    sum_both(a, b, back)
    settle(r)
    sums.middle()
    r.bias_one[...] = sum_rows(r.joined[...].astype(F32))
    r.vecs_one[2:3] = sum_rows(r.g[...] * r.branch[...])
    r.vecs_one[3:4] = sum_rows(r.g16[...].astype(F32))
    r.vecs_one[4:8] = jnp.zeros((4, D), F32)
    weight_grads(r.g_two, r.att, r.whole_two, HW)
    weight_grads(r.second, r.joined, r.whole_one, 3 * HW)
    write_slabs((r.whole_one, 3 * HW), (r.whole_two, HW), r.attn_left, r.attn_right)
    save(r, r.attn_left, r.attn_right)
    sums.end_rows(r.ffn_rows)
    save(r, r.ffn_rows)
    shift, scale = 0.0, 0.0
    for half in (a, b):
        input_grad = half.total()
        normed, inv_std = layer_stats(r.x[half.own, :])
        shift = shift + sum_rows(input_grad)
        scale = scale + sum_rows(input_grad * normed)
        scaled = input_grad * (1.0 + r.vec_one[1:2])
        r.g[half.own, :] = r.g[half.own, :] + layer_back(scaled, normed, inv_std)
    r.vecs_one[0:1] = shift
    r.vecs_one[1:2] = scale
    if last:
        r.out[...] = r.g[...]
        save(r, r.out)
    else:
        grad16 = r.g[...].astype(BF16)
        r.embed_rows[0:16] = dot_tn(r.patches[...], grad16)[EMBED : EMBED + 16]
        r.embed_rows[16:17] = sum_rows(grad16.astype(F32))
        r.embed_rows[17:24] = jnp.zeros((7, D), F32)
        save(r, r.embed_rows)
        r.token_cols[...] = dot_nn(grad16, r.feat[...])
        to_pixels(r.token_cols, r.square, r.latent, EMBED)
    settle(r)


def weight_grads(left_ref, right_ref, whole_ref, width):
    @pl.loop(0, D // 384)
    def _(k):
        at = pl.ds(pl.multiple_of(k * 384, 128), 384)
        whole_ref[at, :width] = dot_tn(left_ref[:, at], right_ref[...])


def write_slabs(one, two, left_ref, right_ref):
    cut = left_ref.shape[3]
    cols = cut + right_ref.shape[3]

    @pl.loop(0, 16)
    def _(k):
        at = pl.ds(pl.multiple_of(k * PART, 8), PART)
        parts = [ref[at, :width] for ref, width in (one, two)]
        spare = cols - one[1] - two[1]
        if spare:
            parts.append(jnp.zeros((PART, spare), F32))
        rows = jnp.concatenate(parts, axis=1)
        rows = jnp.concatenate([rows, jnp.zeros((SLAB - PART, cols), F32)], axis=0).astype(BF16)
        x, z = k // 4, lax.rem(k, 4)
        left_ref[x, z] = rows[:, :cut]
        right_ref[x, z] = rows[:, cut:]


def line_only(lines):
    return [peer for peer, _ in lines[0] + lines[1]]


def slab_specs(cols):
    widths = (CUT[cols], cols - CUT[cols])
    return [((4, 4, SLAB, width), BF16) for width in widths]


def block_backward(near, far, tokens, last, cid):
    vecs = ((8, D), F32)
    attn_left, attn_right = slab_specs(ATT_COLS)
    wide, tile = (8 * tokens, D), (tokens, D)
    outs = dict(vecs_one=vecs, vecs_two=vecs)
    outs.update(bias_one=((1, 3 * HW), F32), bias_two=((1, FW), F32))
    kept = dict(attn_left=attn_left, attn_right=attn_right, ffn_rows=((SLAB, FFN_COLS), BF16))
    scratch = dict(
        g=pltpu.VMEM(tile, F32),
        g16=pltpu.VMEM(tile, BF16),
        square=pltpu.VMEM((128, 128), F32),
        token_cols=pltpu.VMEM((128, 128), F32),
        g_one=pltpu.VMEM(wide, BF16),
        g_two=pltpu.VMEM(wide, BF16),
        pre_all=pltpu.VMEM((8 * tokens, FW), BF16),
        joined=pltpu.VMEM((8 * tokens, 3 * HW), BF16),
        dk=pltpu.VMEM((2, 8 * tokens, HEAD), F32),
        dv=pltpu.VMEM((2, 8 * tokens, HEAD), F32),
        whole_one=pltpu.VMEM((D, FW), F32),
        whole_two=pltpu.VMEM((D, FW), F32),
        ffn_left=pltpu.VMEM(*slab_specs(FFN_COLS)[0]),
        ffn_right=pltpu.VMEM(*slab_specs(FFN_COLS)[1]),
        **ring_scratch(tokens),
        sums_two=rows_out_scratch(FFN_COLS),
    )
    if last:
        outs.update(
            predicted=((16, 8, 32), BF16), unpatch_bias=((8, 128), F32), head_vecs=((2, D), F32)
        )
        kept.update(out=(tile, F32), unpatch_rows=((32, D), F32), grad_ended=((128, D), F32))
        scratch.update(cotangent=pltpu.VMEM((128, 32), BF16))
    else:
        outs.update(latent=((16, 4, 32), F32))
        kept.update(attn_rows=((SLAB, ATT_COLS), BF16), embed_rows=((24, D), F32))
        scratch.update(sums_one=rows_out_scratch(ATT_COLS))
    body = functools.partial(backward_body, tokens=tokens, last=last)
    near_outs, far_outs = launch(body, cid, near, far, outs, kept, scratch, vmem=62 << 20)
    return Results(near_outs, **far_outs)


def shards(
    latent,
    condition,
    routed_ids,
    embed_weight,
    embed_bias,
    modulation_weight,
    modulation_bias,
    attention_weight,
    attention_bias,
    merge_weight,
    merge_bias,
    expand_weight,
    expand_bias,
    reduce_weight,
    reduce_bias,
    final_modulation,
    final_offsets,
    unpatch_weight,
    unpatch_bias,
    pred_cotangent,
):
    tile_rows = latent.shape[1] // 2
    tile_cols = latent.shape[2] // 2
    tile_tokens = tile_rows * tile_cols
    capacity = 7 * tile_tokens // 8
    row_index = lax.axis_index("tx") * tile_rows + jnp.arange(tile_rows, dtype=jnp.int32)
    col_index = lax.axis_index("ty") * tile_cols + jnp.arange(tile_cols, dtype=jnp.int32)
    placed = sincos_table(row_index.astype(F32), col_index.astype(F32), D)
    mod_w = modulation_weight.swapaxes(0, 1)
    got = open_up(
        dict(
            condition=condition,
            ids=routed_ids,
            embed_w=embed_weight,
            embed_b=embed_bias[None],
            unpatch_w=unpatch_weight,
            attn_b=attention_bias,
            merge_b=merge_bias,
            expand_b=expand_bias,
            reduce_b=reduce_bias,
            mod_b=modulation_bias,
            final_b=final_offsets[None],
        ),
        dict(
            mod_w=mod_w,
            final_w=final_modulation,
            attn_w=attention_weight.transpose(1, 2, 0, 3),
            merge_w=merge_weight.swapaxes(0, 1),
            expand_w=expand_weight.swapaxes(0, 1),
            reduce_w=reduce_weight.swapaxes(0, 1),
        ),
    )
    vecs_one = dict(vec_one=got.vec_one_0, vec_two=got.vec_two_0)
    vecs_two = dict(vec_one=got.vec_one_1, vec_two=got.vec_two_1, mask=got.mask)
    kept_one = block_forward(
        dict(
            vecs_one,
            bias_one=got.bias_one_0,
            bias_two=got.bias_two_0,
            pixels=latent.transpose(0, 2, 3, 1)[0],
        ),
        dict(feat=got.feat, placed=placed, rows=got.rows, wqkv=got.wqkv, wm=got.wm),
        tile_tokens,
        2 * ATT_COLS,
        False,
        10,
    )
    weights_two = dict(wqkv=kept_one.next_wqkv, wm=kept_one.next_wm)
    kept_two = block_forward(
        dict(vecs_two, bias_one=got.bias_one_1, bias_two=got.bias_two_1, place=got.place),
        dict(weights_two, rows=got.rows, first=kept_one.out),
        capacity,
        2 * ATT_COLS + FFN_COLS,
        True,
        11,
    )

    def saved(kept, tokens):
        return {name: kept[name] for name in kept_shapes(tokens)}

    back_two = block_backward(
        dict(
            vecs_two,
            place=got.place,
            head_vec=got.head_vec,
            unpatch_b=unpatch_bias[None],
            cotangent_pixels=pred_cotangent.transpose(0, 2, 3, 1)[0],
        ),
        dict(
            saved(kept_two, capacity),
            **weights_two,
            feat=got.feat,
            first=kept_one.out,
            two=kept_two.out,
        ),
        capacity,
        True,
        12,
    )
    back_one = block_backward(
        dict(vecs_one, place=got.place),
        dict(
            saved(kept_one, tile_tokens),
            wqkv=got.wqkv,
            wm=got.wm,
            feat=got.feat,
            patches=kept_one.patches,
            pending_left=back_two.attn_left,
            pending_right=back_two.attn_right,
            grad_two=back_two.out,
            grad_ended=back_two.grad_ended,
        ),
        tile_tokens,
        False,
        13,
    )
    ended = finish(
        dict(
            vecs_one_0=back_one.vecs_one,
            vecs_two_0=back_one.vecs_two,
            vecs_one_1=back_two.vecs_one,
            vecs_two_1=back_two.vecs_two,
            head_vecs=back_two.head_vecs,
            bias_one_0=back_one.bias_one,
            bias_two_0=back_one.bias_two,
            bias_one_1=back_two.bias_one,
            bias_two_1=back_two.bias_two,
            unpatch_bias=back_two.unpatch_bias,
        ),
        dict(
            left=back_one.attn_left,
            right=back_one.attn_right,
            attn_rows=back_one.attn_rows,
            ffn_rows_0=back_one.ffn_rows,
            ffn_rows_1=back_two.ffn_rows,
            unpatch_rows=back_two.unpatch_rows,
            embed_rows=back_one.embed_rows,
        ),
    )
    last = close(
        dict(
            s_in=ended.s_out,
            condition=condition,
            predicted_in=back_two.predicted,
            latent_in=back_one.latent,
        ),
        dict(
            early_in=ended.early_out,
            late_in=ended.late_out,
            m_in=ended.m_out,
            mod_w=mod_w,
            final_w=final_modulation,
        ),
    )
    return (
        last.predicted.transpose(2, 0, 1)[None],
        last.latent.transpose(2, 0, 1)[None],
        last.condition_grad,
        last.embed_w,
        last.embed_b[0],
        last.mod_grad.swapaxes(0, 1),
        last.mod_b,
        last.attn.transpose(2, 0, 1, 3),
        last.attn_b,
        last.merge.swapaxes(0, 1),
        last.merge_b,
        last.expand.swapaxes(0, 1),
        last.expand_b,
        last.reduce.swapaxes(0, 1),
        last.reduce_b,
        last.final_grad,
        last.final_b[0],
        last.unpatch_w,
        last.unpatch_b[0],
    )


def solution(mesh):
    torus = Mesh(
        mesh.devices.reshape(4, 4, mesh.shape["tx"], mesh.shape["ty"]), ("dp_0", "dp_1", "tx", "ty")
    )
    return jax.shard_map(
        shards,
        mesh=torus,
        in_specs=(
            P(DP, "tx", "ty", None),
            P(None, DP_TX_TY),
            P(DP, None),
            P(None, DP_TX_TY),
            P(DP_TX_TY),
            P(None, DP_TX_TY, None),
            P(None, DP_TX_TY),
            P(None, DP_TX_TY, None, None),
            P(None, DP_TX_TY),
            P(None, DP_TX_TY, None),
            P(None, DP_TX_TY),
            P(None, DP_TX_TY, None),
            P(None, DP_TX_TY),
            P(None, DP_TX_TY, None),
            P(None, DP_TX_TY),
            P(DP_TX_TY, None),
            P(DP_TX_TY),
            P(DP_TX_TY, None),
            P(),
            P(DP, "tx", "ty", None),
        ),
        out_specs=(
            P(DP, "tx", "ty", None),
            P(DP, "tx", "ty", None),
            P(None, DP_TX_TY),
            P(None, DP_TX_TY),
            P(DP_TX_TY),
            P(None, DP_TX_TY, None),
            P(None, DP_TX_TY),
            P(None, DP_TX_TY, None, None),
            P(None, DP_TX_TY),
            P(None, DP_TX_TY, None),
            P(None, DP_TX_TY),
            P(None, DP_TX_TY, None),
            P(None, DP_TX_TY),
            P(None, DP_TX_TY, None),
            P(None, DP_TX_TY),
            P(DP_TX_TY, None),
            P(DP_TX_TY),
            P(DP_TX_TY, None),
            P(),
        ),
        check_vma=False,
    )
```

```python
import functools

import jax
import jax.numpy as jnp
import numpy as np
from jax import lax
from jax.experimental import pallas as pl
from jax.experimental.pallas import tpu as pltpu
from jax.sharding import Mesh
from jax.sharding import PartitionSpec as P

D = 1152
HEADS = 16
FF = 4608
HW = D // 8
FW = FF // 8
DP = ("dp_0", "dp_1")
DP_TX_TY = ("dp_0", "dp_1", "tx", "ty")
MESH = pl.DeviceIdType.MESH
VMEM = pl.BlockSpec(memory_space=pltpu.VMEM)
FAR = pl.BlockSpec(memory_space=pl.ANY)
F32 = jnp.float32
BF16 = jnp.bfloat16
ATT_COLS = 640
FFN_COLS = 2 * FW
ALL_COLS = 2 * (ATT_COLS + FFN_COLS)
PIECE = 512
PIECES = ALL_COLS // PIECE


def greet(peers):
    barrier = pltpu.get_barrier_semaphore()
    for peer in peers:
        pl.semaphore_signal(barrier, inc=1, device_id=peer, device_id_type=MESH)


def met(peers):
    pl.semaphore_wait(pltpu.get_barrier_semaphore(), len(peers))


def enter(peers):
    greet(peers)
    met(peers)


def send(src, dst, sems, k, peer):
    copy = pltpu.make_async_remote_copy(
        src_ref=src,
        dst_ref=dst,
        send_sem=sems[0].at[k],
        recv_sem=sems[1].at[k],
        device_id=peer,
        device_id_type=MESH,
    )
    copy.start()
    return copy


def group_peers():
    c, y = lax.axis_index("tx"), lax.axis_index("ty")
    found = []
    for dc in range(2):
        for dy in range(4):
            if dc or dy:
                oc, oy = lax.rem(c + dc, 2), lax.rem(y + dy, 4)
                found.append(({"tx": oc, "ty": oy}, oc * 4 + oy))
    return found


def own_group():
    return lax.axis_index("tx") * 4 + lax.axis_index("ty")


def dma_sems(n):
    return [pltpu.SemaphoreType.DMA((n,)), pltpu.SemaphoreType.DMA((n,))]


def ring_peers():
    c, y = lax.axis_index("tx"), lax.axis_index("ty")
    return (
        {"tx": 1 - c},
        {"ty": lax.rem(y + 1, 4)},
        {"ty": lax.rem(y + 3, 4)},
        {"ty": lax.rem(y + 2, 4)},
    )


def layer_stats(value_rows):
    centered = value_rows - jnp.mean(value_rows, axis=-1, keepdims=True)
    inv_std = lax.rsqrt(jnp.mean(centered * centered, axis=-1, keepdims=True) + 1e-06)
    return (centered * inv_std, inv_std)


def layer_back(upstream, normed, inv_std):
    return inv_std * (
        upstream
        - jnp.mean(upstream, axis=-1, keepdims=True)
        - normed * jnp.mean(upstream * normed, axis=-1, keepdims=True)
    )


def sincos_table(row_pos, col_pos, width):
    quarter = width // 4
    freqs = jnp.power(10000.0, -jnp.arange(quarter, dtype=jnp.float32) / quarter)
    row_angle = row_pos[:, None] * freqs[None, :]
    col_angle = col_pos[:, None] * freqs[None, :]
    row_embed = jnp.concatenate([jnp.sin(row_angle), jnp.cos(row_angle)], axis=-1)
    col_embed = jnp.concatenate([jnp.sin(col_angle), jnp.cos(col_angle)], axis=-1)
    row_full = jnp.broadcast_to(
        row_embed[:, None, :], (row_pos.shape[0], col_pos.shape[0], width // 2)
    )
    col_full = jnp.broadcast_to(
        col_embed[None, :, :], (row_pos.shape[0], col_pos.shape[0], width // 2)
    )
    return jnp.concatenate([row_full, col_full], axis=-1).reshape(
        row_pos.shape[0] * col_pos.shape[0], width
    )


SLAB = 80
PART = D // 16
CUT = {ATT_COLS: 384, FFN_COLS: 640}


def line_peers():
    x, z = lax.axis_index("dp_0"), lax.axis_index("dp_1")
    along_x = [({"dp_0": lax.rem(x + d, 4)}, lax.rem(x + d, 4)) for d in (2, 1, 3)]
    along_z = [({"dp_1": lax.rem(z + d, 4)}, lax.rem(z + d, 4)) for d in (2, 1, 3)]
    return along_x, along_z


class RowsIn:
    def __init__(self, left_ref, right_ref, scratch):
        self.left, self.right = left_ref, right_ref
        self.all_left, self.all_right = scratch[:2]
        self.sems = tuple(scratch[2:4])
        self.x, self.z = lax.axis_index("dp_0"), lax.axis_index("dp_1")
        self.along_x, self.along_z = line_peers()

    def peers(self):
        return [peer for peer, _ in self.along_x + self.along_z]

    def start(self):
        x, z = self.x, self.z
        self.first = []
        for k, (peer, _) in enumerate(self.along_z):
            self.first.append(send(self.left, self.all_left.at[x, z], self.sems, k, peer))
        for k, (peer, _) in enumerate(self.along_x):
            self.first.append(send(self.right, self.all_right.at[x, z], self.sems, 3 + k, peer))
        self.all_left[x, z] = self.left[...]
        self.all_right[x, z] = self.right[...]

    def middle(self):
        left, right = self.all_left.at[self.x], self.all_right.at[:, self.z]
        self.second = []
        for copy in self.first[:3]:
            copy.wait_recv()
        for k, (peer, _) in enumerate(self.along_x):
            self.second.append(send(left, left, self.sems, 6 + k, peer))
        for copy in self.first[3:]:
            copy.wait_recv()
        for k, (peer, _) in enumerate(self.along_z):
            self.second.append(send(right, right, self.sems, 9 + k, peer))

    def end(self, one_ref, two_ref):
        for copy in self.second:
            copy.wait_recv()
        width, other = one_ref.shape[1], two_ref.shape[1]
        cut = self.left.shape[1]

        @pl.loop(0, 8)
        def _(pair):
            x, z = pair // 2, 2 * lax.rem(pair, 2)
            both = []
            for k in range(2):
                parts = [self.all_left[x, z + k], self.all_right[x, z + k]]
                both.append(jnp.concatenate(parts, axis=1).astype(F32)[:PART])
            value = jnp.concatenate(both, axis=0).astype(BF16)
            at = pl.ds(pl.multiple_of(pair * 2 * PART, 16), 2 * PART)
            one_ref[at, :] = value[:, :width]
            two_ref[at, :] = value[:, width : width + other]

        for copy in self.first + self.second:
            copy.wait_send()


def rows_in_scratch(cols):
    left = CUT[cols]
    return [
        pltpu.VMEM((4, 4, SLAB, left), BF16),
        pltpu.VMEM((4, 4, SLAB, cols - left), BF16),
    ] + dma_sems(12)


class RowsOut:
    def __init__(self, left_ref, right_ref, scratch):
        self.left, self.right = left_ref, right_ref
        self.got = scratch[0:2]
        self.mine = scratch[2:4]
        self.last = scratch[4:6]
        self.sems = tuple(scratch[6:8])
        self.x, self.z = lax.axis_index("dp_0"), lax.axis_index("dp_1")
        self.along_x, self.along_z = line_peers()

    def peers(self):
        return [peer for peer, _ in self.along_x + self.along_z]

    def start(self):
        self.first = []
        for k, (peer, at) in enumerate(self.along_x):
            part = self.left.at[at]
            self.first.append(send(part, self.got[0].at[k], self.sems, k, peer))
        for k, (peer, at) in enumerate(self.along_z):
            part = self.right.at[:, at]
            self.first.append(send(part, self.got[1].at[k], self.sems, 3 + k, peer))

    def middle(self):
        self.second = []
        for side, peers in ((0, self.along_z), (1, self.along_x)):
            for copy in self.first[3 * side : 3 * side + 3]:
                copy.wait_recv()
            got, mine = self.got[side], self.mine[side]

            @pl.loop(0, 4)
            def _(k):
                own = self.right[k, self.z] if side else self.left[self.x, k]
                across, below, above = (got[source, k].astype(F32) for source in range(3))
                total = (own.astype(F32) + across) + (below + above)
                mine[k] = total.astype(mine.dtype)

            for k, (peer, at) in enumerate(peers):
                part = mine.at[at]
                copy = send(part, self.last[side].at[k], self.sems, 6 + 3 * side + k, peer)
                self.second.append(copy)

    def end(self):
        for copy in self.second:
            copy.wait_recv()
        totals = []
        for side, own in ((0, self.z), (1, self.x)):
            across, below, above = (self.last[side][source].astype(F32) for source in range(3))
            totals.append((self.mine[side][own].astype(F32) + across) + (below + above))
        return totals

    def end_rows(self, out_ref):
        cut = self.left.shape[3]
        left, right = self.end()
        out_ref[:, :cut] = left.astype(BF16)
        out_ref[:, cut:] = right.astype(BF16)
        self.leave()

    def leave(self):
        for copy in self.first + self.second:
            copy.wait_send()


def rows_out_scratch(cols):
    return sum_scratch([(SLAB, CUT[cols]), (SLAB, cols - CUT[cols])], BF16)


def sum_scratch(shapes, dtype):
    return (
        [pltpu.VMEM((3, 4, *shape), dtype) for shape in shapes]
        + [pltpu.VMEM((4, *shape), dtype) for shape in shapes]
        + [pltpu.VMEM((3, *shape), dtype) for shape in shapes]
        + dma_sems(12)
    )


def slab_views(rows_ref, start, cols):
    cut = start + CUT[cols]
    return rows_ref.at[:, start:cut], rows_ref.at[:, cut : start + cols]


def weight_shapes(cols):
    widths = (3 * HW, HW) if cols == ATT_COLS else (FW, FW)
    return tuple(jax.ShapeDtypeStruct((D, w), BF16) for w in widths)


def dot_nn(left, right):
    return lax.dot_general(left, right, (((1,), (0,)), ((), ())), preferred_element_type=F32)


def dot_nt(left, right):
    return lax.dot_general(left, right, (((1,), (1,)), ((), ())), preferred_element_type=F32)


def dot_tn(left, right):
    return lax.dot_general(left, right, (((0,), (0,)), ((), ())), preferred_element_type=F32)


def gelu_both(pre):
    root = 0.7978845608028654
    square = pre * pre
    bent = jnp.tanh(root * pre * (1.0 + 0.044715 * square))
    value = 0.5 * pre * (1.0 + bent)
    slope = 0.5 * (1.0 + bent) + 0.5 * pre * (1.0 - bent * bent) * root * (1.0 + 0.134145 * square)
    return value, slope


def sum_rows(value):
    return jnp.sum(value, axis=0, keepdims=True)


HEAD = D // HEADS
SCALE = HEAD ** (-0.5)


def head_cols(h, start=0):
    return slice(start + h * HEAD, start + (h + 1) * HEAD)


class Refs:
    pass


class Results(dict):
    __getattr__ = dict.__getitem__


def launch(body, cid, near, far, outs, kept, scratch, vmem=60 << 20):
    twins = {name: (value.shape, value.dtype) for name, value in far.items()}
    twins.update(kept)
    groups, tree = jax.tree.flatten(scratch, is_leaf=lambda entry: not isinstance(entry, (dict, list)))

    def kernel(*refs):
        refs = iter(refs)
        r, hbm = Refs(), {}
        for name in near:
            setattr(r, name, next(refs))
        for name in far:
            hbm[name] = next(refs)
        for name in outs:
            setattr(r, name, next(refs))
        for name in kept:
            hbm[name] = next(refs)
        r.moves, r.moving = {}, {}
        for k, name in enumerate(twins):
            ref = next(refs)
            setattr(r, name, ref)
            r.moves[id(ref)] = (hbm[name], k)
        if twins:
            r.move_sems = next(refs)
        for name, entry in jax.tree.unflatten(tree, list(refs)).items():
            setattr(r, name, entry)
        body(r)

    shapes = [jax.ShapeDtypeStruct(*spec) for spec in (*outs.values(), *kept.values())]
    results = pl.pallas_call(
        kernel,
        out_shape=tuple(shapes),
        in_specs=[VMEM] * len(near) + [FAR] * len(far),
        out_specs=(VMEM,) * len(outs) + (FAR,) * len(kept),
        scratch_shapes=[pltpu.VMEM(*spec) for spec in twins.values()]
        + ([pltpu.SemaphoreType.DMA((len(twins),))] if twins else [])
        + groups,
        compiler_params=pltpu.CompilerParams(
            collective_id=cid, has_side_effects=cid is not None, vmem_limit_bytes=vmem
        ),
    )(*near.values(), *far.values())
    return Results(zip(outs, results)), Results(zip(kept, results[len(outs) :]))


def load_into(r, ref, target):
    source, k = r.moves[id(ref)]
    r.moving[id(ref)] = pltpu.make_async_copy(source, target, r.move_sems.at[k])
    r.moving[id(ref)].start()


def load(r, *refs):
    for ref in refs:
        load_into(r, ref, ref)


def save(r, *refs):
    for ref in refs:
        target, k = r.moves[id(ref)]
        r.moving[id(ref)] = pltpu.make_async_copy(ref, target, r.move_sems.at[k])
        r.moving[id(ref)].start()


def settle(r, *refs):
    for key in [id(ref) for ref in refs] or list(r.moving):
        r.moving.pop(key).wait()


def exact(left, right, dims):
    return lax.dot_general(
        left,
        right,
        ((dims[:1], dims[1:]), ((), ())),
        precision=lax.Precision.HIGHEST,
        preferred_element_type=F32,
    )


def choice(place_ref, capacity):
    tokens = place_ref.shape[1]
    slots = lax.broadcasted_iota(jnp.int32, (capacity, tokens), 0)
    return jnp.where(slots == place_ref[...], 1.0, 0.0).astype(F32)


def spread_back(picks, chosen, others):
    used = exact(picks, jnp.ones((picks.shape[0], 128), F32), (0, 0))[:, :1]
    return exact(picks, chosen, (0, 0)) + others * (1.0 - used)


def modulated(x, vec_ref):
    normed, _ = layer_stats(x)
    return (normed * (1.0 + vec_ref[1:2]) + vec_ref[0:1]).astype(BF16)


def full_width(parts, at):
    height = parts[0].shape[0]
    used = at + sum(part.shape[1] for part in parts)
    if at:
        parts = [jnp.zeros((height, at), F32), *parts]
    if used < 128:
        parts = [*parts, jnp.zeros((height, 128 - used), F32)]
    return jnp.concatenate(parts, axis=1)


def to_tokens(pixels_ref, square, tokens_ref, at):
    wide, depth, high = pixels_ref.shape
    square[...] = jnp.zeros_like(square)
    square[: wide * depth, :high] = pixels_ref[...].astype(F32).reshape(wide * depth, high)
    square[...] = jnp.transpose(square[...])
    size = 2 * depth
    lines = [square[pl.ds(line, high // 2, stride=2), :] for line in range(2)]
    for c in range(wide // 2):
        parts = [value[:, c * size : (c + 1) * size] for value in lines]
        tokens_ref[pl.ds(c, high // 2, stride=wide // 2), :] = full_width(parts, at)


def to_pixels(tokens_ref, square, pixels_ref, at):
    wide, depth, high = pixels_ref.shape
    square[...] = jnp.zeros_like(square)
    size = 2 * depth
    columns = [tokens_ref[pl.ds(c, high // 2, stride=wide // 2), :] for c in range(wide // 2)]
    for line in range(2):
        start = at + line * size
        parts = [value[:, start : start + size] for value in columns]
        square[pl.ds(line, high // 2, stride=2), :] = full_width(parts, 0)
    value = jnp.transpose(square[...])[: wide * depth, :high].reshape(wide, depth, high)
    pixels_ref[...] = value.astype(pixels_ref.dtype)


FIRST = 64
PIECE_ROWS = 32
PLACE_OF = {0: 0, 3: 1, 1: 2, 2: 3}


def half_sizes(tokens):
    return FIRST, tokens - FIRST


def half_local(size):
    return [
        pltpu.VMEM((4, size, D), F32),
        pltpu.VMEM((4, size, D), BF16),
        pltpu.VMEM((3, size, D), BF16),
    ]


def half_remote(size):
    return [
        pltpu.VMEM((4, size, D), BF16),
        pltpu.VMEM((2, size, D), BF16),
        pltpu.VMEM((PIECE_ROWS, D), BF16),
        pltpu.VMEM((size - PIECE_ROWS, D), BF16),
    ] + dma_sems(20)


class Half:
    def __init__(self, which, tokens, x_ref, all_ref, local, remote):
        sizes = half_sizes(tokens)
        self.size = sizes[which]
        self.own = slice(which * FIRST, which * FIRST + self.size)
        self.base = which * 8 * FIRST
        self.x, self.all = x_ref, all_ref
        self.kept, self.sib_out, self.out = local
        self.sib_in, self.got, self.far_low, self.far_high = remote[:4]
        self.sems = tuple(remote[4:6])
        self.sib, self.up, self.down, _ = ring_peers()
        self.low, self.high = slice(0, PIECE_ROWS), slice(PIECE_ROWS, self.size)
        self.sent, self.swaps = [], {}

    def peers(self):
        return [self.sib, self.up, self.down]

    def send(self, src, dst, k, peer):
        copy = send(src, dst, self.sems, k, peer)
        self.sent.append(copy)
        return copy

    def pair(self, d, count=1):
        start = self.base + 2 * PLACE_OF[d] * self.size
        return slice(start, start + 2 * count * self.size)

    def slot(self, d, other, rows=None):
        start = self.base + (2 * PLACE_OF[d] + other) * self.size
        rows = slice(0, self.size) if rows is None else rows
        return self.all.at[start + rows.start : start + rows.stop]

    def source(self, rows):
        return self.x.at[self.own.start + rows.start : self.own.start + rows.stop]

    def issue(self):
        low, high = self.low, self.high
        self.a1 = self.send(self.source(low), self.slot(3, 0, low), 0, self.up)
        self.b1 = self.send(self.source(high), self.slot(1, 0, high), 1, self.down)
        whole = slice(0, self.size)
        self.arrive = {0: self.send(self.source(whole), self.slot(0, 1), 4, self.sib)}
        start = self.base
        self.all[start : start + self.size, :] = self.x[self.own, :]

    def issue_rest(self):
        low, high = self.low, self.high
        self.a2 = self.send(self.source(high), self.slot(3, 0, high), 2, self.up)
        self.b2 = self.send(self.source(low), self.slot(1, 0, low), 3, self.down)

    def forward(self):
        low, high = self.low, self.high
        self.a1.wait_recv()
        self.f1 = self.send(self.slot(3, 0, low), self.slot(2, 0, low), 5, self.up)
        self.b1.wait_recv()
        self.f2 = self.send(self.slot(1, 0, high), self.slot(2, 0, high), 6, self.down)

    def near_arrive(self):
        self.a2.wait_recv()
        self.arrive[3] = self.send(self.slot(3, 0), self.slot(3, 1), 7, self.sib)
        self.b2.wait_recv()
        self.arrive[1] = self.send(self.slot(1, 0), self.slot(1, 1), 8, self.sib)

    def far_arrive(self):
        self.f1.wait_recv()
        self.f2.wait_recv()
        self.arrive[2] = self.send(self.slot(2, 0), self.slot(2, 1), 9, self.sib)

    def ready(self, d):
        self.arrive[d].wait_recv()

    def put(self, d, value):
        self.kept[d] = value[: self.size]
        self.sib_out[d] = value[self.size :].astype(BF16)
        self.swaps[d] = self.send(self.sib_out.at[d], self.sib_in.at[d], 10 + d, self.sib)

    def chip_sum(self, d):
        self.swaps[d].wait_recv()
        return self.kept[d] + self.sib_in[d].astype(F32)

    def near(self):
        low, high = self.low, self.high
        total = self.chip_sum(1)
        self.kept[1] = total
        self.out[0, high] = total[high].astype(BF16)
        self.n1 = self.send(self.out.at[0, high], self.got.at[0, high], 14, self.up)
        total = self.chip_sum(3)
        self.kept[3] = total
        self.out[1, low] = total[low].astype(BF16)
        self.n2 = self.send(self.out.at[1, low], self.got.at[1, low], 15, self.down)

    def far(self):
        self.out[2] = self.chip_sum(2).astype(BF16)
        self.low_sent = self.send(self.out.at[2, self.low], self.far_low, 16, self.up)
        self.high_sent = self.send(self.out.at[2, self.high], self.far_high, 17, self.down)

    def relay(self):
        low, high = self.low, self.high
        self.low_sent.wait_recv()
        self.out[0, low] = (self.kept[1, low] + self.far_low[...].astype(F32)).astype(BF16)
        self.r1 = self.send(self.out.at[0, low], self.got.at[0, low], 18, self.up)
        self.high_sent.wait_recv()
        self.out[1, high] = (self.kept[3, high] + self.far_high[...].astype(F32)).astype(BF16)
        self.r2 = self.send(self.out.at[1, high], self.got.at[1, high], 19, self.down)

    def total(self):
        value = self.chip_sum(0)
        for copy in (self.n1, self.n2, self.r1, self.r2):
            copy.wait_recv()
        value = value + self.got[0].astype(F32) + self.got[1].astype(F32)
        for copy in self.sent:
            copy.wait_send()
        return value


def gather_both(a, b, prepare, visit, between):
    prepare()
    a.ready(0)
    visit(a, 0)
    a.forward()
    b.issue_rest()
    b.ready(0)
    visit(b, 0)
    a.near_arrive()
    b.forward()
    between()
    a.ready(3)
    visit(a, 3)
    a.ready(1)
    visit(a, 1)
    a.far_arrive()
    b.near_arrive()
    b.ready(3)
    visit(b, 3)
    a.ready(2)
    visit(a, 2)
    b.ready(1)
    visit(b, 1)
    b.far_arrive()
    b.ready(2)
    visit(b, 2)


def gather_and_sum(a, b, prepare, visit, between):
    prepare()
    a.ready(0)
    visit(a, 0)
    a.forward()
    b.issue_rest()
    b.ready(0)
    visit(b, 0)
    a.near_arrive()
    b.forward()
    between()
    a.ready(3)
    visit(a, 3)
    a.ready(1)
    visit(a, 1)
    a.far_arrive()
    b.near_arrive()
    a.near()
    b.ready(3)
    visit(b, 3)
    a.ready(2)
    visit(a, 2)
    b.ready(1)
    visit(b, 1)
    a.far()
    b.far_arrive()
    b.near()
    b.ready(2)
    visit(b, 2)
    a.relay()
    b.far()


def sum_both(a, b, make):
    make(a, 2)
    make(b, 2)
    a.far()
    make(a, 1)
    b.far()
    make(a, 3)
    make(a, 0)
    a.near()
    make(b, 1)
    a.relay()
    make(b, 3)
    make(b, 0)
    b.near()
    b.relay()


def nothing():
    pass


def halves(r, tokens, x_ref, all_ref, remote):
    return [Half(k, tokens, x_ref, all_ref, r.local[k], remote[k]) for k in range(2)]


UNPATCH, EMBED, BLOCKS, EMBED_BIAS = 0, 32, 48, 64
WHOLE = 16384


def own_targets():
    group = own_group()
    return group * (D // 16), group * (D // 8)


def bias_table():
    table = np.zeros((8, 1024), np.int32)
    for col in range(3 * HW):
        part, e = divmod(col, HW)
        table[0, col] = (e // 18 + (64 if part == 2 else 0)) * 9 + e % 9 if part != 1 else -(1 << 20)
        table[1, col] = e % 18 // 9
    for e in range(FW):
        table[0, 3 * HW + e] = e // 36 * 9 + e % 9
        table[1, 3 * HW + e] = e % 36 // 9
    return table


def bias_picks(table_ref, cols, shift):
    rows = lax.broadcasted_iota(jnp.int32, (D, cols.stop - cols.start), 0)
    return jnp.where(rows == table_ref[0:1, cols] + shift, 1.0, 0.0).astype(F32)


ATT_BIAS = slice(0, 3 * HW)
FFN_BIAS = slice(3 * HW, 3 * HW + FW)


def mod_places(index):
    e = lax.broadcasted_iota(jnp.int32, (1, 128), 1)
    at = jnp.where(e < 108, 6 * D - 54 + index * 54 + e, 12 * D - 108 + index * 18 + e)
    at = jnp.where(e < 54, index * 54 + e, at)
    at = jnp.where(e < 126, at, -1)
    lines = lax.broadcasted_iota(jnp.int32, (128, 128), 0)
    return lines == lax.shift_right_arithmetic(at, 7), lines == jnp.bitwise_and(at, 127)


def whole_index():
    x, z = lax.axis_index("dp_0"), lax.axis_index("dp_1")
    return (x * 4 + z) * 8 + own_group()


def route(r):
    token = lax.broadcasted_iota(jnp.int32, (128, 512), 0)
    row = lax.axis_index("tx") * 16 + token // 8
    col = lax.axis_index("ty") * 8 + lax.rem(token, 8)
    hits = jnp.where(row * 32 + col == r.ids[...], 1.0, 0.0).astype(BF16)
    flags = dot_nt(jnp.ones((8, 512), BF16), hits)
    lines = lax.broadcasted_iota(jnp.int32, (128, 128), 0)
    lanes = lax.broadcasted_iota(jnp.int32, (128, 128), 1)
    before = dot_nn(flags.astype(BF16), jnp.where(lines <= lanes, 1.0, 0.0).astype(BF16))
    r.place[...] = jnp.where(flags > 0, before - 1.0, -1.0)[0:1].astype(jnp.int32)
    row, col = r.ids[...] // 512, lax.rem(r.ids[...], 32) // 8
    chip = lax.rem(col - lax.axis_index("ty") + 4, 4)
    other = jnp.where(row == lax.axis_index("tx"), 0, 1)
    place = jnp.where(chip == 1, 2, jnp.where(chip == 2, 3, jnp.where(chip == 3, 1, 0)))
    tile = place * 2 + other
    slot = lax.broadcasted_iota(jnp.int32, r.mask.shape, 1)
    used = slot < 0
    for k in range(8):
        count = jnp.sum(jnp.where(tile == k, 1.0, 0.0), axis=1, keepdims=True).astype(jnp.int32)
        for which, size in enumerate(half_sizes(r.mask.shape[1] // 8)):
            at = slot - which * 8 * FIRST - k * size
            used = used | ((at >= 0) & (at < size) & (at + which * FIRST < count))
    r.mask[...] = jnp.where(used, 0.0, -1e30)


def open_body(r):
    group = group_peers()
    sib, up, down, far = ring_peers()
    fetch = RowsIn(*slab_views(r.rows, 0, ATT_COLS), r.fetch)
    mods = RowsOut(r.m_mine.at[:, :, 0:64], r.m_mine.at[:, :, 64:128], r.mods)
    peers = [peer for peer, _ in group] + fetch.peers()
    greet(peers)
    load(r, r.attn_w, r.merge_w, r.expand_w, r.reduce_w, r.unpicks)
    load(r, r.mod_w, r.final_w, r.picks, r.table)
    r.pack[...] = jnp.zeros_like(r.pack)
    settle(r, r.attn_w, r.merge_w, r.expand_w, r.reduce_w)
    attn = [[r.attn_w[:, j, b, :] for j in range(3)] for b in range(2)]
    merge = [r.merge_w[:, b, :] for b in range(2)]
    expand = [r.expand_w[:, b, :] for b in range(2)]
    reduce = [r.reduce_w[:, b, :] for b in range(2)]
    spare = jnp.zeros((9, ATT_COLS - 4 * HW), BF16)
    for p in range(8):
        narrow, wide = slice(p * HW, (p + 1) * HW), slice(p * FW, (p + 1) * FW)
        parts = []
        for b in range(2):
            parts += [attn[b][j][:, narrow] for j in range(3)] + [merge[b][:, narrow], spare]
        for b in range(2):
            parts += [expand[b][:, wide], reduce[b][:, wide]]
        r.pack[p * 16 : p * 16 + 9, :] = jnp.concatenate(parts, axis=1)
    settle(r, r.unpicks)
    packed = jnp.zeros((8 * 64, PIECE), F32)
    for k in range(PIECES):
        packed = packed + dot_tn(r.unpicks[k], r.pack[:, k * PIECE : (k + 1) * PIECE])
    r.w_mine[...] = packed.astype(BF16).reshape(8, 64, PIECE)
    r.lines[...] = jnp.zeros_like(r.lines)
    r.lines[EMBED : EMBED + 16, 0:9] = r.embed_w[...].astype(F32)
    for b in range(2):
        at = BLOCKS + 8 * b
        for j in range(2):
            r.lines[at + j : at + j + 1, 0:9] = r.attn_b[b : b + 1, 9 * j : 9 * j + 9].astype(F32)
        for j in range(4):
            value = r.expand_b[b : b + 1, 9 * j : 9 * j + 9].astype(F32)
            r.lines[at + 2 + j : at + 3 + j, 0:9] = value
        r.lines[at + 6 : at + 7, 0:9] = r.merge_b[b : b + 1].astype(F32)
        r.lines[at + 7 : at + 8, 0:9] = r.reduce_b[b : b + 1].astype(F32)
    r.lines[EMBED_BIAS : EMBED_BIAS + 1, 0:9] = r.embed_b[...].astype(F32)
    r.block[...] = jnp.transpose(r.lines[...])[0:16]
    r.block[0:9, UNPATCH : UNPATCH + 32] = r.unpatch_w[...].astype(F32)
    me, x, z = own_group(), lax.axis_index("dp_0"), lax.axis_index("dp_1")
    r.small[x, z, me] = r.block[...].astype(BF16)
    met(peers)
    sems = (r.ss, r.rs)
    weights = [
        send(r.w_mine.at[at], r.w_got.at[me], sems, k, p) for k, (p, at) in enumerate(group)
    ]
    small = r.small.at[x, z, me]
    first = [send(small, small, sems, 7 + k, p) for k, (p, _) in enumerate(fetch.along_z)]
    r.w_got[me] = r.w_mine[me]

    condition = r.condition[...].astype(F32)
    cond16 = (condition / (1.0 + jnp.exp(-condition))).astype(BF16)
    on_line, on_lane = mod_places(whole_index())
    r.places[...] = jnp.zeros_like(r.places)
    r.places[0:1, 0:54] = r.mod_b[0:1].astype(F32)
    r.places[0:1, 54:108] = r.mod_b[1:2].astype(F32)
    r.places[0:1, 108:126] = r.final_b[...].astype(F32)
    left = jnp.where(on_line, r.places[0:1], 0.0).astype(BF16)
    right = jnp.where(on_lane, 1.0, 0.0).astype(BF16)
    r.placed_bias[...] = dot_nt(left, right)
    r.m_mine[:, :, 126:128] = jnp.zeros((4, 4, 2, 128), F32)
    settle(r, r.mod_w, r.final_w)
    for b in range(3):
        weight = r.mod_w[:, b, :] if b < 2 else r.final_w[...]
        part = dot_nn(cond16, weight)
        for k in range(part.shape[1] // 128):
            line = 54 * b + k
            value = part[:, k * 128 : (k + 1) * 128] + r.placed_bias[line : line + 1]
            r.m_mine[:, :, line, :] = value.reshape(4, 4, 128)
    mods.start()
    for copy in first:
        copy.wait_recv()
    small = r.small.at[x, :, me]
    second = [send(small, small, sems, 10 + k, p) for k, (p, _) in enumerate(fetch.along_x)]
    for copy in weights:
        copy.wait_recv()
    settle(r, r.picks, r.table)
    received = r.w_got[...].reshape(8 * 64, PIECE)
    for k in range(PIECES):
        r.rows[:, k * PIECE : (k + 1) * PIECE] = dot_nn(r.picks[k], received).astype(BF16)
    fetch.start()
    save(r, r.rows)
    for copy in second:
        copy.wait_recv()
    small = r.small.at[:, :, me]
    third = [send(small, small, sems, 13 + k, p) for k, p in enumerate((up, down, far, sib))]
    mods.middle()
    fetch.middle()
    route(r)
    r.m_sum[0:64], r.m_sum[64:128] = mods.end()

    def chunk(ref, index):
        return ref.at[pl.ds(pl.multiple_of(index * 16, 16), 16)]

    m_first = [
        send(chunk(r.m_sum, at), r.m_got.at[me], sems, 20 + k, p) for k, (p, at) in enumerate(group)
    ]
    mine = pl.ds(pl.multiple_of(me * 16, 16), 16)
    r.m_got[me] = r.m_sum[mine, :]
    for copy in m_first:
        copy.wait_recv()
    total = r.m_got[0]
    for k in range(1, 8):
        total = total + r.m_got[k]
    r.m_all[mine, :] = total
    part = chunk(r.m_all, me)
    m_second = [send(part, part, sems, 27 + k, p) for k, (p, _) in enumerate(group)]
    c, y = lax.axis_index("tx"), lax.axis_index("ty")
    fourth = []
    for k, d in enumerate((3, 1, 2)):
        third[k].wait_recv()
        small = r.small.at[:, :, c * 4 + lax.rem(y + d, 4)]
        fourth.append(send(small, small, sems, 17 + k, sib))
    for copy in fourth + third[3:]:
        copy.wait_recv()

    @pl.loop(0, 16)
    def _(k):
        got = r.small[k // 4, lax.rem(k, 4)].reshape(128, 128)
        at = pl.ds(pl.multiple_of(k * PART, 8), PART)
        r.feat32[at, :] = dot_nn(r.pick_small[...], got)[:PART]

    r.feat[...] = r.feat32[...].astype(BF16)
    save(r, r.feat)
    for k in range(9):
        cols = slice(k * 128, (k + 1) * 128)
        r.turned[:, cols] = jnp.transpose(r.feat32[cols, :])
    attn_at, ffn_at = own_targets()
    picks = bias_picks(r.table, ATT_BIAS, attn_at).astype(BF16)
    blocks = r.turned[BLOCKS : BLOCKS + 16].astype(BF16)
    narrow = dot_nn(blocks, picks)
    wide = dot_nn(blocks, bias_picks(r.table, FFN_BIAS, ffn_at).astype(BF16))
    for b, (one, two) in enumerate(((r.bias_one_0, r.bias_two_0), (r.bias_one_1, r.bias_two_1))):
        at, which = 8 * b, r.table[1:2, ATT_BIAS]
        one[...] = jnp.where(which == 0, narrow[at : at + 1], narrow[at + 1 : at + 2])
        value, which = wide[at + 2 : at + 3], r.table[1:2, FFN_BIAS]
        for j in range(1, 4):
            value = jnp.where(which == j, wide[at + 2 + j : at + 3 + j], value)
        two[...] = value
    for copy in m_second:
        copy.wait_recv()

    def mod_line(k):
        return jnp.concatenate([r.m_all[9 * k + i : 9 * k + i + 1] for i in range(9)], axis=1)

    vecs = (r.vec_one_0, r.vec_two_0, r.vec_one_1, r.vec_two_1)
    for k, ref in enumerate(vecs):
        for i in range(3):
            ref[i : i + 1] = mod_line(3 * k + i)
        at = BLOCKS + 8 * (k // 2) + 6 + k % 2
        ref[3:4] = r.turned[at : at + 1]
        ref[4:5] = r.turned[EMBED_BIAS : EMBED_BIAS + 1]
        ref[5:8] = jnp.zeros((3, D), F32)
    r.head_vec[0:1] = mod_line(12)
    r.head_vec[1:2] = mod_line(13)
    fetch.end(r.wqkv, r.wm)
    save(r, r.wqkv, r.wm)
    for copy in weights + first + second + third + fourth + m_first + m_second:
        copy.wait_send()
    mods.leave()
    settle(r)


def picking(pieces, height):
    picks = np.zeros((pieces, SLAB, 8 * height), np.float32)
    for k in range(pieces):
        for row in range(72):
            picks[k, row, row // 9 * height + 9 * k + row % 9] = 1.0
    return picks


def picking_small():
    picks = np.zeros((SLAB, 128), np.float32)
    for row in range(72):
        picks[row, row // 9 * 16 + row % 9] = 1.0
    return picks


def open_up(near, far):
    near = dict(near, pick_small=jnp.asarray(picking_small(), BF16))
    far = dict(
        far,
        unpicks=jnp.asarray(unpicking(PIECES, 64), BF16),
        picks=jnp.asarray(picking(PIECES, 64), BF16),
        table=jnp.asarray(bias_table()),
    )
    vec = ((8, D), F32)
    outs = dict(
        vec_one_0=vec,
        vec_two_0=vec,
        vec_one_1=vec,
        vec_two_1=vec,
        head_vec=((2, D), F32),
        place=((1, 128), jnp.int32),
        mask=((1, 8 * 112), F32),
        bias_one_0=((1, 3 * HW), F32),
        bias_one_1=((1, 3 * HW), F32),
        bias_two_0=((1, FW), F32),
        bias_two_1=((1, FW), F32),
    )
    kept = dict(
        rows=((SLAB, ALL_COLS), BF16),
        wqkv=((D, 3 * HW), BF16),
        wm=((D, HW), BF16),
        feat=((D, 128), BF16),
    )
    scratch = dict(
        pack=pltpu.VMEM((128, ALL_COLS), BF16),
        w_mine=pltpu.VMEM((8, 64, PIECE), BF16),
        w_got=pltpu.VMEM((8, 64, PIECE), BF16),
        lines=pltpu.VMEM((128, 128), F32),
        block=pltpu.VMEM((16, 128), F32),
        small=pltpu.VMEM((4, 4, 8, 16, 128), BF16),
        places=pltpu.VMEM((8, 128), F32),
        placed_bias=pltpu.VMEM((128, 128), F32),
        m_mine=pltpu.VMEM((4, 4, 128, 128), F32),
        m_sum=pltpu.VMEM((128, 128), F32),
        m_got=pltpu.VMEM((8, 16, 128), F32),
        m_all=pltpu.VMEM((128, 128), F32),
        feat32=pltpu.VMEM((D, 128), F32),
        turned=pltpu.VMEM((128, D), F32),
        ss=dma_sems(34)[0],
        rs=dma_sems(34)[1],
        fetch=rows_in_scratch(ATT_COLS),
        mods=sum_scratch([(64, 128), (64, 128)], F32),
    )
    near_outs, far_outs = launch(open_body, 1, near, far, outs, kept, scratch)
    return Results(near_outs, **far_outs)


EARLY = ATT_COLS + 2 * FFN_COLS
EARLY_PIECES = -(-EARLY // PIECE)
LATE_PIECE = 128
LATE_PIECES = ATT_COLS // LATE_PIECE
LATE_ROWS = 48


def packed_rows(picks_ref, parts, piece):
    pieces, _, height = picks_ref.shape
    columns = jnp.concatenate(parts, axis=1)
    spare = pieces * piece - columns.shape[1]
    if spare:
        columns = jnp.concatenate([columns, jnp.zeros((SLAB, spare), BF16)], axis=1)
    total = jnp.zeros((height, piece), F32)
    for k in range(pieces):
        total = total + dot_tn(picks_ref[k], columns[:, k * piece : (k + 1) * piece])
    return total.astype(BF16).reshape(8, height // 8, piece)


def bias_lines(table_ref, cols, shift, biases, count):
    which = table_ref[1:2, cols]
    parts = []
    for bias in biases:
        rest = jnp.concatenate(
            [jnp.where(which == j, bias, 0.0) for j in range(count)]
            + [jnp.zeros((8 - count, bias.shape[1]), F32)],
            axis=0,
        )
        for _ in range(3):
            part = rest.astype(BF16).astype(F32)
            parts.append(part)
            rest = rest - part
    parts = jnp.concatenate(parts, axis=0).astype(BF16)
    found = dot_nt(parts, bias_picks(table_ref, cols, shift).astype(BF16))
    sums = [found[24 * k : 24 * k + 8] for k in range(2)]
    return [
        (sums[k] + found[24 * k + 8 : 24 * k + 16] + found[24 * k + 16 : 24 * k + 24])[:count]
        for k in range(2)
    ]


def finish_body(r):
    group = group_peers()
    sib, up, down, far = ring_peers()
    rows = RowsOut(r.left, r.right, r.rows_sums)
    small = RowsOut(r.small.at[:, :, 0:40], r.small.at[:, :, 40:80], r.small_sums)
    peers = [peer for peer, _ in group] + rows.peers()
    greet(peers)
    me, x, z = own_group(), lax.axis_index("dp_0"), lax.axis_index("dp_1")
    sems = (r.ss, r.rs)
    load(r, r.left, r.right, r.picks, r.late_picks, r.attn_rows, r.ffn_rows_0, r.ffn_rows_1)
    load(r, r.unpatch_rows, r.embed_rows, r.table)
    r.m_mine[...] = jnp.zeros_like(r.m_mine)
    vecs = (r.vecs_one_0, r.vecs_two_0, r.vecs_one_1, r.vecs_two_1, r.head_vecs)
    for k, ref in enumerate(vecs):
        for i in range(3 if k < 4 else 2):
            for j in range(9):
                line = 27 * k + 9 * i + j
                r.m_mine[line // 16, line % 16 : line % 16 + 1] = ref[
                    i : i + 1, j * 128 : (j + 1) * 128
                ]
    met(peers)
    settle(r, r.left, r.right)
    rows.start()
    m_first = [send(r.m_mine.at[at], r.m_got.at[me], sems, k, p) for k, (p, at) in enumerate(group)]
    r.m_got[me] = r.m_mine[me]
    settle(r)
    attn_at, ffn_at = own_targets()
    biases = (r.bias_one_0[...], r.bias_one_1[...])
    narrow = bias_lines(r.table, ATT_BIAS, attn_at, biases, 2)
    biases = (r.bias_two_0[...], r.bias_two_1[...])
    wide = bias_lines(r.table, FFN_BIAS, ffn_at, biases, 4)
    vecs = ((r.vecs_one_0, r.vecs_two_0), (r.vecs_one_1, r.vecs_two_1))
    for k in range(2):
        r.bias_rows[k, 0:2] = narrow[k]
        r.bias_rows[k, 2:6] = wide[k]
        r.bias_rows[k, 6:7] = vecs[k][0][3:4]
        r.bias_rows[k, 7:8] = vecs[k][1][3:4]
    r.turned[...] = jnp.zeros_like(r.turned)
    for k in range(9):
        cols = slice(k * 128, (k + 1) * 128)
        r.lines[...] = jnp.zeros_like(r.lines)
        r.lines[0:32] = r.unpatch_rows[:, cols]
        r.lines[32:48] = r.embed_rows[0:16, cols]
        r.lines[48:56] = r.bias_rows[0, :, cols]
        r.lines[56:64] = r.bias_rows[1, :, cols]
        r.lines[64:72] = r.embed_rows[16:24, cols]
        r.turned[cols, :] = jnp.transpose(r.lines[...])
    for k in range(16):
        r.small[k // 4, k % 4, 0:72] = r.turned[k * PART : (k + 1) * PART, :]
        r.small[k // 4, k % 4, 72:80] = r.unpatch_bias[...]
    small.start()
    r.early[...] = packed_rows(
        r.picks, [r.attn_rows[...], r.ffn_rows_0[...], r.ffn_rows_1[...]], PIECE
    )
    sent = [
        send(r.early.at[at], r.early_out.at[me], sems, 7 + k, p) for k, (p, at) in enumerate(group)
    ]
    r.early_out[me] = r.early[me]
    for copy in m_first:
        copy.wait_recv()
    total = r.m_got[0]
    for k in range(1, 8):
        total = total + r.m_got[k]
    r.m_out[me, x, z] = total.astype(BF16)
    part = r.m_out.at[me, x, z]
    m_second = [send(part, part, sems, 14 + k, p) for k, (p, _) in enumerate(rows.along_z)]
    rows.middle()
    small.middle()
    for copy in m_second:
        copy.wait_recv()
    part = r.m_out.at[me, x]
    m_third = [send(part, part, sems, 17 + k, p) for k, (p, _) in enumerate(rows.along_x)]
    r.s_total[0:40], r.s_total[40:80] = small.end()
    for g in range(8):
        r.s_mine[g, 0:9] = r.s_total[9 * g : 9 * g + 9]
        r.s_mine[g, 9:16] = r.s_total[72:79]
    s_last = [
        send(r.s_mine.at[at], r.s_two.at[me], sems, 20 + k, p) for k, (p, at) in enumerate(group)
    ]
    r.s_two[me] = r.s_mine[me]
    for copy in m_third:
        copy.wait_recv()
    part = r.m_out.at[me]
    m_fourth = [send(part, part, sems, 27 + k, p) for k, p in enumerate((up, down, far, sib))]
    rows.end_rows(r.late_rows)
    r.late[...] = packed_rows(r.late_picks, [r.late_rows[...]], LATE_PIECE)
    later = [
        send(r.late.at[at], r.late_out.at[me], sems, 34 + k, p) for k, (p, at) in enumerate(group)
    ]
    r.late_out[me] = r.late[me]
    c, y = lax.axis_index("tx"), lax.axis_index("ty")
    m_fifth = []
    for k, d in enumerate((3, 1, 2)):
        m_fourth[k].wait_recv()
        part = r.m_out.at[c * 4 + lax.rem(y + d, 4)]
        m_fifth.append(send(part, part, sems, 31 + k, sib))
    for copy in s_last:
        copy.wait_recv()
    total = r.s_two[0]
    for k in range(1, 8):
        total = total + r.s_two[k]
    r.s_out[...] = total
    for copy in sent + m_fourth[3:] + m_fifth + later:
        copy.wait_recv()
    small.leave()
    for copy in m_first + sent + m_second + m_third + s_last + m_fourth + m_fifth + later:
        copy.wait_send()


def finish(near, far):
    far = dict(
        far,
        picks=jnp.asarray(picking(EARLY_PIECES, 64), BF16),
        late_picks=jnp.asarray(picking(LATE_PIECES, LATE_ROWS), BF16),
        table=jnp.asarray(bias_table()),
    )
    outs = dict(
        early_out=((8, 64, PIECE), BF16),
        late_out=((8, LATE_ROWS, LATE_PIECE), BF16),
        m_out=((8, 4, 4, 16, 128), BF16),
        s_out=((16, 128), F32),
    )
    scratch = dict(
        early=pltpu.VMEM((8, 64, PIECE), BF16),
        late=pltpu.VMEM((8, LATE_ROWS, LATE_PIECE), BF16),
        m_mine=pltpu.VMEM((8, 16, 128), F32),
        m_got=pltpu.VMEM((8, 16, 128), F32),
        lines=pltpu.VMEM((128, 128), F32),
        bias_rows=pltpu.VMEM((2, 8, D), F32),
        turned=pltpu.VMEM((D, 128), F32),
        small=pltpu.VMEM((4, 4, 80, 128), F32),
        s_total=pltpu.VMEM((80, 128), F32),
        s_mine=pltpu.VMEM((8, 16, 128), F32),
        s_two=pltpu.VMEM((8, 16, 128), F32),
        late_rows=pltpu.VMEM((SLAB, ATT_COLS), BF16),
        ss=dma_sems(41)[0],
        rs=dma_sems(41)[1],
        rows_sums=rows_out_scratch(ATT_COLS),
        small_sums=sum_scratch([(40, 128), (40, 128)], F32),
    )
    return launch(finish_body, 2, near, far, outs, {}, scratch)[0]


def unpicking(pieces, height):
    picks = np.zeros((pieces, 128, 8 * height), np.float32)
    for k in range(pieces):
        for group in range(8):
            for row in range(9):
                picks[k, group * 16 + row, group * height + 9 * k + row] = 1.0
    return picks


def close_body(r):
    load(r, r.early_in, r.early_picks, r.late_in, r.late_picks, r.m_in, r.mod_w, r.final_w)
    settle(r, r.early_in, r.late_in, r.early_picks, r.late_picks)
    received = r.early_in[...].reshape(8 * 64, PIECE)
    for k in range(EARLY_PIECES):
        r.early[:, k * PIECE : (k + 1) * PIECE] = dot_nn(r.early_picks[k], received)
    received = r.late_in[...].reshape(8 * LATE_ROWS, LATE_PIECE)
    for k in range(LATE_PIECES):
        r.late[:, k * LATE_PIECE : (k + 1) * LATE_PIECE] = dot_nn(r.late_picks[k], received)

    def whole(source, start, width):
        parts = [source[g * 16 : g * 16 + 16, start : start + width] for g in range(8)]
        return jnp.concatenate(parts, axis=1)[:9]

    for b, (source, start) in enumerate(((r.late, 0), (r.early, 0))):
        for j in range(3):
            r.attn[:, j, b, :] = whole(source, start + j * HW, HW)
        r.merge[:, b, :] = whole(source, start + 3 * HW, HW)
    for b, start in enumerate((ATT_COLS, ATT_COLS + FFN_COLS)):
        r.expand[:, b, :] = whole(r.early, start, FW)
        r.reduce[:, b, :] = whole(r.early, start + FW, FW)
    save(r, r.attn, r.merge, r.expand, r.reduce)
    settle(r, r.m_in, r.mod_w, r.final_w)
    for k in range(128):
        value = r.m_in[k // 16, :, :, k % 16, :]
        r.grads[:, k * 128 : (k + 1) * 128] = value.reshape(16, 128)
        r.sums[k : k + 1] = sum_rows(value.reshape(16, 128).astype(F32))
    condition = r.condition[...].astype(F32)
    gate = 1.0 / (1.0 + jnp.exp(-condition))
    cond16 = (condition / (1.0 + jnp.exp(-condition))).astype(BF16)
    terms = jnp.zeros((16, 9), F32)
    for b in range(3):
        grads = r.grads[:, 6 * b * D : min(6 * b + 6, 14) * D]
        weights = r.mod_w[:, b, :] if b < 2 else r.final_w[...]
        product = dot_tn(cond16, grads)
        if b < 2:
            r.mod_grad[:, b, :] = product
        else:
            r.final_grad[...] = product
        terms = terms + dot_nt(grads, weights)
    save(r, r.mod_grad, r.final_grad)
    r.predicted[...] = r.predicted_in[...]
    r.latent[...] = r.latent_in[...]
    r.condition_grad[...] = terms * (gate * (1.0 + condition * (1.0 - gate)))
    on_line, on_lane = mod_places(whole_index())
    found = exact(r.sums[...], jnp.where(on_lane, 1.0, 0.0).astype(F32), (1, 0))
    found = sum_rows(jnp.where(on_line, found, 0.0))
    r.mod_b[0:1] = found[:, 0:54]
    r.mod_b[1:2] = found[:, 54:108]
    r.final_b[...] = found[:, 108:126]
    r.square[...] = jnp.zeros_like(r.square)
    r.square[0:16] = r.s_in[...]
    turned = jnp.transpose(r.square[...])
    r.unpatch_w[...] = r.s_in[0:9, 0:32]
    r.unpatch_b[...] = r.s_in[9:10, 0:32]
    r.embed_w[...] = turned[32:48, 0:9]
    r.embed_b[...] = turned[64:65, 0:9]
    for b in range(2):
        at = BLOCKS + 8 * b
        for j in range(2):
            r.attn_b[b : b + 1, 9 * j : 9 * j + 9] = turned[at + j : at + j + 1, 0:9]
        for j in range(4):
            r.expand_b[b : b + 1, 9 * j : 9 * j + 9] = turned[at + 2 + j : at + 3 + j, 0:9]
        r.merge_b[b : b + 1] = turned[at + 6 : at + 7, 0:9]
        r.reduce_b[b : b + 1] = turned[at + 7 : at + 8, 0:9]
    settle(r)


def close(near, far):
    far = dict(
        far,
        early_picks=jnp.asarray(unpicking(EARLY_PIECES, 64), BF16),
        late_picks=jnp.asarray(unpicking(LATE_PIECES, LATE_ROWS), BF16),
    )
    kept = dict(
        attn=((9, 3, 2, D), F32),
        merge=((9, 2, D), F32),
        expand=((9, 2, FF), F32),
        reduce=((9, 2, FF), F32),
        mod_grad=((9, 2, 6 * D), F32),
        final_grad=((9, 2 * D), F32),
    )
    outs = dict(
        predicted=((16, 8, 32), BF16),
        latent=((16, 4, 32), F32),
        condition_grad=((16, 9), F32),
        mod_b=((2, 54), F32),
        final_b=((1, 18), F32),
        unpatch_w=((9, 32), F32),
        unpatch_b=((1, 32), F32),
        embed_w=((16, 9), F32),
        embed_b=((1, 9), F32),
        attn_b=((2, 18), F32),
        expand_b=((2, 36), F32),
        merge_b=((2, 9), F32),
        reduce_b=((2, 9), F32),
    )
    scratch = dict(
        early=pltpu.VMEM((128, EARLY_PIECES * PIECE), F32),
        late=pltpu.VMEM((128, ATT_COLS), F32),
        grads=pltpu.VMEM((16, WHOLE), BF16),
        sums=pltpu.VMEM((128, 128), F32),
        square=pltpu.VMEM((128, 128), F32),
    )
    near_outs, far_outs = launch(close_body, None, near, far, outs, kept, scratch)
    return Results(near_outs, **far_outs)


def forward_body(r, tokens, start, last):
    a, b = halves(r, tokens, r.x16, r.in_all, r.remote_one)
    fetch = RowsIn(*slab_views(r.rows, start, FFN_COLS), r.fetch_one)
    peers = a.peers() + fetch.peers()
    greet(peers)
    if last:
        load(r, r.first, r.wqkv, r.rows, r.wm)
        settle(r, r.first)
        r.x[...] = exact(choice(r.place, tokens), r.first[...], (1, 0))
    else:
        load(r, r.feat, r.placed, r.wqkv, r.rows, r.wm)
        settle(r, r.feat, r.placed)
        r.token_cols[...] = jnp.zeros_like(r.token_cols)
        to_tokens(r.pixels, r.square, r.token_cols, EMBED)
        r.patches[...] = r.token_cols[...].astype(BF16)
        r.x[...] = dot_nt(r.patches[...], r.feat[...]) + r.vec_one[4:5] + r.placed[...]
    r.x16[...] = modulated(r.x[...], r.vec_one)
    met(peers)
    a.issue()
    a.issue_rest()
    b.issue()
    save(r, r.x)
    if not last:
        save(r, r.patches)

    def prepare():
        settle(r, r.wqkv, r.rows)
        fetch.start()

    def visit(half, d):
        rows = half.pair(d)
        joined = (dot_nn(r.in_all[rows, :], r.wqkv[...]) + r.bias_one[...]).astype(BF16)
        for h in range(2):
            r.q[h, rows, :] = joined[:, head_cols(h)]
            r.k[h, rows, :] = joined[:, head_cols(h, HW)]
            r.v[h, rows, :] = joined[:, head_cols(h, 2 * HW)]

    def attend(half, d):
        rows = half.pair(d)
        parts = []
        for h in range(2):
            scores = dot_nt(r.q[h, rows, :], r.k[h]) * SCALE
            if last:
                scores = scores + r.mask[...]
            highest = jnp.max(scores, axis=-1, keepdims=True)
            shifted = jnp.exp(scores - highest)
            summed = jnp.sum(shifted, axis=-1, keepdims=True)
            probs = (shifted * (1.0 / summed)).astype(BF16)
            r.lse[rows, h : h + 1] = highest + jnp.log(summed)
            parts.append(dot_nn(probs, r.v[h]).astype(BF16))
        attended = jnp.concatenate(parts, axis=1)
        r.att[rows, :] = attended
        half.put(d, dot_nt(attended, r.wm[...]))

    gather_both(a, b, prepare, visit, fetch.middle)
    settle(r, r.wm)
    save(r, r.in_all, r.q, r.k, r.v)
    sum_both(a, b, attend)
    save(r, r.lse, r.att)
    fetch.end(r.we, r.wr)
    save(r, r.we, r.wr)
    follow = halves(r, tokens, r.x16, r.second, r.remote_two)

    def finish_half(half, after):
        branch = half.total() + r.vec_one[3:4]
        middle = r.x[half.own, :] + r.vec_one[2:3] * branch
        r.x16[half.own, :] = modulated(middle, r.vec_two)
        after.issue()
        r.branch[half.own, :] = branch
        r.middle[half.own, :] = middle

    finish_half(a, follow[0])
    follow[0].issue_rest()
    finish_half(b, follow[1])
    save(r, r.branch, r.middle)
    a, b = follow
    fetch = None
    if not last:
        fetch = RowsIn(*slab_views(r.rows, ATT_COLS, ATT_COLS), r.fetch_two)

    def expand(half, d):
        rows = half.pair(d)
        pre = dot_nn(r.second[rows, :], r.we[...]) + r.bias_two[...]
        value, slope = gelu_both(pre)
        hidden = value.astype(BF16)
        r.hid[rows, :] = hidden
        r.slope[rows, :] = slope.astype(BF16)
        half.put(d, dot_nt(hidden, r.wr[...]))

    if fetch:
        gather_and_sum(a, b, fetch.start, expand, fetch.middle)
    else:
        gather_and_sum(a, b, nothing, expand, nothing)
    save(r, r.second, r.hid, r.slope)
    b.relay()
    if fetch:
        fetch.end(r.next_wqkv, r.next_wm)
        save(r, r.next_wqkv, r.next_wm)
    for half in (a, b):
        mlp = half.total() + r.vec_two[3:4]
        r.mlp[half.own, :] = mlp
        r.out[half.own, :] = r.middle[half.own, :] + r.vec_two[2:3] * mlp
    save(r, r.mlp, r.out)
    settle(r)


def ring_scratch(tokens):
    sizes = half_sizes(tokens)
    remote = [half_remote(size) for size in sizes]
    return dict(local=[half_local(size) for size in sizes], remote_one=remote, remote_two=remote)


def kept_shapes(tokens):
    heads = ((2, 8 * tokens, HEAD), BF16)
    wide, tile = ((8 * tokens, D), BF16), ((tokens, D), F32)
    hidden = ((8 * tokens, FW), BF16)
    return dict(
        x=tile,
        in_all=wide,
        q=heads,
        k=heads,
        v=heads,
        lse=((8 * tokens, 2), F32),
        att=((8 * tokens, HW), BF16),
        branch=tile,
        middle=tile,
        second=wide,
        hid=hidden,
        slope=hidden,
        mlp=tile,
        we=((D, FW), BF16),
        wr=((D, FW), BF16),
    )


def block_forward(near, far, tokens, start, last, cid):
    kept = dict(kept_shapes(tokens), out=((tokens, D), F32))
    scratch = dict(
        x16=pltpu.VMEM((tokens, D), BF16),
        **ring_scratch(tokens),
        fetch_one=rows_in_scratch(FFN_COLS),
    )
    if not last:
        kept.update(
            next_wqkv=((D, 3 * HW), BF16), next_wm=((D, HW), BF16), patches=((128, 128), BF16)
        )
        scratch.update(
            square=pltpu.VMEM((128, 128), F32),
            token_cols=pltpu.VMEM((128, 128), F32),
            fetch_two=rows_in_scratch(ATT_COLS),
        )
    body = functools.partial(forward_body, tokens=tokens, start=start, last=last)
    return launch(body, cid, near, far, {}, kept, scratch)[1]


def head(r):
    picks = choice(r.place, r.two.shape[0])
    ended = spread_back(picks, r.two[...], r.first[...])
    normed, inv_std = layer_stats(ended)
    final16 = (normed * (1.0 + r.head_vec[1:2]) + r.head_vec[0:1]).astype(BF16)
    unpatch = r.feat[:, UNPATCH : UNPATCH + 32]
    r.token_cols[...] = jnp.zeros_like(r.token_cols)
    r.token_cols[:, 0:32] = dot_nn(final16, unpatch) + r.unpatch_b[...].astype(F32)
    to_pixels(r.token_cols, r.square, r.predicted, 0)
    to_tokens(r.cotangent_pixels, r.square, r.token_cols, 0)
    r.cotangent[...] = r.token_cols[:, 0:32].astype(BF16)
    r.unpatch_rows[...] = dot_tn(r.cotangent[...], final16)
    r.unpatch_bias[...] = jnp.zeros_like(r.unpatch_bias)
    r.unpatch_bias[0:1, 0:32] = sum_rows(r.cotangent[...].astype(F32))
    grad = dot_nt(r.cotangent[...], unpatch)
    r.head_vecs[0:1] = sum_rows(grad)
    r.head_vecs[1:2] = sum_rows(grad * normed)
    grad = layer_back(grad * (1.0 + r.head_vec[1:2]), normed, inv_std)
    r.grad_ended[...] = grad
    r.g[...] = exact(picks, grad, (1, 0))


def backward_body(r, tokens, last):
    a, b = halves(r, tokens, r.g16, r.g_one, r.remote_one)
    sums = None if last else RowsOut(r.pending_left, r.pending_right, r.sums_one)
    peers = a.peers() + line_only(line_peers())
    greet(peers)
    if last:
        load(r, r.first, r.two, r.feat, r.slope, r.wr, r.we)
    else:
        load(r, r.grad_two, r.grad_ended, r.slope, r.wr, r.we, r.pending_left, r.pending_right)
        load(r, r.feat, r.patches)
    load(r, r.hid, r.second, r.mlp, r.middle)
    load(r, r.q, r.k, r.v, r.lse, r.wm, r.wqkv, r.att, r.x, r.branch)
    if last:
        settle(r, r.first, r.two, r.feat)
        head(r)
    else:
        settle(r, r.grad_two, r.grad_ended)
        picks = choice(r.place, r.grad_two.shape[0])
        r.g[...] = spread_back(picks, r.grad_two[...], r.grad_ended[...])
    r.g16[...] = (r.g[...] * r.vec_two[2:3]).astype(BF16)
    met(peers)
    a.issue()
    a.issue_rest()
    b.issue()
    r.bias_two[...] = jnp.zeros_like(r.bias_two)

    def prepare():
        if sums:
            settle(r, r.pending_left, r.pending_right)
            sums.start()
        settle(r, r.slope, r.wr, r.we)

    def visit(half, d):
        rows = half.pair(d)
        pre_grad = (
            dot_nn(r.g_one[rows, :], r.wr[...]) * r.slope[rows, :].astype(F32)
        ).astype(BF16)
        r.pre_all[rows, :] = pre_grad
        r.bias_two[...] += sum_rows(pre_grad.astype(F32))
        half.put(d, dot_nt(pre_grad, r.we[...]))

    if last:
        save(r, r.grad_ended, r.unpatch_rows)
    gather_and_sum(a, b, prepare, visit, nothing)
    settle(r, r.hid, r.second, r.mlp, r.middle)
    r.vecs_two[2:3] = sum_rows(r.g[...] * r.mlp[...])
    r.vecs_two[3:4] = sum_rows(r.g16[...].astype(F32))
    r.vecs_two[4:8] = jnp.zeros((4, D), F32)
    weight_grads(r.g_one, r.hid, r.whole_two, FW)
    b.relay()
    follow = halves(r, tokens, r.g16, r.g_two, r.remote_two)

    def finish_half(half, after):
        second_grad = half.total()
        normed, inv_std = layer_stats(r.middle[half.own, :])
        grad = r.g[half.own, :] + layer_back(
            second_grad * (1.0 + r.vec_two[1:2]), normed, inv_std
        )
        r.g[half.own, :] = grad
        r.g16[half.own, :] = (grad * r.vec_one[2:3]).astype(BF16)
        after.issue()
        return sum_rows(second_grad), sum_rows(second_grad * normed)

    shift_a, scale_a = finish_half(a, follow[0])
    follow[0].issue_rest()
    if sums:
        sums.middle()
    weight_grads(r.second, r.pre_all, r.whole_one, FW)
    shift_b, scale_b = finish_half(b, follow[1])
    r.vecs_two[0:1] = shift_a + shift_b
    r.vecs_two[1:2] = scale_a + scale_b
    load_into(r, r.in_all, r.second)
    write_slabs((r.whole_one, FW), (r.whole_two, FW), r.ffn_left, r.ffn_right)
    if sums:
        sums.end_rows(r.attn_rows)
        save(r, r.attn_rows)
    a, b = follow
    sums = RowsOut(r.ffn_left, r.ffn_right, r.sums_two)

    def prepare_attention():
        sums.start()
        r.dk[...] = jnp.zeros_like(r.dk)
        r.dv[...] = jnp.zeros_like(r.dv)
        settle(r, r.q, r.k, r.v, r.lse, r.wm)

    def attend(half, d):
        rows = half.pair(0 if d == 3 else 1, 2)
        grad = dot_nn(r.g_two[rows, :], r.wm[...]).astype(BF16)
        queries = []
        for h in range(2):
            part = grad[:, head_cols(h)]
            query = r.q[h, rows, :]
            scores = dot_nt(query, r.k[h]) * SCALE
            if last:
                scores = scores + r.mask[...]
            probs = jnp.exp(scores - r.lse[rows, h : h + 1])
            grad_probs = dot_nt(part, r.v[h])
            weighted = jnp.sum(probs * grad_probs, axis=-1, keepdims=True)
            score_grad = (probs * (grad_probs - weighted)).astype(BF16)
            queries.append((dot_nn(score_grad, r.k[h]) * SCALE).astype(BF16))
            r.dk[h] += dot_tn(score_grad, query)
            r.dv[h] += dot_tn(probs.astype(BF16), part)
        r.joined[rows, 0:HW] = jnp.concatenate(queries, axis=1)

    def back(half, d):
        half.put(d, dot_nt(r.joined[half.pair(d), :], r.wqkv[...]))

    prepare_attention()
    a.forward()
    b.issue_rest()
    a.near_arrive()
    b.forward()
    a.ready(0)
    a.ready(3)
    attend(a, 3)
    a.far_arrive()
    b.near_arrive()
    b.ready(0)
    b.ready(3)
    attend(b, 3)
    a.ready(1)
    a.ready(2)
    b.far_arrive()
    attend(a, 2)
    b.ready(1)
    b.ready(2)
    attend(b, 2)
    settle(r, r.wqkv)
    later = [(r.dk[h] * SCALE).astype(BF16) for h in range(2)]
    later += [r.dv[h].astype(BF16) for h in range(2)]
    r.joined[:, HW : 3 * HW] = jnp.concatenate(later, axis=1)
    sum_both(a, b, back)
    settle(r)
    sums.middle()
    r.bias_one[...] = sum_rows(r.joined[...].astype(F32))
    r.vecs_one[2:3] = sum_rows(r.g[...] * r.branch[...])
    r.vecs_one[3:4] = sum_rows(r.g16[...].astype(F32))
    r.vecs_one[4:8] = jnp.zeros((4, D), F32)
    weight_grads(r.g_two, r.att, r.whole_two, HW)
    weight_grads(r.second, r.joined, r.whole_one, 3 * HW)
    write_slabs((r.whole_one, 3 * HW), (r.whole_two, HW), r.attn_left, r.attn_right)
    save(r, r.attn_left, r.attn_right)
    sums.end_rows(r.ffn_rows)
    save(r, r.ffn_rows)
    shift, scale = 0.0, 0.0
    for half in (a, b):
        input_grad = half.total()
        normed, inv_std = layer_stats(r.x[half.own, :])
        shift = shift + sum_rows(input_grad)
        scale = scale + sum_rows(input_grad * normed)
        scaled = input_grad * (1.0 + r.vec_one[1:2])
        r.g[half.own, :] = r.g[half.own, :] + layer_back(scaled, normed, inv_std)
    r.vecs_one[0:1] = shift
    r.vecs_one[1:2] = scale
    if last:
        r.out[...] = r.g[...]
        save(r, r.out)
    else:
        grad16 = r.g[...].astype(BF16)
        r.embed_rows[0:16] = dot_tn(r.patches[...], grad16)[EMBED : EMBED + 16]
        r.embed_rows[16:17] = sum_rows(grad16.astype(F32))
        r.embed_rows[17:24] = jnp.zeros((7, D), F32)
        save(r, r.embed_rows)
        r.token_cols[...] = dot_nn(grad16, r.feat[...])
        to_pixels(r.token_cols, r.square, r.latent, EMBED)
    settle(r)


def weight_grads(left_ref, right_ref, whole_ref, width):
    @pl.loop(0, D // 384)
    def _(k):
        at = pl.ds(pl.multiple_of(k * 384, 128), 384)
        whole_ref[at, :width] = dot_tn(left_ref[:, at], right_ref[...])


def write_slabs(one, two, left_ref, right_ref):
    cut = left_ref.shape[3]
    cols = cut + right_ref.shape[3]

    @pl.loop(0, 16)
    def _(k):
        at = pl.ds(pl.multiple_of(k * PART, 8), PART)
        parts = [ref[at, :width] for ref, width in (one, two)]
        spare = cols - one[1] - two[1]
        if spare:
            parts.append(jnp.zeros((PART, spare), F32))
        rows = jnp.concatenate(parts, axis=1)
        rows = jnp.concatenate([rows, jnp.zeros((SLAB - PART, cols), F32)], axis=0).astype(BF16)
        x, z = k // 4, lax.rem(k, 4)
        left_ref[x, z] = rows[:, :cut]
        right_ref[x, z] = rows[:, cut:]


def line_only(lines):
    return [peer for peer, _ in lines[0] + lines[1]]


def slab_specs(cols):
    widths = (CUT[cols], cols - CUT[cols])
    return [((4, 4, SLAB, width), BF16) for width in widths]


def block_backward(near, far, tokens, last, cid):
    vecs = ((8, D), F32)
    attn_left, attn_right = slab_specs(ATT_COLS)
    wide, tile = (8 * tokens, D), (tokens, D)
    outs = dict(vecs_one=vecs, vecs_two=vecs)
    outs.update(bias_one=((1, 3 * HW), F32), bias_two=((1, FW), F32))
    kept = dict(attn_left=attn_left, attn_right=attn_right, ffn_rows=((SLAB, FFN_COLS), BF16))
    scratch = dict(
        g=pltpu.VMEM(tile, F32),
        g16=pltpu.VMEM(tile, BF16),
        square=pltpu.VMEM((128, 128), F32),
        token_cols=pltpu.VMEM((128, 128), F32),
        g_one=pltpu.VMEM(wide, BF16),
        g_two=pltpu.VMEM(wide, BF16),
        pre_all=pltpu.VMEM((8 * tokens, FW), BF16),
        joined=pltpu.VMEM((8 * tokens, 3 * HW), BF16),
        dk=pltpu.VMEM((2, 8 * tokens, HEAD), F32),
        dv=pltpu.VMEM((2, 8 * tokens, HEAD), F32),
        whole_one=pltpu.VMEM((D, FW), F32),
        whole_two=pltpu.VMEM((D, FW), F32),
        ffn_left=pltpu.VMEM(*slab_specs(FFN_COLS)[0]),
        ffn_right=pltpu.VMEM(*slab_specs(FFN_COLS)[1]),
        **ring_scratch(tokens),
        sums_two=rows_out_scratch(FFN_COLS),
    )
    if last:
        outs.update(
            predicted=((16, 8, 32), BF16), unpatch_bias=((8, 128), F32), head_vecs=((2, D), F32)
        )
        kept.update(out=(tile, F32), unpatch_rows=((32, D), F32), grad_ended=((128, D), F32))
        scratch.update(cotangent=pltpu.VMEM((128, 32), BF16))
    else:
        outs.update(latent=((16, 4, 32), F32))
        kept.update(attn_rows=((SLAB, ATT_COLS), BF16), embed_rows=((24, D), F32))
        scratch.update(sums_one=rows_out_scratch(ATT_COLS))
    body = functools.partial(backward_body, tokens=tokens, last=last)
    near_outs, far_outs = launch(body, cid, near, far, outs, kept, scratch, vmem=62 << 20)
    return Results(near_outs, **far_outs)


def shards(
    latent,
    condition,
    routed_ids,
    embed_weight,
    embed_bias,
    modulation_weight,
    modulation_bias,
    attention_weight,
    attention_bias,
    merge_weight,
    merge_bias,
    expand_weight,
    expand_bias,
    reduce_weight,
    reduce_bias,
    final_modulation,
    final_offsets,
    unpatch_weight,
    unpatch_bias,
    pred_cotangent,
):
    tile_rows = latent.shape[1] // 2
    tile_cols = latent.shape[2] // 2
    tile_tokens = tile_rows * tile_cols
    capacity = 7 * tile_tokens // 8
    row_index = lax.axis_index("tx") * tile_rows + jnp.arange(tile_rows, dtype=jnp.int32)
    col_index = lax.axis_index("ty") * tile_cols + jnp.arange(tile_cols, dtype=jnp.int32)
    placed = sincos_table(row_index.astype(F32), col_index.astype(F32), D)
    mod_w = modulation_weight.swapaxes(0, 1)
    got = open_up(
        dict(
            condition=condition,
            ids=routed_ids,
            embed_w=embed_weight,
            embed_b=embed_bias[None],
            unpatch_w=unpatch_weight,
            attn_b=attention_bias,
            merge_b=merge_bias,
            expand_b=expand_bias,
            reduce_b=reduce_bias,
            mod_b=modulation_bias,
            final_b=final_offsets[None],
        ),
        dict(
            mod_w=mod_w,
            final_w=final_modulation,
            attn_w=attention_weight.transpose(1, 2, 0, 3),
            merge_w=merge_weight.swapaxes(0, 1),
            expand_w=expand_weight.swapaxes(0, 1),
            reduce_w=reduce_weight.swapaxes(0, 1),
        ),
    )
    vecs_one = dict(vec_one=got.vec_one_0, vec_two=got.vec_two_0)
    vecs_two = dict(vec_one=got.vec_one_1, vec_two=got.vec_two_1, mask=got.mask)
    kept_one = block_forward(
        dict(
            vecs_one,
            bias_one=got.bias_one_0,
            bias_two=got.bias_two_0,
            pixels=latent.transpose(0, 2, 3, 1)[0],
        ),
        dict(feat=got.feat, placed=placed, rows=got.rows, wqkv=got.wqkv, wm=got.wm),
        tile_tokens,
        2 * ATT_COLS,
        False,
        10,
    )
    weights_two = dict(wqkv=kept_one.next_wqkv, wm=kept_one.next_wm)
    kept_two = block_forward(
        dict(vecs_two, bias_one=got.bias_one_1, bias_two=got.bias_two_1, place=got.place),
        dict(weights_two, rows=got.rows, first=kept_one.out),
        capacity,
        2 * ATT_COLS + FFN_COLS,
        True,
        11,
    )

    def saved(kept, tokens):
        return {name: kept[name] for name in kept_shapes(tokens)}

    back_two = block_backward(
        dict(
            vecs_two,
            place=got.place,
            head_vec=got.head_vec,
            unpatch_b=unpatch_bias[None],
            cotangent_pixels=pred_cotangent.transpose(0, 2, 3, 1)[0],
        ),
        dict(
            saved(kept_two, capacity),
            **weights_two,
            feat=got.feat,
            first=kept_one.out,
            two=kept_two.out,
        ),
        capacity,
        True,
        12,
    )
    back_one = block_backward(
        dict(vecs_one, place=got.place),
        dict(
            saved(kept_one, tile_tokens),
            wqkv=got.wqkv,
            wm=got.wm,
            feat=got.feat,
            patches=kept_one.patches,
            pending_left=back_two.attn_left,
            pending_right=back_two.attn_right,
            grad_two=back_two.out,
            grad_ended=back_two.grad_ended,
        ),
        tile_tokens,
        False,
        13,
    )
    ended = finish(
        dict(
            vecs_one_0=back_one.vecs_one,
            vecs_two_0=back_one.vecs_two,
            vecs_one_1=back_two.vecs_one,
            vecs_two_1=back_two.vecs_two,
            head_vecs=back_two.head_vecs,
            bias_one_0=back_one.bias_one,
            bias_two_0=back_one.bias_two,
            bias_one_1=back_two.bias_one,
            bias_two_1=back_two.bias_two,
            unpatch_bias=back_two.unpatch_bias,
        ),
        dict(
            left=back_one.attn_left,
            right=back_one.attn_right,
            attn_rows=back_one.attn_rows,
            ffn_rows_0=back_one.ffn_rows,
            ffn_rows_1=back_two.ffn_rows,
            unpatch_rows=back_two.unpatch_rows,
            embed_rows=back_one.embed_rows,
        ),
    )
    last = close(
        dict(
            s_in=ended.s_out,
            condition=condition,
            predicted_in=back_two.predicted,
            latent_in=back_one.latent,
        ),
        dict(
            early_in=ended.early_out,
            late_in=ended.late_out,
            m_in=ended.m_out,
            mod_w=mod_w,
            final_w=final_modulation,
        ),
    )
    return (
        last.predicted.transpose(2, 0, 1)[None],
        last.latent.transpose(2, 0, 1)[None],
        last.condition_grad,
        last.embed_w,
        last.embed_b[0],
        last.mod_grad.swapaxes(0, 1),
        last.mod_b,
        last.attn.transpose(2, 0, 1, 3),
        last.attn_b,
        last.merge.swapaxes(0, 1),
        last.merge_b,
        last.expand.swapaxes(0, 1),
        last.expand_b,
        last.reduce.swapaxes(0, 1),
        last.reduce_b,
        last.final_grad,
        last.final_b[0],
        last.unpatch_w,
        last.unpatch_b[0],
    )


def solution(mesh):
    torus = Mesh(
        mesh.devices.reshape(4, 4, mesh.shape["tx"], mesh.shape["ty"]), ("dp_0", "dp_1", "tx", "ty")
    )
    return jax.shard_map(
        shards,
        mesh=torus,
        in_specs=(
            P(DP, "tx", "ty", None),
            P(None, DP_TX_TY),
            P(DP, None),
            P(None, DP_TX_TY),
            P(DP_TX_TY),
            P(None, DP_TX_TY, None),
            P(None, DP_TX_TY),
            P(None, DP_TX_TY, None, None),
            P(None, DP_TX_TY),
            P(None, DP_TX_TY, None),
            P(None, DP_TX_TY),
            P(None, DP_TX_TY, None),
            P(None, DP_TX_TY),
            P(None, DP_TX_TY, None),
            P(None, DP_TX_TY),
            P(DP_TX_TY, None),
            P(DP_TX_TY),
            P(DP_TX_TY, None),
            P(),
            P(DP, "tx", "ty", None),
        ),
        out_specs=(
            P(DP, "tx", "ty", None),
            P(DP, "tx", "ty", None),
            P(None, DP_TX_TY),
            P(None, DP_TX_TY),
            P(DP_TX_TY),
            P(None, DP_TX_TY, None),
            P(None, DP_TX_TY),
            P(None, DP_TX_TY, None, None),
            P(None, DP_TX_TY),
            P(None, DP_TX_TY, None),
            P(None, DP_TX_TY),
            P(None, DP_TX_TY, None),
            P(None, DP_TX_TY),
            P(None, DP_TX_TY, None),
            P(None, DP_TX_TY),
            P(DP_TX_TY, None),
            P(DP_TX_TY),
            P(DP_TX_TY, None),
            P(),
        ),
        check_vma=False,
    )
```

```python
import functools

import jax
import jax.numpy as jnp
import numpy as np
from jax import lax
from jax.experimental import pallas as pl
from jax.experimental.pallas import tpu as pltpu
from jax.sharding import Mesh
from jax.sharding import PartitionSpec as P

D = 1152
HEADS = 16
FF = 4608
HW = D // 8
FW = FF // 8
DP = ("dp_0", "dp_1")
DP_TX_TY = ("dp_0", "dp_1", "tx", "ty")
MESH = pl.DeviceIdType.MESH
VMEM = pl.BlockSpec(memory_space=pltpu.VMEM)
FAR = pl.BlockSpec(memory_space=pl.ANY)
F32 = jnp.float32
BF16 = jnp.bfloat16
ATT_COLS = 640
FFN_COLS = 2 * FW
ALL_COLS = 2 * (ATT_COLS + FFN_COLS)
PIECE = 512
PIECES = ALL_COLS // PIECE


def greet(peers):
    barrier = pltpu.get_barrier_semaphore()
    for peer in peers:
        pl.semaphore_signal(barrier, inc=1, device_id=peer, device_id_type=MESH)


def met(peers):
    pl.semaphore_wait(pltpu.get_barrier_semaphore(), len(peers))


def enter(peers):
    greet(peers)
    met(peers)


def send(src, dst, sems, k, peer):
    copy = pltpu.make_async_remote_copy(
        src_ref=src,
        dst_ref=dst,
        send_sem=sems[0].at[k],
        recv_sem=sems[1].at[k],
        device_id=peer,
        device_id_type=MESH,
    )
    copy.start()
    return copy


def group_peers():
    c, y = lax.axis_index("tx"), lax.axis_index("ty")
    found = []
    for dc in range(2):
        for dy in range(4):
            if dc or dy:
                oc, oy = lax.rem(c + dc, 2), lax.rem(y + dy, 4)
                found.append(({"tx": oc, "ty": oy}, oc * 4 + oy))
    return found


def own_group():
    return lax.axis_index("tx") * 4 + lax.axis_index("ty")


def dma_sems(n):
    return [pltpu.SemaphoreType.DMA((n,)), pltpu.SemaphoreType.DMA((n,))]


def ring_peers():
    c, y = lax.axis_index("tx"), lax.axis_index("ty")
    return (
        {"tx": 1 - c},
        {"ty": lax.rem(y + 1, 4)},
        {"ty": lax.rem(y + 3, 4)},
        {"ty": lax.rem(y + 2, 4)},
    )


def layer_stats(value_rows):
    centered = value_rows - jnp.mean(value_rows, axis=-1, keepdims=True)
    inv_std = lax.rsqrt(jnp.mean(centered * centered, axis=-1, keepdims=True) + 1e-06)
    return (centered * inv_std, inv_std)


def layer_back(upstream, normed, inv_std):
    return inv_std * (
        upstream
        - jnp.mean(upstream, axis=-1, keepdims=True)
        - normed * jnp.mean(upstream * normed, axis=-1, keepdims=True)
    )


def sincos_table(row_pos, col_pos, width):
    quarter = width // 4
    freqs = jnp.power(10000.0, -jnp.arange(quarter, dtype=jnp.float32) / quarter)
    row_angle = row_pos[:, None] * freqs[None, :]
    col_angle = col_pos[:, None] * freqs[None, :]
    row_embed = jnp.concatenate([jnp.sin(row_angle), jnp.cos(row_angle)], axis=-1)
    col_embed = jnp.concatenate([jnp.sin(col_angle), jnp.cos(col_angle)], axis=-1)
    row_full = jnp.broadcast_to(
        row_embed[:, None, :], (row_pos.shape[0], col_pos.shape[0], width // 2)
    )
    col_full = jnp.broadcast_to(
        col_embed[None, :, :], (row_pos.shape[0], col_pos.shape[0], width // 2)
    )
    return jnp.concatenate([row_full, col_full], axis=-1).reshape(
        row_pos.shape[0] * col_pos.shape[0], width
    )


SLAB = 80
PART = D // 16
CUT = {ATT_COLS: 384, FFN_COLS: 640}


def line_peers():
    x, z = lax.axis_index("dp_0"), lax.axis_index("dp_1")
    along_x = [({"dp_0": lax.rem(x + d, 4)}, lax.rem(x + d, 4)) for d in (2, 1, 3)]
    along_z = [({"dp_1": lax.rem(z + d, 4)}, lax.rem(z + d, 4)) for d in (2, 1, 3)]
    return along_x, along_z


class RowsIn:
    def __init__(self, left_ref, right_ref, scratch):
        self.left, self.right = left_ref, right_ref
        self.all_left, self.all_right = scratch[:2]
        self.sems = tuple(scratch[2:4])
        self.x, self.z = lax.axis_index("dp_0"), lax.axis_index("dp_1")
        self.along_x, self.along_z = line_peers()

    def peers(self):
        return [peer for peer, _ in self.along_x + self.along_z]

    def start(self):
        x, z = self.x, self.z
        self.first = []
        for k, (peer, _) in enumerate(self.along_z):
            self.first.append(send(self.left, self.all_left.at[x, z], self.sems, k, peer))
        for k, (peer, _) in enumerate(self.along_x):
            self.first.append(send(self.right, self.all_right.at[x, z], self.sems, 3 + k, peer))
        self.all_left[x, z] = self.left[...]
        self.all_right[x, z] = self.right[...]

    def middle(self):
        left, right = self.all_left.at[self.x], self.all_right.at[:, self.z]
        self.second = []
        for copy in self.first[:3]:
            copy.wait_recv()
        for k, (peer, _) in enumerate(self.along_x):
            self.second.append(send(left, left, self.sems, 6 + k, peer))
        for copy in self.first[3:]:
            copy.wait_recv()
        for k, (peer, _) in enumerate(self.along_z):
            self.second.append(send(right, right, self.sems, 9 + k, peer))

    def end(self, one_ref, two_ref):
        for copy in self.second:
            copy.wait_recv()
        width, other = one_ref.shape[1], two_ref.shape[1]
        cut = self.left.shape[1]

        @pl.loop(0, 8)
        def _(pair):
            x, z = pair // 2, 2 * lax.rem(pair, 2)
            both = []
            for k in range(2):
                parts = [self.all_left[x, z + k], self.all_right[x, z + k]]
                both.append(jnp.concatenate(parts, axis=1).astype(F32)[:PART])
            value = jnp.concatenate(both, axis=0).astype(BF16)
            at = pl.ds(pl.multiple_of(pair * 2 * PART, 16), 2 * PART)
            one_ref[at, :] = value[:, :width]
            two_ref[at, :] = value[:, width : width + other]

        for copy in self.first + self.second:
            copy.wait_send()


def rows_in_scratch(cols):
    left = CUT[cols]
    return [
        pltpu.VMEM((4, 4, SLAB, left), BF16),
        pltpu.VMEM((4, 4, SLAB, cols - left), BF16),
    ] + dma_sems(12)


class RowsOut:
    def __init__(self, left_ref, right_ref, scratch):
        self.left, self.right = left_ref, right_ref
        self.got = scratch[0:2]
        self.mine = scratch[2:4]
        self.last = scratch[4:6]
        self.sems = tuple(scratch[6:8])
        self.x, self.z = lax.axis_index("dp_0"), lax.axis_index("dp_1")
        self.along_x, self.along_z = line_peers()

    def peers(self):
        return [peer for peer, _ in self.along_x + self.along_z]

    def start(self):
        self.first = []
        for k, (peer, at) in enumerate(self.along_x):
            part = self.left.at[at]
            self.first.append(send(part, self.got[0].at[k], self.sems, k, peer))
        for k, (peer, at) in enumerate(self.along_z):
            part = self.right.at[:, at]
            self.first.append(send(part, self.got[1].at[k], self.sems, 3 + k, peer))

    def middle(self):
        self.second = []
        for side, peers in ((0, self.along_z), (1, self.along_x)):
            for copy in self.first[3 * side : 3 * side + 3]:
                copy.wait_recv()
            got, mine = self.got[side], self.mine[side]

            @pl.loop(0, 4)
            def _(k):
                own = self.right[k, self.z] if side else self.left[self.x, k]
                across, below, above = (got[source, k].astype(F32) for source in range(3))
                total = (own.astype(F32) + across) + (below + above)
                mine[k] = total.astype(mine.dtype)

            for k, (peer, at) in enumerate(peers):
                part = mine.at[at]
                copy = send(part, self.last[side].at[k], self.sems, 6 + 3 * side + k, peer)
                self.second.append(copy)

    def end(self):
        for copy in self.second:
            copy.wait_recv()
        totals = []
        for side, own in ((0, self.z), (1, self.x)):
            across, below, above = (self.last[side][source].astype(F32) for source in range(3))
            totals.append((self.mine[side][own].astype(F32) + across) + (below + above))
        return totals

    def end_rows(self, out_ref):
        cut = self.left.shape[3]
        left, right = self.end()
        out_ref[:, :cut] = left.astype(BF16)
        out_ref[:, cut:] = right.astype(BF16)
        self.leave()

    def leave(self):
        for copy in self.first + self.second:
            copy.wait_send()


def rows_out_scratch(cols):
    return sum_scratch([(SLAB, CUT[cols]), (SLAB, cols - CUT[cols])], BF16)


def sum_scratch(shapes, dtype):
    return (
        [pltpu.VMEM((3, 4, *shape), dtype) for shape in shapes]
        + [pltpu.VMEM((4, *shape), dtype) for shape in shapes]
        + [pltpu.VMEM((3, *shape), dtype) for shape in shapes]
        + dma_sems(12)
    )


def slab_views(rows_ref, start, cols):
    cut = start + CUT[cols]
    return rows_ref.at[:, start:cut], rows_ref.at[:, cut : start + cols]


def weight_shapes(cols):
    widths = (3 * HW, HW) if cols == ATT_COLS else (FW, FW)
    return tuple(jax.ShapeDtypeStruct((D, w), BF16) for w in widths)


def dot_nn(left, right):
    return lax.dot_general(left, right, (((1,), (0,)), ((), ())), preferred_element_type=F32)


def dot_nt(left, right):
    return lax.dot_general(left, right, (((1,), (1,)), ((), ())), preferred_element_type=F32)


def dot_tn(left, right):
    return lax.dot_general(left, right, (((0,), (0,)), ((), ())), preferred_element_type=F32)


def gelu_both(pre):
    root = 0.7978845608028654
    square = pre * pre
    bent = jnp.tanh(root * pre * (1.0 + 0.044715 * square))
    value = 0.5 * pre * (1.0 + bent)
    slope = 0.5 * (1.0 + bent) + 0.5 * pre * (1.0 - bent * bent) * root * (1.0 + 0.134145 * square)
    return value, slope


def sum_rows(value):
    return jnp.sum(value, axis=0, keepdims=True)


HEAD = D // HEADS
SCALE = HEAD ** (-0.5)


def head_cols(h, start=0):
    return slice(start + h * HEAD, start + (h + 1) * HEAD)


class Refs:
    pass


class Results(dict):
    __getattr__ = dict.__getitem__


def launch(body, cid, near, far, outs, kept, scratch, vmem=60 << 20):
    twins = {name: (value.shape, value.dtype) for name, value in far.items()}
    twins.update(kept)
    groups, tree = jax.tree.flatten(scratch, is_leaf=lambda entry: not isinstance(entry, (dict, list)))

    def kernel(*refs):
        refs = iter(refs)
        r, hbm = Refs(), {}
        for name in near:
            setattr(r, name, next(refs))
        for name in far:
            hbm[name] = next(refs)
        for name in outs:
            setattr(r, name, next(refs))
        for name in kept:
            hbm[name] = next(refs)
        r.moves, r.moving = {}, {}
        for k, name in enumerate(twins):
            ref = next(refs)
            setattr(r, name, ref)
            r.moves[id(ref)] = (hbm[name], k)
        if twins:
            r.move_sems = next(refs)
        for name, entry in jax.tree.unflatten(tree, list(refs)).items():
            setattr(r, name, entry)
        body(r)

    shapes = [jax.ShapeDtypeStruct(*spec) for spec in (*outs.values(), *kept.values())]
    results = pl.pallas_call(
        kernel,
        out_shape=tuple(shapes),
        in_specs=[VMEM] * len(near) + [FAR] * len(far),
        out_specs=(VMEM,) * len(outs) + (FAR,) * len(kept),
        scratch_shapes=[pltpu.VMEM(*spec) for spec in twins.values()]
        + ([pltpu.SemaphoreType.DMA((len(twins),))] if twins else [])
        + groups,
        compiler_params=pltpu.CompilerParams(
            collective_id=cid, has_side_effects=cid is not None, vmem_limit_bytes=vmem
        ),
    )(*near.values(), *far.values())
    return Results(zip(outs, results)), Results(zip(kept, results[len(outs) :]))


def load_into(r, ref, target):
    source, k = r.moves[id(ref)]
    r.moving[id(ref)] = pltpu.make_async_copy(source, target, r.move_sems.at[k])
    r.moving[id(ref)].start()


def load(r, *refs):
    for ref in refs:
        load_into(r, ref, ref)


def save(r, *refs):
    for ref in refs:
        target, k = r.moves[id(ref)]
        r.moving[id(ref)] = pltpu.make_async_copy(ref, target, r.move_sems.at[k])
        r.moving[id(ref)].start()


def settle(r, *refs):
    for key in [id(ref) for ref in refs] or list(r.moving):
        r.moving.pop(key).wait()


def exact(left, right, dims):
    return lax.dot_general(
        left,
        right,
        ((dims[:1], dims[1:]), ((), ())),
        precision=lax.Precision.HIGHEST,
        preferred_element_type=F32,
    )


def choice(place_ref, capacity):
    tokens = place_ref.shape[1]
    slots = lax.broadcasted_iota(jnp.int32, (capacity, tokens), 0)
    return jnp.where(slots == place_ref[...], 1.0, 0.0).astype(F32)


def spread_back(picks, chosen, others):
    used = exact(picks, jnp.ones((picks.shape[0], 128), F32), (0, 0))[:, :1]
    return exact(picks, chosen, (0, 0)) + others * (1.0 - used)


def modulated(x, vec_ref):
    normed, _ = layer_stats(x)
    return (normed * (1.0 + vec_ref[1:2]) + vec_ref[0:1]).astype(BF16)


def full_width(parts, at):
    height = parts[0].shape[0]
    used = at + sum(part.shape[1] for part in parts)
    if at:
        parts = [jnp.zeros((height, at), F32), *parts]
    if used < 128:
        parts = [*parts, jnp.zeros((height, 128 - used), F32)]
    return jnp.concatenate(parts, axis=1)


def to_tokens(pixels_ref, square, tokens_ref, at):
    wide, depth, high = pixels_ref.shape
    square[...] = jnp.zeros_like(square)
    square[: wide * depth, :high] = pixels_ref[...].astype(F32).reshape(wide * depth, high)
    square[...] = jnp.transpose(square[...])
    size = 2 * depth
    lines = [square[pl.ds(line, high // 2, stride=2), :] for line in range(2)]
    for c in range(wide // 2):
        parts = [value[:, c * size : (c + 1) * size] for value in lines]
        tokens_ref[pl.ds(c, high // 2, stride=wide // 2), :] = full_width(parts, at)


def to_pixels(tokens_ref, square, pixels_ref, at):
    wide, depth, high = pixels_ref.shape
    square[...] = jnp.zeros_like(square)
    size = 2 * depth
    columns = [tokens_ref[pl.ds(c, high // 2, stride=wide // 2), :] for c in range(wide // 2)]
    for line in range(2):
        start = at + line * size
        parts = [value[:, start : start + size] for value in columns]
        square[pl.ds(line, high // 2, stride=2), :] = full_width(parts, 0)
    value = jnp.transpose(square[...])[: wide * depth, :high].reshape(wide, depth, high)
    pixels_ref[...] = value.astype(pixels_ref.dtype)


FIRST = 64
PIECE_ROWS = 32
PLACE_OF = {0: 0, 3: 1, 1: 2, 2: 3}


def half_sizes(tokens):
    return FIRST, tokens - FIRST


def half_local(size):
    return [
        pltpu.VMEM((4, size, D), F32),
        pltpu.VMEM((4, size, D), BF16),
        pltpu.VMEM((3, size, D), BF16),
    ]


def half_remote(size):
    return [
        pltpu.VMEM((4, size, D), BF16),
        pltpu.VMEM((2, size, D), BF16),
        pltpu.VMEM((PIECE_ROWS, D), BF16),
        pltpu.VMEM((size - PIECE_ROWS, D), BF16),
    ] + dma_sems(20)


class Half:
    def __init__(self, which, tokens, x_ref, all_ref, local, remote):
        sizes = half_sizes(tokens)
        self.size = sizes[which]
        self.own = slice(which * FIRST, which * FIRST + self.size)
        self.base = which * 8 * FIRST
        self.x, self.all = x_ref, all_ref
        self.kept, self.sib_out, self.out = local
        self.sib_in, self.got, self.far_low, self.far_high = remote[:4]
        self.sems = tuple(remote[4:6])
        self.sib, self.up, self.down, _ = ring_peers()
        self.low, self.high = slice(0, PIECE_ROWS), slice(PIECE_ROWS, self.size)
        self.sent, self.swaps = [], {}

    def peers(self):
        return [self.sib, self.up, self.down]

    def send(self, src, dst, k, peer):
        copy = send(src, dst, self.sems, k, peer)
        self.sent.append(copy)
        return copy

    def pair(self, d, count=1):
        start = self.base + 2 * PLACE_OF[d] * self.size
        return slice(start, start + 2 * count * self.size)

    def slot(self, d, other, rows=None):
        start = self.base + (2 * PLACE_OF[d] + other) * self.size
        rows = slice(0, self.size) if rows is None else rows
        return self.all.at[start + rows.start : start + rows.stop]

    def source(self, rows):
        return self.x.at[self.own.start + rows.start : self.own.start + rows.stop]

    def issue(self):
        low, high = self.low, self.high
        self.a1 = self.send(self.source(low), self.slot(3, 0, low), 0, self.up)
        self.b1 = self.send(self.source(high), self.slot(1, 0, high), 1, self.down)
        whole = slice(0, self.size)
        self.arrive = {0: self.send(self.source(whole), self.slot(0, 1), 4, self.sib)}
        start = self.base
        self.all[start : start + self.size, :] = self.x[self.own, :]

    def issue_rest(self):
        low, high = self.low, self.high
        self.a2 = self.send(self.source(high), self.slot(3, 0, high), 2, self.up)
        self.b2 = self.send(self.source(low), self.slot(1, 0, low), 3, self.down)

    def forward(self):
        low, high = self.low, self.high
        self.a1.wait_recv()
        self.f1 = self.send(self.slot(3, 0, low), self.slot(2, 0, low), 5, self.up)
        self.b1.wait_recv()
        self.f2 = self.send(self.slot(1, 0, high), self.slot(2, 0, high), 6, self.down)

    def near_arrive(self):
        self.a2.wait_recv()
        self.arrive[3] = self.send(self.slot(3, 0), self.slot(3, 1), 7, self.sib)
        self.b2.wait_recv()
        self.arrive[1] = self.send(self.slot(1, 0), self.slot(1, 1), 8, self.sib)

    def far_arrive(self):
        self.f1.wait_recv()
        self.f2.wait_recv()
        self.arrive[2] = self.send(self.slot(2, 0), self.slot(2, 1), 9, self.sib)

    def ready(self, d):
        self.arrive[d].wait_recv()

    def put(self, d, value):
        self.kept[d] = value[: self.size]
        self.sib_out[d] = value[self.size :].astype(BF16)
        self.swaps[d] = self.send(self.sib_out.at[d], self.sib_in.at[d], 10 + d, self.sib)

    def chip_sum(self, d):
        self.swaps[d].wait_recv()
        return self.kept[d] + self.sib_in[d].astype(F32)

    def near(self):
        low, high = self.low, self.high
        total = self.chip_sum(1)
        self.kept[1] = total
        self.out[0, high] = total[high].astype(BF16)
        self.n1 = self.send(self.out.at[0, high], self.got.at[0, high], 14, self.up)
        total = self.chip_sum(3)
        self.kept[3] = total
        self.out[1, low] = total[low].astype(BF16)
        self.n2 = self.send(self.out.at[1, low], self.got.at[1, low], 15, self.down)

    def far(self):
        self.out[2] = self.chip_sum(2).astype(BF16)
        self.low_sent = self.send(self.out.at[2, self.low], self.far_low, 16, self.up)
        self.high_sent = self.send(self.out.at[2, self.high], self.far_high, 17, self.down)

    def relay(self):
        low, high = self.low, self.high
        self.low_sent.wait_recv()
        self.out[0, low] = (self.kept[1, low] + self.far_low[...].astype(F32)).astype(BF16)
        self.r1 = self.send(self.out.at[0, low], self.got.at[0, low], 18, self.up)
        self.high_sent.wait_recv()
        self.out[1, high] = (self.kept[3, high] + self.far_high[...].astype(F32)).astype(BF16)
        self.r2 = self.send(self.out.at[1, high], self.got.at[1, high], 19, self.down)

    def total(self):
        value = self.chip_sum(0)
        for copy in (self.n1, self.n2, self.r1, self.r2):
            copy.wait_recv()
        value = value + self.got[0].astype(F32) + self.got[1].astype(F32)
        for copy in self.sent:
            copy.wait_send()
        return value


def gather_both(a, b, prepare, visit, between):
    prepare()
    a.ready(0)
    visit(a, 0)
    a.forward()
    b.issue_rest()
    b.ready(0)
    visit(b, 0)
    a.near_arrive()
    b.forward()
    between()
    a.ready(3)
    visit(a, 3)
    a.ready(1)
    visit(a, 1)
    a.far_arrive()
    b.near_arrive()
    b.ready(3)
    visit(b, 3)
    a.ready(2)
    visit(a, 2)
    b.ready(1)
    visit(b, 1)
    b.far_arrive()
    b.ready(2)
    visit(b, 2)


def gather_and_sum(a, b, prepare, visit, between):
    prepare()
    a.ready(0)
    visit(a, 0)
    a.forward()
    b.issue_rest()
    b.ready(0)
    visit(b, 0)
    a.near_arrive()
    b.forward()
    between()
    a.ready(3)
    visit(a, 3)
    a.ready(1)
    visit(a, 1)
    a.far_arrive()
    b.near_arrive()
    a.near()
    b.ready(3)
    visit(b, 3)
    a.ready(2)
    visit(a, 2)
    b.ready(1)
    visit(b, 1)
    a.far()
    b.far_arrive()
    b.near()
    b.ready(2)
    visit(b, 2)
    a.relay()
    b.far()


def sum_both(a, b, make):
    make(a, 2)
    make(b, 2)
    a.far()
    make(a, 1)
    b.far()
    make(a, 3)
    make(a, 0)
    a.near()
    make(b, 1)
    a.relay()
    make(b, 3)
    make(b, 0)
    b.near()
    b.relay()


def nothing():
    pass


def halves(r, tokens, x_ref, all_ref, remote):
    return [Half(k, tokens, x_ref, all_ref, r.local[k], remote[k]) for k in range(2)]


UNPATCH, EMBED, BLOCKS, EMBED_BIAS = 0, 32, 48, 64
WHOLE = 16384


def own_targets():
    group = own_group()
    return group * (D // 16), group * (D // 8)


def bias_table():
    table = np.zeros((8, 1024), np.int32)
    for col in range(3 * HW):
        part, e = divmod(col, HW)
        table[0, col] = (e // 18 + (64 if part == 2 else 0)) * 9 + e % 9 if part != 1 else -(1 << 20)
        table[1, col] = e % 18 // 9
    for e in range(FW):
        table[0, 3 * HW + e] = e // 36 * 9 + e % 9
        table[1, 3 * HW + e] = e % 36 // 9
    return table


def bias_picks(table_ref, cols, shift):
    rows = lax.broadcasted_iota(jnp.int32, (D, cols.stop - cols.start), 0)
    return jnp.where(rows == table_ref[0:1, cols] + shift, 1.0, 0.0).astype(F32)


ATT_BIAS = slice(0, 3 * HW)
FFN_BIAS = slice(3 * HW, 3 * HW + FW)


def mod_places(index):
    e = lax.broadcasted_iota(jnp.int32, (1, 128), 1)
    at = jnp.where(e < 108, 6 * D - 54 + index * 54 + e, 12 * D - 108 + index * 18 + e)
    at = jnp.where(e < 54, index * 54 + e, at)
    at = jnp.where(e < 126, at, -1)
    lines = lax.broadcasted_iota(jnp.int32, (128, 128), 0)
    return lines == lax.shift_right_arithmetic(at, 7), lines == jnp.bitwise_and(at, 127)


def whole_index():
    x, z = lax.axis_index("dp_0"), lax.axis_index("dp_1")
    return (x * 4 + z) * 8 + own_group()


def route(r):
    token = lax.broadcasted_iota(jnp.int32, (128, 512), 0)
    row = lax.axis_index("tx") * 16 + token // 8
    col = lax.axis_index("ty") * 8 + lax.rem(token, 8)
    hits = jnp.where(row * 32 + col == r.ids[...], 1.0, 0.0).astype(BF16)
    flags = dot_nt(jnp.ones((8, 512), BF16), hits)
    lines = lax.broadcasted_iota(jnp.int32, (128, 128), 0)
    lanes = lax.broadcasted_iota(jnp.int32, (128, 128), 1)
    before = dot_nn(flags.astype(BF16), jnp.where(lines <= lanes, 1.0, 0.0).astype(BF16))
    r.place[...] = jnp.where(flags > 0, before - 1.0, -1.0)[0:1].astype(jnp.int32)
    row, col = r.ids[...] // 512, lax.rem(r.ids[...], 32) // 8
    chip = lax.rem(col - lax.axis_index("ty") + 4, 4)
    other = jnp.where(row == lax.axis_index("tx"), 0, 1)
    place = jnp.where(chip == 1, 2, jnp.where(chip == 2, 3, jnp.where(chip == 3, 1, 0)))
    tile = place * 2 + other
    slot = lax.broadcasted_iota(jnp.int32, r.mask.shape, 1)
    used = slot < 0
    for k in range(8):
        count = jnp.sum(jnp.where(tile == k, 1.0, 0.0), axis=1, keepdims=True).astype(jnp.int32)
        for which, size in enumerate(half_sizes(r.mask.shape[1] // 8)):
            at = slot - which * 8 * FIRST - k * size
            used = used | ((at >= 0) & (at < size) & (at + which * FIRST < count))
    r.mask[...] = jnp.where(used, 0.0, -1e30)


def open_body(r):
    group = group_peers()
    sib, up, down, far = ring_peers()
    fetch = RowsIn(*slab_views(r.rows, 0, ATT_COLS), r.fetch)
    mods = RowsOut(r.m_mine.at[:, :, 0:64], r.m_mine.at[:, :, 64:128], r.mods)
    peers = [peer for peer, _ in group] + fetch.peers()
    greet(peers)
    load(r, r.attn_w, r.merge_w, r.expand_w, r.reduce_w, r.unpicks)
    load(r, r.mod_w, r.final_w, r.picks, r.table)
    r.pack[...] = jnp.zeros_like(r.pack)
    settle(r, r.attn_w, r.merge_w, r.expand_w, r.reduce_w)
    attn = [[r.attn_w[:, j, b, :] for j in range(3)] for b in range(2)]
    merge = [r.merge_w[:, b, :] for b in range(2)]
    expand = [r.expand_w[:, b, :] for b in range(2)]
    reduce = [r.reduce_w[:, b, :] for b in range(2)]
    spare = jnp.zeros((9, ATT_COLS - 4 * HW), BF16)
    for p in range(8):
        narrow, wide = slice(p * HW, (p + 1) * HW), slice(p * FW, (p + 1) * FW)
        parts = []
        for b in range(2):
            parts += [attn[b][j][:, narrow] for j in range(3)] + [merge[b][:, narrow], spare]
        for b in range(2):
            parts += [expand[b][:, wide], reduce[b][:, wide]]
        r.pack[p * 16 : p * 16 + 9, :] = jnp.concatenate(parts, axis=1)
    settle(r, r.unpicks)
    packed = jnp.zeros((8 * 64, PIECE), F32)
    for k in range(PIECES):
        packed = packed + dot_tn(r.unpicks[k], r.pack[:, k * PIECE : (k + 1) * PIECE])
    r.w_mine[...] = packed.astype(BF16).reshape(8, 64, PIECE)
    r.lines[...] = jnp.zeros_like(r.lines)
    r.lines[EMBED : EMBED + 16, 0:9] = r.embed_w[...].astype(F32)
    for b in range(2):
        at = BLOCKS + 8 * b
        for j in range(2):
            r.lines[at + j : at + j + 1, 0:9] = r.attn_b[b : b + 1, 9 * j : 9 * j + 9].astype(F32)
        for j in range(4):
            value = r.expand_b[b : b + 1, 9 * j : 9 * j + 9].astype(F32)
            r.lines[at + 2 + j : at + 3 + j, 0:9] = value
        r.lines[at + 6 : at + 7, 0:9] = r.merge_b[b : b + 1].astype(F32)
        r.lines[at + 7 : at + 8, 0:9] = r.reduce_b[b : b + 1].astype(F32)
    r.lines[EMBED_BIAS : EMBED_BIAS + 1, 0:9] = r.embed_b[...].astype(F32)
    r.block[...] = jnp.transpose(r.lines[...])[0:16]
    r.block[0:9, UNPATCH : UNPATCH + 32] = r.unpatch_w[...].astype(F32)
    me, x, z = own_group(), lax.axis_index("dp_0"), lax.axis_index("dp_1")
    r.small[x, z, me] = r.block[...].astype(BF16)
    met(peers)
    sems = (r.ss, r.rs)
    weights = [
        send(r.w_mine.at[at], r.w_got.at[me], sems, k, p) for k, (p, at) in enumerate(group)
    ]
    small = r.small.at[x, z, me]
    first = [send(small, small, sems, 7 + k, p) for k, (p, _) in enumerate(fetch.along_z)]
    r.w_got[me] = r.w_mine[me]

    condition = r.condition[...].astype(F32)
    cond16 = (condition / (1.0 + jnp.exp(-condition))).astype(BF16)
    on_line, on_lane = mod_places(whole_index())
    r.places[...] = jnp.zeros_like(r.places)
    r.places[0:1, 0:54] = r.mod_b[0:1].astype(F32)
    r.places[0:1, 54:108] = r.mod_b[1:2].astype(F32)
    r.places[0:1, 108:126] = r.final_b[...].astype(F32)
    left = jnp.where(on_line, r.places[0:1], 0.0).astype(BF16)
    right = jnp.where(on_lane, 1.0, 0.0).astype(BF16)
    r.placed_bias[...] = dot_nt(left, right)
    r.m_mine[:, :, 126:128] = jnp.zeros((4, 4, 2, 128), F32)
    settle(r, r.mod_w, r.final_w)
    for b in range(3):
        weight = r.mod_w[:, b, :] if b < 2 else r.final_w[...]
        part = dot_nn(cond16, weight)
        for k in range(part.shape[1] // 128):
            line = 54 * b + k
            value = part[:, k * 128 : (k + 1) * 128] + r.placed_bias[line : line + 1]
            r.m_mine[:, :, line, :] = value.reshape(4, 4, 128)
    mods.start()
    for copy in first:
        copy.wait_recv()
    small = r.small.at[x, :, me]
    second = [send(small, small, sems, 10 + k, p) for k, (p, _) in enumerate(fetch.along_x)]
    for copy in weights:
        copy.wait_recv()
    settle(r, r.picks, r.table)
    received = r.w_got[...].reshape(8 * 64, PIECE)
    for k in range(PIECES):
        r.rows[:, k * PIECE : (k + 1) * PIECE] = dot_nn(r.picks[k], received).astype(BF16)
    fetch.start()
    save(r, r.rows)
    for copy in second:
        copy.wait_recv()
    small = r.small.at[:, :, me]
    third = [send(small, small, sems, 13 + k, p) for k, p in enumerate((up, down, far, sib))]
    mods.middle()
    fetch.middle()
    route(r)
    r.m_sum[0:64], r.m_sum[64:128] = mods.end()

    def chunk(ref, index):
        return ref.at[pl.ds(pl.multiple_of(index * 16, 16), 16)]

    m_first = [
        send(chunk(r.m_sum, at), r.m_got.at[me], sems, 20 + k, p) for k, (p, at) in enumerate(group)
    ]
    mine = pl.ds(pl.multiple_of(me * 16, 16), 16)
    r.m_got[me] = r.m_sum[mine, :]
    for copy in m_first:
        copy.wait_recv()
    total = r.m_got[0]
    for k in range(1, 8):
        total = total + r.m_got[k]
    r.m_all[mine, :] = total
    part = chunk(r.m_all, me)
    m_second = [send(part, part, sems, 27 + k, p) for k, (p, _) in enumerate(group)]
    c, y = lax.axis_index("tx"), lax.axis_index("ty")
    fourth = []
    for k, d in enumerate((3, 1, 2)):
        third[k].wait_recv()
        small = r.small.at[:, :, c * 4 + lax.rem(y + d, 4)]
        fourth.append(send(small, small, sems, 17 + k, sib))
    for copy in fourth + third[3:]:
        copy.wait_recv()

    @pl.loop(0, 16)
    def _(k):
        got = r.small[k // 4, lax.rem(k, 4)].reshape(128, 128)
        at = pl.ds(pl.multiple_of(k * PART, 8), PART)
        r.feat32[at, :] = dot_nn(r.pick_small[...], got)[:PART]

    r.feat[...] = r.feat32[...].astype(BF16)
    save(r, r.feat)
    for k in range(9):
        cols = slice(k * 128, (k + 1) * 128)
        r.turned[:, cols] = jnp.transpose(r.feat32[cols, :])
    attn_at, ffn_at = own_targets()
    picks = bias_picks(r.table, ATT_BIAS, attn_at).astype(BF16)
    blocks = r.turned[BLOCKS : BLOCKS + 16].astype(BF16)
    narrow = dot_nn(blocks, picks)
    wide = dot_nn(blocks, bias_picks(r.table, FFN_BIAS, ffn_at).astype(BF16))
    for b, (one, two) in enumerate(((r.bias_one_0, r.bias_two_0), (r.bias_one_1, r.bias_two_1))):
        at, which = 8 * b, r.table[1:2, ATT_BIAS]
        one[...] = jnp.where(which == 0, narrow[at : at + 1], narrow[at + 1 : at + 2])
        value, which = wide[at + 2 : at + 3], r.table[1:2, FFN_BIAS]
        for j in range(1, 4):
            value = jnp.where(which == j, wide[at + 2 + j : at + 3 + j], value)
        two[...] = value
    for copy in m_second:
        copy.wait_recv()

    def mod_line(k):
        return jnp.concatenate([r.m_all[9 * k + i : 9 * k + i + 1] for i in range(9)], axis=1)

    vecs = (r.vec_one_0, r.vec_two_0, r.vec_one_1, r.vec_two_1)
    for k, ref in enumerate(vecs):
        for i in range(3):
            ref[i : i + 1] = mod_line(3 * k + i)
        at = BLOCKS + 8 * (k // 2) + 6 + k % 2
        ref[3:4] = r.turned[at : at + 1]
        ref[4:5] = r.turned[EMBED_BIAS : EMBED_BIAS + 1]
        ref[5:8] = jnp.zeros((3, D), F32)
    r.head_vec[0:1] = mod_line(12)
    r.head_vec[1:2] = mod_line(13)
    fetch.end(r.wqkv, r.wm)
    save(r, r.wqkv, r.wm)
    for copy in weights + first + second + third + fourth + m_first + m_second:
        copy.wait_send()
    mods.leave()
    settle(r)


def picking(pieces, height):
    picks = np.zeros((pieces, SLAB, 8 * height), np.float32)
    for k in range(pieces):
        for row in range(72):
            picks[k, row, row // 9 * height + 9 * k + row % 9] = 1.0
    return picks


def picking_small():
    picks = np.zeros((SLAB, 128), np.float32)
    for row in range(72):
        picks[row, row // 9 * 16 + row % 9] = 1.0
    return picks


def open_up(near, far):
    near = dict(near, pick_small=jnp.asarray(picking_small(), BF16))
    far = dict(
        far,
        unpicks=jnp.asarray(unpicking(PIECES, 64), BF16),
        picks=jnp.asarray(picking(PIECES, 64), BF16),
        table=jnp.asarray(bias_table()),
    )
    vec = ((8, D), F32)
    outs = dict(
        vec_one_0=vec,
        vec_two_0=vec,
        vec_one_1=vec,
        vec_two_1=vec,
        head_vec=((2, D), F32),
        place=((1, 128), jnp.int32),
        mask=((1, 8 * 112), F32),
        bias_one_0=((1, 3 * HW), F32),
        bias_one_1=((1, 3 * HW), F32),
        bias_two_0=((1, FW), F32),
        bias_two_1=((1, FW), F32),
    )
    kept = dict(
        rows=((SLAB, ALL_COLS), BF16),
        wqkv=((D, 3 * HW), BF16),
        wm=((D, HW), BF16),
        feat=((D, 128), BF16),
    )
    scratch = dict(
        pack=pltpu.VMEM((128, ALL_COLS), BF16),
        w_mine=pltpu.VMEM((8, 64, PIECE), BF16),
        w_got=pltpu.VMEM((8, 64, PIECE), BF16),
        lines=pltpu.VMEM((128, 128), F32),
        block=pltpu.VMEM((16, 128), F32),
        small=pltpu.VMEM((4, 4, 8, 16, 128), BF16),
        places=pltpu.VMEM((8, 128), F32),
        placed_bias=pltpu.VMEM((128, 128), F32),
        m_mine=pltpu.VMEM((4, 4, 128, 128), F32),
        m_sum=pltpu.VMEM((128, 128), F32),
        m_got=pltpu.VMEM((8, 16, 128), F32),
        m_all=pltpu.VMEM((128, 128), F32),
        feat32=pltpu.VMEM((D, 128), F32),
        turned=pltpu.VMEM((128, D), F32),
        ss=dma_sems(34)[0],
        rs=dma_sems(34)[1],
        fetch=rows_in_scratch(ATT_COLS),
        mods=sum_scratch([(64, 128), (64, 128)], F32),
    )
    near_outs, far_outs = launch(open_body, 1, near, far, outs, kept, scratch)
    return Results(near_outs, **far_outs)


EARLY = ATT_COLS + 2 * FFN_COLS
EARLY_PIECES = -(-EARLY // PIECE)
LATE_PIECE = 128
LATE_PIECES = ATT_COLS // LATE_PIECE
LATE_ROWS = 48


def packed_rows(picks_ref, parts, piece):
    pieces, _, height = picks_ref.shape
    columns = jnp.concatenate(parts, axis=1)
    spare = pieces * piece - columns.shape[1]
    if spare:
        columns = jnp.concatenate([columns, jnp.zeros((SLAB, spare), BF16)], axis=1)
    total = jnp.zeros((height, piece), F32)
    for k in range(pieces):
        total = total + dot_tn(picks_ref[k], columns[:, k * piece : (k + 1) * piece])
    return total.astype(BF16).reshape(8, height // 8, piece)


def bias_lines(table_ref, cols, shift, biases, count):
    which = table_ref[1:2, cols]
    parts = []
    for bias in biases:
        rest = jnp.concatenate(
            [jnp.where(which == j, bias, 0.0) for j in range(count)]
            + [jnp.zeros((8 - count, bias.shape[1]), F32)],
            axis=0,
        )
        for _ in range(3):
            part = rest.astype(BF16).astype(F32)
            parts.append(part)
            rest = rest - part
    parts = jnp.concatenate(parts, axis=0).astype(BF16)
    found = dot_nt(parts, bias_picks(table_ref, cols, shift).astype(BF16))
    sums = [found[24 * k : 24 * k + 8] for k in range(2)]
    return [
        (sums[k] + found[24 * k + 8 : 24 * k + 16] + found[24 * k + 16 : 24 * k + 24])[:count]
        for k in range(2)
    ]


def finish_body(r):
    group = group_peers()
    sib, up, down, far = ring_peers()
    rows = RowsOut(r.left, r.right, r.rows_sums)
    small = RowsOut(r.small.at[:, :, 0:40], r.small.at[:, :, 40:80], r.small_sums)
    peers = [peer for peer, _ in group] + rows.peers()
    greet(peers)
    me, x, z = own_group(), lax.axis_index("dp_0"), lax.axis_index("dp_1")
    sems = (r.ss, r.rs)
    load(r, r.left, r.right, r.picks, r.late_picks, r.attn_rows, r.ffn_rows_0, r.ffn_rows_1)
    load(r, r.unpatch_rows, r.embed_rows, r.table)
    r.m_mine[...] = jnp.zeros_like(r.m_mine)
    vecs = (r.vecs_one_0, r.vecs_two_0, r.vecs_one_1, r.vecs_two_1, r.head_vecs)
    for k, ref in enumerate(vecs):
        for i in range(3 if k < 4 else 2):
            for j in range(9):
                line = 27 * k + 9 * i + j
                r.m_mine[line // 16, line % 16 : line % 16 + 1] = ref[
                    i : i + 1, j * 128 : (j + 1) * 128
                ]
    met(peers)
    settle(r, r.left, r.right)
    rows.start()
    m_first = [send(r.m_mine.at[at], r.m_got.at[me], sems, k, p) for k, (p, at) in enumerate(group)]
    r.m_got[me] = r.m_mine[me]
    settle(r)
    attn_at, ffn_at = own_targets()
    biases = (r.bias_one_0[...], r.bias_one_1[...])
    narrow = bias_lines(r.table, ATT_BIAS, attn_at, biases, 2)
    biases = (r.bias_two_0[...], r.bias_two_1[...])
    wide = bias_lines(r.table, FFN_BIAS, ffn_at, biases, 4)
    vecs = ((r.vecs_one_0, r.vecs_two_0), (r.vecs_one_1, r.vecs_two_1))
    for k in range(2):
        r.bias_rows[k, 0:2] = narrow[k]
        r.bias_rows[k, 2:6] = wide[k]
        r.bias_rows[k, 6:7] = vecs[k][0][3:4]
        r.bias_rows[k, 7:8] = vecs[k][1][3:4]
    r.turned[...] = jnp.zeros_like(r.turned)
    for k in range(9):
        cols = slice(k * 128, (k + 1) * 128)
        r.lines[...] = jnp.zeros_like(r.lines)
        r.lines[0:32] = r.unpatch_rows[:, cols]
        r.lines[32:48] = r.embed_rows[0:16, cols]
        r.lines[48:56] = r.bias_rows[0, :, cols]
        r.lines[56:64] = r.bias_rows[1, :, cols]
        r.lines[64:72] = r.embed_rows[16:24, cols]
        r.turned[cols, :] = jnp.transpose(r.lines[...])
    for k in range(16):
        r.small[k // 4, k % 4, 0:72] = r.turned[k * PART : (k + 1) * PART, :]
        r.small[k // 4, k % 4, 72:80] = r.unpatch_bias[...]
    small.start()
    r.early[...] = packed_rows(
        r.picks, [r.attn_rows[...], r.ffn_rows_0[...], r.ffn_rows_1[...]], PIECE
    )
    sent = [
        send(r.early.at[at], r.early_out.at[me], sems, 7 + k, p) for k, (p, at) in enumerate(group)
    ]
    r.early_out[me] = r.early[me]
    for copy in m_first:
        copy.wait_recv()
    total = r.m_got[0]
    for k in range(1, 8):
        total = total + r.m_got[k]
    r.m_out[me, x, z] = total.astype(BF16)
    part = r.m_out.at[me, x, z]
    m_second = [send(part, part, sems, 14 + k, p) for k, (p, _) in enumerate(rows.along_z)]
    rows.middle()
    small.middle()
    for copy in m_second:
        copy.wait_recv()
    part = r.m_out.at[me, x]
    m_third = [send(part, part, sems, 17 + k, p) for k, (p, _) in enumerate(rows.along_x)]
    r.s_total[0:40], r.s_total[40:80] = small.end()
    for g in range(8):
        r.s_mine[g, 0:9] = r.s_total[9 * g : 9 * g + 9]
        r.s_mine[g, 9:16] = r.s_total[72:79]
    s_last = [
        send(r.s_mine.at[at], r.s_two.at[me], sems, 20 + k, p) for k, (p, at) in enumerate(group)
    ]
    r.s_two[me] = r.s_mine[me]
    for copy in m_third:
        copy.wait_recv()
    part = r.m_out.at[me]
    m_fourth = [send(part, part, sems, 27 + k, p) for k, p in enumerate((up, down, far, sib))]
    rows.end_rows(r.late_rows)
    r.late[...] = packed_rows(r.late_picks, [r.late_rows[...]], LATE_PIECE)
    later = [
        send(r.late.at[at], r.late_out.at[me], sems, 34 + k, p) for k, (p, at) in enumerate(group)
    ]
    r.late_out[me] = r.late[me]
    c, y = lax.axis_index("tx"), lax.axis_index("ty")
    m_fifth = []
    for k, d in enumerate((3, 1, 2)):
        m_fourth[k].wait_recv()
        part = r.m_out.at[c * 4 + lax.rem(y + d, 4)]
        m_fifth.append(send(part, part, sems, 31 + k, sib))
    for copy in s_last:
        copy.wait_recv()
    total = r.s_two[0]
    for k in range(1, 8):
        total = total + r.s_two[k]
    r.s_out[...] = total
    for copy in sent + m_fourth[3:] + m_fifth + later:
        copy.wait_recv()
    small.leave()
    for copy in m_first + sent + m_second + m_third + s_last + m_fourth + m_fifth + later:
        copy.wait_send()


def finish(near, far):
    far = dict(
        far,
        picks=jnp.asarray(picking(EARLY_PIECES, 64), BF16),
        late_picks=jnp.asarray(picking(LATE_PIECES, LATE_ROWS), BF16),
        table=jnp.asarray(bias_table()),
    )
    outs = dict(
        early_out=((8, 64, PIECE), BF16),
        late_out=((8, LATE_ROWS, LATE_PIECE), BF16),
        m_out=((8, 4, 4, 16, 128), BF16),
        s_out=((16, 128), F32),
    )
    scratch = dict(
        early=pltpu.VMEM((8, 64, PIECE), BF16),
        late=pltpu.VMEM((8, LATE_ROWS, LATE_PIECE), BF16),
        m_mine=pltpu.VMEM((8, 16, 128), F32),
        m_got=pltpu.VMEM((8, 16, 128), F32),
        lines=pltpu.VMEM((128, 128), F32),
        bias_rows=pltpu.VMEM((2, 8, D), F32),
        turned=pltpu.VMEM((D, 128), F32),
        small=pltpu.VMEM((4, 4, 80, 128), F32),
        s_total=pltpu.VMEM((80, 128), F32),
        s_mine=pltpu.VMEM((8, 16, 128), F32),
        s_two=pltpu.VMEM((8, 16, 128), F32),
        late_rows=pltpu.VMEM((SLAB, ATT_COLS), BF16),
        ss=dma_sems(41)[0],
        rs=dma_sems(41)[1],
        rows_sums=rows_out_scratch(ATT_COLS),
        small_sums=sum_scratch([(40, 128), (40, 128)], F32),
    )
    return launch(finish_body, 2, near, far, outs, {}, scratch)[0]


def unpicking(pieces, height):
    picks = np.zeros((pieces, 128, 8 * height), np.float32)
    for k in range(pieces):
        for group in range(8):
            for row in range(9):
                picks[k, group * 16 + row, group * height + 9 * k + row] = 1.0
    return picks


def close_body(r):
    load(r, r.early_in, r.early_picks, r.late_in, r.late_picks, r.m_in, r.mod_w, r.final_w)
    settle(r, r.early_in, r.late_in, r.early_picks, r.late_picks)
    received = r.early_in[...].reshape(8 * 64, PIECE)
    for k in range(EARLY_PIECES):
        r.early[:, k * PIECE : (k + 1) * PIECE] = dot_nn(r.early_picks[k], received)
    received = r.late_in[...].reshape(8 * LATE_ROWS, LATE_PIECE)
    for k in range(LATE_PIECES):
        r.late[:, k * LATE_PIECE : (k + 1) * LATE_PIECE] = dot_nn(r.late_picks[k], received)

    def whole(source, start, width):
        parts = [source[g * 16 : g * 16 + 16, start : start + width] for g in range(8)]
        return jnp.concatenate(parts, axis=1)[:9]

    for b, (source, start) in enumerate(((r.late, 0), (r.early, 0))):
        for j in range(3):
            r.attn[:, j, b, :] = whole(source, start + j * HW, HW)
        r.merge[:, b, :] = whole(source, start + 3 * HW, HW)
    for b, start in enumerate((ATT_COLS, ATT_COLS + FFN_COLS)):
        r.expand[:, b, :] = whole(r.early, start, FW)
        r.reduce[:, b, :] = whole(r.early, start + FW, FW)
    save(r, r.attn, r.merge, r.expand, r.reduce)
    settle(r, r.m_in, r.mod_w, r.final_w)
    for k in range(128):
        value = r.m_in[k // 16, :, :, k % 16, :]
        r.grads[:, k * 128 : (k + 1) * 128] = value.reshape(16, 128)
        r.sums[k : k + 1] = sum_rows(value.reshape(16, 128).astype(F32))
    condition = r.condition[...].astype(F32)
    gate = 1.0 / (1.0 + jnp.exp(-condition))
    cond16 = (condition / (1.0 + jnp.exp(-condition))).astype(BF16)
    terms = jnp.zeros((16, 9), F32)
    for b in range(3):
        grads = r.grads[:, 6 * b * D : min(6 * b + 6, 14) * D]
        weights = r.mod_w[:, b, :] if b < 2 else r.final_w[...]
        product = dot_tn(cond16, grads)
        if b < 2:
            r.mod_grad[:, b, :] = product
        else:
            r.final_grad[...] = product
        terms = terms + dot_nt(grads, weights)
    save(r, r.mod_grad, r.final_grad)
    r.predicted[...] = r.predicted_in[...]
    r.latent[...] = r.latent_in[...]
    r.condition_grad[...] = terms * (gate * (1.0 + condition * (1.0 - gate)))
    on_line, on_lane = mod_places(whole_index())
    found = exact(r.sums[...], jnp.where(on_lane, 1.0, 0.0).astype(F32), (1, 0))
    found = sum_rows(jnp.where(on_line, found, 0.0))
    r.mod_b[0:1] = found[:, 0:54]
    r.mod_b[1:2] = found[:, 54:108]
    r.final_b[...] = found[:, 108:126]
    r.square[...] = jnp.zeros_like(r.square)
    r.square[0:16] = r.s_in[...]
    turned = jnp.transpose(r.square[...])
    r.unpatch_w[...] = r.s_in[0:9, 0:32]
    r.unpatch_b[...] = r.s_in[9:10, 0:32]
    r.embed_w[...] = turned[32:48, 0:9]
    r.embed_b[...] = turned[64:65, 0:9]
    for b in range(2):
        at = BLOCKS + 8 * b
        for j in range(2):
            r.attn_b[b : b + 1, 9 * j : 9 * j + 9] = turned[at + j : at + j + 1, 0:9]
        for j in range(4):
            r.expand_b[b : b + 1, 9 * j : 9 * j + 9] = turned[at + 2 + j : at + 3 + j, 0:9]
        r.merge_b[b : b + 1] = turned[at + 6 : at + 7, 0:9]
        r.reduce_b[b : b + 1] = turned[at + 7 : at + 8, 0:9]
    settle(r)


def close(near, far):
    far = dict(
        far,
        early_picks=jnp.asarray(unpicking(EARLY_PIECES, 64), BF16),
        late_picks=jnp.asarray(unpicking(LATE_PIECES, LATE_ROWS), BF16),
    )
    kept = dict(
        attn=((9, 3, 2, D), F32),
        merge=((9, 2, D), F32),
        expand=((9, 2, FF), F32),
        reduce=((9, 2, FF), F32),
        mod_grad=((9, 2, 6 * D), F32),
        final_grad=((9, 2 * D), F32),
    )
    outs = dict(
        predicted=((16, 8, 32), BF16),
        latent=((16, 4, 32), F32),
        condition_grad=((16, 9), F32),
        mod_b=((2, 54), F32),
        final_b=((1, 18), F32),
        unpatch_w=((9, 32), F32),
        unpatch_b=((1, 32), F32),
        embed_w=((16, 9), F32),
        embed_b=((1, 9), F32),
        attn_b=((2, 18), F32),
        expand_b=((2, 36), F32),
        merge_b=((2, 9), F32),
        reduce_b=((2, 9), F32),
    )
    scratch = dict(
        early=pltpu.VMEM((128, EARLY_PIECES * PIECE), F32),
        late=pltpu.VMEM((128, ATT_COLS), F32),
        grads=pltpu.VMEM((16, WHOLE), BF16),
        sums=pltpu.VMEM((128, 128), F32),
        square=pltpu.VMEM((128, 128), F32),
    )
    near_outs, far_outs = launch(close_body, None, near, far, outs, kept, scratch)
    return Results(near_outs, **far_outs)


def forward_body(r, tokens, start, last):
    a, b = halves(r, tokens, r.x16, r.in_all, r.remote_one)
    fetch = RowsIn(*slab_views(r.rows, start, FFN_COLS), r.fetch_one)
    peers = a.peers() + fetch.peers()
    greet(peers)
    if last:
        load(r, r.first, r.wqkv, r.rows, r.wm)
        settle(r, r.first)
        r.x[...] = exact(choice(r.place, tokens), r.first[...], (1, 0))
    else:
        load(r, r.feat, r.placed, r.wqkv, r.rows, r.wm)
        settle(r, r.feat, r.placed)
        r.token_cols[...] = jnp.zeros_like(r.token_cols)
        to_tokens(r.pixels, r.square, r.token_cols, EMBED)
        r.patches[...] = r.token_cols[...].astype(BF16)
        r.x[...] = dot_nt(r.patches[...], r.feat[...]) + r.vec_one[4:5] + r.placed[...]
    r.x16[...] = modulated(r.x[...], r.vec_one)
    met(peers)
    a.issue()
    a.issue_rest()
    b.issue()
    save(r, r.x)
    if not last:
        save(r, r.patches)

    def prepare():
        settle(r, r.wqkv, r.rows)
        fetch.start()

    def visit(half, d):
        rows = half.pair(d)
        joined = (dot_nn(r.in_all[rows, :], r.wqkv[...]) + r.bias_one[...]).astype(BF16)
        for h in range(2):
            r.q[h, rows, :] = joined[:, head_cols(h)]
            r.k[h, rows, :] = joined[:, head_cols(h, HW)]
            r.v[h, rows, :] = joined[:, head_cols(h, 2 * HW)]

    def attend(half, d):
        rows = half.pair(d)
        parts = []
        for h in range(2):
            scores = dot_nt(r.q[h, rows, :], r.k[h]) * SCALE
            if last:
                scores = scores + r.mask[...]
            highest = jnp.max(scores, axis=-1, keepdims=True)
            shifted = jnp.exp(scores - highest)
            summed = jnp.sum(shifted, axis=-1, keepdims=True)
            probs = (shifted * (1.0 / summed)).astype(BF16)
            r.lse[rows, h : h + 1] = highest + jnp.log(summed)
            parts.append(dot_nn(probs, r.v[h]).astype(BF16))
        attended = jnp.concatenate(parts, axis=1)
        r.att[rows, :] = attended
        half.put(d, dot_nt(attended, r.wm[...]))

    gather_both(a, b, prepare, visit, fetch.middle)
    settle(r, r.wm)
    save(r, r.in_all, r.q, r.k, r.v)
    sum_both(a, b, attend)
    save(r, r.lse, r.att)
    fetch.end(r.we, r.wr)
    save(r, r.we, r.wr)
    follow = halves(r, tokens, r.x16, r.second, r.remote_two)

    def finish_half(half, after):
        branch = half.total() + r.vec_one[3:4]
        middle = r.x[half.own, :] + r.vec_one[2:3] * branch
        r.x16[half.own, :] = modulated(middle, r.vec_two)
        after.issue()
        r.branch[half.own, :] = branch
        r.middle[half.own, :] = middle

    finish_half(a, follow[0])
    follow[0].issue_rest()
    finish_half(b, follow[1])
    save(r, r.branch, r.middle)
    a, b = follow
    fetch = None
    if not last:
        fetch = RowsIn(*slab_views(r.rows, ATT_COLS, ATT_COLS), r.fetch_two)

    def expand(half, d):
        rows = half.pair(d)
        pre = dot_nn(r.second[rows, :], r.we[...]) + r.bias_two[...]
        value, slope = gelu_both(pre)
        hidden = value.astype(BF16)
        r.hid[rows, :] = hidden
        r.slope[rows, :] = slope.astype(BF16)
        half.put(d, dot_nt(hidden, r.wr[...]))

    if fetch:
        gather_and_sum(a, b, fetch.start, expand, fetch.middle)
    else:
        gather_and_sum(a, b, nothing, expand, nothing)
    save(r, r.second, r.hid, r.slope)
    b.relay()
    if fetch:
        fetch.end(r.next_wqkv, r.next_wm)
        save(r, r.next_wqkv, r.next_wm)
    for half in (a, b):
        mlp = half.total() + r.vec_two[3:4]
        r.mlp[half.own, :] = mlp
        r.out[half.own, :] = r.middle[half.own, :] + r.vec_two[2:3] * mlp
    save(r, r.mlp, r.out)
    settle(r)


def ring_scratch(tokens):
    sizes = half_sizes(tokens)
    remote = [half_remote(size) for size in sizes]
    return dict(local=[half_local(size) for size in sizes], remote_one=remote, remote_two=remote)


def kept_shapes(tokens):
    heads = ((2, 8 * tokens, HEAD), BF16)
    wide, tile = ((8 * tokens, D), BF16), ((tokens, D), F32)
    hidden = ((8 * tokens, FW), BF16)
    return dict(
        x=tile,
        in_all=wide,
        q=heads,
        k=heads,
        v=heads,
        lse=((8 * tokens, 2), F32),
        att=((8 * tokens, HW), BF16),
        branch=tile,
        middle=tile,
        second=wide,
        hid=hidden,
        slope=hidden,
        mlp=tile,
        we=((D, FW), BF16),
        wr=((D, FW), BF16),
    )


def block_forward(near, far, tokens, start, last, cid):
    kept = dict(kept_shapes(tokens), out=((tokens, D), F32))
    scratch = dict(
        x16=pltpu.VMEM((tokens, D), BF16),
        **ring_scratch(tokens),
        fetch_one=rows_in_scratch(FFN_COLS),
    )
    if not last:
        kept.update(
            next_wqkv=((D, 3 * HW), BF16), next_wm=((D, HW), BF16), patches=((128, 128), BF16)
        )
        scratch.update(
            square=pltpu.VMEM((128, 128), F32),
            token_cols=pltpu.VMEM((128, 128), F32),
            fetch_two=rows_in_scratch(ATT_COLS),
        )
    body = functools.partial(forward_body, tokens=tokens, start=start, last=last)
    return launch(body, cid, near, far, {}, kept, scratch)[1]


def head(r):
    picks = choice(r.place, r.two.shape[0])
    ended = spread_back(picks, r.two[...], r.first[...])
    normed, inv_std = layer_stats(ended)
    final16 = (normed * (1.0 + r.head_vec[1:2]) + r.head_vec[0:1]).astype(BF16)
    unpatch = r.feat[:, UNPATCH : UNPATCH + 32]
    r.token_cols[...] = jnp.zeros_like(r.token_cols)
    r.token_cols[:, 0:32] = dot_nn(final16, unpatch) + r.unpatch_b[...].astype(F32)
    to_pixels(r.token_cols, r.square, r.predicted, 0)
    to_tokens(r.cotangent_pixels, r.square, r.token_cols, 0)
    r.cotangent[...] = r.token_cols[:, 0:32].astype(BF16)
    r.unpatch_rows[...] = dot_tn(r.cotangent[...], final16)
    r.unpatch_bias[...] = jnp.zeros_like(r.unpatch_bias)
    r.unpatch_bias[0:1, 0:32] = sum_rows(r.cotangent[...].astype(F32))
    grad = dot_nt(r.cotangent[...], unpatch)
    r.head_vecs[0:1] = sum_rows(grad)
    r.head_vecs[1:2] = sum_rows(grad * normed)
    grad = layer_back(grad * (1.0 + r.head_vec[1:2]), normed, inv_std)
    r.grad_ended[...] = grad
    r.g[...] = exact(picks, grad, (1, 0))


def backward_body(r, tokens, last):
    a, b = halves(r, tokens, r.g16, r.g_one, r.remote_one)
    sums = None if last else RowsOut(r.pending_left, r.pending_right, r.sums_one)
    peers = a.peers() + line_only(line_peers())
    greet(peers)
    if last:
        load(r, r.first, r.two, r.feat, r.slope, r.wr, r.we)
    else:
        load(r, r.grad_two, r.grad_ended, r.slope, r.wr, r.we, r.pending_left, r.pending_right)
        load(r, r.feat, r.patches)
    load(r, r.hid, r.second, r.mlp, r.middle)
    load(r, r.q, r.k, r.v, r.lse, r.wm, r.wqkv, r.att, r.x, r.branch)
    if last:
        settle(r, r.first, r.two, r.feat)
        head(r)
    else:
        settle(r, r.grad_two, r.grad_ended)
        picks = choice(r.place, r.grad_two.shape[0])
        r.g[...] = spread_back(picks, r.grad_two[...], r.grad_ended[...])
    r.g16[...] = (r.g[...] * r.vec_two[2:3]).astype(BF16)
    met(peers)
    a.issue()
    a.issue_rest()
    b.issue()
    r.bias_two[...] = jnp.zeros_like(r.bias_two)

    def prepare():
        if sums:
            settle(r, r.pending_left, r.pending_right)
            sums.start()
        settle(r, r.slope, r.wr, r.we)

    def visit(half, d):
        rows = half.pair(d)
        pre_grad = (
            dot_nn(r.g_one[rows, :], r.wr[...]) * r.slope[rows, :].astype(F32)
        ).astype(BF16)
        r.pre_all[rows, :] = pre_grad
        r.bias_two[...] += sum_rows(pre_grad.astype(F32))
        half.put(d, dot_nt(pre_grad, r.we[...]))

    if last:
        save(r, r.grad_ended, r.unpatch_rows)
    gather_and_sum(a, b, prepare, visit, nothing)
    settle(r, r.hid, r.second, r.mlp, r.middle)
    r.vecs_two[2:3] = sum_rows(r.g[...] * r.mlp[...])
    r.vecs_two[3:4] = sum_rows(r.g16[...].astype(F32))
    r.vecs_two[4:8] = jnp.zeros((4, D), F32)
    weight_grads(r.g_one, r.hid, r.whole_two, FW)
    b.relay()
    follow = halves(r, tokens, r.g16, r.g_two, r.remote_two)

    def finish_half(half, after):
        second_grad = half.total()
        normed, inv_std = layer_stats(r.middle[half.own, :])
        grad = r.g[half.own, :] + layer_back(
            second_grad * (1.0 + r.vec_two[1:2]), normed, inv_std
        )
        r.g[half.own, :] = grad
        r.g16[half.own, :] = (grad * r.vec_one[2:3]).astype(BF16)
        after.issue()
        return sum_rows(second_grad), sum_rows(second_grad * normed)

    shift_a, scale_a = finish_half(a, follow[0])
    follow[0].issue_rest()
    if sums:
        sums.middle()
    weight_grads(r.second, r.pre_all, r.whole_one, FW)
    shift_b, scale_b = finish_half(b, follow[1])
    r.vecs_two[0:1] = shift_a + shift_b
    r.vecs_two[1:2] = scale_a + scale_b
    load_into(r, r.in_all, r.second)
    write_slabs((r.whole_one, FW), (r.whole_two, FW), r.ffn_left, r.ffn_right)
    if sums:
        sums.end_rows(r.attn_rows)
        save(r, r.attn_rows)
    a, b = follow
    sums = RowsOut(r.ffn_left, r.ffn_right, r.sums_two)

    def prepare_attention():
        sums.start()
        r.dk[...] = jnp.zeros_like(r.dk)
        r.dv[...] = jnp.zeros_like(r.dv)
        settle(r, r.q, r.k, r.v, r.lse, r.wm)

    def attend(half, d):
        rows = half.pair(0 if d == 3 else 1, 2)
        grad = dot_nn(r.g_two[rows, :], r.wm[...]).astype(BF16)
        queries = []
        for h in range(2):
            part = grad[:, head_cols(h)]
            query = r.q[h, rows, :]
            scores = dot_nt(query, r.k[h]) * SCALE
            if last:
                scores = scores + r.mask[...]
            probs = jnp.exp(scores - r.lse[rows, h : h + 1])
            grad_probs = dot_nt(part, r.v[h])
            weighted = jnp.sum(probs * grad_probs, axis=-1, keepdims=True)
            score_grad = (probs * (grad_probs - weighted)).astype(BF16)
            queries.append((dot_nn(score_grad, r.k[h]) * SCALE).astype(BF16))
            r.dk[h] += dot_tn(score_grad, query)
            r.dv[h] += dot_tn(probs.astype(BF16), part)
        r.joined[rows, 0:HW] = jnp.concatenate(queries, axis=1)

    def back(half, low, high):
        value = dot_nt(r.joined[half.pair(low, 2), :], r.wqkv[...])
        half.put(high, value[2 * half.size :])
        half.put(low, value[: 2 * half.size])

    prepare_attention()
    a.forward()
    b.issue_rest()
    a.near_arrive()
    b.forward()
    a.ready(0)
    a.ready(3)
    attend(a, 3)
    a.far_arrive()
    b.near_arrive()
    b.ready(0)
    b.ready(3)
    attend(b, 3)
    a.ready(1)
    a.ready(2)
    b.far_arrive()
    attend(a, 2)
    b.ready(1)
    b.ready(2)
    attend(b, 2)
    settle(r, r.wqkv)
    later = [(r.dk[h] * SCALE).astype(BF16) for h in range(2)]
    later += [r.dv[h].astype(BF16) for h in range(2)]
    r.joined[:, HW : 3 * HW] = jnp.concatenate(later, axis=1)
    back(a, 1, 2)
    back(b, 1, 2)
    a.far()
    back(a, 0, 3)
    b.far()
    a.near()
    back(b, 0, 3)
    a.relay()
    b.near()
    b.relay()
    settle(r)
    sums.middle()
    r.bias_one[...] = sum_rows(r.joined[...].astype(F32))
    r.vecs_one[2:3] = sum_rows(r.g[...] * r.branch[...])
    r.vecs_one[3:4] = sum_rows(r.g16[...].astype(F32))
    r.vecs_one[4:8] = jnp.zeros((4, D), F32)
    weight_grads(r.g_two, r.att, r.whole_two, HW)
    weight_grads(r.second, r.joined, r.whole_one, 3 * HW)
    write_slabs((r.whole_one, 3 * HW), (r.whole_two, HW), r.attn_left, r.attn_right)
    save(r, r.attn_left, r.attn_right)
    sums.end_rows(r.ffn_rows)
    save(r, r.ffn_rows)
    shift, scale = 0.0, 0.0
    for half in (a, b):
        input_grad = half.total()
        normed, inv_std = layer_stats(r.x[half.own, :])
        shift = shift + sum_rows(input_grad)
        scale = scale + sum_rows(input_grad * normed)
        scaled = input_grad * (1.0 + r.vec_one[1:2])
        r.g[half.own, :] = r.g[half.own, :] + layer_back(scaled, normed, inv_std)
    r.vecs_one[0:1] = shift
    r.vecs_one[1:2] = scale
    if last:
        r.out[...] = r.g[...]
        save(r, r.out)
    else:
        grad16 = r.g[...].astype(BF16)
        r.embed_rows[0:16] = dot_tn(r.patches[...], grad16)[EMBED : EMBED + 16]
        r.embed_rows[16:17] = sum_rows(grad16.astype(F32))
        r.embed_rows[17:24] = jnp.zeros((7, D), F32)
        save(r, r.embed_rows)
        r.token_cols[...] = dot_nn(grad16, r.feat[...])
        to_pixels(r.token_cols, r.square, r.latent, EMBED)
    settle(r)


def weight_grads(left_ref, right_ref, whole_ref, width):
    @pl.loop(0, D // 384)
    def _(k):
        at = pl.ds(pl.multiple_of(k * 384, 128), 384)
        whole_ref[at, :width] = dot_tn(left_ref[:, at], right_ref[...])


def write_slabs(one, two, left_ref, right_ref):
    cut = left_ref.shape[3]
    cols = cut + right_ref.shape[3]

    @pl.loop(0, 16)
    def _(k):
        at = pl.ds(pl.multiple_of(k * PART, 8), PART)
        parts = [ref[at, :width] for ref, width in (one, two)]
        spare = cols - one[1] - two[1]
        if spare:
            parts.append(jnp.zeros((PART, spare), F32))
        rows = jnp.concatenate(parts, axis=1)
        rows = jnp.concatenate([rows, jnp.zeros((SLAB - PART, cols), F32)], axis=0).astype(BF16)
        x, z = k // 4, lax.rem(k, 4)
        left_ref[x, z] = rows[:, :cut]
        right_ref[x, z] = rows[:, cut:]


def line_only(lines):
    return [peer for peer, _ in lines[0] + lines[1]]


def slab_specs(cols):
    widths = (CUT[cols], cols - CUT[cols])
    return [((4, 4, SLAB, width), BF16) for width in widths]


def block_backward(near, far, tokens, last, cid):
    vecs = ((8, D), F32)
    attn_left, attn_right = slab_specs(ATT_COLS)
    wide, tile = (8 * tokens, D), (tokens, D)
    outs = dict(vecs_one=vecs, vecs_two=vecs)
    outs.update(bias_one=((1, 3 * HW), F32), bias_two=((1, FW), F32))
    kept = dict(attn_left=attn_left, attn_right=attn_right, ffn_rows=((SLAB, FFN_COLS), BF16))
    scratch = dict(
        g=pltpu.VMEM(tile, F32),
        g16=pltpu.VMEM(tile, BF16),
        square=pltpu.VMEM((128, 128), F32),
        token_cols=pltpu.VMEM((128, 128), F32),
        g_one=pltpu.VMEM(wide, BF16),
        g_two=pltpu.VMEM(wide, BF16),
        pre_all=pltpu.VMEM((8 * tokens, FW), BF16),
        joined=pltpu.VMEM((8 * tokens, 3 * HW), BF16),
        dk=pltpu.VMEM((2, 8 * tokens, HEAD), F32),
        dv=pltpu.VMEM((2, 8 * tokens, HEAD), F32),
        whole_one=pltpu.VMEM((D, FW), F32),
        whole_two=pltpu.VMEM((D, FW), F32),
        ffn_left=pltpu.VMEM(*slab_specs(FFN_COLS)[0]),
        ffn_right=pltpu.VMEM(*slab_specs(FFN_COLS)[1]),
        **ring_scratch(tokens),
        sums_two=rows_out_scratch(FFN_COLS),
    )
    if last:
        outs.update(
            predicted=((16, 8, 32), BF16), unpatch_bias=((8, 128), F32), head_vecs=((2, D), F32)
        )
        kept.update(out=(tile, F32), unpatch_rows=((32, D), F32), grad_ended=((128, D), F32))
        scratch.update(cotangent=pltpu.VMEM((128, 32), BF16))
    else:
        outs.update(latent=((16, 4, 32), F32))
        kept.update(attn_rows=((SLAB, ATT_COLS), BF16), embed_rows=((24, D), F32))
        scratch.update(sums_one=rows_out_scratch(ATT_COLS))
    body = functools.partial(backward_body, tokens=tokens, last=last)
    near_outs, far_outs = launch(body, cid, near, far, outs, kept, scratch, vmem=62 << 20)
    return Results(near_outs, **far_outs)


def shards(
    latent,
    condition,
    routed_ids,
    embed_weight,
    embed_bias,
    modulation_weight,
    modulation_bias,
    attention_weight,
    attention_bias,
    merge_weight,
    merge_bias,
    expand_weight,
    expand_bias,
    reduce_weight,
    reduce_bias,
    final_modulation,
    final_offsets,
    unpatch_weight,
    unpatch_bias,
    pred_cotangent,
):
    tile_rows = latent.shape[1] // 2
    tile_cols = latent.shape[2] // 2
    tile_tokens = tile_rows * tile_cols
    capacity = 7 * tile_tokens // 8
    row_index = lax.axis_index("tx") * tile_rows + jnp.arange(tile_rows, dtype=jnp.int32)
    col_index = lax.axis_index("ty") * tile_cols + jnp.arange(tile_cols, dtype=jnp.int32)
    placed = sincos_table(row_index.astype(F32), col_index.astype(F32), D)
    mod_w = modulation_weight.swapaxes(0, 1)
    got = open_up(
        dict(
            condition=condition,
            ids=routed_ids,
            embed_w=embed_weight,
            embed_b=embed_bias[None],
            unpatch_w=unpatch_weight,
            attn_b=attention_bias,
            merge_b=merge_bias,
            expand_b=expand_bias,
            reduce_b=reduce_bias,
            mod_b=modulation_bias,
            final_b=final_offsets[None],
        ),
        dict(
            mod_w=mod_w,
            final_w=final_modulation,
            attn_w=attention_weight.transpose(1, 2, 0, 3),
            merge_w=merge_weight.swapaxes(0, 1),
            expand_w=expand_weight.swapaxes(0, 1),
            reduce_w=reduce_weight.swapaxes(0, 1),
        ),
    )
    vecs_one = dict(vec_one=got.vec_one_0, vec_two=got.vec_two_0)
    vecs_two = dict(vec_one=got.vec_one_1, vec_two=got.vec_two_1, mask=got.mask)
    kept_one = block_forward(
        dict(
            vecs_one,
            bias_one=got.bias_one_0,
            bias_two=got.bias_two_0,
            pixels=latent.transpose(0, 2, 3, 1)[0],
        ),
        dict(feat=got.feat, placed=placed, rows=got.rows, wqkv=got.wqkv, wm=got.wm),
        tile_tokens,
        2 * ATT_COLS,
        False,
        10,
    )
    weights_two = dict(wqkv=kept_one.next_wqkv, wm=kept_one.next_wm)
    kept_two = block_forward(
        dict(vecs_two, bias_one=got.bias_one_1, bias_two=got.bias_two_1, place=got.place),
        dict(weights_two, rows=got.rows, first=kept_one.out),
        capacity,
        2 * ATT_COLS + FFN_COLS,
        True,
        11,
    )

    def saved(kept, tokens):
        return {name: kept[name] for name in kept_shapes(tokens)}

    back_two = block_backward(
        dict(
            vecs_two,
            place=got.place,
            head_vec=got.head_vec,
            unpatch_b=unpatch_bias[None],
            cotangent_pixels=pred_cotangent.transpose(0, 2, 3, 1)[0],
        ),
        dict(
            saved(kept_two, capacity),
            **weights_two,
            feat=got.feat,
            first=kept_one.out,
            two=kept_two.out,
        ),
        capacity,
        True,
        12,
    )
    back_one = block_backward(
        dict(vecs_one, place=got.place),
        dict(
            saved(kept_one, tile_tokens),
            wqkv=got.wqkv,
            wm=got.wm,
            feat=got.feat,
            patches=kept_one.patches,
            pending_left=back_two.attn_left,
            pending_right=back_two.attn_right,
            grad_two=back_two.out,
            grad_ended=back_two.grad_ended,
        ),
        tile_tokens,
        False,
        13,
    )
    ended = finish(
        dict(
            vecs_one_0=back_one.vecs_one,
            vecs_two_0=back_one.vecs_two,
            vecs_one_1=back_two.vecs_one,
            vecs_two_1=back_two.vecs_two,
            head_vecs=back_two.head_vecs,
            bias_one_0=back_one.bias_one,
            bias_two_0=back_one.bias_two,
            bias_one_1=back_two.bias_one,
            bias_two_1=back_two.bias_two,
            unpatch_bias=back_two.unpatch_bias,
        ),
        dict(
            left=back_one.attn_left,
            right=back_one.attn_right,
            attn_rows=back_one.attn_rows,
            ffn_rows_0=back_one.ffn_rows,
            ffn_rows_1=back_two.ffn_rows,
            unpatch_rows=back_two.unpatch_rows,
            embed_rows=back_one.embed_rows,
        ),
    )
    last = close(
        dict(
            s_in=ended.s_out,
            condition=condition,
            predicted_in=back_two.predicted,
            latent_in=back_one.latent,
        ),
        dict(
            early_in=ended.early_out,
            late_in=ended.late_out,
            m_in=ended.m_out,
            mod_w=mod_w,
            final_w=final_modulation,
        ),
    )
    return (
        last.predicted.transpose(2, 0, 1)[None],
        last.latent.transpose(2, 0, 1)[None],
        last.condition_grad,
        last.embed_w,
        last.embed_b[0],
        last.mod_grad.swapaxes(0, 1),
        last.mod_b,
        last.attn.transpose(2, 0, 1, 3),
        last.attn_b,
        last.merge.swapaxes(0, 1),
        last.merge_b,
        last.expand.swapaxes(0, 1),
        last.expand_b,
        last.reduce.swapaxes(0, 1),
        last.reduce_b,
        last.final_grad,
        last.final_b[0],
        last.unpatch_w,
        last.unpatch_b[0],
    )


def solution(mesh):
    torus = Mesh(
        mesh.devices.reshape(4, 4, mesh.shape["tx"], mesh.shape["ty"]), ("dp_0", "dp_1", "tx", "ty")
    )
    return jax.shard_map(
        shards,
        mesh=torus,
        in_specs=(
            P(DP, "tx", "ty", None),
            P(None, DP_TX_TY),
            P(DP, None),
            P(None, DP_TX_TY),
            P(DP_TX_TY),
            P(None, DP_TX_TY, None),
            P(None, DP_TX_TY),
            P(None, DP_TX_TY, None, None),
            P(None, DP_TX_TY),
            P(None, DP_TX_TY, None),
            P(None, DP_TX_TY),
            P(None, DP_TX_TY, None),
            P(None, DP_TX_TY),
            P(None, DP_TX_TY, None),
            P(None, DP_TX_TY),
            P(DP_TX_TY, None),
            P(DP_TX_TY),
            P(DP_TX_TY, None),
            P(),
            P(DP, "tx", "ty", None),
        ),
        out_specs=(
            P(DP, "tx", "ty", None),
            P(DP, "tx", "ty", None),
            P(None, DP_TX_TY),
            P(None, DP_TX_TY),
            P(DP_TX_TY),
            P(None, DP_TX_TY, None),
            P(None, DP_TX_TY),
            P(None, DP_TX_TY, None, None),
            P(None, DP_TX_TY),
            P(None, DP_TX_TY, None),
            P(None, DP_TX_TY),
            P(None, DP_TX_TY, None),
            P(None, DP_TX_TY),
            P(None, DP_TX_TY, None),
            P(None, DP_TX_TY),
            P(DP_TX_TY, None),
            P(DP_TX_TY),
            P(DP_TX_TY, None),
            P(),
        ),
        check_vma=False,
    )
```
